32 devices in a mesh: rows: 16 (over z, y, x), cols: 2 (over core).
Axes of the slice: x: 2, y: 2, z: 4, core: 2. Of those that a mesh axis runs over, the one named last changes fastest.
Arguments:
- canvas: bfloat16 [128, 256, 256], P('rows', 'cols'), may hold values from -16 to 16
- conv_weight: bfloat16 [3, 3, 256, 512], replicated, may hold values from -0.125 to 0.125
- conv_bias: bfloat16 [512], replicated, may hold values from -3 to 3
- target_gram: float32 [512, 512], P(('rows', 'cols')), may hold values from -6 to 6
Outputs:
- gram: float32 [512, 512], P(('rows', 'cols'))
- grad_canvas: bfloat16 [128, 256, 256], P('rows', 'cols')
The draws below stay inside these ranges and needn't reach their ends.
All inputs are finite; a program needn't handle non-finite values.
Results may differ from the reference program's by a relative error of at most 0.009.
Values may be sent and summed in bfloat16 or wider, within the bound.
No kernel may reach another device: no remote copies, remote signals or barrier semaphores. Data moves between devices by JAX's collectives and lax.ppermute only.
A program may use at most 64 MiB of HBM per device.

```python
import math
import jax
import jax.numpy as jnp
from jax import lax

CI = 256
CO = 512
TR = 8
TC = 128
H = 128
W = 256
NPIX = 32768
N_ROWS = 16


def draw_canvas(key, part):
    key_base = jax.random.fold_in(key, 11)
    key_rough = jax.random.fold_in(key, 12)
    key_chan = jax.random.fold_in(key, 13)
    key_heavy = jax.random.fold_in(key, 15)
    row_place = jnp.arange(H, dtype=jnp.float32) / H
    rough = jax.random.uniform(key_rough, (H, 1, 1), jnp.float32, -0.6, 0.6)
    row_scale = jnp.exp(0.55 * (2.0 * row_place[:, None, None] - 1.0) + rough)
    chan_scale = jnp.exp(jax.random.uniform(key_chan, (1, 1, CI), jnp.float32, -0.5, 0.5))
    band_count = H // TR
    strip_count = W // TC
    heavy_strip = jax.random.randint(key_heavy, (band_count,), 0, strip_count)
    band_of_row = jnp.arange(H, dtype=jnp.int32) // TR
    strip_of_col = jnp.arange(W, dtype=jnp.int32) // TC
    chosen = heavy_strip[band_of_row]
    heavy = (band_of_row[:, None] % 4 == 0) & (strip_of_col[None, :] == chosen[:, None])
    heavy_scale = jnp.where(heavy, 4.0, 1.0).astype(jnp.float32)[:, :, None]
    base = jax.random.normal(key_base, (H, W, CI), jnp.float32)
    return jnp.clip(base * row_scale * chan_scale * heavy_scale, -16.0, 16.0).astype(jnp.bfloat16)


def level_of(rng, dims, split, low, largest):
    def one(position, blocks):
        draws = jax.random.uniform(jax.random.fold_in(jax.random.fold_in(rng, 6), position), (blocks,), jnp.float32, low / len(split), largest / len(split))
        return jnp.repeat(jnp.exp(draws), dims[position] // blocks).reshape((-1,) + (1,) * (len(dims) - position - 1))

    gain = one(*split[0])
    for cut in split[1:]:
        gain = gain * one(*cut)
    return gain


def scatter_about(key, dims, deviation, most, split=(), kind=jnp.bfloat16):
    entries = jax.random.normal(key, dims, jnp.float32) * deviation
    if len(split) > 0:
        entries = level_of(key, dims, split, -0.22, 0.18) * entries
    return jnp.clip(entries, min=-most, max=most).astype(kind)


def setup_inputs(seed: int = 0) -> dict:
    seeds = jax.random.split(jax.random.key(seed), 5)
    return {
        "canvas": draw_canvas(jax.random.fold_in(seeds[4], 71), 0),
        "conv_weight": scatter_about(seeds[1], (3, 3, CI, CO), (9 * CI) ** -0.5, 0.125),
        "conv_bias": scatter_about(seeds[2], (CO,), 0.5, 3.0),
        "target_gram": scatter_about(seeds[3], (CO, CO), 1.0, 6.0, ((0, 32),), jnp.float32),
    }


gelu_scale = math.sqrt(2.0 / math.pi)

def gelu_grad(value):
    tangent = jnp.tanh(gelu_scale * (value + 0.044715 * value * value * value))
    return 0.5 * (1.0 + tangent) + 0.5 * value * (1.0 - tangent * tangent) * gelu_scale * (1.0 + 3.0 * 0.044715 * value * value)

def patches(padded, tile_rows, tile_cols):
    pieces = [padded[row_off:row_off + tile_rows, col_off:col_off + tile_cols, :] for row_off in range(3) for col_off in range(3)]
    return jnp.concatenate(pieces, axis=2).reshape(tile_rows * tile_cols, -1)

def reference(canvas, conv_weight, conv_bias, target_gram):
    padded = jnp.pad(canvas, ((1, 1), (1, 1), (0, 0)))
    kernel = conv_weight.reshape(9 * CI, CO)
    flipped = conv_weight[::-1, ::-1].transpose(0, 1, 3, 2).reshape(9 * CO, CI)
    bands = jnp.arange(N_ROWS, dtype=jnp.int32)

    def preact_band(band_index):
        begin = (band_index * TR).astype(jnp.int32)
        window = lax.dynamic_slice_in_dim(padded, begin, TR + 2, 0)
        return jnp.dot(patches(window, TR, W), kernel, preferred_element_type=jnp.float32) + conv_bias.astype(jnp.float32)

    def feature_band(band_index):
        return jax.nn.gelu(preact_band(band_index), approximate=True).astype(jnp.bfloat16)
    features = lax.map(feature_band, bands).reshape(H * W, CO)
    gram = lax.dot_general(features, features, (((0,), (0,)), ((), ())), preferred_element_type=jnp.float32) / NPIX
    error = gram - target_gram
    symmetric = (error + error.T).astype(jnp.bfloat16)

    def grad_band(band_index):
        preact = preact_band(band_index)
        begin = (band_index * TR * W).astype(jnp.int32)
        own_rows = lax.dynamic_slice_in_dim(features, begin, TR * W, 0)
        upstream = jnp.dot(own_rows, symmetric, preferred_element_type=jnp.float32) / math.sqrt(CO)
        return (upstream * gelu_grad(preact)).astype(jnp.bfloat16)
    grad_pre = lax.map(grad_band, bands).reshape(H, W, CO)
    grad_padded = jnp.pad(grad_pre, ((1, 1), (1, 1), (0, 0)))

    def input_band(band_index):
        begin = (band_index * TR).astype(jnp.int32)
        window = lax.dynamic_slice_in_dim(grad_padded, begin, TR + 2, 0)
        return jnp.dot(patches(window, TR, W), flipped, preferred_element_type=jnp.float32).astype(jnp.bfloat16)
    grad_canvas = lax.map(input_band, bands).reshape(H, W, CI)
    return (gram, grad_canvas)
```

```python
import functools
import math

import jax
import jax.numpy as jnp
from jax import lax
from jax.experimental import pallas as pl
from jax.experimental.pallas import tpu as pltpu
from jax.sharding import PartitionSpec as P

gelu_scale = math.sqrt(2.0 / math.pi)
tile = 128
edge = 16
f32, bf16 = jnp.float32, jnp.bfloat16


def tile_pairs(width):
    count = width // tile
    return [(i, j) for i in range(count) for j in range(i, count)]


def exchange(block, axis, dim, width):
    count = lax.axis_size(axis)
    last = lax.slice_in_dim(block, block.shape[dim] - width, None, axis=dim)
    first = lax.slice_in_dim(block, 0, width, axis=dim)
    if count == 2:
        here = lax.axis_index(axis)
        other = lax.ppermute(jnp.where(here == 0, last, first), axis, [(0, 1), (1, 0)])
        none = jnp.zeros_like(other)
        return jnp.where(here == 0, none, other), jnp.where(here == 0, other, none)
    forward = [(i, i + 1) for i in range(count - 1)]
    backward = [(target, source) for source, target in forward]
    return lax.ppermute(last, axis, forward), lax.ppermute(first, axis, backward)


def device_index():
    return lax.axis_index("rows") * lax.axis_size("cols") + lax.axis_index("cols")


def swap(value, bit):
    total = lax.axis_size("rows") * lax.axis_size("cols")
    return lax.ppermute(value, ("rows", "cols"), [(i, i ^ (1 << bit)) for i in range(total)])


def sum_all(packed):
    bits = (lax.axis_size("rows") * lax.axis_size("cols")).bit_length() - 1
    me = device_index()
    halving = [bit for bit in range(min(3, bits))]
    mine = packed
    for bit in halving:
        half = mine.shape[0] // 2
        side = (me >> bit) & 1
        send = lax.dynamic_slice_in_dim(mine, (1 - side) * half, half, axis=0).astype(bf16)
        keep = lax.dynamic_slice_in_dim(mine, side * half, half, axis=0)
        mine = keep + swap(send, bit).astype(f32)
    for bit in range(len(halving), bits):
        send = mine.astype(bf16)
        mine = send.astype(f32) + swap(send, bit).astype(f32)
    mine = mine.astype(bf16)
    for bit in reversed(halving):
        side = (me >> bit) & 1
        other = swap(mine, bit)
        mine = jnp.where(
            side == 0, jnp.concatenate([mine, other]), jnp.concatenate([other, mine])
        )
    return mine


def gelu_pair(value):
    square = value * value
    tangent = jnp.tanh(value * (gelu_scale + gelu_scale * 0.044715 * square))
    half = 0.5 * value
    plus = 0.5 + 0.5 * tangent
    grad = plus + half * (1.0 - tangent * tangent) * (
        gelu_scale + gelu_scale * 3.0 * 0.044715 * square
    )
    return value * plus, grad


def forward_kernel(
    shape, own_ref, low_ref, high_ref, left_ref, right_ref, kernel_ref, bias_ref,
    feat_ref, slope_ref, gram_ref, cat_ref, edge_ref,
):
    tile_rows, tile_cols, in_width, out_width, step = shape
    first = (lax.axis_index("rows") > 0).astype(f32)
    last = (lax.axis_index("rows") < lax.axis_size("rows") - 1).astype(f32)
    left = (lax.axis_index("cols") > 0).astype(f32)
    right = (lax.axis_index("cols") < lax.axis_size("cols") - 1).astype(f32)
    place = lax.broadcasted_iota(jnp.int32, (tile_cols, in_width), 0)
    lefts = [left_ref[b].astype(f32) for b in range(3)]
    rights = [right_ref[b].astype(f32) for b in range(3)]
    span = 3 * in_width
    for r in range(tile_rows + 4):
        if r < 2:
            row = low_ref[r]
        elif r < tile_rows + 2:
            row = own_ref[r - 2]
        else:
            row = high_ref[r - tile_rows - 2]
        wide = row.astype(f32)
        at = slice(r * tile_cols, (r + 1) * tile_cols)
        before = jnp.where(place == 0, lefts[1][r : r + 1], pltpu.roll(wide, 1, 0))
        after = jnp.where(
            place == tile_cols - 1, rights[1][r : r + 1], pltpu.roll(wide, tile_cols - 1, 0)
        )
        cat_ref[at, 0:in_width] = before.astype(bf16)
        cat_ref[at, in_width : 2 * in_width] = row
        cat_ref[at, 2 * in_width : span] = after.astype(bf16)
    blank = jnp.zeros((edge - tile_rows - 2, in_width), f32)
    for a in range(3):
        for b in range(3):
            piece = jnp.concatenate(
                [lefts[b][a : a + tile_rows + 2], blank, rights[b][a : a + tile_rows + 2], blank],
                axis=0,
            )
            at = (3 * a + b) * in_width
            edge_ref[:, at : at + in_width] = piece.astype(bf16)
    bias = bias_ref[...].astype(f32)
    root = 1.0 / math.sqrt(out_width)
    main = (tile_rows + 2) * tile_cols
    for h in range(0, tile_rows + 2, step):
        total = bias
        for a in range(3):
            total = total + jnp.dot(
                cat_ref[(h + a) * tile_cols : (h + a + step) * tile_cols, :],
                kernel_ref[a * span : (a + 1) * span, :],
                preferred_element_type=f32,
            )
        features, slope = gelu_pair(total)
        slope = slope * root
        at = slice(h * tile_cols, (h + step) * tile_cols)
        feat_ref[at, :] = features.astype(bf16)
        if h == 0:
            slope_ref[0:tile_cols, :] = (slope[:tile_cols] * first).astype(bf16)
            slope_ref[tile_cols : step * tile_cols, :] = slope[tile_cols:].astype(bf16)
        elif h + step == tile_rows + 2:
            slope_ref[at, :] = slope.astype(bf16)
            slope_ref[main - tile_cols : main, :] = (slope[-tile_cols:] * last).astype(bf16)
        else:
            slope_ref[at, :] = slope.astype(bf16)
    total = bias + jnp.dot(edge_ref[...], kernel_ref[...], preferred_element_type=f32)
    features, slope = gelu_pair(total)
    line = lax.broadcasted_iota(jnp.int32, (2 * edge, out_width), 0)
    weight = jnp.where(line < edge, left, right)
    weight = jnp.where(line % edge == 0, weight * first, weight)
    weight = jnp.where(line % edge == tile_rows + 1, weight * last, weight)
    feat_ref[main : main + 2 * edge, :] = features.astype(bf16)
    slope_ref[main : main + 2 * edge, :] = (slope * root * weight).astype(bf16)

    inside = slice(tile_cols, main - tile_cols)
    half = out_width // 2
    upper = lax.dot_general(
        feat_ref[inside, 0:half], feat_ref[inside, :], (((0,), (0,)), ((), ())),
        preferred_element_type=f32,
    )
    lower = lax.dot_general(
        feat_ref[inside, half:], feat_ref[inside, half:], (((0,), (0,)), ((), ())),
        preferred_element_type=f32,
    )
    for n, (i, j) in enumerate(tile_pairs(out_width)):
        if i * tile < half:
            part = upper[i * tile : (i + 1) * tile, j * tile : (j + 1) * tile]
        else:
            part = lower[
                i * tile - half : (i + 1) * tile - half, j * tile - half : (j + 1) * tile - half
            ]
        gram_ref[n * tile : (n + 1) * tile, :] = part


def backward_kernel(
    shape, pixel_total, gram_ref, target_ref, feat_ref, slope_ref, kernel_ref,
    own_gram_ref, out_ref, full_ref, sym_ref, cat_ref,
):
    tile_rows, tile_cols, in_width, out_width, step = shape
    for n, (i, j) in enumerate(tile_pairs(out_width)):
        at_i, at_j = slice(i * tile, (i + 1) * tile), slice(j * tile, (j + 1) * tile)
        gram = gram_ref[n * tile : (n + 1) * tile, :].astype(f32) * (1.0 / pixel_total)
        both = 2.0 * gram - (target_ref[at_i, at_j].astype(f32) + target_ref[at_j, at_i].astype(f32).T)
        full_ref[at_i, at_j] = gram
        sym_ref[at_i, at_j] = both.astype(bf16)
        if i != j:
            full_ref[at_j, at_i] = gram.T
            sym_ref[at_j, at_i] = both.T.astype(bf16)
    share = own_gram_ref.shape[0]
    start = device_index() * share
    if share % 8 == 0:
        own_gram_ref[...] = full_ref[pl.ds(pl.multiple_of(start, 8), share), :]
    else:
        group = full_ref[pl.ds(pl.multiple_of(start // 8 * 8, 8), 8), :]
        picked = group[0:share]
        for k in range(share, 8, share):
            picked = jnp.where(start % 8 == k, group[k : k + share], picked)
        own_gram_ref[...] = picked

    main = (tile_rows + 2) * tile_cols
    edges = (
        jnp.dot(feat_ref[main : main + 2 * edge, :], sym_ref[...], preferred_element_type=f32)
        * slope_ref[main : main + 2 * edge, :].astype(f32)
    )
    place = lax.broadcasted_iota(jnp.int32, (tile_cols, out_width), 0)
    for h in range(0, tile_rows + 2, step):
        at = slice(h * tile_cols, (h + step) * tile_cols)
        grad = jnp.dot(feat_ref[at, :], sym_ref[...], preferred_element_type=f32) * slope_ref[
            at, :
        ].astype(f32)
        cat_ref[at, out_width : 2 * out_width] = grad.astype(bf16)
        for k in range(step):
            r = h + k
            row = grad[k * tile_cols : (k + 1) * tile_cols]
            to = slice(r * tile_cols, (r + 1) * tile_cols)
            after = jnp.where(
                place == tile_cols - 1,
                edges[edge + r : edge + r + 1],
                pltpu.roll(row, tile_cols - 1, 0),
            )
            before = jnp.where(place == 0, edges[r : r + 1], pltpu.roll(row, 1, 0))
            cat_ref[to, 0:out_width] = after.astype(bf16)
            cat_ref[to, 2 * out_width :] = before.astype(bf16)
    for h in range(0, tile_rows, step):
        total = jnp.zeros((step * tile_cols, in_width), f32)
        for a in range(3):
            for b in range(3):
                total = total + lax.dot_general(
                    cat_ref[
                        (h + 2 - a) * tile_cols : (h + 2 - a + step) * tile_cols,
                        b * out_width : (b + 1) * out_width,
                    ],
                    kernel_ref[(3 * a + b) * in_width : (3 * a + b + 1) * in_width, :],
                    (((1,), (1,)), ((), ())),
                    preferred_element_type=f32,
                )
        out_ref[h * tile_cols : (h + step) * tile_cols, :] = total.astype(bf16)


def on_device(canvas, conv_weight, conv_bias, target_gram):
    tile_rows, tile_cols, in_width = canvas.shape
    out_width = conv_weight.shape[3]
    pixel_total = tile_rows * tile_cols * lax.axis_size("rows") * lax.axis_size("cols")
    shape = (tile_rows, tile_cols, in_width, out_width, 2)
    lines = (tile_rows + 2) * tile_cols + 2 * edge
    target_full = lax.all_gather(target_gram.astype(bf16), ("rows", "cols"), axis=0, tiled=True)

    low, high = exchange(canvas, "rows", 0, 2)
    sides = lambda part: jnp.concatenate([low[:, part], canvas[:, part], high[:, part]], axis=0)
    rim = jnp.concatenate([sides(slice(0, 2)), sides(slice(tile_cols - 2, tile_cols))], axis=1)
    left, right = exchange(rim, "cols", 1, 2)
    left = jnp.concatenate([left, rim[:, 0:1]], axis=1).transpose(1, 0, 2)
    right = jnp.concatenate([rim[:, 3:4], right], axis=1).transpose(1, 0, 2)

    kernel = conv_weight.reshape(9 * in_width, out_width)
    params = pltpu.CompilerParams(vmem_limit_bytes=32 * 1024 * 1024)
    features, slope, gram = pl.pallas_call(
        functools.partial(forward_kernel, shape),
        out_shape=(
            jax.ShapeDtypeStruct((lines, out_width), bf16),
            jax.ShapeDtypeStruct((lines, out_width), bf16),
            jax.ShapeDtypeStruct((len(tile_pairs(out_width)) * tile, tile), f32),
        ),
        scratch_shapes=[
            pltpu.VMEM(((tile_rows + 4) * tile_cols, 3 * in_width), bf16),
            pltpu.VMEM((2 * edge, 9 * in_width), bf16),
        ],
        compiler_params=params,
        name="conv_gelu_gram",
    )(canvas, low, high, left, right, kernel, conv_bias.reshape(1, out_width))

    packed = sum_all(gram)

    own_gram, grad = pl.pallas_call(
        functools.partial(backward_kernel, shape, pixel_total),
        out_shape=(
            jax.ShapeDtypeStruct(target_gram.shape, f32),
            jax.ShapeDtypeStruct((tile_rows * tile_cols, in_width), bf16),
        ),
        scratch_shapes=[
            pltpu.VMEM((out_width, out_width), f32),
            pltpu.VMEM((out_width, out_width), bf16),
            pltpu.VMEM(((tile_rows + 2) * tile_cols, 3 * out_width), bf16),
        ],
        compiler_params=params,
        name="grad_conv",
    )(packed, target_full, features, slope, kernel)
    return own_gram, grad.reshape(tile_rows, tile_cols, in_width)


def solution(mesh):
    return jax.shard_map(
        on_device,
        mesh=mesh,
        in_specs=(P("rows", "cols", None), P(), P(), P(("rows", "cols"), None)),
        out_specs=(P(("rows", "cols"), None), P("rows", "cols", None)),
        check_vma=False,
    )
```

```python
import functools
import math

import jax
import jax.numpy as jnp
from jax import lax
from jax.experimental import pallas as pl
from jax.experimental.pallas import tpu as pltpu
from jax.sharding import PartitionSpec as P

gelu_scale = math.sqrt(2.0 / math.pi)
tile = 128
edge = 16
f32, bf16 = jnp.float32, jnp.bfloat16


def tile_pairs(width):
    count = width // tile
    return [(i, j) for i in range(count) for j in range(i, count)]


def exchange(block, axis, dim, width):
    count = lax.axis_size(axis)
    last = lax.slice_in_dim(block, block.shape[dim] - width, None, axis=dim)
    first = lax.slice_in_dim(block, 0, width, axis=dim)
    if count == 2:
        here = lax.axis_index(axis)
        other = lax.ppermute(jnp.where(here == 0, last, first), axis, [(0, 1), (1, 0)])
        none = jnp.zeros_like(other)
        return jnp.where(here == 0, none, other), jnp.where(here == 0, other, none)
    forward = [(i, i + 1) for i in range(count - 1)]
    backward = [(target, source) for source, target in forward]
    return lax.ppermute(last, axis, forward), lax.ppermute(first, axis, backward)


def device_index():
    return lax.axis_index("rows") * lax.axis_size("cols") + lax.axis_index("cols")


def swap(value, bit):
    total = lax.axis_size("rows") * lax.axis_size("cols")
    return lax.ppermute(value, ("rows", "cols"), [(i, i ^ (1 << bit)) for i in range(total)])


def sum_all(packed):
    count, lanes = lax.axis_size("rows"), packed.shape[1]
    bits = lax.axis_size("cols").bit_length() - 1
    me = lax.axis_index("cols")
    mine = packed
    for bit in range(bits):
        half = mine.shape[0] // 2
        side = (me >> bit) & 1
        send = lax.dynamic_slice_in_dim(mine, (1 - side) * half, half, axis=0).astype(bf16)
        keep = lax.dynamic_slice_in_dim(mine, side * half, half, axis=0)
        mine = keep + swap(send, bit).astype(f32)
    share = mine.shape[0] // count
    parts = lax.all_to_all(
        mine.astype(bf16).reshape(count, share, lanes), "rows", split_axis=0, concat_axis=0
    )
    mine = jnp.sum(parts.astype(f32), axis=0).astype(bf16)
    mine = lax.all_to_all(
        jnp.broadcast_to(mine[None], (count, share, lanes)), "rows", split_axis=0, concat_axis=0
    ).reshape(count * share, lanes)
    for bit in reversed(range(bits)):
        side = (me >> bit) & 1
        other = swap(mine, bit)
        mine = jnp.where(
            side == 0, jnp.concatenate([mine, other]), jnp.concatenate([other, mine])
        )
    return mine


def gather_all(mine):
    bits = (lax.axis_size("rows") * lax.axis_size("cols")).bit_length() - 1
    share, width = mine.shape
    mine = mine[None]
    for bit in reversed(range(bits)):
        side = (device_index() >> bit) & 1
        other = swap(mine, bit)
        mine = jnp.where(
            side == 0, jnp.stack([mine, other], axis=1), jnp.stack([other, mine], axis=1)
        ).reshape(-1, share, width)
    return mine.reshape(-1, width)


def gelu_pair(value):
    square = value * value
    tangent = jnp.tanh(value * (gelu_scale + gelu_scale * 0.044715 * square))
    half = 0.5 * value
    plus = 0.5 + 0.5 * tangent
    grad = plus + half * (1.0 - tangent * tangent) * (
        gelu_scale + gelu_scale * 3.0 * 0.044715 * square
    )
    return value * plus, grad


def forward_kernel(
    shape, own_ref, low_ref, high_ref, left_ref, right_ref, kernel_ref, bias_ref,
    feat_ref, slope_ref, gram_ref, cat_ref, edge_ref,
):
    tile_rows, tile_cols, in_width, out_width, step = shape
    first = (lax.axis_index("rows") > 0).astype(f32)
    last = (lax.axis_index("rows") < lax.axis_size("rows") - 1).astype(f32)
    left = (lax.axis_index("cols") > 0).astype(f32)
    right = (lax.axis_index("cols") < lax.axis_size("cols") - 1).astype(f32)
    place = lax.broadcasted_iota(jnp.int32, (tile_cols, in_width), 0)
    lefts = [left_ref[b].astype(f32) for b in range(3)]
    rights = [right_ref[b].astype(f32) for b in range(3)]
    span = 3 * in_width
    for r in range(tile_rows + 4):
        if r < 2:
            row = low_ref[r]
        elif r < tile_rows + 2:
            row = own_ref[r - 2]
        else:
            row = high_ref[r - tile_rows - 2]
        wide = row.astype(f32)
        at = slice(r * tile_cols, (r + 1) * tile_cols)
        before = jnp.where(place == 0, lefts[1][r : r + 1], pltpu.roll(wide, 1, 0))
        after = jnp.where(
            place == tile_cols - 1, rights[1][r : r + 1], pltpu.roll(wide, tile_cols - 1, 0)
        )
        cat_ref[at, 0:in_width] = before.astype(bf16)
        cat_ref[at, in_width : 2 * in_width] = row
        cat_ref[at, 2 * in_width : span] = after.astype(bf16)
    blank = jnp.zeros((edge - tile_rows - 2, in_width), f32)
    for a in range(3):
        for b in range(3):
            piece = jnp.concatenate(
                [lefts[b][a : a + tile_rows + 2], blank, rights[b][a : a + tile_rows + 2], blank],
                axis=0,
            )
            at = (3 * a + b) * in_width
            edge_ref[:, at : at + in_width] = piece.astype(bf16)
    bias = bias_ref[...].astype(f32)
    root = 1.0 / math.sqrt(out_width)
    main = (tile_rows + 2) * tile_cols
    for h in range(0, tile_rows + 2, step):
        total = bias
        for a in range(3):
            total = total + jnp.dot(
                cat_ref[(h + a) * tile_cols : (h + a + step) * tile_cols, :],
                kernel_ref[a * span : (a + 1) * span, :],
                preferred_element_type=f32,
            )
        features, slope = gelu_pair(total)
        slope = slope * root
        at = slice(h * tile_cols, (h + step) * tile_cols)
        feat_ref[at, :] = features.astype(bf16)
        if h == 0:
            slope_ref[0:tile_cols, :] = (slope[:tile_cols] * first).astype(bf16)
            slope_ref[tile_cols : step * tile_cols, :] = slope[tile_cols:].astype(bf16)
        elif h + step == tile_rows + 2:
            slope_ref[at, :] = slope.astype(bf16)
            slope_ref[main - tile_cols : main, :] = (slope[-tile_cols:] * last).astype(bf16)
        else:
            slope_ref[at, :] = slope.astype(bf16)
    total = bias + jnp.dot(edge_ref[...], kernel_ref[...], preferred_element_type=f32)
    features, slope = gelu_pair(total)
    line = lax.broadcasted_iota(jnp.int32, (2 * edge, out_width), 0)
    weight = jnp.where(line < edge, left, right)
    weight = jnp.where(line % edge == 0, weight * first, weight)
    weight = jnp.where(line % edge == tile_rows + 1, weight * last, weight)
    feat_ref[main : main + 2 * edge, :] = features.astype(bf16)
    slope_ref[main : main + 2 * edge, :] = (slope * root * weight).astype(bf16)

    inside = slice(tile_cols, main - tile_cols)
    half = out_width // 2
    upper = lax.dot_general(
        feat_ref[inside, 0:half], feat_ref[inside, :], (((0,), (0,)), ((), ())),
        preferred_element_type=f32,
    )
    lower = lax.dot_general(
        feat_ref[inside, half:], feat_ref[inside, half:], (((0,), (0,)), ((), ())),
        preferred_element_type=f32,
    )
    for n, (i, j) in enumerate(tile_pairs(out_width)):
        if i * tile < half:
            part = upper[i * tile : (i + 1) * tile, j * tile : (j + 1) * tile]
        else:
            part = lower[
                i * tile - half : (i + 1) * tile - half, j * tile - half : (j + 1) * tile - half
            ]
        gram_ref[n * tile : (n + 1) * tile, :] = part


def backward_kernel(
    shape, pixel_total, gram_ref, target_ref, feat_ref, slope_ref, kernel_ref,
    own_gram_ref, out_ref, full_ref, sym_ref, cat_ref,
):
    tile_rows, tile_cols, in_width, out_width, step = shape
    for n, (i, j) in enumerate(tile_pairs(out_width)):
        at_i, at_j = slice(i * tile, (i + 1) * tile), slice(j * tile, (j + 1) * tile)
        gram = gram_ref[n * tile : (n + 1) * tile, :].astype(f32) * (1.0 / pixel_total)
        both = 2.0 * gram - (target_ref[at_i, at_j].astype(f32) + target_ref[at_j, at_i].astype(f32).T)
        full_ref[at_i, at_j] = gram
        sym_ref[at_i, at_j] = both.astype(bf16)
        if i != j:
            full_ref[at_j, at_i] = gram.T
            sym_ref[at_j, at_i] = both.T.astype(bf16)
    share = own_gram_ref.shape[0]
    start = device_index() * share
    if share % 8 == 0:
        own_gram_ref[...] = full_ref[pl.ds(pl.multiple_of(start, 8), share), :]
    else:
        group = full_ref[pl.ds(pl.multiple_of(start // 8 * 8, 8), 8), :]
        picked = group[0:share]
        for k in range(share, 8, share):
            picked = jnp.where(start % 8 == k, group[k : k + share], picked)
        own_gram_ref[...] = picked

    main = (tile_rows + 2) * tile_cols
    edges = (
        jnp.dot(feat_ref[main : main + 2 * edge, :], sym_ref[...], preferred_element_type=f32)
        * slope_ref[main : main + 2 * edge, :].astype(f32)
    )
    place = lax.broadcasted_iota(jnp.int32, (tile_cols, out_width), 0)
    for h in range(0, tile_rows + 2, step):
        at = slice(h * tile_cols, (h + step) * tile_cols)
        grad = jnp.dot(feat_ref[at, :], sym_ref[...], preferred_element_type=f32) * slope_ref[
            at, :
        ].astype(f32)
        cat_ref[at, out_width : 2 * out_width] = grad.astype(bf16)
        for k in range(step):
            r = h + k
            row = grad[k * tile_cols : (k + 1) * tile_cols]
            to = slice(r * tile_cols, (r + 1) * tile_cols)
            after = jnp.where(
                place == tile_cols - 1,
                edges[edge + r : edge + r + 1],
                pltpu.roll(row, tile_cols - 1, 0),
            )
            before = jnp.where(place == 0, edges[r : r + 1], pltpu.roll(row, 1, 0))
            cat_ref[to, 0:out_width] = after.astype(bf16)
            cat_ref[to, 2 * out_width :] = before.astype(bf16)
    for h in range(0, tile_rows, step):
        total = jnp.zeros((step * tile_cols, in_width), f32)
        for a in range(3):
            for b in range(3):
                total = total + lax.dot_general(
                    cat_ref[
                        (h + 2 - a) * tile_cols : (h + 2 - a + step) * tile_cols,
                        b * out_width : (b + 1) * out_width,
                    ],
                    kernel_ref[(3 * a + b) * in_width : (3 * a + b + 1) * in_width, :],
                    (((1,), (1,)), ((), ())),
                    preferred_element_type=f32,
                )
        out_ref[h * tile_cols : (h + step) * tile_cols, :] = total.astype(bf16)


def on_device(canvas, conv_weight, conv_bias, target_gram):
    tile_rows, tile_cols, in_width = canvas.shape
    out_width = conv_weight.shape[3]
    pixel_total = tile_rows * tile_cols * lax.axis_size("rows") * lax.axis_size("cols")
    shape = (tile_rows, tile_cols, in_width, out_width, 2)
    lines = (tile_rows + 2) * tile_cols + 2 * edge
    target_full = gather_all(target_gram.astype(bf16))

    low, high = exchange(canvas, "rows", 0, 2)
    sides = lambda part: jnp.concatenate([low[:, part], canvas[:, part], high[:, part]], axis=0)
    rim = jnp.concatenate([sides(slice(0, 2)), sides(slice(tile_cols - 2, tile_cols))], axis=1)
    left, right = exchange(rim, "cols", 1, 2)
    left = jnp.concatenate([left, rim[:, 0:1]], axis=1).transpose(1, 0, 2)
    right = jnp.concatenate([rim[:, 3:4], right], axis=1).transpose(1, 0, 2)

    kernel = conv_weight.reshape(9 * in_width, out_width)
    params = pltpu.CompilerParams(vmem_limit_bytes=32 * 1024 * 1024)
    features, slope, gram = pl.pallas_call(
        functools.partial(forward_kernel, shape),
        out_shape=(
            jax.ShapeDtypeStruct((lines, out_width), bf16),
            jax.ShapeDtypeStruct((lines, out_width), bf16),
            jax.ShapeDtypeStruct((len(tile_pairs(out_width)) * tile, tile), f32),
        ),
        scratch_shapes=[
            pltpu.VMEM(((tile_rows + 4) * tile_cols, 3 * in_width), bf16),
            pltpu.VMEM((2 * edge, 9 * in_width), bf16),
        ],
        compiler_params=params,
        name="conv_gelu_gram",
    )(canvas, low, high, left, right, kernel, conv_bias.reshape(1, out_width))

    packed = sum_all(gram)

    own_gram, grad = pl.pallas_call(
        functools.partial(backward_kernel, shape, pixel_total),
        out_shape=(
            jax.ShapeDtypeStruct(target_gram.shape, f32),
            jax.ShapeDtypeStruct((tile_rows * tile_cols, in_width), bf16),
        ),
        scratch_shapes=[
            pltpu.VMEM((out_width, out_width), f32),
            pltpu.VMEM((out_width, out_width), bf16),
            pltpu.VMEM(((tile_rows + 2) * tile_cols, 3 * out_width), bf16),
        ],
        compiler_params=params,
        name="grad_conv",
    )(packed, target_full, features, slope, kernel)
    return own_gram, grad.reshape(tile_rows, tile_cols, in_width)


def solution(mesh):
    return jax.shard_map(
        on_device,
        mesh=mesh,
        in_specs=(P("rows", "cols", None), P(), P(), P(("rows", "cols"), None)),
        out_specs=(P(("rows", "cols"), None), P("rows", "cols", None)),
        check_vma=False,
    )
```

```python
import functools
import math

import jax
import jax.numpy as jnp
from jax import lax
from jax.experimental import pallas as pl
from jax.experimental.pallas import tpu as pltpu
from jax.sharding import PartitionSpec as P

gelu_scale = math.sqrt(2.0 / math.pi)
tile = 128
edge = 16
f32, bf16 = jnp.float32, jnp.bfloat16


def tile_pairs(width):
    count = width // tile
    return [(i, j) for i in range(count) for j in range(i, count)]


def shift_rows(last, first):
    count = lax.axis_size("rows")
    forward = [(i, i + 1) for i in range(count - 1)]
    backward = [(target, source) for source, target in forward]
    return lax.ppermute(last, "rows", forward), lax.ppermute(first, "rows", backward)


def shift_cols(last, first):
    count = lax.axis_size("cols")
    if count == 2:
        here = lax.axis_index("cols")
        other = lax.ppermute(jnp.where(here == 0, last, first), "cols", [(0, 1), (1, 0)])
        none = jnp.zeros_like(other)
        return jnp.where(here == 0, none, other), jnp.where(here == 0, other, none)
    forward = [(i, i + 1) for i in range(count - 1)]
    backward = [(target, source) for source, target in forward]
    return lax.ppermute(last, "cols", forward), lax.ppermute(first, "cols", backward)


def device_index():
    return lax.axis_index("rows") * lax.axis_size("cols") + lax.axis_index("cols")


def swap(value, bit):
    total = lax.axis_size("rows") * lax.axis_size("cols")
    return lax.ppermute(value, ("rows", "cols"), [(i, i ^ (1 << bit)) for i in range(total)])


def sum_all(packed, target):
    count, lanes = lax.axis_size("rows"), packed.shape[1]
    bits = lax.axis_size("cols").bit_length() - 1
    me = lax.axis_index("cols")
    mine = packed
    for bit in range(bits):
        half = mine.shape[0] // 2
        side = (me >> bit) & 1
        send = lax.dynamic_slice_in_dim(mine, (1 - side) * half, half, axis=0).astype(bf16)
        keep = lax.dynamic_slice_in_dim(mine, side * half, half, axis=0)
        mine = keep + swap(send, bit).astype(f32)
    plane = 4
    near = [list(range(i, i + plane)) for i in range(0, count, plane)]
    far = [list(range(i, count, plane)) for i in range(plane)]
    share = mine.shape[0] // plane
    trade = functools.partial(lax.all_to_all, axis_name="rows", split_axis=0, concat_axis=0)
    copies = lambda value, n: jnp.broadcast_to(value[None], (n, *value.shape))
    parts = trade(mine.astype(bf16).reshape(plane, share, lanes), axis_index_groups=near)
    mine = jnp.sum(parts.astype(f32), axis=0).astype(bf16)
    parts = trade(copies(mine, count // plane), axis_index_groups=far)
    mine = jnp.sum(parts.astype(f32), axis=0).astype(bf16)
    mine = trade(copies(mine, plane), axis_index_groups=near).reshape(plane * share, lanes)
    for bit in reversed(range(bits)):
        side = (me >> bit) & 1
        other = swap(mine, bit)
        mine = jnp.where(
            side == 0, jnp.concatenate([mine, other]), jnp.concatenate([other, mine])
        )
    return mine, gather_all(target)


def gather_all(mine):
    bits = (lax.axis_size("rows") * lax.axis_size("cols")).bit_length() - 1
    share, width = mine.shape
    mine = mine[None]
    for bit in reversed(range(bits)):
        side = (device_index() >> bit) & 1
        other = swap(mine, bit)
        mine = jnp.where(
            side == 0, jnp.stack([mine, other], axis=1), jnp.stack([other, mine], axis=1)
        ).reshape(-1, share, width)
    return mine.reshape(-1, width)


def gelu_pair(value):
    square = value * value
    tangent = jnp.tanh(value * (gelu_scale + gelu_scale * 0.044715 * square))
    half = 0.5 * value
    plus = 0.5 + 0.5 * tangent
    grad = plus + half * (1.0 - tangent * tangent) * (
        gelu_scale + gelu_scale * 3.0 * 0.044715 * square
    )
    return value * plus, grad


def start_weights(source_ref, held_ref, sems):
    rows = source_ref.shape[0] // 3
    copies = []
    for a in range(3):
        at = slice(a * rows, (a + 1) * rows)
        copies.append(pltpu.make_async_copy(source_ref.at[at], held_ref.at[at], sems.at[a]))
        copies[a].start()
    return copies


def fill_row(cat_ref, r, row, before, after):
    cols, width = row.shape
    wide = row.astype(f32)
    place = lax.broadcasted_iota(jnp.int32, (cols, width), 0)
    at = slice(r * cols, (r + 1) * cols)
    moved = jnp.where(place == 0, before, pltpu.roll(wide, 1, 0))
    cat_ref[at, 0:width] = moved.astype(bf16)
    cat_ref[at, width : 2 * width] = row.astype(bf16)
    moved = jnp.where(place == cols - 1, after, pltpu.roll(wide, cols - 1, 0))
    cat_ref[at, 2 * width : 3 * width] = moved.astype(bf16)


def gram_tiles(feat, gram_ref, base_ref=None):
    width = feat.shape[1]
    half = width // 2
    product = functools.partial(
        lax.dot_general,
        dimension_numbers=(((0,), (0,)), ((), ())),
        preferred_element_type=f32,
    )
    upper = product(feat[:, :half], feat)
    lower = product(feat[:, half:], feat[:, half:])
    for n, (i, j) in enumerate(tile_pairs(width)):
        at = slice(n * tile, (n + 1) * tile)
        if i * tile < half:
            part = upper[i * tile : (i + 1) * tile, j * tile : (j + 1) * tile]
        else:
            k, m = i * tile - half, j * tile - half
            part = lower[k : k + tile, m : m + tile]
        gram_ref[at, :] = part if base_ref is None else part + base_ref[at, :]


def inner_kernel(
    shape, own_ref, left_ref, right_ref, kernel_ref, bias_ref,
    feat_ref, slope_ref, gram_ref, cat_ref, held_ref, sems,
):
    tile_rows, tile_cols, in_width, out_width, step = shape
    copies = start_weights(kernel_ref, held_ref, sems)
    lefts, rights = left_ref[...].astype(f32), right_ref[...].astype(f32)
    for r in range(tile_rows):
        fill_row(cat_ref, r, own_ref[r], lefts[r : r + 1], rights[r : r + 1])
    bias = bias_ref[...].astype(f32)
    root = 1.0 / math.sqrt(out_width)
    span = 3 * in_width
    for h in range(0, tile_rows - 2, step):
        total = bias
        for a in range(3):
            if h == 0:
                copies[a].wait()
            total = total + jnp.dot(
                cat_ref[(h + a) * tile_cols : (h + a + step) * tile_cols, :],
                held_ref[a * span : (a + 1) * span, :],
                preferred_element_type=f32,
            )
        features, slope = gelu_pair(total)
        at = slice(h * tile_cols, (h + step) * tile_cols)
        feat_ref[at, :] = features.astype(bf16)
        slope_ref[at, :] = (slope * root).astype(bf16)
    gram_tiles(feat_ref[...], gram_ref)


def outer_kernel(
    shape, own_ref, low_ref, high_ref, left_ref, right_ref, kernel_ref, bias_ref, base_ref,
    feat_ref, slope_ref, gram_ref, cat_ref, edge_ref, held_ref, sems,
):
    tile_rows, tile_cols, in_width, out_width, step = shape
    copies = start_weights(kernel_ref, held_ref, sems)
    first = (lax.axis_index("rows") > 0).astype(f32)
    last = (lax.axis_index("rows") < lax.axis_size("rows") - 1).astype(f32)
    left = (lax.axis_index("cols") > 0).astype(f32)
    right = (lax.axis_index("cols") < lax.axis_size("cols") - 1).astype(f32)
    lefts = [left_ref[b].astype(f32) for b in range(3)]
    rights = [right_ref[b].astype(f32) for b in range(3)]
    span = 3 * in_width
    lines = [0, 1, 2, 3, tile_rows, tile_rows + 1, tile_rows + 2, tile_rows + 3]
    for r, line in enumerate(lines):
        if line < 2:
            row = low_ref[line, 0:tile_cols]
        elif line < tile_rows + 2:
            row = own_ref[line - 2]
        else:
            row = high_ref[line - tile_rows - 2, 0:tile_cols]
        fill_row(cat_ref, r, row, lefts[1][line : line + 1], rights[1][line : line + 1])
    blank = jnp.zeros((edge - tile_rows - 2, in_width), f32)
    for a in range(3):
        for b in range(3):
            piece = jnp.concatenate(
                [lefts[b][a : a + tile_rows + 2], blank, rights[b][a : a + tile_rows + 2], blank],
                axis=0,
            )
            at = (3 * a + b) * in_width
            edge_ref[:, at : at + in_width] = piece.astype(bf16)
    bias = bias_ref[...].astype(f32)
    root = 1.0 / math.sqrt(out_width)
    totals = [bias, bias, bias]
    for a in range(3):
        copies[a].wait()
        weights = held_ref[a * span : (a + 1) * span, :]
        for k in range(2):
            totals[k] = totals[k] + jnp.dot(
                cat_ref[(4 * k + a) * tile_cols : (4 * k + a + 2) * tile_cols, :],
                weights,
                preferred_element_type=f32,
            )
        totals[2] = totals[2] + jnp.dot(
            edge_ref[:, a * span : (a + 1) * span], weights, preferred_element_type=f32
        )
    main = 2 * tile_cols
    for k in range(2):
        features, slope = gelu_pair(totals[k])
        slope = slope * root
        at = k * main
        feat_ref[at : at + main, :] = features.astype(bf16)
        scale = (first, 1.0) if k == 0 else (1.0, last)
        slope_ref[at : at + tile_cols, :] = (slope[:tile_cols] * scale[0]).astype(bf16)
        slope_ref[at + tile_cols : at + main, :] = (slope[tile_cols:] * scale[1]).astype(bf16)
    features, slope = gelu_pair(totals[2])
    line = lax.broadcasted_iota(jnp.int32, (2 * edge, out_width), 0)
    weight = jnp.where(line < edge, left, right)
    weight = jnp.where(line % edge == 0, weight * first, weight)
    weight = jnp.where(line % edge == tile_rows + 1, weight * last, weight)
    feat_ref[2 * main :, :] = features.astype(bf16)
    slope_ref[2 * main :, :] = (slope * root * weight).astype(bf16)
    gram_tiles(feat_ref[tile_cols : 3 * tile_cols, :], gram_ref, base_ref)


def backward_kernel(
    shape, pixel_total, gram_ref, target_ref, in_feat_ref, in_slope_ref, out_feat_ref, out_slope_ref,
    kernel_ref, own_gram_ref, out_ref, full_ref, sym_ref, cat_ref, held_ref, sems,
):
    tile_rows, tile_cols, in_width, out_width, step = shape
    copies = start_weights(kernel_ref, held_ref, sems)
    for n, (i, j) in enumerate(tile_pairs(out_width)):
        at_i, at_j = slice(i * tile, (i + 1) * tile), slice(j * tile, (j + 1) * tile)
        gram = gram_ref[n * tile : (n + 1) * tile, :].astype(f32) * (1.0 / pixel_total)
        both = 2.0 * gram - (target_ref[at_i, at_j].astype(f32) + target_ref[at_j, at_i].astype(f32).T)
        full_ref[at_i, at_j] = gram
        sym_ref[at_i, at_j] = both.astype(bf16)
        if i != j:
            full_ref[at_j, at_i] = gram.T
            sym_ref[at_j, at_i] = both.T.astype(bf16)
    share = own_gram_ref.shape[0]
    start = device_index() * share
    if share % 8 == 0:
        own_gram_ref[...] = full_ref[pl.ds(pl.multiple_of(start, 8), share), :]
    else:
        group = full_ref[pl.ds(pl.multiple_of(start // 8 * 8, 8), 8), :]
        picked = group[0:share]
        for k in range(share, 8, share):
            picked = jnp.where(start % 8 == k, group[k : k + share], picked)
        own_gram_ref[...] = picked

    def grad_of(feat_ref, slope_ref, at):
        product = jnp.dot(feat_ref[at, :], sym_ref[...], preferred_element_type=f32)
        return product * slope_ref[at, :].astype(f32)

    main = 2 * tile_cols
    edges = grad_of(out_feat_ref, out_slope_ref, slice(2 * main, None))
    lines = [
        (out_feat_ref, out_slope_ref, 0, 0),
        (out_feat_ref, out_slope_ref, main, tile_rows),
    ] + [
        (in_feat_ref, in_slope_ref, h * tile_cols, h + 2) for h in range(0, tile_rows - 2, step)
    ]
    for feat_ref, slope_ref, begin, r in lines:
        grad = grad_of(feat_ref, slope_ref, slice(begin, begin + step * tile_cols))
        for k in range(step):
            fill_row(
                cat_ref, r + k, grad[k * tile_cols : (k + 1) * tile_cols],
                edges[r + k : r + k + 1], edges[edge + r + k : edge + r + k + 1],
            )
    for a in range(3):
        copies[a].wait()
    for h in range(0, tile_rows, step):
        total = jnp.zeros((step * tile_cols, in_width), f32)
        for a in range(3):
            for b in range(3):
                total = total + lax.dot_general(
                    cat_ref[
                        (h + 2 - a) * tile_cols : (h + 2 - a + step) * tile_cols,
                        (2 - b) * out_width : (3 - b) * out_width,
                    ],
                    held_ref[(3 * a + b) * in_width : (3 * a + b + 1) * in_width, :],
                    (((1,), (1,)), ((), ())),
                    preferred_element_type=f32,
                )
        out_ref[h * tile_cols : (h + step) * tile_cols, :] = total.astype(bf16)


def on_device(canvas, conv_weight, conv_bias, target_gram):
    tile_rows, tile_cols, in_width = canvas.shape
    out_width = conv_weight.shape[3]
    pixel_total = tile_rows * tile_cols * lax.axis_size("rows") * lax.axis_size("cols")
    shape = (tile_rows, tile_cols, in_width, out_width, 2)
    kernel = conv_weight.reshape(9 * in_width, out_width)
    bias = conv_bias.reshape(1, out_width)
    params = pltpu.CompilerParams(vmem_limit_bytes=24 * 1024 * 1024)
    vmem, hbm = pl.BlockSpec(memory_space=pltpu.VMEM), pl.BlockSpec(memory_space=pltpu.HBM)
    held = [pltpu.VMEM(kernel.shape, bf16), pltpu.SemaphoreType.DMA((3,))]
    packed_shape = jax.ShapeDtypeStruct((len(tile_pairs(out_width)) * tile, tile), f32)

    begin, end = canvas[:, :2], canvas[:, tile_cols - 2 :]
    left, right = shift_cols(end, begin)
    whole = lambda rows: jnp.concatenate([canvas[rows], left[rows], right[rows]], axis=1)
    low, high = shift_rows(whole(slice(tile_rows - 2, tile_rows)), whole(slice(0, 2)))

    inner = (tile_rows - 2) * tile_cols
    in_feat, in_slope, in_gram = pl.pallas_call(
        functools.partial(inner_kernel, shape),
        out_shape=(
            jax.ShapeDtypeStruct((inner, out_width), bf16),
            jax.ShapeDtypeStruct((inner, out_width), bf16),
            packed_shape,
        ),
        in_specs=[vmem, vmem, vmem, hbm, vmem],
        scratch_shapes=[pltpu.VMEM((tile_rows * tile_cols, 3 * in_width), bf16), *held],
        compiler_params=params,
        name="inner_rows",
        cost_estimate=pl.CostEstimate(
            flops=2 * inner * (9 * in_width + out_width) * out_width,
            bytes_accessed=6_000_000,
            transcendentals=inner * out_width,
        ),
    )(canvas, left[:, 1], right[:, 0], kernel, bias)

    sides = lambda at: jnp.concatenate([low[:, at], canvas_rim[:, at - tile_cols], high[:, at]], axis=0)
    canvas_rim = jnp.concatenate([left, right], axis=1)
    ends = lambda at: jnp.concatenate([low[:, at], canvas[:, at], high[:, at]], axis=0)
    lefts = jnp.stack([sides(tile_cols), sides(tile_cols + 1), ends(0)])
    rights = jnp.stack([ends(tile_cols - 1), sides(tile_cols + 2), sides(tile_cols + 3)])
    outer = 4 * tile_cols + 2 * edge
    out_feat, out_slope, gram = pl.pallas_call(
        functools.partial(outer_kernel, shape),
        out_shape=(
            jax.ShapeDtypeStruct((outer, out_width), bf16),
            jax.ShapeDtypeStruct((outer, out_width), bf16),
            packed_shape,
        ),
        in_specs=[vmem, vmem, vmem, vmem, vmem, hbm, vmem, vmem],
        scratch_shapes=[
            pltpu.VMEM((8 * tile_cols, 3 * in_width), bf16),
            pltpu.VMEM((2 * edge, 9 * in_width), bf16),
            *held,
        ],
        compiler_params=params,
        name="outer_rows",
    )(canvas, low, high, lefts, rights, kernel, bias, in_gram)

    packed, target_full = sum_all(gram, target_gram.astype(bf16))

    own_gram, grad = pl.pallas_call(
        functools.partial(backward_kernel, shape, pixel_total),
        out_shape=(
            jax.ShapeDtypeStruct(target_gram.shape, f32),
            jax.ShapeDtypeStruct((tile_rows * tile_cols, in_width), bf16),
        ),
        in_specs=[vmem] * 6 + [hbm],
        scratch_shapes=[
            pltpu.VMEM((out_width, out_width), f32),
            pltpu.VMEM((out_width, out_width), bf16),
            pltpu.VMEM(((tile_rows + 2) * tile_cols, 3 * out_width), bf16),
            *held,
        ],
        compiler_params=params,
        name="grad_conv",
    )(packed, target_full, in_feat, in_slope, out_feat, out_slope, kernel)
    return own_gram, grad.reshape(tile_rows, tile_cols, in_width)


def solution(mesh):
    return jax.shard_map(
        on_device,
        mesh=mesh,
        in_specs=(P("rows", "cols", None), P(), P(), P(("rows", "cols"), None)),
        out_specs=(P(("rows", "cols"), None), P("rows", "cols", None)),
        check_vma=False,
    )
```

```python
import functools
import math

import jax
import jax.numpy as jnp
from jax import lax
from jax.experimental import pallas as pl
from jax.experimental.pallas import tpu as pltpu
from jax.sharding import PartitionSpec as P

gelu_scale = math.sqrt(2.0 / math.pi)
tile = 128
edge = 16
f32, bf16 = jnp.float32, jnp.bfloat16


def tile_pairs(width):
    count = width // tile
    return [(i, j) for i in range(count) for j in range(i, count)]


def shift_rows(last, first):
    count = lax.axis_size("rows")
    forward = [(i, i + 1) for i in range(count - 1)]
    backward = [(target, source) for source, target in forward]
    return lax.ppermute(last, "rows", forward), lax.ppermute(first, "rows", backward)


def shift_cols(last, first):
    count = lax.axis_size("cols")
    if count == 2:
        here = lax.axis_index("cols")
        other = lax.ppermute(jnp.where(here == 0, last, first), "cols", [(0, 1), (1, 0)])
        none = jnp.zeros_like(other)
        return jnp.where(here == 0, none, other), jnp.where(here == 0, other, none)
    forward = [(i, i + 1) for i in range(count - 1)]
    backward = [(target, source) for source, target in forward]
    return lax.ppermute(last, "cols", forward), lax.ppermute(first, "cols", backward)


def device_index():
    return lax.axis_index("rows") * lax.axis_size("cols") + lax.axis_index("cols")


def swap(value, bit):
    total = lax.axis_size("rows") * lax.axis_size("cols")
    return lax.ppermute(value, ("rows", "cols"), [(i, i ^ (1 << bit)) for i in range(total)])


def join(side, mine, other):
    return jnp.where(side == 0, jnp.stack([mine, other], axis=1), jnp.stack([other, mine], axis=1))


def sum_and_gather(packed, target):
    bits = (lax.axis_size("rows") * lax.axis_size("cols")).bit_length() - 1
    me = device_index()
    lanes = packed.shape[1]
    halving = list(range(min(3, bits)))
    share, width = target.shape
    held = {"bits": list(reversed(range(bits))), "rows": target[None]}

    def step(send, bit):
        if not held["bits"]:
            return swap(send, bit)
        other_bit = held["bits"].pop(0)
        send, rows = lax.optimization_barrier((send, held["rows"]))
        got = swap(send, bit)
        more = swap(rows, other_bit)
        side = (me >> other_bit) & 1
        held["rows"] = join(side, rows, more).reshape(-1, share, width)
        return got

    mine = packed
    for bit in halving:
        half = mine.shape[0] // 2
        side = (me >> bit) & 1
        send = lax.dynamic_slice_in_dim(mine, (1 - side) * half, half, axis=0).astype(bf16)
        keep = lax.dynamic_slice_in_dim(mine, side * half, half, axis=0)
        mine = keep + step(send, bit).astype(f32)
    for bit in range(len(halving), bits):
        send = mine.astype(bf16)
        mine = send.astype(f32) + step(send, bit).astype(f32)
    mine = mine.astype(bf16)
    for bit in reversed(halving):
        side = (me >> bit) & 1
        other = step(mine, bit)
        mine = jnp.where(
            side == 0, jnp.concatenate([mine, other]), jnp.concatenate([other, mine])
        )
    return mine, held["rows"].reshape(-1, width)


def gelu_pair(value):
    square = value * value
    tangent = jnp.tanh(value * (gelu_scale + gelu_scale * 0.044715 * square))
    half = 0.5 * value
    plus = 0.5 + 0.5 * tangent
    grad = plus + half * (1.0 - tangent * tangent) * (
        gelu_scale + gelu_scale * 3.0 * 0.044715 * square
    )
    return value * plus, grad


def column(value, c):
    return jnp.concatenate([value[r, c : c + 1] for r in range(value.shape[0])], axis=0)


def rim_kernel(canvas_ref, begin_ref, end_ref):
    cols = canvas_ref.shape[1]
    begin = canvas_ref[:, 0:16, :].astype(f32)
    end = canvas_ref[:, cols - 16 :, :].astype(f32)
    for c in range(2):
        begin_ref[c] = column(begin, c).astype(bf16)
        end_ref[c] = column(end, 14 + c).astype(bf16)


def fill_row(cat_ref, r, row, before, after):
    cols, width = row.shape
    wide = row.astype(f32)
    place = lax.broadcasted_iota(jnp.int32, (cols, width), 0)
    at = slice(r * cols, (r + 1) * cols)
    moved = jnp.where(place == 0, before, pltpu.roll(wide, 1, 0))
    cat_ref[at, 0:width] = moved.astype(bf16)
    cat_ref[at, width : 2 * width] = row.astype(bf16)
    moved = jnp.where(place == cols - 1, after, pltpu.roll(wide, cols - 1, 0))
    cat_ref[at, 2 * width : 3 * width] = moved.astype(bf16)


def gram_tiles(feat, gram_ref, base_ref=None):
    width = feat.shape[1]
    half = width // 2
    product = functools.partial(
        lax.dot_general,
        dimension_numbers=(((0,), (0,)), ((), ())),
        preferred_element_type=f32,
    )
    upper = product(feat[:, :half], feat)
    lower = product(feat[:, half:], feat[:, half:])
    for n, (i, j) in enumerate(tile_pairs(width)):
        at = slice(n * tile, (n + 1) * tile)
        if i * tile < half:
            part = upper[i * tile : (i + 1) * tile, j * tile : (j + 1) * tile]
        else:
            k, m = i * tile - half, j * tile - half
            part = lower[k : k + tile, m : m + tile]
        gram_ref[at, :] = part if base_ref is None else part + base_ref[at, :]


def inner_kernel(
    shape, own_ref, left_ref, right_ref, kernel_ref, bias_ref, target_ref,
    feat_ref, slope_ref, gram_ref, row_ref, half_ref, cat_ref,
):
    row_ref[...] = bias_ref[...].astype(f32).reshape(row_ref.shape)
    half_ref[...] = target_ref[...].astype(bf16)
    tile_rows, tile_cols, in_width, out_width, step = shape
    lefts, rights = left_ref[1].astype(f32), right_ref[0].astype(f32)
    for r in range(tile_rows):
        fill_row(cat_ref, r, own_ref[r], lefts[r : r + 1], rights[r : r + 1])
    bias = row_ref[...]
    root = 1.0 / math.sqrt(out_width)
    span = 3 * in_width
    for h in range(0, tile_rows - 2, step):
        total = bias
        for a in range(3):
            total = total + jnp.dot(
                cat_ref[(h + a) * tile_cols : (h + a + step) * tile_cols, :],
                kernel_ref[a * span : (a + 1) * span, :],
                preferred_element_type=f32,
            )
        features, slope = gelu_pair(total)
        at = slice(h * tile_cols, (h + step) * tile_cols)
        feat_ref[at, :] = features.astype(bf16)
        slope_ref[at, :] = (slope * root).astype(bf16)
    gram_tiles(feat_ref[...], gram_ref)


def outer_kernel(
    shape, own_ref, low_ref, high_ref, left_ref, right_ref, kernel_ref, bias_ref, base_ref,
    feat_ref, slope_ref, gram_ref, cat_ref, edge_ref,
):
    tile_rows, tile_cols, in_width, out_width, step = shape
    first = (lax.axis_index("rows") > 0).astype(f32)
    last = (lax.axis_index("rows") < lax.axis_size("rows") - 1).astype(f32)
    left = (lax.axis_index("cols") > 0).astype(f32)
    right = (lax.axis_index("cols") < lax.axis_size("cols") - 1).astype(f32)
    main = 2 * tile_cols
    low_rim, high_rim = low_ref[main:, :].astype(f32), high_ref[main:, :].astype(f32)
    own_begin = column(own_ref[:, 0:16, :].astype(f32), 0)
    own_end = column(own_ref[:, tile_cols - 16 :, :].astype(f32), 15)

    def sides(c, own):
        return jnp.concatenate(
            [low_rim[c : c + 1], low_rim[4 + c : 5 + c], own, high_rim[c : c + 1], high_rim[4 + c : 5 + c]],
            axis=0,
        )

    def ends(c, own):
        c16 = c // 16 * 16
        piece = lambda ref, k: ref[k + c16 : k + c16 + 16, :].astype(f32)[c - c16 : c - c16 + 1]
        rows = [piece(low_ref, 0), piece(low_ref, tile_cols), own]
        return jnp.concatenate([*rows, piece(high_ref, 0), piece(high_ref, tile_cols)], axis=0)

    lefts = [
        sides(0, left_ref[0].astype(f32)), sides(1, left_ref[1].astype(f32)), ends(0, own_begin)
    ]
    rights = [
        ends(tile_cols - 1, own_end), sides(2, right_ref[0].astype(f32)), sides(3, right_ref[1].astype(f32))
    ]
    span = 3 * in_width
    lines = [0, 1, 2, 3, tile_rows, tile_rows + 1, tile_rows + 2, tile_rows + 3]
    for r, line in enumerate(lines):
        if line < 2:
            row = low_ref[line * tile_cols : (line + 1) * tile_cols, :]
        elif line < tile_rows + 2:
            row = own_ref[line - 2]
        else:
            k = line - tile_rows - 2
            row = high_ref[k * tile_cols : (k + 1) * tile_cols, :]
        fill_row(cat_ref, r, row, lefts[1][line : line + 1], rights[1][line : line + 1])
    blank = jnp.zeros((edge - tile_rows - 2, in_width), f32)
    for a in range(3):
        for b in range(3):
            piece = jnp.concatenate(
                [lefts[b][a : a + tile_rows + 2], blank, rights[b][a : a + tile_rows + 2], blank],
                axis=0,
            )
            at = (3 * a + b) * in_width
            edge_ref[:, at : at + in_width] = piece.astype(bf16)
    bias = bias_ref[...]
    root = 1.0 / math.sqrt(out_width)
    totals = [bias, bias, bias]
    for a in range(3):
        weights = kernel_ref[a * span : (a + 1) * span, :]
        for k in range(2):
            totals[k] = totals[k] + jnp.dot(
                cat_ref[(4 * k + a) * tile_cols : (4 * k + a + 2) * tile_cols, :],
                weights,
                preferred_element_type=f32,
            )
        totals[2] = totals[2] + jnp.dot(
            edge_ref[:, a * span : (a + 1) * span], weights, preferred_element_type=f32
        )
    for k in range(2):
        features, slope = gelu_pair(totals[k])
        slope = slope * root
        at = k * main
        feat_ref[at : at + main, :] = features.astype(bf16)
        scale = (first, 1.0) if k == 0 else (1.0, last)
        slope_ref[at : at + tile_cols, :] = (slope[:tile_cols] * scale[0]).astype(bf16)
        slope_ref[at + tile_cols : at + main, :] = (slope[tile_cols:] * scale[1]).astype(bf16)
    features, slope = gelu_pair(totals[2])
    line = lax.broadcasted_iota(jnp.int32, (2 * edge, out_width), 0)
    weight = jnp.where(line < edge, left, right)
    weight = jnp.where(line % edge == 0, weight * first, weight)
    weight = jnp.where(line % edge == tile_rows + 1, weight * last, weight)
    feat_ref[2 * main :, :] = features.astype(bf16)
    slope_ref[2 * main :, :] = (slope * root * weight).astype(bf16)
    gram_tiles(feat_ref[tile_cols : 3 * tile_cols, :], gram_ref, base_ref)


def backward_kernel(
    shape, pixel_total, gram_ref, target_ref, in_feat_ref, in_slope_ref, out_feat_ref, out_slope_ref,
    kernel_ref, own_gram_ref, out_ref, full_ref, sym_ref, cat_ref,
):
    tile_rows, tile_cols, in_width, out_width, step = shape
    for n, (i, j) in enumerate(tile_pairs(out_width)):
        at_i, at_j = slice(i * tile, (i + 1) * tile), slice(j * tile, (j + 1) * tile)
        gram = gram_ref[n * tile : (n + 1) * tile, :].astype(f32) * (1.0 / pixel_total)
        both = 2.0 * gram - (target_ref[at_i, at_j].astype(f32) + target_ref[at_j, at_i].astype(f32).T)
        full_ref[at_i, at_j] = gram
        sym_ref[at_i, at_j] = both.astype(bf16)
        if i != j:
            full_ref[at_j, at_i] = gram.T
            sym_ref[at_j, at_i] = both.T.astype(bf16)
    share = own_gram_ref.shape[0]
    start = device_index() * share
    if share % 8 == 0:
        own_gram_ref[...] = full_ref[pl.ds(pl.multiple_of(start, 8), share), :]
    else:
        group = full_ref[pl.ds(pl.multiple_of(start // 8 * 8, 8), 8), :]
        picked = group[0:share]
        for k in range(share, 8, share):
            picked = jnp.where(start % 8 == k, group[k : k + share], picked)
        own_gram_ref[...] = picked

    def grad_of(feat_ref, slope_ref, at):
        product = jnp.dot(feat_ref[at, :], sym_ref[...], preferred_element_type=f32)
        return product * slope_ref[at, :].astype(f32)

    main = 2 * tile_cols
    edges = grad_of(out_feat_ref, out_slope_ref, slice(2 * main, None))
    lines = [
        (out_feat_ref, out_slope_ref, 0, 0),
        (out_feat_ref, out_slope_ref, main, tile_rows),
    ] + [
        (in_feat_ref, in_slope_ref, h * tile_cols, h + 2) for h in range(0, tile_rows - 2, step)
    ]
    for feat_ref, slope_ref, begin, r in lines:
        grad = grad_of(feat_ref, slope_ref, slice(begin, begin + step * tile_cols))
        for k in range(step):
            fill_row(
                cat_ref, r + k, grad[k * tile_cols : (k + 1) * tile_cols],
                edges[r + k : r + k + 1], edges[edge + r + k : edge + r + k + 1],
            )
    for h in range(0, tile_rows, step):
        total = jnp.zeros((step * tile_cols, in_width), f32)
        for a in range(3):
            for b in range(3):
                total = total + lax.dot_general(
                    cat_ref[
                        (h + 2 - a) * tile_cols : (h + 2 - a + step) * tile_cols,
                        (2 - b) * out_width : (3 - b) * out_width,
                    ],
                    kernel_ref[(3 * a + b) * in_width : (3 * a + b + 1) * in_width, :],
                    (((1,), (1,)), ((), ())),
                    preferred_element_type=f32,
                )
        out_ref[h * tile_cols : (h + step) * tile_cols, :] = total.astype(bf16)


def on_device(canvas, conv_weight, conv_bias, target_gram):
    tile_rows, tile_cols, in_width = canvas.shape
    out_width = conv_weight.shape[3]
    pixel_total = tile_rows * tile_cols * lax.axis_size("rows") * lax.axis_size("cols")
    shape = (tile_rows, tile_cols, in_width, out_width, 2)
    kernel = conv_weight.reshape(9 * in_width, out_width)
    params = pltpu.CompilerParams(vmem_limit_bytes=24 * 1024 * 1024)
    vmem = pl.BlockSpec(memory_space=pltpu.VMEM)
    packed_shape = jax.ShapeDtypeStruct((len(tile_pairs(out_width)) * tile, tile), f32)

    rim_shape = jax.ShapeDtypeStruct((2, tile_rows, in_width), bf16)
    begin, end = pl.pallas_call(
        rim_kernel,
        out_shape=(rim_shape, rim_shape),
        in_specs=[vmem],
        compiler_params=params,
        name="column_rims",
        cost_estimate=pl.CostEstimate(flops=4_000_000_000, bytes_accessed=600_000, transcendentals=0),
    )(canvas)
    left, right = shift_cols(end, begin)

    def payload(r):
        rim = [part[c, r + k] for k in range(2) for part in (left, right) for c in range(2)]
        main = canvas[r : r + 2].reshape(2 * tile_cols, in_width)
        return jnp.concatenate([main, jnp.stack(rim)], axis=0)

    low, high = shift_rows(payload(tile_rows - 2), payload(0))

    inner = (tile_rows - 2) * tile_cols
    in_feat, in_slope, in_gram, bias, target = pl.pallas_call(
        functools.partial(inner_kernel, shape),
        out_shape=(
            jax.ShapeDtypeStruct((inner, out_width), bf16),
            jax.ShapeDtypeStruct((inner, out_width), bf16),
            packed_shape,
            jax.ShapeDtypeStruct((1, out_width), f32),
            jax.ShapeDtypeStruct(target_gram.shape, bf16),
        ),
        in_specs=[vmem] * 6,
        scratch_shapes=[pltpu.VMEM((tile_rows * tile_cols, 3 * in_width), bf16)],
        compiler_params=params,
        name="inner_rows",
        cost_estimate=pl.CostEstimate(
            flops=2 * inner * (9 * in_width + out_width) * out_width,
            bytes_accessed=6_000_000,
            transcendentals=inner * out_width,
        ),
    )(canvas, left, right, kernel, conv_bias, target_gram)

    outer = 4 * tile_cols + 2 * edge
    out_feat, out_slope, gram = pl.pallas_call(
        functools.partial(outer_kernel, shape),
        out_shape=(
            jax.ShapeDtypeStruct((outer, out_width), bf16),
            jax.ShapeDtypeStruct((outer, out_width), bf16),
            packed_shape,
        ),
        in_specs=[vmem] * 8,
        scratch_shapes=[
            pltpu.VMEM((8 * tile_cols, 3 * in_width), bf16),
            pltpu.VMEM((2 * edge, 9 * in_width), bf16),
        ],
        compiler_params=params,
        name="outer_rows",
    )(canvas, low, high, left, right, kernel, bias, in_gram)

    packed, target_full = sum_and_gather(gram, target)

    own_gram, grad = pl.pallas_call(
        functools.partial(backward_kernel, shape, pixel_total),
        out_shape=(
            jax.ShapeDtypeStruct(target_gram.shape, f32),
            jax.ShapeDtypeStruct((tile_rows * tile_cols, in_width), bf16),
        ),
        in_specs=[vmem] * 7,
        scratch_shapes=[
            pltpu.VMEM((out_width, out_width), f32),
            pltpu.VMEM((out_width, out_width), bf16),
            pltpu.VMEM(((tile_rows + 2) * tile_cols, 3 * out_width), bf16),
        ],
        compiler_params=params,
        name="grad_conv",
    )(packed, target_full, in_feat, in_slope, out_feat, out_slope, kernel)
    return own_gram, grad.reshape(tile_rows, tile_cols, in_width)


def solution(mesh):
    return jax.shard_map(
        on_device,
        mesh=mesh,
        in_specs=(P("rows", "cols", None), P(), P(), P(("rows", "cols"), None)),
        out_specs=(P(("rows", "cols"), None), P("rows", "cols", None)),
        check_vma=False,
    )
```

```python
import functools
import math

import jax
import jax.numpy as jnp
from jax import lax
from jax.experimental import pallas as pl
from jax.experimental.pallas import tpu as pltpu
from jax.sharding import PartitionSpec as P

gelu_scale = math.sqrt(2.0 / math.pi)
tile = 128
edge = 16
f32, bf16 = jnp.float32, jnp.bfloat16


def tile_pairs(width):
    count = width // tile
    return [(i, j) for i in range(count) for j in range(i, count)]


def shift_rows(last, first):
    count = lax.axis_size("rows")
    forward = [(i, i + 1) for i in range(count - 1)]
    backward = [(target, source) for source, target in forward]
    return lax.ppermute(last, "rows", forward), lax.ppermute(first, "rows", backward)


def shift_cols(last, first):
    count = lax.axis_size("cols")
    forward = [(i, i + 1) for i in range(count - 1)]
    backward = [(target, source) for source, target in forward]
    return lax.ppermute(last, "cols", forward), lax.ppermute(first, "cols", backward)


def device_index():
    return lax.axis_index("rows") * lax.axis_size("cols") + lax.axis_index("cols")


def swap(value, bit):
    total = lax.axis_size("rows") * lax.axis_size("cols")
    return lax.ppermute(value, ("rows", "cols"), [(i, i ^ (1 << bit)) for i in range(total)])


def local(body, out_shape, name, *operands, **kwargs):
    return pl.pallas_call(
        body,
        out_shape=out_shape,
        in_specs=[pl.BlockSpec(memory_space=pltpu.VMEM)] * len(operands),
        compiler_params=pltpu.CompilerParams(vmem_limit_bytes=8 * 1024 * 1024),
        name=name,
        **kwargs,
    )(*operands)


def side_of(bit):
    return lax.rem(device_index() // (1 << bit), 2)


def rows_at(index, count):
    return pl.ds(pl.multiple_of(index * count, count), count)


def halve(keep, got, bit):
    half = keep.shape[0] // 2

    def body(keep_ref, got_ref, send_ref, stay_ref):
        side = side_of(bit)
        away, here = rows_at(1 - side, half), rows_at(side, half)
        send_ref[...] = (keep_ref[away, :] + got_ref[away, :].astype(f32)).astype(bf16)
        stay_ref[...] = keep_ref[here, :] + got_ref[here, :].astype(f32)

    shape = (half, keep.shape[1])
    return local(
        body,
        (jax.ShapeDtypeStruct(shape, bf16), jax.ShapeDtypeStruct(shape, f32)),
        "halve",
        keep,
        got,
    )


def add(keep, got):
    def body(keep_ref, got_ref, sum_ref):
        sum_ref[...] = (keep_ref[...].astype(f32) + got_ref[...].astype(f32)).astype(bf16)

    return local(body, jax.ShapeDtypeStruct(got.shape, bf16), "add", keep, got)


def join(mine, other, bit):
    def body(mine_ref, other_ref, both_ref):
        side = side_of(bit)
        both_ref[:, pl.ds(side, 1)] = mine_ref[...][:, None]
        both_ref[:, pl.ds(1 - side, 1)] = other_ref[...][:, None]

    shape = (mine.shape[0], 2, *mine.shape[1:])
    return local(body, jax.ShapeDtypeStruct(shape, mine.dtype), "join", mine, other)


class Gather:
    def __init__(self, rows):
        self.rows, self.done = rows, []

    def step(self, bit, after):
        share = self.rows.shape[-2:]
        send, _ = lax.optimization_barrier((self.rows, after))
        got = swap(send, bit)
        lead = 1 << sum(other > bit for other in self.done)
        parts = [part.reshape(lead, -1, *share) for part in (send, got)]
        self.rows = join(*parts, bit).reshape(-1, *share)
        self.done.append(bit)


def sum_all(send, keep, gather, order):
    bits = (lax.axis_size("rows") * lax.axis_size("cols")).bit_length() - 1
    halving = list(range(min(3, bits)))
    order = list(order)

    def step(value, bit):
        beside = order.pop(0) if order else None
        got = swap(value, bit)
        if beside is not None:
            gather.step(beside, value)
        return got

    got = step(send, 0)
    for bit in halving[1:]:
        send, keep = halve(keep, got, bit)
        got = step(send, bit)
    mine = add(keep, got)
    for bit in range(len(halving), bits):
        mine = add(mine, step(mine, bit))
    for bit in reversed(halving[1:]):
        got = step(mine, bit)
        mine = join(mine[None], got[None], bit).reshape(-1, mine.shape[1])
    return mine, step(mine, 0), order


def gelu_pair(value):
    square = value * value
    tangent = jnp.tanh(value * (gelu_scale + gelu_scale * 0.044715 * square))
    half = 0.5 * value
    plus = 0.5 + 0.5 * tangent
    grad = plus + half * (1.0 - tangent * tangent) * (
        gelu_scale + gelu_scale * 3.0 * 0.044715 * square
    )
    return value * plus, grad


def column(value, c):
    return jnp.concatenate([value[r, c : c + 1] for r in range(value.shape[0])], axis=0)


def rim_kernel(canvas_ref, *out_refs):
    cols = canvas_ref.shape[1]
    begin = canvas_ref[:, 0:16, :].astype(f32)
    end = canvas_ref[:, cols - 16 :, :].astype(f32)
    for c in range(2):
        pair = column(begin, c), column(end, 14 + c)
        if len(out_refs) == 1:
            out_refs[0][c] = jnp.where(lax.axis_index("cols") == 0, pair[1], pair[0]).astype(bf16)
        else:
            out_refs[0][c], out_refs[1][c] = pair[0].astype(bf16), pair[1].astype(bf16)


def payload_kernel(canvas_ref, *refs):
    first_ref, last_ref, left_ref, right_ref = refs[-4:]
    rows, cols, width = canvas_ref.shape
    if len(refs) == 5:
        here = lax.axis_index("cols")
        other = refs[0][...].astype(f32)
        left_ref[...] = jnp.where(here == 0, 0.0, other).astype(bf16)
        right_ref[...] = jnp.where(here == 0, other, 0.0).astype(bf16)
    else:
        left_ref[...], right_ref[...] = refs[0][...], refs[1][...]
    beyond = [ref[c].astype(f32) for ref in (left_ref, right_ref) for c in range(2)]
    for ref, r in ((first_ref, 0), (last_ref, rows - 2)):
        for k in range(2):
            ref[k * cols : (k + 1) * cols, :] = canvas_ref[r + k]
        rim = [part[r + k : r + k + 1] for k in range(2) for part in beyond]
        rim = jnp.concatenate([*rim, jnp.zeros((8, width), f32)], axis=0)
        ref[2 * cols :, :] = rim.astype(bf16)


def fill_row(cat_ref, r, row, before, after):
    cols, width = row.shape
    wide = row.astype(f32)
    place = lax.broadcasted_iota(jnp.int32, (cols, width), 0)
    at = slice(r * cols, (r + 1) * cols)
    moved = jnp.where(place == 0, before, pltpu.roll(wide, 1, 0))
    cat_ref[at, 0:width] = moved.astype(bf16)
    cat_ref[at, width : 2 * width] = row.astype(bf16)
    moved = jnp.where(place == cols - 1, after, pltpu.roll(wide, cols - 1, 0))
    cat_ref[at, 2 * width : 3 * width] = moved.astype(bf16)


def gram_tiles(feat, gram_ref, base_ref=None):
    width = feat.shape[1]
    half = width // 2
    product = functools.partial(
        lax.dot_general,
        dimension_numbers=(((0,), (0,)), ((), ())),
        preferred_element_type=f32,
    )
    upper = product(feat[:, :half], feat)
    lower = product(feat[:, half:], feat[:, half:])
    for n, (i, j) in enumerate(tile_pairs(width)):
        at = slice(n * tile, (n + 1) * tile)
        if i * tile < half:
            part = upper[i * tile : (i + 1) * tile, j * tile : (j + 1) * tile]
        else:
            k, m = i * tile - half, j * tile - half
            part = lower[k : k + tile, m : m + tile]
        gram_ref[at, :] = part if base_ref is None else part + base_ref[at, :]


def inner_kernel(
    shape, own_ref, left_ref, right_ref, kernel_ref, bias_ref,
    feat_ref, slope_ref, gram_ref, row_ref, cat_ref,
):
    row_ref[...] = bias_ref[...].astype(f32).reshape(row_ref.shape)
    tile_rows, tile_cols, in_width, out_width, step = shape
    lefts, rights = left_ref[1].astype(f32), right_ref[0].astype(f32)
    for r in range(tile_rows):
        fill_row(cat_ref, r, own_ref[r], lefts[r : r + 1], rights[r : r + 1])
    bias = row_ref[...]
    root = 1.0 / math.sqrt(out_width)
    span = 3 * in_width
    for h in range(0, tile_rows - 2, step):
        total = bias
        for a in range(3):
            total = total + jnp.dot(
                cat_ref[(h + a) * tile_cols : (h + a + step) * tile_cols, :],
                kernel_ref[a * span : (a + 1) * span, :],
                preferred_element_type=f32,
            )
        features, slope = gelu_pair(total)
        at = slice(h * tile_cols, (h + step) * tile_cols)
        feat_ref[at, :] = features.astype(bf16)
        slope_ref[at, :] = (slope * root).astype(bf16)
    gram_tiles(feat_ref[...], gram_ref)


def outer_kernel(
    shape, own_ref, low_ref, high_ref, left_ref, right_ref, kernel_ref, bias_ref, base_ref,
    feat_ref, slope_ref, send_ref, keep_ref, cat_ref, edge_ref, gram_ref,
):
    tile_rows, tile_cols, in_width, out_width, step = shape
    first = (lax.axis_index("rows") > 0).astype(f32)
    last = (lax.axis_index("rows") < lax.axis_size("rows") - 1).astype(f32)
    left = (lax.axis_index("cols") > 0).astype(f32)
    right = (lax.axis_index("cols") < lax.axis_size("cols") - 1).astype(f32)
    main = 2 * tile_cols
    low_rim, high_rim = low_ref[main:, :].astype(f32), high_ref[main:, :].astype(f32)
    own_begin = column(own_ref[:, 0:16, :].astype(f32), 0)
    own_end = column(own_ref[:, tile_cols - 16 :, :].astype(f32), 15)

    def sides(c, own):
        return jnp.concatenate(
            [low_rim[c : c + 1], low_rim[4 + c : 5 + c], own, high_rim[c : c + 1], high_rim[4 + c : 5 + c]],
            axis=0,
        )

    def ends(c, own):
        c16 = c // 16 * 16
        piece = lambda ref, k: ref[k + c16 : k + c16 + 16, :].astype(f32)[c - c16 : c - c16 + 1]
        rows = [piece(low_ref, 0), piece(low_ref, tile_cols), own]
        return jnp.concatenate([*rows, piece(high_ref, 0), piece(high_ref, tile_cols)], axis=0)

    lefts = [
        sides(0, left_ref[0].astype(f32)), sides(1, left_ref[1].astype(f32)), ends(0, own_begin)
    ]
    rights = [
        ends(tile_cols - 1, own_end), sides(2, right_ref[0].astype(f32)), sides(3, right_ref[1].astype(f32))
    ]
    span = 3 * in_width
    lines = [0, 1, 2, 3, tile_rows, tile_rows + 1, tile_rows + 2, tile_rows + 3]
    for r, line in enumerate(lines):
        if line < 2:
            row = low_ref[line * tile_cols : (line + 1) * tile_cols, :]
        elif line < tile_rows + 2:
            row = own_ref[line - 2]
        else:
            k = line - tile_rows - 2
            row = high_ref[k * tile_cols : (k + 1) * tile_cols, :]
        fill_row(cat_ref, r, row, lefts[1][line : line + 1], rights[1][line : line + 1])
    blank = jnp.zeros((edge - tile_rows - 2, in_width), f32)
    for a in range(3):
        for b in range(3):
            piece = jnp.concatenate(
                [lefts[b][a : a + tile_rows + 2], blank, rights[b][a : a + tile_rows + 2], blank],
                axis=0,
            )
            at = (3 * a + b) * in_width
            edge_ref[:, at : at + in_width] = piece.astype(bf16)
    bias = bias_ref[...]
    root = 1.0 / math.sqrt(out_width)
    totals = [bias, bias, bias]
    for a in range(3):
        weights = kernel_ref[a * span : (a + 1) * span, :]
        for k in range(2):
            totals[k] = totals[k] + jnp.dot(
                cat_ref[(4 * k + a) * tile_cols : (4 * k + a + 2) * tile_cols, :],
                weights,
                preferred_element_type=f32,
            )
        totals[2] = totals[2] + jnp.dot(
            edge_ref[:, a * span : (a + 1) * span], weights, preferred_element_type=f32
        )
    for k in range(2):
        features, slope = gelu_pair(totals[k])
        slope = slope * root
        at = k * main
        feat_ref[at : at + main, :] = features.astype(bf16)
        scale = (first, 1.0) if k == 0 else (1.0, last)
        slope_ref[at : at + tile_cols, :] = (slope[:tile_cols] * scale[0]).astype(bf16)
        slope_ref[at + tile_cols : at + main, :] = (slope[tile_cols:] * scale[1]).astype(bf16)
    features, slope = gelu_pair(totals[2])
    line = lax.broadcasted_iota(jnp.int32, (2 * edge, out_width), 0)
    weight = jnp.where(line < edge, left, right)
    weight = jnp.where(line % edge == 0, weight * first, weight)
    weight = jnp.where(line % edge == tile_rows + 1, weight * last, weight)
    feat_ref[2 * main :, :] = features.astype(bf16)
    slope_ref[2 * main :, :] = (slope * root * weight).astype(bf16)
    gram_tiles(feat_ref[tile_cols : 3 * tile_cols, :], gram_ref, base_ref)
    half = send_ref.shape[0]
    side = side_of(0)
    send_ref[...] = gram_ref[rows_at(1 - side, half), :].astype(bf16)
    keep_ref[...] = gram_ref[rows_at(side, half), :]


def backward_kernel(
    shape, pixel_total, mine_ref, other_ref, target_ref, in_feat_ref, in_slope_ref, out_feat_ref, out_slope_ref,
    kernel_ref, own_gram_ref, out_ref, gram_ref, full_ref, sym_ref, cat_ref,
):
    tile_rows, tile_cols, in_width, out_width, step = shape
    half = mine_ref.shape[0]
    side = side_of(0)
    gram_ref[rows_at(side, half), :] = mine_ref[...].astype(f32)
    gram_ref[rows_at(1 - side, half), :] = other_ref[...].astype(f32)
    for n, (i, j) in enumerate(tile_pairs(out_width)):
        at_i, at_j = slice(i * tile, (i + 1) * tile), slice(j * tile, (j + 1) * tile)
        gram = gram_ref[n * tile : (n + 1) * tile, :] * (1.0 / pixel_total)
        both = 2.0 * gram - (target_ref[at_i, at_j].astype(f32) + target_ref[at_j, at_i].astype(f32).T)
        full_ref[at_i, at_j] = gram
        sym_ref[at_i, at_j] = both.astype(bf16)
        if i != j:
            full_ref[at_j, at_i] = gram.T
            sym_ref[at_j, at_i] = both.T.astype(bf16)
    share = own_gram_ref.shape[0]
    start = device_index() * share
    if share % 8 == 0:
        own_gram_ref[...] = full_ref[pl.ds(pl.multiple_of(start, 8), share), :]
    else:
        group = full_ref[pl.ds(pl.multiple_of(start // 8 * 8, 8), 8), :]
        picked = group[0:share]
        for k in range(share, 8, share):
            picked = jnp.where(start % 8 == k, group[k : k + share], picked)
        own_gram_ref[...] = picked

    def grad_of(feat_ref, slope_ref, at):
        product = jnp.dot(feat_ref[at, :], sym_ref[...], preferred_element_type=f32)
        return product * slope_ref[at, :].astype(f32)

    main = 2 * tile_cols
    edges = grad_of(out_feat_ref, out_slope_ref, slice(2 * main, None))
    lines = [
        (out_feat_ref, out_slope_ref, 0, 0),
        (out_feat_ref, out_slope_ref, main, tile_rows),
    ] + [
        (in_feat_ref, in_slope_ref, h * tile_cols, h + 2) for h in range(0, tile_rows - 2, step)
    ]
    for feat_ref, slope_ref, begin, r in lines:
        grad = grad_of(feat_ref, slope_ref, slice(begin, begin + step * tile_cols))
        for k in range(step):
            fill_row(
                cat_ref, r + k, grad[k * tile_cols : (k + 1) * tile_cols],
                edges[r + k : r + k + 1], edges[edge + r + k : edge + r + k + 1],
            )
    for h in range(0, tile_rows, step):
        total = jnp.zeros((step * tile_cols, in_width), f32)
        for a in range(3):
            for b in range(3):
                total = total + lax.dot_general(
                    cat_ref[
                        (h + 2 - a) * tile_cols : (h + 2 - a + step) * tile_cols,
                        (2 - b) * out_width : (3 - b) * out_width,
                    ],
                    kernel_ref[(3 * a + b) * in_width : (3 * a + b + 1) * in_width, :],
                    (((1,), (1,)), ((), ())),
                    preferred_element_type=f32,
                )
        out_ref[h * tile_cols : (h + step) * tile_cols, :] = total.astype(bf16)


def on_device(canvas, conv_weight, conv_bias, target_gram):
    tile_rows, tile_cols, in_width = canvas.shape
    out_width = conv_weight.shape[3]
    pixel_total = tile_rows * tile_cols * lax.axis_size("rows") * lax.axis_size("cols")
    shape = (tile_rows, tile_cols, in_width, out_width, 2)
    kernel = conv_weight.reshape(9 * in_width, out_width)
    params = pltpu.CompilerParams(vmem_limit_bytes=24 * 1024 * 1024)
    vmem = pl.BlockSpec(memory_space=pltpu.VMEM)
    packed_shape = jax.ShapeDtypeStruct((len(tile_pairs(out_width)) * tile, tile), f32)

    bits = (lax.axis_size("rows") * lax.axis_size("cols")).bit_length() - 1
    rim_shape = jax.ShapeDtypeStruct((2, tile_rows, in_width), bf16)
    two = lax.axis_size("cols") == 2
    rims = local(
        rim_kernel,
        (rim_shape,) * (1 if two else 2),
        "column_rims",
        canvas,
        cost_estimate=pl.CostEstimate(flops=4_000_000_000, bytes_accessed=600_000, transcendentals=0),
    )
    if two:
        beyond = [lax.ppermute(rims[0], "cols", [(0, 1), (1, 0)])]
    else:
        beyond = shift_cols(rims[1], rims[0])
    payload_shape = jax.ShapeDtypeStruct((2 * tile_cols + edge, in_width), bf16)
    first, last, left, right = local(
        payload_kernel, (payload_shape, payload_shape, rim_shape, rim_shape), "row_payload", canvas, *beyond
    )
    low, high = shift_rows(last, first)
    gather = Gather(target_gram.astype(bf16)[None])
    gather.step(bits - 1, first)

    inner = (tile_rows - 2) * tile_cols
    in_feat, in_slope, in_gram, bias = pl.pallas_call(
        functools.partial(inner_kernel, shape),
        out_shape=(
            jax.ShapeDtypeStruct((inner, out_width), bf16),
            jax.ShapeDtypeStruct((inner, out_width), bf16),
            packed_shape,
            jax.ShapeDtypeStruct((1, out_width), f32),
        ),
        in_specs=[vmem] * 5,
        scratch_shapes=[pltpu.VMEM((tile_rows * tile_cols, 3 * in_width), bf16)],
        compiler_params=params,
        name="inner_rows",
        cost_estimate=pl.CostEstimate(
            flops=2 * inner * (9 * in_width + out_width) * out_width,
            bytes_accessed=6_000_000,
            transcendentals=inner * out_width,
        ),
    )(canvas, left, right, kernel, conv_bias)

    outer = 4 * tile_cols + 2 * edge
    half_shape = (packed_shape.shape[0] // 2, tile)
    out_feat, out_slope, send, keep = pl.pallas_call(
        functools.partial(outer_kernel, shape),
        out_shape=(
            jax.ShapeDtypeStruct((outer, out_width), bf16),
            jax.ShapeDtypeStruct((outer, out_width), bf16),
            jax.ShapeDtypeStruct(half_shape, bf16),
            jax.ShapeDtypeStruct(half_shape, f32),
        ),
        in_specs=[vmem] * 8,
        scratch_shapes=[
            pltpu.VMEM((8 * tile_cols, 3 * in_width), bf16),
            pltpu.VMEM((2 * edge, 9 * in_width), bf16),
            pltpu.VMEM(packed_shape.shape, f32),
        ],
        compiler_params=params,
        name="outer_rows",
    )(canvas, low, high, left, right, kernel, bias, in_gram)

    rest = [bit for bit in range(bits - 2, 2, -1)]
    order = [*rest, *([None] * max(0, 2 - len(rest))), 1, 2, 0]
    mine, other, left_over = sum_all(send, keep, gather, order)
    for bit in left_over:
        gather.step(bit, other)
    target_full = gather.rows.reshape(out_width, out_width)

    own_gram, grad = pl.pallas_call(
        functools.partial(backward_kernel, shape, pixel_total),
        out_shape=(
            jax.ShapeDtypeStruct(target_gram.shape, f32),
            jax.ShapeDtypeStruct((tile_rows * tile_cols, in_width), bf16),
        ),
        in_specs=[vmem] * 8,
        scratch_shapes=[
            pltpu.VMEM(packed_shape.shape, f32),
            pltpu.VMEM((out_width, out_width), f32),
            pltpu.VMEM((out_width, out_width), bf16),
            pltpu.VMEM(((tile_rows + 2) * tile_cols, 3 * out_width), bf16),
        ],
        compiler_params=params,
        name="grad_conv",
    )(mine, other, target_full, in_feat, in_slope, out_feat, out_slope, kernel)
    return own_gram, grad.reshape(tile_rows, tile_cols, in_width)


def solution(mesh):
    return jax.shard_map(
        on_device,
        mesh=mesh,
        in_specs=(P("rows", "cols", None), P(), P(), P(("rows", "cols"), None)),
        out_specs=(P(("rows", "cols"), None), P("rows", "cols", None)),
        check_vma=False,
    )
```

```python
import functools
import math

import jax
import jax.numpy as jnp
from jax import lax
from jax.experimental import pallas as pl
from jax.experimental.pallas import tpu as pltpu
from jax.sharding import PartitionSpec as P

gelu_scale = math.sqrt(2.0 / math.pi)
tile = 128
edge = 16
f32, bf16 = jnp.float32, jnp.bfloat16


def tile_pairs(width):
    count = width // tile
    return [(i, j) for i in range(count) for j in range(i, count)]


def swap_rows(pairs, values):
    perm = lambda low: [(i, i + 1) for i in low] + [(i + 1, i) for i in low]
    return [lax.ppermute(value, "rows", perm(low)) for low, value in zip(pairs, values)]


def shift_cols(last, first):
    count = lax.axis_size("cols")
    forward = [(i, i + 1) for i in range(count - 1)]
    backward = [(target, source) for source, target in forward]
    return lax.ppermute(last, "cols", forward), lax.ppermute(first, "cols", backward)


def device_index():
    return lax.axis_index("rows") * lax.axis_size("cols") + lax.axis_index("cols")


def swap(value, bit, core=None):
    total = lax.axis_size("rows") * lax.axis_size("cols")
    perm = [(i, i ^ (1 << bit)) for i in range(total) if core is None or i % 2 == core]
    return lax.ppermute(value, ("rows", "cols"), perm)


def hand_over(value, core):
    total = lax.axis_size("rows") * lax.axis_size("cols")
    perm = [(i, i ^ 1) for i in range(total) if i % 2 == core]
    return lax.ppermute(value, ("rows", "cols"), perm)


def local(body, out_shape, name, *operands, **kwargs):
    return pl.pallas_call(
        body,
        out_shape=out_shape,
        in_specs=[pl.BlockSpec(memory_space=pltpu.VMEM)] * len(operands),
        compiler_params=pltpu.CompilerParams(vmem_limit_bytes=8 * 1024 * 1024),
        name=name,
        **kwargs,
    )(*operands)


def side_of(bit):
    return lax.rem(device_index() // (1 << bit), 2)


def rows_at(index, count):
    return pl.ds(pl.multiple_of(index * count, count), count)


def halve(keep, got, bit):
    half = keep.shape[0] // 2

    def body(keep_ref, got_ref, send_ref, stay_ref):
        side = side_of(bit)
        away, here = rows_at(1 - side, half), rows_at(side, half)
        send_ref[...] = (keep_ref[away, :] + got_ref[away, :].astype(f32)).astype(bf16)
        stay_ref[...] = keep_ref[here, :] + got_ref[here, :].astype(f32)

    shape = (half, keep.shape[1])
    return local(
        body,
        (jax.ShapeDtypeStruct(shape, bf16), jax.ShapeDtypeStruct(shape, f32)),
        "halve",
        keep,
        got,
    )


def add(keep, got):
    def body(keep_ref, got_ref, sum_ref):
        sum_ref[...] = (keep_ref[...].astype(f32) + got_ref[...].astype(f32)).astype(bf16)

    return local(body, jax.ShapeDtypeStruct(got.shape, bf16), "add", keep, got)


def join(mine, other, bit):
    def body(mine_ref, other_ref, both_ref):
        side = side_of(bit)
        both_ref[:, pl.ds(side, 1)] = mine_ref[...][:, None]
        both_ref[:, pl.ds(1 - side, 1)] = other_ref[...][:, None]

    shape = (mine.shape[0], 2, *mine.shape[1:])
    return local(body, jax.ShapeDtypeStruct(shape, mine.dtype), "join", mine, other)


def gather_step(rows, bit, after, core=None):
    share = rows.shape[-2:]
    send, _ = lax.optimization_barrier((rows, after))
    got = swap(send, bit, core)
    lead = max(1, rows.shape[0] // 2)
    return join(send.reshape(lead, -1, *share), got.reshape(lead, -1, *share), bit).reshape(-1, *share)


def sum_all(send, keep, rows):
    bits = (lax.axis_size("rows") * lax.axis_size("cols")).bit_length() - 1
    halving = list(range(1, min(3, bits)))
    order = list(reversed(range(1, bits)))

    def step(value, bit):
        nonlocal rows
        got = swap(value, bit, 1)
        if order:
            rows = gather_step(rows, order.pop(0), value, 0)
        return got

    got = hand_over(send, 0)
    for bit in halving:
        send, keep = halve(keep, got, bit)
        got = step(send, bit)
    mine = add(keep, got)
    for bit in range(len(halving) + 1, bits):
        mine = add(mine, step(mine, bit))
    for bit in reversed(halving):
        before = mine
        mine = join(mine[None], step(mine, bit)[None], bit).reshape(-1, mine.shape[1])
    rows, _ = lax.optimization_barrier((rows, before))
    return mine, hand_over(mine, 1), rows, hand_over(rows, 0)


def gelu_pair(value):
    square = value * value
    tangent = jnp.tanh(value * (gelu_scale + gelu_scale * 0.044715 * square))
    half = 0.5 * value
    plus = 0.5 + 0.5 * tangent
    grad = plus + half * (1.0 - tangent * tangent) * (
        gelu_scale + gelu_scale * 3.0 * 0.044715 * square
    )
    return value * plus, grad


def column(value, c):
    return jnp.concatenate([value[r, c : c + 1] for r in range(value.shape[0])], axis=0)


def rim_kernel(canvas_ref, *out_refs):
    cols = canvas_ref.shape[1]
    begin = canvas_ref[:, 0:16, :].astype(f32)
    end = canvas_ref[:, cols - 16 :, :].astype(f32)
    for c in range(2):
        pair = column(begin, c), column(end, 14 + c)
        if len(out_refs) == 1:
            out_refs[0][c] = jnp.where(lax.axis_index("cols") == 0, pair[1], pair[0]).astype(bf16)
        else:
            out_refs[0][c], out_refs[1][c] = pair[0].astype(bf16), pair[1].astype(bf16)


def payload_kernel(canvas_ref, target_ref, *refs):
    even_ref, odd_ref, left_ref, right_ref, half_ref = refs[-5:]
    rows, cols, width = canvas_ref.shape
    half_ref[0] = target_ref[...].astype(bf16)
    if len(refs) == 6:
        here = lax.axis_index("cols")
        other = refs[0][...].astype(f32)
        left_ref[...] = jnp.where(here == 0, 0.0, other).astype(bf16)
        right_ref[...] = jnp.where(here == 0, other, 0.0).astype(bf16)
    else:
        left_ref[...], right_ref[...] = refs[0][...], refs[1][...]
    beyond = [ref[c].astype(f32) for ref in (left_ref, right_ref) for c in range(2)]

    def fill(ref, r):
        for k in range(2):
            ref[k * cols : (k + 1) * cols, :] = canvas_ref[r + k]
        rim = [part[r + k : r + k + 1] for k in range(2) for part in beyond]
        rim = jnp.concatenate([*rim, jnp.zeros((8, width), f32)], axis=0)
        ref[2 * cols :, :] = rim.astype(bf16)

    odd = lax.rem(lax.axis_index("rows"), 2)

    @pl.when(odd == 0)
    def _():
        fill(even_ref, rows - 2)
        fill(odd_ref, 0)

    @pl.when(odd == 1)
    def _():
        fill(even_ref, 0)
        fill(odd_ref, rows - 2)


def fill_row(cat_ref, r, row, before, after):
    cols, width = row.shape
    wide = row.astype(f32)
    place = lax.broadcasted_iota(jnp.int32, (cols, width), 0)
    at = slice(r * cols, (r + 1) * cols)
    moved = jnp.where(place == 0, before, pltpu.roll(wide, 1, 0))
    cat_ref[at, 0:width] = moved.astype(bf16)
    cat_ref[at, width : 2 * width] = row.astype(bf16)
    moved = jnp.where(place == cols - 1, after, pltpu.roll(wide, cols - 1, 0))
    cat_ref[at, 2 * width : 3 * width] = moved.astype(bf16)


def gram_tiles(feat, gram_ref, base_ref=None):
    width = feat.shape[1]
    half = width // 2
    product = functools.partial(
        lax.dot_general,
        dimension_numbers=(((0,), (0,)), ((), ())),
        preferred_element_type=f32,
    )
    upper = product(feat[:, :half], feat)
    lower = product(feat[:, half:], feat[:, half:])
    for n, (i, j) in enumerate(tile_pairs(width)):
        at = slice(n * tile, (n + 1) * tile)
        if i * tile < half:
            part = upper[i * tile : (i + 1) * tile, j * tile : (j + 1) * tile]
        else:
            k, m = i * tile - half, j * tile - half
            part = lower[k : k + tile, m : m + tile]
        gram_ref[at, :] = part if base_ref is None else part + base_ref[at, :]


def inner_kernel(
    shape, own_ref, left_ref, right_ref, kernel_ref, bias_ref,
    feat_ref, slope_ref, gram_ref, row_ref, cat_ref,
):
    row_ref[...] = bias_ref[...].astype(f32).reshape(row_ref.shape)
    tile_rows, tile_cols, in_width, out_width, step = shape
    lefts, rights = left_ref[1].astype(f32), right_ref[0].astype(f32)
    for r in range(tile_rows):
        fill_row(cat_ref, r, own_ref[r], lefts[r : r + 1], rights[r : r + 1])
    bias = row_ref[...]
    root = 1.0 / math.sqrt(out_width)
    span = 3 * in_width
    for h in range(0, tile_rows - 2, step):
        total = bias
        for a in range(3):
            total = total + jnp.dot(
                cat_ref[(h + a) * tile_cols : (h + a + step) * tile_cols, :],
                kernel_ref[a * span : (a + 1) * span, :],
                preferred_element_type=f32,
            )
        features, slope = gelu_pair(total)
        at = slice(h * tile_cols, (h + step) * tile_cols)
        feat_ref[at, :] = features.astype(bf16)
        slope_ref[at, :] = (slope * root).astype(bf16)
    gram_tiles(feat_ref[...], gram_ref)


def outer_kernel(
    shape, own_ref, even_ref, odd_ref, left_ref, right_ref, kernel_ref, bias_ref, base_ref,
    feat_ref, slope_ref, send_ref, keep_ref, cat_ref, edge_ref, low_ref, high_ref,
):
    tile_rows, tile_cols, in_width, out_width, step = shape
    odd = lax.rem(lax.axis_index("rows"), 2)
    low_ref[...] = jnp.where(odd == 0, odd_ref[...], even_ref[...])
    high_ref[...] = jnp.where(odd == 0, even_ref[...], odd_ref[...])
    first = (lax.axis_index("rows") > 0).astype(f32)
    last = (lax.axis_index("rows") < lax.axis_size("rows") - 1).astype(f32)
    left = (lax.axis_index("cols") > 0).astype(f32)
    right = (lax.axis_index("cols") < lax.axis_size("cols") - 1).astype(f32)
    main = 2 * tile_cols
    low_rim, high_rim = low_ref[main:, :].astype(f32), high_ref[main:, :].astype(f32)
    own_begin = column(own_ref[:, 0:16, :].astype(f32), 0)
    own_end = column(own_ref[:, tile_cols - 16 :, :].astype(f32), 15)

    def sides(c, own):
        return jnp.concatenate(
            [low_rim[c : c + 1], low_rim[4 + c : 5 + c], own, high_rim[c : c + 1], high_rim[4 + c : 5 + c]],
            axis=0,
        )

    def ends(c, own):
        c16 = c // 16 * 16
        piece = lambda ref, k: ref[k + c16 : k + c16 + 16, :].astype(f32)[c - c16 : c - c16 + 1]
        rows = [piece(low_ref, 0), piece(low_ref, tile_cols), own]
        return jnp.concatenate([*rows, piece(high_ref, 0), piece(high_ref, tile_cols)], axis=0)

    lefts = [
        sides(0, left_ref[0].astype(f32)), sides(1, left_ref[1].astype(f32)), ends(0, own_begin)
    ]
    rights = [
        ends(tile_cols - 1, own_end), sides(2, right_ref[0].astype(f32)), sides(3, right_ref[1].astype(f32))
    ]
    span = 3 * in_width
    lines = [0, 1, 2, 3, tile_rows, tile_rows + 1, tile_rows + 2, tile_rows + 3]
    for r, line in enumerate(lines):
        if line < 2:
            row = low_ref[line * tile_cols : (line + 1) * tile_cols, :]
        elif line < tile_rows + 2:
            row = own_ref[line - 2]
        else:
            k = line - tile_rows - 2
            row = high_ref[k * tile_cols : (k + 1) * tile_cols, :]
        fill_row(cat_ref, r, row, lefts[1][line : line + 1], rights[1][line : line + 1])
    blank = jnp.zeros((edge - tile_rows - 2, in_width), f32)
    for a in range(3):
        for b in range(3):
            piece = jnp.concatenate(
                [lefts[b][a : a + tile_rows + 2], blank, rights[b][a : a + tile_rows + 2], blank],
                axis=0,
            )
            at = (3 * a + b) * in_width
            edge_ref[:, at : at + in_width] = piece.astype(bf16)
    bias = bias_ref[...]
    root = 1.0 / math.sqrt(out_width)
    totals = [bias, bias, bias]
    for a in range(3):
        weights = kernel_ref[a * span : (a + 1) * span, :]
        for k in range(2):
            totals[k] = totals[k] + jnp.dot(
                cat_ref[(4 * k + a) * tile_cols : (4 * k + a + 2) * tile_cols, :],
                weights,
                preferred_element_type=f32,
            )
        totals[2] = totals[2] + jnp.dot(
            edge_ref[:, a * span : (a + 1) * span], weights, preferred_element_type=f32
        )
    for k in range(2):
        features, slope = gelu_pair(totals[k])
        slope = slope * root
        at = k * main
        feat_ref[at : at + main, :] = features.astype(bf16)
        scale = (first, 1.0) if k == 0 else (1.0, last)
        slope_ref[at : at + tile_cols, :] = (slope[:tile_cols] * scale[0]).astype(bf16)
        slope_ref[at + tile_cols : at + main, :] = (slope[tile_cols:] * scale[1]).astype(bf16)
    features, slope = gelu_pair(totals[2])
    line = lax.broadcasted_iota(jnp.int32, (2 * edge, out_width), 0)
    weight = jnp.where(line < edge, left, right)
    weight = jnp.where(line % edge == 0, weight * first, weight)
    weight = jnp.where(line % edge == tile_rows + 1, weight * last, weight)
    feat_ref[2 * main :, :] = features.astype(bf16)
    slope_ref[2 * main :, :] = (slope * root * weight).astype(bf16)
    gram_tiles(feat_ref[tile_cols : 3 * tile_cols, :], keep_ref, base_ref)
    send_ref[...] = keep_ref[...].astype(bf16)


def backward_kernel(
    shape, pixel_total, mine_ref, other_ref, rows_ref, other_rows_ref, in_feat_ref, in_slope_ref, out_feat_ref, out_slope_ref,
    kernel_ref, own_gram_ref, out_ref, target_ref, full_ref, sym_ref, cat_ref,
):
    tile_rows, tile_cols, in_width, out_width, step = shape
    core = side_of(0)
    target_ref[...] = jnp.where(core == 0, rows_ref[...], other_rows_ref[...])
    for n, (i, j) in enumerate(tile_pairs(out_width)):
        at_i, at_j = slice(i * tile, (i + 1) * tile), slice(j * tile, (j + 1) * tile)
        at = slice(n * tile, (n + 1) * tile)
        gram = jnp.where(core == 1, mine_ref[at, :], other_ref[at, :]).astype(f32) * (1.0 / pixel_total)
        both = 2.0 * gram - (target_ref[at_i, at_j].astype(f32) + target_ref[at_j, at_i].astype(f32).T)
        full_ref[at_i, at_j] = gram
        sym_ref[at_i, at_j] = both.astype(bf16)
        if i != j:
            full_ref[at_j, at_i] = gram.T
            sym_ref[at_j, at_i] = both.T.astype(bf16)
    share = own_gram_ref.shape[0]
    start = device_index() * share
    if share % 8 == 0:
        own_gram_ref[...] = full_ref[pl.ds(pl.multiple_of(start, 8), share), :]
    else:
        group = full_ref[pl.ds(pl.multiple_of(start // 8 * 8, 8), 8), :]
        picked = group[0:share]
        for k in range(share, 8, share):
            picked = jnp.where(start % 8 == k, group[k : k + share], picked)
        own_gram_ref[...] = picked

    def grad_of(feat_ref, slope_ref, at):
        product = jnp.dot(feat_ref[at, :], sym_ref[...], preferred_element_type=f32)
        return product * slope_ref[at, :].astype(f32)

    main = 2 * tile_cols
    edges = grad_of(out_feat_ref, out_slope_ref, slice(2 * main, None))
    lines = [
        (out_feat_ref, out_slope_ref, 0, 0),
        (out_feat_ref, out_slope_ref, main, tile_rows),
    ] + [
        (in_feat_ref, in_slope_ref, h * tile_cols, h + 2) for h in range(0, tile_rows - 2, step)
    ]
    for feat_ref, slope_ref, begin, r in lines:
        grad = grad_of(feat_ref, slope_ref, slice(begin, begin + step * tile_cols))
        for k in range(step):
            fill_row(
                cat_ref, r + k, grad[k * tile_cols : (k + 1) * tile_cols],
                edges[r + k : r + k + 1], edges[edge + r + k : edge + r + k + 1],
            )
    for h in range(0, tile_rows, step):
        total = jnp.zeros((step * tile_cols, in_width), f32)
        for a in range(3):
            for b in range(3):
                total = total + lax.dot_general(
                    cat_ref[
                        (h + 2 - a) * tile_cols : (h + 2 - a + step) * tile_cols,
                        (2 - b) * out_width : (3 - b) * out_width,
                    ],
                    kernel_ref[(3 * a + b) * in_width : (3 * a + b + 1) * in_width, :],
                    (((1,), (1,)), ((), ())),
                    preferred_element_type=f32,
                )
        out_ref[h * tile_cols : (h + step) * tile_cols, :] = total.astype(bf16)


def on_device(canvas, conv_weight, conv_bias, target_gram):
    tile_rows, tile_cols, in_width = canvas.shape
    out_width = conv_weight.shape[3]
    pixel_total = tile_rows * tile_cols * lax.axis_size("rows") * lax.axis_size("cols")
    shape = (tile_rows, tile_cols, in_width, out_width, 2)
    kernel = conv_weight.reshape(9 * in_width, out_width)
    params = pltpu.CompilerParams(vmem_limit_bytes=24 * 1024 * 1024)
    vmem = pl.BlockSpec(memory_space=pltpu.VMEM)
    packed_shape = jax.ShapeDtypeStruct((len(tile_pairs(out_width)) * tile, tile), f32)

    rim_shape = jax.ShapeDtypeStruct((2, tile_rows, in_width), bf16)
    two = lax.axis_size("cols") == 2
    rims = local(
        rim_kernel,
        (rim_shape,) * (1 if two else 2),
        "column_rims",
        canvas,
        cost_estimate=pl.CostEstimate(flops=4_000_000_000, bytes_accessed=600_000, transcendentals=0),
    )
    if two:
        beyond = [lax.ppermute(rims[0], "cols", [(0, 1), (1, 0)])]
    else:
        beyond = shift_cols(rims[1], rims[0])
    payload_shape = jax.ShapeDtypeStruct((2 * tile_cols + edge, in_width), bf16)
    half_shape = jax.ShapeDtypeStruct((1, *target_gram.shape), bf16)
    even, odd, left, right, rows = local(
        payload_kernel,
        (payload_shape, payload_shape, rim_shape, rim_shape, half_shape),
        "row_payload",
        canvas,
        target_gram,
        *beyond,
    )
    count = lax.axis_size("rows")
    even, odd = swap_rows([range(0, count - 1, 2), range(1, count - 1, 2)], [even, odd])
    rows = gather_step(rows, 0, left)

    inner = (tile_rows - 2) * tile_cols
    in_feat, in_slope, in_gram, bias = pl.pallas_call(
        functools.partial(inner_kernel, shape),
        out_shape=(
            jax.ShapeDtypeStruct((inner, out_width), bf16),
            jax.ShapeDtypeStruct((inner, out_width), bf16),
            packed_shape,
            jax.ShapeDtypeStruct((1, out_width), f32),
        ),
        in_specs=[vmem] * 5,
        scratch_shapes=[pltpu.VMEM((tile_rows * tile_cols, 3 * in_width), bf16)],
        compiler_params=params,
        name="inner_rows",
        cost_estimate=pl.CostEstimate(
            flops=2 * inner * (9 * in_width + out_width) * out_width,
            bytes_accessed=6_000_000,
            transcendentals=inner * out_width,
        ),
    )(canvas, left, right, kernel, conv_bias)

    in_gram, rows = lax.optimization_barrier((in_gram, rows))
    outer = 4 * tile_cols + 2 * edge
    out_feat, out_slope, send, keep = pl.pallas_call(
        functools.partial(outer_kernel, shape),
        out_shape=(
            jax.ShapeDtypeStruct((outer, out_width), bf16),
            jax.ShapeDtypeStruct((outer, out_width), bf16),
            jax.ShapeDtypeStruct(packed_shape.shape, bf16),
            packed_shape,
        ),
        in_specs=[vmem] * 8,
        scratch_shapes=[
            pltpu.VMEM((8 * tile_cols, 3 * in_width), bf16),
            pltpu.VMEM((2 * edge, 9 * in_width), bf16),
            pltpu.VMEM(payload_shape.shape, bf16),
            pltpu.VMEM(payload_shape.shape, bf16),
        ],
        compiler_params=params,
        name="outer_rows",
    )(canvas, even, odd, left, right, kernel, bias, in_gram)

    mine, other, rows, other_rows = sum_all(send, keep, rows)
    rows, other_rows = (part.reshape(out_width, out_width) for part in (rows, other_rows))

    own_gram, grad = pl.pallas_call(
        functools.partial(backward_kernel, shape, pixel_total),
        out_shape=(
            jax.ShapeDtypeStruct(target_gram.shape, f32),
            jax.ShapeDtypeStruct((tile_rows * tile_cols, in_width), bf16),
        ),
        in_specs=[vmem] * 9,
        scratch_shapes=[
            pltpu.VMEM((out_width, out_width), bf16),
            pltpu.VMEM((out_width, out_width), f32),
            pltpu.VMEM((out_width, out_width), bf16),
            pltpu.VMEM(((tile_rows + 2) * tile_cols, 3 * out_width), bf16),
        ],
        compiler_params=params,
        name="grad_conv",
    )(mine, other, rows, other_rows, in_feat, in_slope, out_feat, out_slope, kernel)
    return own_gram, grad.reshape(tile_rows, tile_cols, in_width)


def solution(mesh):
    return jax.shard_map(
        on_device,
        mesh=mesh,
        in_specs=(P("rows", "cols", None), P(), P(), P(("rows", "cols"), None)),
        out_specs=(P(("rows", "cols"), None), P("rows", "cols", None)),
        check_vma=False,
    )
```

```python
import functools
import math

import jax
import jax.numpy as jnp
from jax import lax
from jax.experimental import pallas as pl
from jax.experimental.pallas import tpu as pltpu
from jax.sharding import PartitionSpec as P

gelu_scale = math.sqrt(2.0 / math.pi)
tile = 128
edge = 16
f32, bf16 = jnp.float32, jnp.bfloat16


def tile_pairs(width):
    count = width // tile
    return [(i, j) for i in range(count) for j in range(i, count)]


def swap_rows(pairs, values):
    count = lax.axis_size("rows")

    def perm(low):
        partner = {i: i for i in range(count)}
        partner.update({i: i + 1 for i in low})
        partner.update({i + 1: i for i in low})
        return list(partner.items())

    return [lax.ppermute(value, "rows", perm(low)) for low, value in zip(pairs, values)]


def shift_cols(last, first):
    count = lax.axis_size("cols")
    forward = [(i, i + 1) for i in range(count - 1)]
    backward = [(target, source) for source, target in forward]
    return lax.ppermute(last, "cols", forward), lax.ppermute(first, "cols", backward)


def device_index():
    return lax.axis_index("rows") * lax.axis_size("cols") + lax.axis_index("cols")


def swap(value, bit, core=None):
    total = lax.axis_size("rows") * lax.axis_size("cols")
    takes_part = lambda i: core is None or i % 2 == core
    perm = [(i, i ^ (1 << bit) if takes_part(i) else i) for i in range(total)]
    return lax.ppermute(value, ("rows", "cols"), perm)


def local(body, out_shape, name, *operands, **kwargs):
    return pl.pallas_call(
        body,
        out_shape=out_shape,
        in_specs=[pl.BlockSpec(memory_space=pltpu.VMEM)] * len(operands),
        compiler_params=pltpu.CompilerParams(vmem_limit_bytes=8 * 1024 * 1024),
        name=name,
        **kwargs,
    )(*operands)


def side_of(bit):
    return lax.rem(device_index() // (1 << bit), 2)


def rows_at(index, count):
    return pl.ds(pl.multiple_of(index * count, count), count)


def halve(keep, got, bit):
    half = keep.shape[0] // 2

    def body(keep_ref, got_ref, send_ref, stay_ref):
        side = side_of(bit)
        away, here = rows_at(1 - side, half), rows_at(side, half)
        send_ref[...] = (keep_ref[away, :] + got_ref[away, :].astype(f32)).astype(bf16)
        stay_ref[...] = keep_ref[here, :] + got_ref[here, :].astype(f32)

    shape = (half, keep.shape[1])
    return local(
        body,
        (jax.ShapeDtypeStruct(shape, bf16), jax.ShapeDtypeStruct(shape, f32)),
        "halve",
        keep,
        got,
    )


def add(keep, got):
    def body(keep_ref, got_ref, sum_ref):
        sum_ref[...] = (keep_ref[...].astype(f32) + got_ref[...].astype(f32)).astype(bf16)

    return local(body, jax.ShapeDtypeStruct(got.shape, bf16), "add", keep, got)


def join(mine, other, bit):
    def body(mine_ref, other_ref, both_ref):
        side = side_of(bit)
        both_ref[:, pl.ds(side, 1)] = mine_ref[...][:, None]
        both_ref[:, pl.ds(1 - side, 1)] = other_ref[...][:, None]

    shape = (mine.shape[0], 2, *mine.shape[1:])
    return local(body, jax.ShapeDtypeStruct(shape, mine.dtype), "join", mine, other)


def gather_step(rows, bit, after, core=None):
    share = rows.shape[-2:]
    send, _ = lax.optimization_barrier((rows, after))
    got = swap(send, bit, core)
    lead = max(1, rows.shape[0] // 2)
    return join(send.reshape(lead, -1, *share), got.reshape(lead, -1, *share), bit).reshape(-1, *share)


def sum_all(send, keep, rows):
    bits = (lax.axis_size("rows") * lax.axis_size("cols")).bit_length() - 1
    halving = list(range(1, min(3, bits)))
    order = list(reversed(range(1, bits)))

    def step(value, bit):
        nonlocal rows
        got = swap(value, bit, 1)
        if order:
            rows = gather_step(rows, order.pop(0), value, 0)
        return got

    got = swap(send, 0)
    for bit in halving:
        send, keep = halve(keep, got, bit)
        got = step(send, bit)
    mine = add(keep, got)
    for bit in range(len(halving) + 1, bits):
        mine = add(mine, step(mine, bit))
    for bit in reversed(halving):
        before = mine
        mine = join(mine[None], step(mine, bit)[None], bit).reshape(-1, mine.shape[1])
    rows, _ = lax.optimization_barrier((rows, before))
    return mine, swap(mine, 0), rows, swap(rows, 0)


def gelu_pair(value):
    square = value * value
    tangent = jnp.tanh(value * (gelu_scale + gelu_scale * 0.044715 * square))
    half = 0.5 * value
    plus = 0.5 + 0.5 * tangent
    grad = plus + half * (1.0 - tangent * tangent) * (
        gelu_scale + gelu_scale * 3.0 * 0.044715 * square
    )
    return value * plus, grad


def column(value, c):
    return jnp.concatenate([value[r, c : c + 1] for r in range(value.shape[0])], axis=0)


def rim_kernel(canvas_ref, *out_refs):
    cols = canvas_ref.shape[1]
    begin = canvas_ref[:, 0:16, :].astype(f32)
    end = canvas_ref[:, cols - 16 :, :].astype(f32)
    for c in range(2):
        pair = column(begin, c), column(end, 14 + c)
        if len(out_refs) == 1:
            out_refs[0][c] = jnp.where(lax.axis_index("cols") == 0, pair[1], pair[0]).astype(bf16)
        else:
            out_refs[0][c], out_refs[1][c] = pair[0].astype(bf16), pair[1].astype(bf16)


def payload_kernel(canvas_ref, target_ref, *refs):
    even_ref, odd_ref, left_ref, right_ref, half_ref = refs[-5:]
    rows, cols, width = canvas_ref.shape
    half_ref[0] = target_ref[...].astype(bf16)
    if len(refs) == 6:
        here = lax.axis_index("cols")
        other = refs[0][...].astype(f32)
        left_ref[...] = jnp.where(here == 0, 0.0, other).astype(bf16)
        right_ref[...] = jnp.where(here == 0, other, 0.0).astype(bf16)
    else:
        left_ref[...], right_ref[...] = refs[0][...], refs[1][...]
    beyond = [ref[c].astype(f32) for ref in (left_ref, right_ref) for c in range(2)]

    def fill(ref, r):
        for k in range(2):
            ref[k * cols : (k + 1) * cols, :] = canvas_ref[r + k]
        rim = [part[r + k : r + k + 1] for k in range(2) for part in beyond]
        rim = jnp.concatenate([*rim, jnp.zeros((8, width), f32)], axis=0)
        ref[2 * cols :, :] = rim.astype(bf16)

    odd = lax.rem(lax.axis_index("rows"), 2)

    @pl.when(odd == 0)
    def _():
        fill(even_ref, rows - 2)
        fill(odd_ref, 0)

    @pl.when(odd == 1)
    def _():
        fill(even_ref, 0)
        fill(odd_ref, rows - 2)


def fill_row(cat_ref, r, row, before, after):
    cols, width = row.shape
    wide = row.astype(f32)
    place = lax.broadcasted_iota(jnp.int32, (cols, width), 0)
    at = slice(r * cols, (r + 1) * cols)
    moved = jnp.where(place == 0, before, pltpu.roll(wide, 1, 0))
    cat_ref[at, 0:width] = moved.astype(bf16)
    cat_ref[at, width : 2 * width] = row.astype(bf16)
    moved = jnp.where(place == cols - 1, after, pltpu.roll(wide, cols - 1, 0))
    cat_ref[at, 2 * width : 3 * width] = moved.astype(bf16)


def gram_tiles(feat, gram_ref, base_ref=None):
    width = feat.shape[1]
    half = width // 2
    product = functools.partial(
        lax.dot_general,
        dimension_numbers=(((0,), (0,)), ((), ())),
        preferred_element_type=f32,
    )
    upper = product(feat[:, :half], feat)
    lower = product(feat[:, half:], feat[:, half:])
    for n, (i, j) in enumerate(tile_pairs(width)):
        at = slice(n * tile, (n + 1) * tile)
        if i * tile < half:
            part = upper[i * tile : (i + 1) * tile, j * tile : (j + 1) * tile]
        else:
            k, m = i * tile - half, j * tile - half
            part = lower[k : k + tile, m : m + tile]
        gram_ref[at, :] = part if base_ref is None else part + base_ref[at, :]


def inner_kernel(
    shape, own_ref, left_ref, right_ref, kernel_ref, bias_ref,
    feat_ref, slope_ref, gram_ref, row_ref, cat_ref,
):
    row_ref[...] = bias_ref[...].astype(f32).reshape(row_ref.shape)
    tile_rows, tile_cols, in_width, out_width, step = shape
    lefts, rights = left_ref[1].astype(f32), right_ref[0].astype(f32)
    for r in range(tile_rows):
        fill_row(cat_ref, r, own_ref[r], lefts[r : r + 1], rights[r : r + 1])
    bias = row_ref[...]
    root = 1.0 / math.sqrt(out_width)
    span = 3 * in_width
    for h in range(0, tile_rows - 2, step):
        total = bias
        for a in range(3):
            total = total + jnp.dot(
                cat_ref[(h + a) * tile_cols : (h + a + step) * tile_cols, :],
                kernel_ref[a * span : (a + 1) * span, :],
                preferred_element_type=f32,
            )
        features, slope = gelu_pair(total)
        at = slice(h * tile_cols, (h + step) * tile_cols)
        feat_ref[at, :] = features.astype(bf16)
        slope_ref[at, :] = (slope * root).astype(bf16)
    gram_tiles(feat_ref[...], gram_ref)


def outer_kernel(
    shape, own_ref, even_ref, odd_ref, left_ref, right_ref, kernel_ref, bias_ref, base_ref,
    feat_ref, slope_ref, send_ref, keep_ref, cat_ref, edge_ref, low_ref, high_ref,
):
    tile_rows, tile_cols, in_width, out_width, step = shape
    odd = lax.rem(lax.axis_index("rows"), 2)
    row = lax.axis_index("rows")
    low_ref[...] = jnp.where(odd == 0, odd_ref[...], even_ref[...])
    high_ref[...] = jnp.where(odd == 0, even_ref[...], odd_ref[...])

    @pl.when(row == 0)
    def _():
        low_ref[...] = jnp.zeros_like(low_ref)

    @pl.when(row == lax.axis_size("rows") - 1)
    def _():
        high_ref[...] = jnp.zeros_like(high_ref)

    first = (lax.axis_index("rows") > 0).astype(f32)
    last = (lax.axis_index("rows") < lax.axis_size("rows") - 1).astype(f32)
    left = (lax.axis_index("cols") > 0).astype(f32)
    right = (lax.axis_index("cols") < lax.axis_size("cols") - 1).astype(f32)
    main = 2 * tile_cols
    low_rim, high_rim = low_ref[main:, :].astype(f32), high_ref[main:, :].astype(f32)
    own_begin = column(own_ref[:, 0:16, :].astype(f32), 0)
    own_end = column(own_ref[:, tile_cols - 16 :, :].astype(f32), 15)

    def sides(c, own):
        return jnp.concatenate(
            [low_rim[c : c + 1], low_rim[4 + c : 5 + c], own, high_rim[c : c + 1], high_rim[4 + c : 5 + c]],
            axis=0,
        )

    def ends(c, own):
        c16 = c // 16 * 16
        piece = lambda ref, k: ref[k + c16 : k + c16 + 16, :].astype(f32)[c - c16 : c - c16 + 1]
        rows = [piece(low_ref, 0), piece(low_ref, tile_cols), own]
        return jnp.concatenate([*rows, piece(high_ref, 0), piece(high_ref, tile_cols)], axis=0)

    lefts = [
        sides(0, left_ref[0].astype(f32)), sides(1, left_ref[1].astype(f32)), ends(0, own_begin)
    ]
    rights = [
        ends(tile_cols - 1, own_end), sides(2, right_ref[0].astype(f32)), sides(3, right_ref[1].astype(f32))
    ]
    span = 3 * in_width
    lines = [0, 1, 2, 3, tile_rows, tile_rows + 1, tile_rows + 2, tile_rows + 3]
    for r, line in enumerate(lines):
        if line < 2:
            row = low_ref[line * tile_cols : (line + 1) * tile_cols, :]
        elif line < tile_rows + 2:
            row = own_ref[line - 2]
        else:
            k = line - tile_rows - 2
            row = high_ref[k * tile_cols : (k + 1) * tile_cols, :]
        fill_row(cat_ref, r, row, lefts[1][line : line + 1], rights[1][line : line + 1])
    blank = jnp.zeros((edge - tile_rows - 2, in_width), f32)
    for a in range(3):
        for b in range(3):
            piece = jnp.concatenate(
                [lefts[b][a : a + tile_rows + 2], blank, rights[b][a : a + tile_rows + 2], blank],
                axis=0,
            )
            at = (3 * a + b) * in_width
            edge_ref[:, at : at + in_width] = piece.astype(bf16)
    bias = bias_ref[...]
    root = 1.0 / math.sqrt(out_width)
    totals = [bias, bias, bias]
    for a in range(3):
        weights = kernel_ref[a * span : (a + 1) * span, :]
        for k in range(2):
            totals[k] = totals[k] + jnp.dot(
                cat_ref[(4 * k + a) * tile_cols : (4 * k + a + 2) * tile_cols, :],
                weights,
                preferred_element_type=f32,
            )
        totals[2] = totals[2] + jnp.dot(
            edge_ref[:, a * span : (a + 1) * span], weights, preferred_element_type=f32
        )
    for k in range(2):
        features, slope = gelu_pair(totals[k])
        slope = slope * root
        at = k * main
        feat_ref[at : at + main, :] = features.astype(bf16)
        scale = (first, 1.0) if k == 0 else (1.0, last)
        slope_ref[at : at + tile_cols, :] = (slope[:tile_cols] * scale[0]).astype(bf16)
        slope_ref[at + tile_cols : at + main, :] = (slope[tile_cols:] * scale[1]).astype(bf16)
    features, slope = gelu_pair(totals[2])
    line = lax.broadcasted_iota(jnp.int32, (2 * edge, out_width), 0)
    weight = jnp.where(line < edge, left, right)
    weight = jnp.where(line % edge == 0, weight * first, weight)
    weight = jnp.where(line % edge == tile_rows + 1, weight * last, weight)
    feat_ref[2 * main :, :] = features.astype(bf16)
    slope_ref[2 * main :, :] = (slope * root * weight).astype(bf16)
    gram_tiles(feat_ref[tile_cols : 3 * tile_cols, :], keep_ref, base_ref)
    send_ref[...] = keep_ref[...].astype(bf16)


def backward_kernel(
    shape, pixel_total, mine_ref, other_ref, rows_ref, other_rows_ref, in_feat_ref, in_slope_ref, out_feat_ref, out_slope_ref,
    kernel_ref, own_gram_ref, out_ref, target_ref, full_ref, sym_ref, cat_ref,
):
    tile_rows, tile_cols, in_width, out_width, step = shape
    core = side_of(0)
    target_ref[...] = jnp.where(core == 0, rows_ref[...], other_rows_ref[...])
    for n, (i, j) in enumerate(tile_pairs(out_width)):
        at_i, at_j = slice(i * tile, (i + 1) * tile), slice(j * tile, (j + 1) * tile)
        at = slice(n * tile, (n + 1) * tile)
        gram = jnp.where(core == 1, mine_ref[at, :], other_ref[at, :]).astype(f32) * (1.0 / pixel_total)
        both = 2.0 * gram - (target_ref[at_i, at_j].astype(f32) + target_ref[at_j, at_i].astype(f32).T)
        full_ref[at_i, at_j] = gram
        sym_ref[at_i, at_j] = both.astype(bf16)
        if i != j:
            full_ref[at_j, at_i] = gram.T
            sym_ref[at_j, at_i] = both.T.astype(bf16)
    share = own_gram_ref.shape[0]
    start = device_index() * share
    if share % 8 == 0:
        own_gram_ref[...] = full_ref[pl.ds(pl.multiple_of(start, 8), share), :]
    else:
        group = full_ref[pl.ds(pl.multiple_of(start // 8 * 8, 8), 8), :]
        picked = group[0:share]
        for k in range(share, 8, share):
            picked = jnp.where(start % 8 == k, group[k : k + share], picked)
        own_gram_ref[...] = picked

    def grad_of(feat_ref, slope_ref, at):
        product = jnp.dot(feat_ref[at, :], sym_ref[...], preferred_element_type=f32)
        return product * slope_ref[at, :].astype(f32)

    main = 2 * tile_cols
    edges = grad_of(out_feat_ref, out_slope_ref, slice(2 * main, None))
    lines = [
        (out_feat_ref, out_slope_ref, 0, 0),
        (out_feat_ref, out_slope_ref, main, tile_rows),
    ] + [
        (in_feat_ref, in_slope_ref, h * tile_cols, h + 2) for h in range(0, tile_rows - 2, step)
    ]
    for feat_ref, slope_ref, begin, r in lines:
        grad = grad_of(feat_ref, slope_ref, slice(begin, begin + step * tile_cols))
        for k in range(step):
            fill_row(
                cat_ref, r + k, grad[k * tile_cols : (k + 1) * tile_cols],
                edges[r + k : r + k + 1], edges[edge + r + k : edge + r + k + 1],
            )
    for h in range(0, tile_rows, step):
        total = jnp.zeros((step * tile_cols, in_width), f32)
        for a in range(3):
            for b in range(3):
                total = total + lax.dot_general(
                    cat_ref[
                        (h + 2 - a) * tile_cols : (h + 2 - a + step) * tile_cols,
                        (2 - b) * out_width : (3 - b) * out_width,
                    ],
                    kernel_ref[(3 * a + b) * in_width : (3 * a + b + 1) * in_width, :],
                    (((1,), (1,)), ((), ())),
                    preferred_element_type=f32,
                )
        out_ref[h * tile_cols : (h + step) * tile_cols, :] = total.astype(bf16)


def on_device(canvas, conv_weight, conv_bias, target_gram):
    tile_rows, tile_cols, in_width = canvas.shape
    out_width = conv_weight.shape[3]
    pixel_total = tile_rows * tile_cols * lax.axis_size("rows") * lax.axis_size("cols")
    shape = (tile_rows, tile_cols, in_width, out_width, 2)
    kernel = conv_weight.reshape(9 * in_width, out_width)
    params = pltpu.CompilerParams(vmem_limit_bytes=24 * 1024 * 1024)
    vmem = pl.BlockSpec(memory_space=pltpu.VMEM)
    packed_shape = jax.ShapeDtypeStruct((len(tile_pairs(out_width)) * tile, tile), f32)

    rim_shape = jax.ShapeDtypeStruct((2, tile_rows, in_width), bf16)
    two = lax.axis_size("cols") == 2
    rims = local(
        rim_kernel,
        (rim_shape,) * (1 if two else 2),
        "column_rims",
        canvas,
        cost_estimate=pl.CostEstimate(flops=4_000_000_000, bytes_accessed=600_000, transcendentals=0),
    )
    if two:
        beyond = [lax.ppermute(rims[0], "cols", [(0, 1), (1, 0)])]
    else:
        beyond = shift_cols(rims[1], rims[0])
    payload_shape = jax.ShapeDtypeStruct((2 * tile_cols + edge, in_width), bf16)
    half_shape = jax.ShapeDtypeStruct((1, *target_gram.shape), bf16)
    even, odd, left, right, rows = local(
        payload_kernel,
        (payload_shape, payload_shape, rim_shape, rim_shape, half_shape),
        "row_payload",
        canvas,
        target_gram,
        *beyond,
    )
    count = lax.axis_size("rows")
    even, odd = swap_rows([range(0, count - 1, 2), range(1, count - 1, 2)], [even, odd])
    rows = gather_step(rows, 0, left)

    inner = (tile_rows - 2) * tile_cols
    in_feat, in_slope, in_gram, bias = pl.pallas_call(
        functools.partial(inner_kernel, shape),
        out_shape=(
            jax.ShapeDtypeStruct((inner, out_width), bf16),
            jax.ShapeDtypeStruct((inner, out_width), bf16),
            packed_shape,
            jax.ShapeDtypeStruct((1, out_width), f32),
        ),
        in_specs=[vmem] * 5,
        scratch_shapes=[pltpu.VMEM((tile_rows * tile_cols, 3 * in_width), bf16)],
        compiler_params=params,
        name="inner_rows",
        cost_estimate=pl.CostEstimate(
            flops=2 * inner * (9 * in_width + out_width) * out_width,
            bytes_accessed=6_000_000,
            transcendentals=inner * out_width,
        ),
    )(canvas, left, right, kernel, conv_bias)

    in_gram, rows = lax.optimization_barrier((in_gram, rows))
    outer = 4 * tile_cols + 2 * edge
    out_feat, out_slope, send, keep = pl.pallas_call(
        functools.partial(outer_kernel, shape),
        out_shape=(
            jax.ShapeDtypeStruct((outer, out_width), bf16),
            jax.ShapeDtypeStruct((outer, out_width), bf16),
            jax.ShapeDtypeStruct(packed_shape.shape, bf16),
            packed_shape,
        ),
        in_specs=[vmem] * 8,
        scratch_shapes=[
            pltpu.VMEM((8 * tile_cols, 3 * in_width), bf16),
            pltpu.VMEM((2 * edge, 9 * in_width), bf16),
            pltpu.VMEM(payload_shape.shape, bf16),
            pltpu.VMEM(payload_shape.shape, bf16),
        ],
        compiler_params=params,
        name="outer_rows",
    )(canvas, even, odd, left, right, kernel, bias, in_gram)

    mine, other, rows, other_rows = sum_all(send, keep, rows)
    rows, other_rows = (part.reshape(out_width, out_width) for part in (rows, other_rows))

    own_gram, grad = pl.pallas_call(
        functools.partial(backward_kernel, shape, pixel_total),
        out_shape=(
            jax.ShapeDtypeStruct(target_gram.shape, f32),
            jax.ShapeDtypeStruct((tile_rows * tile_cols, in_width), bf16),
        ),
        in_specs=[vmem] * 9,
        scratch_shapes=[
            pltpu.VMEM((out_width, out_width), bf16),
            pltpu.VMEM((out_width, out_width), f32),
            pltpu.VMEM((out_width, out_width), bf16),
            pltpu.VMEM(((tile_rows + 2) * tile_cols, 3 * out_width), bf16),
        ],
        compiler_params=params,
        name="grad_conv",
    )(mine, other, rows, other_rows, in_feat, in_slope, out_feat, out_slope, kernel)
    return own_gram, grad.reshape(tile_rows, tile_cols, in_width)


def solution(mesh):
    return jax.shard_map(
        on_device,
        mesh=mesh,
        in_specs=(P("rows", "cols", None), P(), P(), P(("rows", "cols"), None)),
        out_specs=(P(("rows", "cols"), None), P("rows", "cols", None)),
        check_vma=False,
    )
```

```python
import functools
import math

import jax
import jax.numpy as jnp
from jax import lax
from jax.experimental import pallas as pl
from jax.experimental.pallas import tpu as pltpu
from jax.sharding import PartitionSpec as P

gelu_scale = math.sqrt(2.0 / math.pi)
tile = 128
edge = 16
f32, bf16 = jnp.float32, jnp.bfloat16


def tile_pairs(width):
    count = width // tile
    return [(i, j) for i in range(count) for j in range(i, count)]


def swap_rows(pairs, values):
    count = lax.axis_size("rows")

    def perm(low):
        partner = {i: i for i in range(count)}
        partner.update({i: i + 1 for i in low})
        partner.update({i + 1: i for i in low})
        return list(partner.items())

    return [lax.ppermute(value, "rows", perm(low)) for low, value in zip(pairs, values)]


def shift_cols(last, first):
    count = lax.axis_size("cols")
    forward = [(i, i + 1) for i in range(count - 1)]
    backward = [(target, source) for source, target in forward]
    return lax.ppermute(last, "cols", forward), lax.ppermute(first, "cols", backward)


def device_index():
    return lax.axis_index("rows") * lax.axis_size("cols") + lax.axis_index("cols")


def swap(value, bit):
    total = lax.axis_size("rows") * lax.axis_size("cols")
    return lax.ppermute(value, ("rows", "cols"), [(i, i ^ (1 << bit | 1)) for i in range(total)])


def local(body, out_shape, name, *operands, **kwargs):
    return pl.pallas_call(
        body,
        out_shape=out_shape,
        in_specs=[pl.BlockSpec(memory_space=pltpu.VMEM)] * len(operands),
        compiler_params=pltpu.CompilerParams(vmem_limit_bytes=8 * 1024 * 1024),
        name=name,
        **kwargs,
    )(*operands)


def side_of(bit):
    index = device_index()
    if bit > 0:
        return lax.rem(index // (1 << bit), 2)
    bits = (lax.axis_size("rows") * lax.axis_size("cols")).bit_length() - 1
    return lax.rem(sum(lax.rem(index // (1 << k), 2) for k in range(bits)), 2)


def rows_at(index, count):
    return pl.ds(pl.multiple_of(index * count, count), count)


def halve(keep, got, bit):
    half = keep.shape[0] // 2

    def body(keep_ref, got_ref, send_ref, stay_ref):
        side = side_of(bit)
        away, here = rows_at(1 - side, half), rows_at(side, half)
        send_ref[...] = (keep_ref[away, :] + got_ref[away, :].astype(f32)).astype(bf16)
        stay_ref[...] = keep_ref[here, :] + got_ref[here, :].astype(f32)

    shape = (half, keep.shape[1])
    return local(
        body,
        (jax.ShapeDtypeStruct(shape, bf16), jax.ShapeDtypeStruct(shape, f32)),
        "halve",
        keep,
        got,
    )


def add(keep, got):
    def body(keep_ref, got_ref, sum_ref):
        sum_ref[...] = (keep_ref[...].astype(f32) + got_ref[...].astype(f32)).astype(bf16)

    return local(body, jax.ShapeDtypeStruct(got.shape, bf16), "add", keep, got)


def join(mine, other, bit):
    def body(mine_ref, other_ref, both_ref):
        side = side_of(bit)
        both_ref[:, pl.ds(side, 1)] = mine_ref[...][:, None]
        both_ref[:, pl.ds(1 - side, 1)] = other_ref[...][:, None]

    shape = (mine.shape[0], 2, *mine.shape[1:])
    return local(body, jax.ShapeDtypeStruct(shape, mine.dtype), "join", mine, other)


def join_cores(mine, other):
    def body(mine_ref, other_ref, both_ref):
        side = side_of(0)
        for chip in range(mine.shape[0]):
            core = lax.rem(side + chip.bit_count(), 2)
            both_ref[chip, pl.ds(core, 1)] = mine_ref[chip][None]
            both_ref[chip, pl.ds(1 - core, 1)] = other_ref[chip][None]

    shape = (mine.shape[0], 2, *mine.shape[1:])
    return local(body, jax.ShapeDtypeStruct(shape, mine.dtype), "join_cores", mine, other)


def gather_step(rows, bit, after):
    share = rows.shape[-2:]
    send, _ = lax.optimization_barrier((rows, after))
    got = swap(send, bit)
    both = join(send, got, bit) if bit > 0 else join_cores(send, got)
    return both.reshape(-1, *share)


def sum_all(send, keep, rows):
    bits = (lax.axis_size("rows") * lax.axis_size("cols")).bit_length() - 1
    halving = list(range(1, min(3, bits)))
    order = list(reversed(range(bits)))

    def step(value, bit):
        nonlocal rows
        got = swap(value, bit)
        if order:
            rows = gather_step(rows, order.pop(0), value)
        return got

    got = swap(send, 0)
    for bit in halving:
        send, keep = halve(keep, got, bit)
        got = step(send, bit)
    mine = add(keep, got)
    for bit in range(len(halving) + 1, bits):
        mine = add(mine, step(mine, bit))
    for bit in reversed(halving):
        mine = join(mine[None], step(mine, bit)[None], bit).reshape(-1, mine.shape[1])
    other = swap(mine, 0)
    for bit in order:
        rows = gather_step(rows, bit, mine)
    return mine, other, rows


def gelu_pair(value):
    square = value * value
    tangent = jnp.tanh(value * (gelu_scale + gelu_scale * 0.044715 * square))
    half = 0.5 * value
    plus = 0.5 + 0.5 * tangent
    grad = plus + half * (1.0 - tangent * tangent) * (
        gelu_scale + gelu_scale * 3.0 * 0.044715 * square
    )
    return value * plus, grad


def column(value, c):
    return jnp.concatenate([value[r, c : c + 1] for r in range(value.shape[0])], axis=0)


def rim_kernel(canvas_ref, *out_refs):
    cols = canvas_ref.shape[1]
    begin = canvas_ref[:, 0:16, :].astype(f32)
    end = canvas_ref[:, cols - 16 :, :].astype(f32)
    for c in range(2):
        pair = column(begin, c), column(end, 14 + c)
        if len(out_refs) == 1:
            out_refs[0][c] = jnp.where(lax.axis_index("cols") == 0, pair[1], pair[0]).astype(bf16)
        else:
            out_refs[0][c], out_refs[1][c] = pair[0].astype(bf16), pair[1].astype(bf16)


def payload_kernel(canvas_ref, target_ref, *refs):
    even_ref, odd_ref, left_ref, right_ref, half_ref = refs[-5:]
    rows, cols, width = canvas_ref.shape
    half_ref[0] = target_ref[...].astype(bf16)
    if len(refs) == 6:
        here = lax.axis_index("cols")
        other = refs[0][...].astype(f32)
        left_ref[...] = jnp.where(here == 0, 0.0, other).astype(bf16)
        right_ref[...] = jnp.where(here == 0, other, 0.0).astype(bf16)
    else:
        left_ref[...], right_ref[...] = refs[0][...], refs[1][...]
    beyond = [ref[c].astype(f32) for ref in (left_ref, right_ref) for c in range(2)]

    def fill(ref, r):
        for k in range(2):
            ref[k * cols : (k + 1) * cols, :] = canvas_ref[r + k]
        rim = [part[r + k : r + k + 1] for k in range(2) for part in beyond]
        rim = jnp.concatenate([*rim, jnp.zeros((8, width), f32)], axis=0)
        ref[2 * cols :, :] = rim.astype(bf16)

    odd = lax.rem(lax.axis_index("rows"), 2)

    @pl.when(odd == 0)
    def _():
        fill(even_ref, rows - 2)
        fill(odd_ref, 0)

    @pl.when(odd == 1)
    def _():
        fill(even_ref, 0)
        fill(odd_ref, rows - 2)


def fill_row(cat_ref, r, row, before, after):
    cols, width = row.shape
    wide = row.astype(f32)
    place = lax.broadcasted_iota(jnp.int32, (cols, width), 0)
    at = slice(r * cols, (r + 1) * cols)
    moved = jnp.where(place == 0, before, pltpu.roll(wide, 1, 0))
    cat_ref[at, 0:width] = moved.astype(bf16)
    cat_ref[at, width : 2 * width] = row.astype(bf16)
    moved = jnp.where(place == cols - 1, after, pltpu.roll(wide, cols - 1, 0))
    cat_ref[at, 2 * width : 3 * width] = moved.astype(bf16)


def gram_tiles(feat, gram_ref, base_ref=None):
    width = feat.shape[1]
    half = width // 2
    product = functools.partial(
        lax.dot_general,
        dimension_numbers=(((0,), (0,)), ((), ())),
        preferred_element_type=f32,
    )
    upper = product(feat[:, :half], feat)
    lower = product(feat[:, half:], feat[:, half:])
    for n, (i, j) in enumerate(tile_pairs(width)):
        at = slice(n * tile, (n + 1) * tile)
        if i * tile < half:
            part = upper[i * tile : (i + 1) * tile, j * tile : (j + 1) * tile]
        else:
            k, m = i * tile - half, j * tile - half
            part = lower[k : k + tile, m : m + tile]
        gram_ref[at, :] = part if base_ref is None else part + base_ref[at, :]


def inner_kernel(
    shape, own_ref, left_ref, right_ref, kernel_ref, bias_ref,
    feat_ref, slope_ref, gram_ref, row_ref, cat_ref,
):
    row_ref[...] = bias_ref[...].astype(f32).reshape(row_ref.shape)
    tile_rows, tile_cols, in_width, out_width, step = shape
    lefts, rights = left_ref[1].astype(f32), right_ref[0].astype(f32)
    for r in range(tile_rows):
        fill_row(cat_ref, r, own_ref[r], lefts[r : r + 1], rights[r : r + 1])
    bias = row_ref[...]
    root = 1.0 / math.sqrt(out_width)
    span = 3 * in_width
    for h in range(0, tile_rows - 2, step):
        total = bias
        for a in range(3):
            total = total + jnp.dot(
                cat_ref[(h + a) * tile_cols : (h + a + step) * tile_cols, :],
                kernel_ref[a * span : (a + 1) * span, :],
                preferred_element_type=f32,
            )
        features, slope = gelu_pair(total)
        at = slice(h * tile_cols, (h + step) * tile_cols)
        feat_ref[at, :] = features.astype(bf16)
        slope_ref[at, :] = (slope * root).astype(bf16)
    gram_tiles(feat_ref[...], gram_ref)


def outer_kernel(
    shape, own_ref, even_ref, odd_ref, left_ref, right_ref, kernel_ref, bias_ref, base_ref,
    feat_ref, slope_ref, send_ref, keep_ref, cat_ref, edge_ref, low_ref, high_ref, gram_ref,
):
    tile_rows, tile_cols, in_width, out_width, step = shape
    odd = lax.rem(lax.axis_index("rows"), 2)
    row = lax.axis_index("rows")
    low_ref[...] = jnp.where(odd == 0, odd_ref[...], even_ref[...])
    high_ref[...] = jnp.where(odd == 0, even_ref[...], odd_ref[...])

    @pl.when(row == 0)
    def _():
        low_ref[...] = jnp.zeros_like(low_ref)

    @pl.when(row == lax.axis_size("rows") - 1)
    def _():
        high_ref[...] = jnp.zeros_like(high_ref)

    first = (lax.axis_index("rows") > 0).astype(f32)
    last = (lax.axis_index("rows") < lax.axis_size("rows") - 1).astype(f32)
    left = (lax.axis_index("cols") > 0).astype(f32)
    right = (lax.axis_index("cols") < lax.axis_size("cols") - 1).astype(f32)
    main = 2 * tile_cols
    low_rim, high_rim = low_ref[main:, :].astype(f32), high_ref[main:, :].astype(f32)
    own_begin = column(own_ref[:, 0:16, :].astype(f32), 0)
    own_end = column(own_ref[:, tile_cols - 16 :, :].astype(f32), 15)

    def sides(c, own):
        return jnp.concatenate(
            [low_rim[c : c + 1], low_rim[4 + c : 5 + c], own, high_rim[c : c + 1], high_rim[4 + c : 5 + c]],
            axis=0,
        )

    def ends(c, own):
        c16 = c // 16 * 16
        piece = lambda ref, k: ref[k + c16 : k + c16 + 16, :].astype(f32)[c - c16 : c - c16 + 1]
        rows = [piece(low_ref, 0), piece(low_ref, tile_cols), own]
        return jnp.concatenate([*rows, piece(high_ref, 0), piece(high_ref, tile_cols)], axis=0)

    lefts = [
        sides(0, left_ref[0].astype(f32)), sides(1, left_ref[1].astype(f32)), ends(0, own_begin)
    ]
    rights = [
        ends(tile_cols - 1, own_end), sides(2, right_ref[0].astype(f32)), sides(3, right_ref[1].astype(f32))
    ]
    span = 3 * in_width
    lines = [0, 1, 2, 3, tile_rows, tile_rows + 1, tile_rows + 2, tile_rows + 3]
    for r, line in enumerate(lines):
        if line < 2:
            row = low_ref[line * tile_cols : (line + 1) * tile_cols, :]
        elif line < tile_rows + 2:
            row = own_ref[line - 2]
        else:
            k = line - tile_rows - 2
            row = high_ref[k * tile_cols : (k + 1) * tile_cols, :]
        fill_row(cat_ref, r, row, lefts[1][line : line + 1], rights[1][line : line + 1])
    blank = jnp.zeros((edge - tile_rows - 2, in_width), f32)
    for a in range(3):
        for b in range(3):
            piece = jnp.concatenate(
                [lefts[b][a : a + tile_rows + 2], blank, rights[b][a : a + tile_rows + 2], blank],
                axis=0,
            )
            at = (3 * a + b) * in_width
            edge_ref[:, at : at + in_width] = piece.astype(bf16)
    bias = bias_ref[...]
    root = 1.0 / math.sqrt(out_width)
    totals = [bias, bias, bias]
    for a in range(3):
        weights = kernel_ref[a * span : (a + 1) * span, :]
        for k in range(2):
            totals[k] = totals[k] + jnp.dot(
                cat_ref[(4 * k + a) * tile_cols : (4 * k + a + 2) * tile_cols, :],
                weights,
                preferred_element_type=f32,
            )
        totals[2] = totals[2] + jnp.dot(
            edge_ref[:, a * span : (a + 1) * span], weights, preferred_element_type=f32
        )
    for k in range(2):
        features, slope = gelu_pair(totals[k])
        slope = slope * root
        at = k * main
        feat_ref[at : at + main, :] = features.astype(bf16)
        scale = (first, 1.0) if k == 0 else (1.0, last)
        slope_ref[at : at + tile_cols, :] = (slope[:tile_cols] * scale[0]).astype(bf16)
        slope_ref[at + tile_cols : at + main, :] = (slope[tile_cols:] * scale[1]).astype(bf16)
    features, slope = gelu_pair(totals[2])
    line = lax.broadcasted_iota(jnp.int32, (2 * edge, out_width), 0)
    weight = jnp.where(line < edge, left, right)
    weight = jnp.where(line % edge == 0, weight * first, weight)
    weight = jnp.where(line % edge == tile_rows + 1, weight * last, weight)
    feat_ref[2 * main :, :] = features.astype(bf16)
    slope_ref[2 * main :, :] = (slope * root * weight).astype(bf16)
    gram_tiles(feat_ref[tile_cols : 3 * tile_cols, :], gram_ref, base_ref)
    half = send_ref.shape[0]
    side = side_of(0)
    send_ref[...] = gram_ref[rows_at(1 - side, half), :].astype(bf16)
    keep_ref[...] = gram_ref[rows_at(side, half), :]


def backward_kernel(
    shape, pixel_total, mine_ref, other_ref, target_ref, in_feat_ref, in_slope_ref, out_feat_ref, out_slope_ref,
    kernel_ref, own_gram_ref, out_ref, gram_ref, full_ref, sym_ref, cat_ref,
):
    tile_rows, tile_cols, in_width, out_width, step = shape
    half = mine_ref.shape[0]
    side = side_of(0)
    gram_ref[rows_at(side, half), :] = mine_ref[...].astype(f32)
    gram_ref[rows_at(1 - side, half), :] = other_ref[...].astype(f32)
    for n, (i, j) in enumerate(tile_pairs(out_width)):
        at_i, at_j = slice(i * tile, (i + 1) * tile), slice(j * tile, (j + 1) * tile)
        at = slice(n * tile, (n + 1) * tile)
        gram = gram_ref[at, :] * (1.0 / pixel_total)
        both = 2.0 * gram - (target_ref[at_i, at_j].astype(f32) + target_ref[at_j, at_i].astype(f32).T)
        full_ref[at_i, at_j] = gram
        sym_ref[at_i, at_j] = both.astype(bf16)
        if i != j:
            full_ref[at_j, at_i] = gram.T
            sym_ref[at_j, at_i] = both.T.astype(bf16)
    share = own_gram_ref.shape[0]
    start = device_index() * share
    if share % 8 == 0:
        own_gram_ref[...] = full_ref[pl.ds(pl.multiple_of(start, 8), share), :]
    else:
        group = full_ref[pl.ds(pl.multiple_of(start // 8 * 8, 8), 8), :]
        picked = group[0:share]
        for k in range(share, 8, share):
            picked = jnp.where(start % 8 == k, group[k : k + share], picked)
        own_gram_ref[...] = picked

    def grad_of(feat_ref, slope_ref, at):
        product = jnp.dot(feat_ref[at, :], sym_ref[...], preferred_element_type=f32)
        return product * slope_ref[at, :].astype(f32)

    main = 2 * tile_cols
    edges = grad_of(out_feat_ref, out_slope_ref, slice(2 * main, None))
    lines = [
        (out_feat_ref, out_slope_ref, 0, 0),
        (out_feat_ref, out_slope_ref, main, tile_rows),
    ] + [
        (in_feat_ref, in_slope_ref, h * tile_cols, h + 2) for h in range(0, tile_rows - 2, step)
    ]
    for feat_ref, slope_ref, begin, r in lines:
        grad = grad_of(feat_ref, slope_ref, slice(begin, begin + step * tile_cols))
        for k in range(step):
            fill_row(
                cat_ref, r + k, grad[k * tile_cols : (k + 1) * tile_cols],
                edges[r + k : r + k + 1], edges[edge + r + k : edge + r + k + 1],
            )
    for h in range(0, tile_rows, step):
        total = jnp.zeros((step * tile_cols, in_width), f32)
        for a in range(3):
            for b in range(3):
                total = total + lax.dot_general(
                    cat_ref[
                        (h + 2 - a) * tile_cols : (h + 2 - a + step) * tile_cols,
                        (2 - b) * out_width : (3 - b) * out_width,
                    ],
                    kernel_ref[(3 * a + b) * in_width : (3 * a + b + 1) * in_width, :],
                    (((1,), (1,)), ((), ())),
                    preferred_element_type=f32,
                )
        out_ref[h * tile_cols : (h + step) * tile_cols, :] = total.astype(bf16)


def on_device(canvas, conv_weight, conv_bias, target_gram):
    tile_rows, tile_cols, in_width = canvas.shape
    out_width = conv_weight.shape[3]
    pixel_total = tile_rows * tile_cols * lax.axis_size("rows") * lax.axis_size("cols")
    shape = (tile_rows, tile_cols, in_width, out_width, 2)
    kernel = conv_weight.reshape(9 * in_width, out_width)
    params = pltpu.CompilerParams(vmem_limit_bytes=24 * 1024 * 1024)
    vmem = pl.BlockSpec(memory_space=pltpu.VMEM)
    packed_shape = jax.ShapeDtypeStruct((len(tile_pairs(out_width)) * tile, tile), f32)

    rim_shape = jax.ShapeDtypeStruct((2, tile_rows, in_width), bf16)
    two = lax.axis_size("cols") == 2
    rims = local(
        rim_kernel,
        (rim_shape,) * (1 if two else 2),
        "column_rims",
        canvas,
        cost_estimate=pl.CostEstimate(flops=4_000_000_000, bytes_accessed=600_000, transcendentals=0),
    )
    if two:
        beyond = [lax.ppermute(rims[0], "cols", [(0, 1), (1, 0)])]
    else:
        beyond = shift_cols(rims[1], rims[0])
    payload_shape = jax.ShapeDtypeStruct((2 * tile_cols + edge, in_width), bf16)
    half_shape = jax.ShapeDtypeStruct((1, *target_gram.shape), bf16)
    even, odd, left, right, rows = local(
        payload_kernel,
        (payload_shape, payload_shape, rim_shape, rim_shape, half_shape),
        "row_payload",
        canvas,
        target_gram,
        *beyond,
    )
    count = lax.axis_size("rows")
    even, odd = swap_rows([range(0, count - 1, 2), range(1, count - 1, 2)], [even, odd])

    inner = (tile_rows - 2) * tile_cols
    in_feat, in_slope, in_gram, bias = pl.pallas_call(
        functools.partial(inner_kernel, shape),
        out_shape=(
            jax.ShapeDtypeStruct((inner, out_width), bf16),
            jax.ShapeDtypeStruct((inner, out_width), bf16),
            packed_shape,
            jax.ShapeDtypeStruct((1, out_width), f32),
        ),
        in_specs=[vmem] * 5,
        scratch_shapes=[pltpu.VMEM((tile_rows * tile_cols, 3 * in_width), bf16)],
        compiler_params=params,
        name="inner_rows",
        cost_estimate=pl.CostEstimate(
            flops=2 * inner * (9 * in_width + out_width) * out_width,
            bytes_accessed=6_000_000,
            transcendentals=inner * out_width,
        ),
    )(canvas, left, right, kernel, conv_bias)

    outer = 4 * tile_cols + 2 * edge
    half_gram = (packed_shape.shape[0] // 2, tile)
    out_feat, out_slope, send, keep = pl.pallas_call(
        functools.partial(outer_kernel, shape),
        out_shape=(
            jax.ShapeDtypeStruct((outer, out_width), bf16),
            jax.ShapeDtypeStruct((outer, out_width), bf16),
            jax.ShapeDtypeStruct(half_gram, bf16),
            jax.ShapeDtypeStruct(half_gram, f32),
        ),
        in_specs=[vmem] * 8,
        scratch_shapes=[
            pltpu.VMEM((8 * tile_cols, 3 * in_width), bf16),
            pltpu.VMEM((2 * edge, 9 * in_width), bf16),
            pltpu.VMEM(payload_shape.shape, bf16),
            pltpu.VMEM(payload_shape.shape, bf16),
            pltpu.VMEM(packed_shape.shape, f32),
        ],
        compiler_params=params,
        name="outer_rows",
    )(canvas, even, odd, left, right, kernel, bias, in_gram)

    mine, other, rows = sum_all(send, keep, rows)

    own_gram, grad = pl.pallas_call(
        functools.partial(backward_kernel, shape, pixel_total),
        out_shape=(
            jax.ShapeDtypeStruct(target_gram.shape, f32),
            jax.ShapeDtypeStruct((tile_rows * tile_cols, in_width), bf16),
        ),
        in_specs=[vmem] * 8,
        scratch_shapes=[
            pltpu.VMEM(packed_shape.shape, f32),
            pltpu.VMEM((out_width, out_width), f32),
            pltpu.VMEM((out_width, out_width), bf16),
            pltpu.VMEM(((tile_rows + 2) * tile_cols, 3 * out_width), bf16),
        ],
        compiler_params=params,
        name="grad_conv",
    )(mine, other, rows.reshape(out_width, out_width), in_feat, in_slope, out_feat, out_slope, kernel)
    return own_gram, grad.reshape(tile_rows, tile_cols, in_width)


def solution(mesh):
    return jax.shard_map(
        on_device,
        mesh=mesh,
        in_specs=(P("rows", "cols", None), P(), P(), P(("rows", "cols"), None)),
        out_specs=(P(("rows", "cols"), None), P("rows", "cols", None)),
        check_vma=False,
    )
```

```python
import functools
import math

import jax
import jax.numpy as jnp
from jax import lax
from jax.experimental import pallas as pl
from jax.experimental.pallas import tpu as pltpu
from jax.sharding import PartitionSpec as P

gelu_scale = math.sqrt(2.0 / math.pi)
tile = 128
edge = 16
f32, bf16 = jnp.float32, jnp.bfloat16


def tile_pairs(width):
    count = width // tile
    return [(i, j) for i in range(count) for j in range(i, count)]


def swap_rows(pairs, values):
    count = lax.axis_size("rows")

    def perm(low):
        partner = {i: i for i in range(count)}
        partner.update({i: i + 1 for i in low})
        partner.update({i + 1: i for i in low})
        return list(partner.items())

    return [lax.ppermute(value, "rows", perm(low)) for low, value in zip(pairs, values)]


def shift_cols(last, first):
    count = lax.axis_size("cols")
    forward = [(i, i + 1) for i in range(count - 1)]
    backward = [(target, source) for source, target in forward]
    return lax.ppermute(last, "cols", forward), lax.ppermute(first, "cols", backward)


def device_index():
    return lax.axis_index("rows") * lax.axis_size("cols") + lax.axis_index("cols")


def swap(value, bit):
    total = lax.axis_size("rows") * lax.axis_size("cols")
    return lax.ppermute(value, ("rows", "cols"), [(i, i ^ (1 << bit | 1)) for i in range(total)])


def local(body, out_shape, name, *operands, **kwargs):
    return pl.pallas_call(
        body,
        out_shape=out_shape,
        in_specs=[pl.BlockSpec(memory_space=pltpu.VMEM)] * len(operands),
        compiler_params=pltpu.CompilerParams(vmem_limit_bytes=8 * 1024 * 1024),
        name=name,
        **kwargs,
    )(*operands)


def side_of(bit):
    index = device_index()
    if bit > 0:
        return lax.rem(index // (1 << bit), 2)
    bits = (lax.axis_size("rows") * lax.axis_size("cols")).bit_length() - 1
    return lax.rem(sum(lax.rem(index // (1 << k), 2) for k in range(bits)), 2)


def rows_at(index, count):
    return pl.ds(pl.multiple_of(index * count, count), count)


def halve(keep, got, bit):
    half = keep.shape[0] // 2

    def body(keep_ref, got_ref, send_ref, stay_ref):
        side = side_of(bit)
        away, here = rows_at(1 - side, half), rows_at(side, half)
        send_ref[...] = (keep_ref[away, :] + got_ref[away, :].astype(f32)).astype(bf16)
        stay_ref[...] = keep_ref[here, :] + got_ref[here, :].astype(f32)

    shape = (half, keep.shape[1])
    return local(
        body,
        (jax.ShapeDtypeStruct(shape, bf16), jax.ShapeDtypeStruct(shape, f32)),
        "halve",
        keep,
        got,
    )


def add(keep, got):
    def body(keep_ref, got_ref, sum_ref):
        sum_ref[...] = (keep_ref[...].astype(f32) + got_ref[...].astype(f32)).astype(bf16)

    return local(body, jax.ShapeDtypeStruct(got.shape, bf16), "add", keep, got)


def join(mine, other, bit):
    def body(mine_ref, other_ref, both_ref):
        side = side_of(bit)
        both_ref[:, pl.ds(side, 1)] = mine_ref[...][:, None]
        both_ref[:, pl.ds(1 - side, 1)] = other_ref[...][:, None]

    shape = (mine.shape[0], 2, *mine.shape[1:])
    return local(body, jax.ShapeDtypeStruct(shape, mine.dtype), "join", mine, other)


def join_cores(mine, other):
    def body(mine_ref, other_ref, both_ref):
        side = side_of(0)
        for chip in range(mine.shape[0]):
            core = lax.rem(side + chip.bit_count(), 2)
            both_ref[chip, pl.ds(core, 1)] = mine_ref[chip][None]
            both_ref[chip, pl.ds(1 - core, 1)] = other_ref[chip][None]

    shape = (mine.shape[0], 2, *mine.shape[1:])
    return local(body, jax.ShapeDtypeStruct(shape, mine.dtype), "join_cores", mine, other)


class Gather:
    def __init__(self, rows):
        self.rows, self.done = rows, []

    def step(self, bit, after, until=None):
        share = self.rows.shape[-2:]
        send, _ = lax.optimization_barrier((self.rows, after))
        got = swap(send, bit)
        if until is not None:
            got, _ = lax.optimization_barrier((got, until))
        if bit > 0:
            lead = 1 << sum(other > bit for other in self.done)
            send, got = (part.reshape(lead, -1, *share) for part in (send, got))
            self.rows = join(send, got, bit).reshape(-1, *share)
        else:
            self.rows = join_cores(send, got).reshape(-1, *share)
        self.done.append(bit)

    def before(self, value):
        value, self.rows = lax.optimization_barrier((value, self.rows))
        return value


def sum_all(send, keep, beside):
    bits = (lax.axis_size("rows") * lax.axis_size("cols")).bit_length() - 1
    halving = list(range(1, min(3, bits)))

    def step(value, bit, name):
        got = swap(value, bit)
        return beside(name, value, got)

    got = step(send, 0, "cores")
    for bit in halving:
        send, keep = halve(keep, got, bit)
        got = step(send, bit, f"halve {bit}")
    mine = add(keep, got)
    for bit in range(len(halving) + 1, bits):
        mine = add(mine, step(mine, bit, f"add {bit}"))
    for bit in reversed(halving):
        got = step(mine, bit, f"join {bit}")
        mine = join(mine[None], got[None], bit).reshape(-1, mine.shape[1])
    return mine, step(mine, 0, "halves")


def gelu_pair(value):
    square = value * value
    tangent = jnp.tanh(value * (gelu_scale + gelu_scale * 0.044715 * square))
    half = 0.5 * value
    plus = 0.5 + 0.5 * tangent
    grad = plus + half * (1.0 - tangent * tangent) * (
        gelu_scale + gelu_scale * 3.0 * 0.044715 * square
    )
    return value * plus, grad


def column(value, c):
    return jnp.concatenate([value[r, c : c + 1] for r in range(value.shape[0])], axis=0)


def rim_kernel(canvas_ref, *out_refs):
    cols = canvas_ref.shape[1]
    begin = canvas_ref[:, 0:16, :].astype(f32)
    end = canvas_ref[:, cols - 16 :, :].astype(f32)
    for c in range(2):
        pair = column(begin, c), column(end, 14 + c)
        if len(out_refs) == 1:
            out_refs[0][c] = jnp.where(lax.axis_index("cols") == 0, pair[1], pair[0]).astype(bf16)
        else:
            out_refs[0][c], out_refs[1][c] = pair[0].astype(bf16), pair[1].astype(bf16)


def payload_kernel(canvas_ref, target_ref, *refs):
    even_ref, odd_ref, left_ref, right_ref, half_ref = refs[-5:]
    rows, cols, width = canvas_ref.shape
    half_ref[0] = target_ref[...].astype(bf16)
    if len(refs) == 6:
        here = lax.axis_index("cols")
        other = refs[0][...].astype(f32)
        left_ref[...] = jnp.where(here == 0, 0.0, other).astype(bf16)
        right_ref[...] = jnp.where(here == 0, other, 0.0).astype(bf16)
    else:
        left_ref[...], right_ref[...] = refs[0][...], refs[1][...]
    beyond = [ref[c].astype(f32) for ref in (left_ref, right_ref) for c in range(2)]

    def fill(ref, r):
        for k in range(2):
            ref[k * cols : (k + 1) * cols, :] = canvas_ref[r + k]
        rim = [part[r + k : r + k + 1] for k in range(2) for part in beyond]
        rim = jnp.concatenate([*rim, jnp.zeros((8, width), f32)], axis=0)
        ref[2 * cols :, :] = rim.astype(bf16)

    odd = lax.rem(lax.axis_index("rows"), 2)

    @pl.when(odd == 0)
    def _():
        fill(even_ref, rows - 2)
        fill(odd_ref, 0)

    @pl.when(odd == 1)
    def _():
        fill(even_ref, 0)
        fill(odd_ref, rows - 2)


def moved_rows(row, before, after):
    cols, width = row.shape
    wide = row.astype(f32)
    place = lax.broadcasted_iota(jnp.int32, (cols, width), 0)
    right = jnp.where(place == 0, before, pltpu.roll(wide, 1, 0))
    left = jnp.where(place == cols - 1, after, pltpu.roll(wide, cols - 1, 0))
    return right.astype(bf16), row.astype(bf16), left.astype(bf16)


def fill_row(cat_ref, r, row, before, after):
    cols, width = row.shape
    for b, part in enumerate(moved_rows(row, before, after)):
        cat_ref[r * cols : (r + 1) * cols, b * width : (b + 1) * width] = part


def fill_patches(cat_ref, spots, row, before, after):
    cols, width = row.shape
    for b, part in enumerate(moved_rows(row, before, after)):
        for r, a in spots:
            at = (3 * a + b) * width
            cat_ref[r * cols : (r + 1) * cols, at : at + width] = part


def gram_tiles(feat, gram_ref, base_ref=None):
    width = feat.shape[1]
    half = width // 2
    product = functools.partial(
        lax.dot_general,
        dimension_numbers=(((0,), (0,)), ((), ())),
        preferred_element_type=f32,
    )
    upper = product(feat[:, :half], feat)
    lower = product(feat[:, half:], feat[:, half:])
    for n, (i, j) in enumerate(tile_pairs(width)):
        at = slice(n * tile, (n + 1) * tile)
        if i * tile < half:
            part = upper[i * tile : (i + 1) * tile, j * tile : (j + 1) * tile]
        else:
            k, m = i * tile - half, j * tile - half
            part = lower[k : k + tile, m : m + tile]
        gram_ref[at, :] = part if base_ref is None else part + base_ref[at, :]


def inner_kernel(
    shape, own_ref, left_ref, right_ref, kernel_ref, bias_ref,
    feat_ref, slope_ref, gram_ref, row_ref, cat_ref,
):
    row_ref[...] = bias_ref[...].astype(f32).reshape(row_ref.shape)
    tile_rows, tile_cols, in_width, out_width, step = shape
    lefts, rights = left_ref[1].astype(f32), right_ref[0].astype(f32)
    for r in range(tile_rows):
        spots = [(r - a, a) for a in range(3) if 0 <= r - a < tile_rows - 2]
        fill_patches(cat_ref, spots, own_ref[r], lefts[r : r + 1], rights[r : r + 1])
    root = 1.0 / math.sqrt(out_width)
    for at in (slice(0, out_width // 2), slice(out_width // 2, out_width)):
        total = row_ref[:, at] + jnp.dot(
            cat_ref[...], kernel_ref[:, at], preferred_element_type=f32
        )
        features, slope = gelu_pair(total)
        feat_ref[:, at] = features.astype(bf16)
        slope_ref[:, at] = (slope * root).astype(bf16)
    gram_tiles(feat_ref[...], gram_ref)


def outer_kernel(
    shape, own_ref, even_ref, odd_ref, left_ref, right_ref, kernel_ref, bias_ref, base_ref,
    feat_ref, slope_ref, send_ref, keep_ref, cat_ref, low_ref, high_ref, gram_ref,
):
    tile_rows, tile_cols, in_width, out_width, step = shape
    odd = lax.rem(lax.axis_index("rows"), 2)
    row = lax.axis_index("rows")
    low_ref[...] = jnp.where(odd == 0, odd_ref[...], even_ref[...])
    high_ref[...] = jnp.where(odd == 0, even_ref[...], odd_ref[...])

    @pl.when(row == 0)
    def _():
        low_ref[...] = jnp.zeros_like(low_ref)

    @pl.when(row == lax.axis_size("rows") - 1)
    def _():
        high_ref[...] = jnp.zeros_like(high_ref)

    first = (lax.axis_index("rows") > 0).astype(f32)
    last = (lax.axis_index("rows") < lax.axis_size("rows") - 1).astype(f32)
    left = (lax.axis_index("cols") > 0).astype(f32)
    right = (lax.axis_index("cols") < lax.axis_size("cols") - 1).astype(f32)
    main = 2 * tile_cols
    low_rim, high_rim = low_ref[main:, :].astype(f32), high_ref[main:, :].astype(f32)
    own_begin = column(own_ref[:, 0:16, :].astype(f32), 0)
    own_end = column(own_ref[:, tile_cols - 16 :, :].astype(f32), 15)

    def sides(c, own):
        return jnp.concatenate(
            [low_rim[c : c + 1], low_rim[4 + c : 5 + c], own, high_rim[c : c + 1], high_rim[4 + c : 5 + c]],
            axis=0,
        )

    def ends(c, own):
        c16 = c // 16 * 16
        piece = lambda ref, k: ref[k + c16 : k + c16 + 16, :].astype(f32)[c - c16 : c - c16 + 1]
        rows = [piece(low_ref, 0), piece(low_ref, tile_cols), own]
        return jnp.concatenate([*rows, piece(high_ref, 0), piece(high_ref, tile_cols)], axis=0)

    lefts = [
        sides(0, left_ref[0].astype(f32)), sides(1, left_ref[1].astype(f32)), ends(0, own_begin)
    ]
    rights = [
        ends(tile_cols - 1, own_end), sides(2, right_ref[0].astype(f32)), sides(3, right_ref[1].astype(f32))
    ]
    lines = [0, 1, 2, 3, tile_rows, tile_rows + 1, tile_rows + 2, tile_rows + 3]
    for r, line in enumerate(lines):
        if line < 2:
            row = low_ref[line * tile_cols : (line + 1) * tile_cols, :]
        elif line < tile_rows + 2:
            row = own_ref[line - 2]
        else:
            k = line - tile_rows - 2
            row = high_ref[k * tile_cols : (k + 1) * tile_cols, :]
        group, r = r // 4, r % 4
        spots = [(2 * group + r - a, a) for a in range(3) if 0 <= r - a < 2]
        fill_patches(cat_ref, spots, row, lefts[1][line : line + 1], rights[1][line : line + 1])
    blank = jnp.zeros((edge - tile_rows - 2, in_width), f32)
    for a in range(3):
        for b in range(3):
            piece = jnp.concatenate(
                [lefts[b][a : a + tile_rows + 2], blank, rights[b][a : a + tile_rows + 2], blank],
                axis=0,
            )
            at = (3 * a + b) * in_width
            cat_ref[2 * main :, at : at + in_width] = piece.astype(bf16)
    root = 1.0 / math.sqrt(out_width)
    line = lax.broadcasted_iota(jnp.int32, (2 * edge, out_width // 2), 0)
    weight = jnp.where(line < edge, left, right)
    weight = jnp.where(line % edge == 0, weight * first, weight)
    weight = jnp.where(line % edge == tile_rows + 1, weight * last, weight)
    for at in (slice(0, out_width // 2), slice(out_width // 2, out_width)):
        total = bias_ref[:, at] + jnp.dot(
            cat_ref[...], kernel_ref[:, at], preferred_element_type=f32
        )
        features, slope = gelu_pair(total)
        slope = slope * root
        feat_ref[:, at] = features.astype(bf16)
        slope_ref[0:tile_cols, at] = (slope[:tile_cols] * first).astype(bf16)
        slope_ref[tile_cols : 3 * tile_cols, at] = slope[tile_cols : 3 * tile_cols].astype(bf16)
        slope_ref[3 * tile_cols : 2 * main, at] = (slope[3 * tile_cols : 2 * main] * last).astype(bf16)
        slope_ref[2 * main :, at] = (slope[2 * main :] * weight).astype(bf16)
    gram_tiles(feat_ref[tile_cols : 3 * tile_cols, :], gram_ref, base_ref)
    half = send_ref.shape[0]
    side = side_of(0)
    send_ref[...] = gram_ref[rows_at(1 - side, half), :].astype(bf16)
    keep_ref[...] = gram_ref[rows_at(side, half), :]


def prepare_kernel(kernel_ref, target_ref, turned_ref, both_ref):
    taps, in_width, out_width = 9, kernel_ref.shape[0] // 9, kernel_ref.shape[1]
    for n in range(taps):
        to = (n // 3 * 3 + 2 - n % 3) * out_width
        turned_ref[to : to + out_width, :] = kernel_ref[n * in_width : (n + 1) * in_width, :].T
    for i, j in tile_pairs(out_width):
        at_i, at_j = slice(i * tile, (i + 1) * tile), slice(j * tile, (j + 1) * tile)
        both = target_ref[at_i, at_j].astype(f32) + target_ref[at_j, at_i].astype(f32).T
        both_ref[at_i, at_j] = both
        if i != j:
            both_ref[at_j, at_i] = both.T


def backward_kernel(
    shape, pixel_total, mine_ref, other_ref, both_ref, in_feat_ref, in_slope_ref, out_feat_ref, out_slope_ref,
    turned_ref, own_gram_ref, out_ref, gram_ref, full_ref, sym_ref, cat_ref,
):
    tile_rows, tile_cols, in_width, out_width, step = shape
    half = mine_ref.shape[0]
    side = side_of(0)
    gram_ref[rows_at(side, half), :] = mine_ref[...].astype(f32)
    gram_ref[rows_at(1 - side, half), :] = other_ref[...].astype(f32)
    for n, (i, j) in enumerate(tile_pairs(out_width)):
        at_i, at_j = slice(i * tile, (i + 1) * tile), slice(j * tile, (j + 1) * tile)
        gram = gram_ref[n * tile : (n + 1) * tile, :] * (1.0 / pixel_total)
        full_ref[at_i, at_j] = gram
        sym_ref[at_i, at_j] = (2.0 * gram - both_ref[at_i, at_j]).astype(bf16)
        if i != j:
            gram = gram.T
            full_ref[at_j, at_i] = gram
            sym_ref[at_j, at_i] = (2.0 * gram - both_ref[at_j, at_i]).astype(bf16)
    share = own_gram_ref.shape[0]
    start = device_index() * share
    if share % 8 == 0:
        own_gram_ref[...] = full_ref[pl.ds(pl.multiple_of(start, 8), share), :]
    else:
        group = full_ref[pl.ds(pl.multiple_of(start // 8 * 8, 8), 8), :]
        picked = group[0:share]
        for k in range(share, 8, share):
            picked = jnp.where(start % 8 == k, group[k : k + share], picked)
        own_gram_ref[...] = picked

    def grad_of(feat_ref, slope_ref, at):
        product = jnp.dot(feat_ref[at, :], sym_ref[...], preferred_element_type=f32)
        return product * slope_ref[at, :].astype(f32)

    main = 2 * tile_cols
    edges = grad_of(out_feat_ref, out_slope_ref, slice(2 * main, None))
    lines = [
        (out_feat_ref, out_slope_ref, 0, 0),
        (out_feat_ref, out_slope_ref, main, tile_rows),
    ] + [
        (in_feat_ref, in_slope_ref, h * tile_cols, h + 2) for h in range(0, tile_rows - 2, step)
    ]
    for feat_ref, slope_ref, begin, r in lines:
        grad = grad_of(feat_ref, slope_ref, slice(begin, begin + step * tile_cols))
        for k in range(step):
            fill_row(
                cat_ref, r + k, grad[k * tile_cols : (k + 1) * tile_cols],
                edges[r + k : r + k + 1], edges[edge + r + k : edge + r + k + 1],
            )
    total = 0.0
    span = 3 * out_width
    for a in range(3):
        total = total + jnp.dot(
            cat_ref[(2 - a) * tile_cols : (2 - a + tile_rows) * tile_cols, :],
            turned_ref[a * span : (a + 1) * span, :],
            preferred_element_type=f32,
        )
    out_ref[...] = total.astype(bf16)


def on_device(canvas, conv_weight, conv_bias, target_gram):
    tile_rows, tile_cols, in_width = canvas.shape
    out_width = conv_weight.shape[3]
    pixel_total = tile_rows * tile_cols * lax.axis_size("rows") * lax.axis_size("cols")
    shape = (tile_rows, tile_cols, in_width, out_width, 2)
    kernel = conv_weight.reshape(9 * in_width, out_width)
    params = pltpu.CompilerParams(vmem_limit_bytes=24 * 1024 * 1024)
    vmem = pl.BlockSpec(memory_space=pltpu.VMEM)
    packed_shape = jax.ShapeDtypeStruct((len(tile_pairs(out_width)) * tile, tile), f32)

    rim_shape = jax.ShapeDtypeStruct((2, tile_rows, in_width), bf16)
    two = lax.axis_size("cols") == 2
    rims = local(
        rim_kernel,
        (rim_shape,) * (1 if two else 2),
        "column_rims",
        canvas,
        cost_estimate=pl.CostEstimate(flops=4_000_000_000, bytes_accessed=600_000, transcendentals=0),
    )
    if two:
        beyond = [lax.ppermute(rims[0], "cols", [(0, 1), (1, 0)])]
    else:
        beyond = shift_cols(rims[1], rims[0])
    payload_shape = jax.ShapeDtypeStruct((2 * tile_cols + edge, in_width), bf16)
    half_shape = jax.ShapeDtypeStruct((1, *target_gram.shape), bf16)
    even, odd, left, right, rows = local(
        payload_kernel,
        (payload_shape, payload_shape, rim_shape, rim_shape, half_shape),
        "row_payload",
        canvas,
        target_gram,
        *beyond,
    )
    count = lax.axis_size("rows")
    even, odd = swap_rows([range(0, count - 1, 2), range(1, count - 1, 2)], [even, odd])

    bits = (lax.axis_size("rows") * lax.axis_size("cols")).bit_length() - 1
    gather = Gather(rows)
    far = list(reversed(range(3, bits)))
    gather.step(far[0], left)
    inner = (tile_rows - 2) * tile_cols
    in_feat, in_slope, in_gram, bias = pl.pallas_call(
        functools.partial(inner_kernel, shape),
        out_shape=(
            jax.ShapeDtypeStruct((inner, out_width), bf16),
            jax.ShapeDtypeStruct((inner, out_width), bf16),
            packed_shape,
            jax.ShapeDtypeStruct((1, out_width), f32),
        ),
        in_specs=[vmem] * 5,
        scratch_shapes=[pltpu.VMEM((inner, 9 * in_width), bf16)],
        compiler_params=params,
        name="inner_rows",
        cost_estimate=pl.CostEstimate(
            flops=2 * inner * (9 * in_width + out_width) * out_width,
            bytes_accessed=6_000_000,
            transcendentals=inner * out_width,
        ),
    )(canvas, left, right, kernel, conv_bias)

    in_gram = gather.before(in_gram)
    outer = 4 * tile_cols + 2 * edge
    half_gram = (packed_shape.shape[0] // 2, tile)
    out_feat, out_slope, send, keep = pl.pallas_call(
        functools.partial(outer_kernel, shape),
        out_shape=(
            jax.ShapeDtypeStruct((outer, out_width), bf16),
            jax.ShapeDtypeStruct((outer, out_width), bf16),
            jax.ShapeDtypeStruct(half_gram, bf16),
            jax.ShapeDtypeStruct(half_gram, f32),
        ),
        in_specs=[vmem] * 8,
        scratch_shapes=[
            pltpu.VMEM((outer, 9 * in_width), bf16),
            pltpu.VMEM(payload_shape.shape, bf16),
            pltpu.VMEM(payload_shape.shape, bf16),
            pltpu.VMEM(packed_shape.shape, f32),
        ],
        compiler_params=params,
        name="outer_rows",
    )(canvas, even, odd, left, right, kernel, bias, in_gram)

    exchanges = {"cores": far[1:2], "halve 2": [*far[2:], 1], "add 3": [2], "add 4": [0]}
    prepared = []

    def beside(name, sent, got):
        for bit in exchanges.get(name, []):
            gather.step(bit, sent, got)
        if name != "join 1":
            return got
        rows, _ = lax.optimization_barrier((gather.rows, sent))
        prepared.extend(
            pl.pallas_call(
                prepare_kernel,
                out_shape=(
                    jax.ShapeDtypeStruct((9 * out_width, in_width), bf16),
                    jax.ShapeDtypeStruct((out_width, out_width), f32),
                ),
                in_specs=[vmem] * 2,
                compiler_params=params,
                name="prepare",
                cost_estimate=pl.CostEstimate(
                    flops=2_000_000_000, bytes_accessed=6_000_000, transcendentals=0
                ),
            )(kernel, rows.reshape(out_width, out_width))
        )
        return lax.optimization_barrier((got, *prepared))[0]

    mine, other = sum_all(send, keep, beside)
    turned, both = prepared
    own_gram, grad = pl.pallas_call(
        functools.partial(backward_kernel, shape, pixel_total),
        out_shape=(
            jax.ShapeDtypeStruct(target_gram.shape, f32),
            jax.ShapeDtypeStruct((tile_rows * tile_cols, in_width), bf16),
        ),
        in_specs=[vmem] * 8,
        scratch_shapes=[
            pltpu.VMEM(packed_shape.shape, f32),
            pltpu.VMEM((out_width, out_width), f32),
            pltpu.VMEM((out_width, out_width), bf16),
            pltpu.VMEM(((tile_rows + 2) * tile_cols, 3 * out_width), bf16),
        ],
        compiler_params=params,
        name="grad_conv",
    )(mine, other, both, in_feat, in_slope, out_feat, out_slope, turned)
    return own_gram, grad.reshape(tile_rows, tile_cols, in_width)


def solution(mesh):
    return jax.shard_map(
        on_device,
        mesh=mesh,
        in_specs=(P("rows", "cols", None), P(), P(), P(("rows", "cols"), None)),
        out_specs=(P(("rows", "cols"), None), P("rows", "cols", None)),
        check_vma=False,
    )
```

```python
import functools
import math

import jax
import jax.numpy as jnp
from jax import lax
from jax.experimental import pallas as pl
from jax.experimental.pallas import tpu as pltpu
from jax.sharding import PartitionSpec as P

gelu_scale = math.sqrt(2.0 / math.pi)
tile = 128
edge = 16
f32, bf16 = jnp.float32, jnp.bfloat16


def tile_pairs(width):
    count = width // tile
    return [(i, j) for i in range(count) for j in range(i, count)]


def swap_rows(pairs, values):
    count = lax.axis_size("rows")

    def perm(low):
        partner = {i: i for i in range(count)}
        partner.update({i: i + 1 for i in low})
        partner.update({i + 1: i for i in low})
        return list(partner.items())

    return [lax.ppermute(value, "rows", perm(low)) for low, value in zip(pairs, values)]


def shift_cols(last, first):
    count = lax.axis_size("cols")
    forward = [(i, i + 1) for i in range(count - 1)]
    backward = [(target, source) for source, target in forward]
    return lax.ppermute(last, "cols", forward), lax.ppermute(first, "cols", backward)


def device_index():
    return lax.axis_index("rows") * lax.axis_size("cols") + lax.axis_index("cols")


def swap(value, bit):
    total = lax.axis_size("rows") * lax.axis_size("cols")
    return lax.ppermute(value, ("rows", "cols"), [(i, i ^ (1 << bit | 1)) for i in range(total)])


def local(body, out_shape, name, *operands, **kwargs):
    return pl.pallas_call(
        body,
        out_shape=out_shape,
        in_specs=[pl.BlockSpec(memory_space=pltpu.VMEM)] * len(operands),
        compiler_params=pltpu.CompilerParams(vmem_limit_bytes=8 * 1024 * 1024),
        name=name,
        **kwargs,
    )(*operands)


def side_of(bit):
    index = device_index()
    if bit > 0:
        return lax.rem(index // (1 << bit), 2)
    bits = (lax.axis_size("rows") * lax.axis_size("cols")).bit_length() - 1
    return lax.rem(sum(lax.rem(index // (1 << k), 2) for k in range(bits)), 2)


def rows_at(index, count):
    return pl.ds(pl.multiple_of(index * count, count), count)


waiting = pl.CostEstimate(flops=1_500_000_000, bytes_accessed=100_000, transcendentals=0)
chained = pl.CostEstimate(flops=8_000_000_000, bytes_accessed=100_000, transcendentals=0)


def halve(keep, got, bit):
    half = keep.shape[0] // 2

    def body(keep_ref, got_ref, send_ref, stay_ref):
        side = side_of(bit)
        away, here = rows_at(1 - side, half), rows_at(side, half)
        send_ref[...] = (keep_ref[away, :] + got_ref[away, :].astype(f32)).astype(bf16)
        stay_ref[...] = keep_ref[here, :] + got_ref[here, :].astype(f32)

    shape = (half, keep.shape[1])
    return local(
        body,
        (jax.ShapeDtypeStruct(shape, bf16), jax.ShapeDtypeStruct(shape, f32)),
        "halve",
        keep,
        got,
        cost_estimate=chained,
    )


def add(keep, got):
    def body(keep_ref, got_ref, sum_ref):
        sum_ref[...] = (keep_ref[...].astype(f32) + got_ref[...].astype(f32)).astype(bf16)

    return local(body, jax.ShapeDtypeStruct(got.shape, bf16), "add", keep, got, cost_estimate=chained)


def join(mine, other, bit, **kwargs):
    def body(mine_ref, other_ref, both_ref):
        side = side_of(bit)
        both_ref[:, pl.ds(side, 1)] = mine_ref[...][:, None]
        both_ref[:, pl.ds(1 - side, 1)] = other_ref[...][:, None]

    shape = (mine.shape[0], 2, *mine.shape[1:])
    return local(body, jax.ShapeDtypeStruct(shape, mine.dtype), "join", mine, other, **kwargs)


def join_cores(mine, other, **kwargs):
    def body(mine_ref, other_ref, both_ref):
        side = side_of(0)
        for chip in range(mine.shape[0]):
            core = lax.rem(side + chip.bit_count(), 2)
            both_ref[chip, pl.ds(core, 1)] = mine_ref[chip][None]
            both_ref[chip, pl.ds(1 - core, 1)] = other_ref[chip][None]

    shape = (mine.shape[0], 2, *mine.shape[1:])
    return local(body, jax.ShapeDtypeStruct(shape, mine.dtype), "join_cores", mine, other, **kwargs)


class Gather:
    def __init__(self, rows):
        self.rows, self.got, self.done = rows, None, []

    def settle(self, after):
        if self.got is None:
            self.rows, _ = lax.optimization_barrier((self.rows, after))
            return
        share = self.rows.shape[-2:]
        got, _ = lax.optimization_barrier((self.got, after))
        bit = self.done[-1]
        if bit > 0:
            lead = 1 << sum(other > bit for other in self.done)
            mine, got = (part.reshape(lead, -1, *share) for part in (self.rows, got))
            both = join(mine, got, bit, cost_estimate=waiting)
        else:
            both = join_cores(self.rows, got, cost_estimate=waiting)
        self.rows, self.got = both.reshape(-1, *share), None

    def step(self, bit, after):
        self.settle(after)
        self.got = swap(self.rows, bit)
        self.done.append(bit)


def sum_all(send, keep, beside):
    bits = (lax.axis_size("rows") * lax.axis_size("cols")).bit_length() - 1
    halving = list(range(1, min(3, bits)))

    def step(value, bit, name):
        got = swap(value, bit)
        return beside(name, value, got)

    got = step(send, 0, "cores")
    for bit in halving:
        send, keep = halve(keep, got, bit)
        got = step(send, bit, f"halve {bit}")
    mine = add(keep, got)
    for bit in range(len(halving) + 1, bits):
        mine = add(mine, step(mine, bit, f"add {bit}"))
    for bit in reversed(halving):
        got = step(mine, bit, f"join {bit}")
        mine = join(mine[None], got[None], bit, cost_estimate=chained).reshape(-1, mine.shape[1])
    return mine, step(mine, 0, "halves")


def gelu_pair(value):
    square = value * value
    tangent = jnp.tanh(value * (gelu_scale + gelu_scale * 0.044715 * square))
    half = 0.5 * value
    plus = 0.5 + 0.5 * tangent
    grad = plus + half * (1.0 - tangent * tangent) * (
        gelu_scale + gelu_scale * 3.0 * 0.044715 * square
    )
    return value * plus, grad


def column(value, c):
    return jnp.concatenate([value[r, c : c + 1] for r in range(value.shape[0])], axis=0)


def rim_kernel(canvas_ref, *out_refs):
    cols = canvas_ref.shape[1]
    begin = canvas_ref[:, 0:16, :].astype(f32)
    end = canvas_ref[:, cols - 16 :, :].astype(f32)
    for c in range(2):
        pair = column(begin, c), column(end, 14 + c)
        if len(out_refs) == 1:
            out_refs[0][c] = jnp.where(lax.axis_index("cols") == 0, pair[1], pair[0]).astype(bf16)
        else:
            out_refs[0][c], out_refs[1][c] = pair[0].astype(bf16), pair[1].astype(bf16)


def payload_kernel(canvas_ref, target_ref, *refs):
    even_ref, odd_ref, left_ref, right_ref, half_ref = refs[-5:]
    rows, cols, width = canvas_ref.shape
    half_ref[0] = target_ref[...].astype(bf16)
    if len(refs) == 6:
        here = lax.axis_index("cols")
        other = refs[0][...].astype(f32)
        left_ref[...] = jnp.where(here == 0, 0.0, other).astype(bf16)
        right_ref[...] = jnp.where(here == 0, other, 0.0).astype(bf16)
    else:
        left_ref[...], right_ref[...] = refs[0][...], refs[1][...]
    beyond = [ref[c].astype(f32) for ref in (left_ref, right_ref) for c in range(2)]

    def fill(ref, r):
        for k in range(2):
            ref[k * cols : (k + 1) * cols, :] = canvas_ref[r + k]
        rim = [part[r + k : r + k + 1] for k in range(2) for part in beyond]
        rim = jnp.concatenate([*rim, jnp.zeros((8, width), f32)], axis=0)
        ref[2 * cols :, :] = rim.astype(bf16)

    odd = lax.rem(lax.axis_index("rows"), 2)

    @pl.when(odd == 0)
    def _():
        fill(even_ref, rows - 2)
        fill(odd_ref, 0)

    @pl.when(odd == 1)
    def _():
        fill(even_ref, 0)
        fill(odd_ref, rows - 2)


def moved_rows(row, before, after):
    cols, width = row.shape
    wide = row.astype(f32)
    place = lax.broadcasted_iota(jnp.int32, (cols, width), 0)
    right = jnp.where(place == 0, before, pltpu.roll(wide, 1, 0))
    left = jnp.where(place == cols - 1, after, pltpu.roll(wide, cols - 1, 0))
    return right.astype(bf16), row.astype(bf16), left.astype(bf16)


def fill_row(cat_ref, r, row, before, after):
    cols, width = row.shape
    for b, part in enumerate(moved_rows(row, before, after)):
        cat_ref[r * cols : (r + 1) * cols, b * width : (b + 1) * width] = part


def fill_patches(cat_ref, spots, row, before, after):
    cols, width = row.shape
    for b, part in enumerate(moved_rows(row, before, after)):
        for r, a in spots:
            at = (3 * a + b) * width
            cat_ref[r * cols : (r + 1) * cols, at : at + width] = part


def gram_tiles(feat, gram_ref, base_ref=None):
    width = feat.shape[1]
    half = width // 2
    product = functools.partial(
        lax.dot_general,
        dimension_numbers=(((0,), (0,)), ((), ())),
        preferred_element_type=f32,
    )
    upper = product(feat[:, :half], feat)
    lower = product(feat[:, half:], feat[:, half:])
    for n, (i, j) in enumerate(tile_pairs(width)):
        at = slice(n * tile, (n + 1) * tile)
        if i * tile < half:
            part = upper[i * tile : (i + 1) * tile, j * tile : (j + 1) * tile]
        else:
            k, m = i * tile - half, j * tile - half
            part = lower[k : k + tile, m : m + tile]
        gram_ref[at, :] = part if base_ref is None else part + base_ref[at, :]


def inner_kernel(
    shape, own_ref, left_ref, right_ref, kernel_ref, bias_ref,
    feat_ref, slope_ref, gram_ref, row_ref, cat_ref,
):
    row_ref[...] = bias_ref[...].astype(f32).reshape(row_ref.shape)
    tile_rows, tile_cols, in_width, out_width, step = shape
    lefts, rights = left_ref[1].astype(f32), right_ref[0].astype(f32)
    for r in range(tile_rows):
        fill_row(cat_ref, r, own_ref[r], lefts[r : r + 1], rights[r : r + 1])
    bias = row_ref[...]
    root = 1.0 / math.sqrt(out_width)
    span = 3 * in_width
    for h in range(0, tile_rows - 2, step):
        total = bias
        for a in range(3):
            total = total + jnp.dot(
                cat_ref[(h + a) * tile_cols : (h + a + step) * tile_cols, :],
                kernel_ref[a * span : (a + 1) * span, :],
                preferred_element_type=f32,
            )
        features, slope = gelu_pair(total)
        at = slice(h * tile_cols, (h + step) * tile_cols)
        feat_ref[at, :] = features.astype(bf16)
        slope_ref[at, :] = (slope * root).astype(bf16)
    gram_tiles(feat_ref[...], gram_ref)


def outer_kernel(
    shape, own_ref, even_ref, odd_ref, left_ref, right_ref, kernel_ref, bias_ref, base_ref,
    feat_ref, slope_ref, send_ref, keep_ref, cat_ref, low_ref, high_ref, gram_ref,
):
    tile_rows, tile_cols, in_width, out_width, step = shape
    odd = lax.rem(lax.axis_index("rows"), 2)
    row = lax.axis_index("rows")
    low_ref[...] = jnp.where(odd == 0, odd_ref[...], even_ref[...])
    high_ref[...] = jnp.where(odd == 0, even_ref[...], odd_ref[...])

    @pl.when(row == 0)
    def _():
        low_ref[...] = jnp.zeros_like(low_ref)

    @pl.when(row == lax.axis_size("rows") - 1)
    def _():
        high_ref[...] = jnp.zeros_like(high_ref)

    first = (lax.axis_index("rows") > 0).astype(f32)
    last = (lax.axis_index("rows") < lax.axis_size("rows") - 1).astype(f32)
    left = (lax.axis_index("cols") > 0).astype(f32)
    right = (lax.axis_index("cols") < lax.axis_size("cols") - 1).astype(f32)
    main = 2 * tile_cols
    low_rim, high_rim = low_ref[main:, :].astype(f32), high_ref[main:, :].astype(f32)
    own_begin = column(own_ref[:, 0:16, :].astype(f32), 0)
    own_end = column(own_ref[:, tile_cols - 16 :, :].astype(f32), 15)

    def sides(c, own):
        return jnp.concatenate(
            [low_rim[c : c + 1], low_rim[4 + c : 5 + c], own, high_rim[c : c + 1], high_rim[4 + c : 5 + c]],
            axis=0,
        )

    def ends(c, own):
        c16 = c // 16 * 16
        piece = lambda ref, k: ref[k + c16 : k + c16 + 16, :].astype(f32)[c - c16 : c - c16 + 1]
        rows = [piece(low_ref, 0), piece(low_ref, tile_cols), own]
        return jnp.concatenate([*rows, piece(high_ref, 0), piece(high_ref, tile_cols)], axis=0)

    lefts = [
        sides(0, left_ref[0].astype(f32)), sides(1, left_ref[1].astype(f32)), ends(0, own_begin)
    ]
    rights = [
        ends(tile_cols - 1, own_end), sides(2, right_ref[0].astype(f32)), sides(3, right_ref[1].astype(f32))
    ]
    lines = [0, 1, 2, 3, tile_rows, tile_rows + 1, tile_rows + 2, tile_rows + 3]
    for r, line in enumerate(lines):
        if line < 2:
            row = low_ref[line * tile_cols : (line + 1) * tile_cols, :]
        elif line < tile_rows + 2:
            row = own_ref[line - 2]
        else:
            k = line - tile_rows - 2
            row = high_ref[k * tile_cols : (k + 1) * tile_cols, :]
        group, r = r // 4, r % 4
        spots = [(2 * group + r - a, a) for a in range(3) if 0 <= r - a < 2]
        fill_patches(cat_ref, spots, row, lefts[1][line : line + 1], rights[1][line : line + 1])
    blank = jnp.zeros((edge - tile_rows - 2, in_width), f32)
    for a in range(3):
        for b in range(3):
            piece = jnp.concatenate(
                [lefts[b][a : a + tile_rows + 2], blank, rights[b][a : a + tile_rows + 2], blank],
                axis=0,
            )
            at = (3 * a + b) * in_width
            cat_ref[2 * main :, at : at + in_width] = piece.astype(bf16)
    root = 1.0 / math.sqrt(out_width)
    line = lax.broadcasted_iota(jnp.int32, (2 * edge, out_width // 2), 0)
    weight = jnp.where(line < edge, left, right)
    weight = jnp.where(line % edge == 0, weight * first, weight)
    weight = jnp.where(line % edge == tile_rows + 1, weight * last, weight)
    for at in (slice(0, out_width // 2), slice(out_width // 2, out_width)):
        total = bias_ref[:, at] + jnp.dot(
            cat_ref[...], kernel_ref[:, at], preferred_element_type=f32
        )
        features, slope = gelu_pair(total)
        slope = slope * root
        feat_ref[:, at] = features.astype(bf16)
        slope_ref[0:tile_cols, at] = (slope[:tile_cols] * first).astype(bf16)
        slope_ref[tile_cols : 3 * tile_cols, at] = slope[tile_cols : 3 * tile_cols].astype(bf16)
        slope_ref[3 * tile_cols : 2 * main, at] = (slope[3 * tile_cols : 2 * main] * last).astype(bf16)
        slope_ref[2 * main :, at] = (slope[2 * main :] * weight).astype(bf16)
    gram_tiles(feat_ref[tile_cols : 3 * tile_cols, :], gram_ref, base_ref)
    half = send_ref.shape[0]
    side = side_of(0)
    send_ref[...] = gram_ref[rows_at(1 - side, half), :].astype(bf16)
    keep_ref[...] = gram_ref[rows_at(side, half), :]


def prepare_kernel(kernel_ref, target_ref, turned_ref, both_ref):
    taps, in_width, out_width = 9, kernel_ref.shape[0] // 9, kernel_ref.shape[1]
    for n in range(taps):
        to = (n // 3 * 3 + 2 - n % 3) * out_width
        turned_ref[to : to + out_width, :] = kernel_ref[n * in_width : (n + 1) * in_width, :].T
    for i, j in tile_pairs(out_width):
        at_i, at_j = slice(i * tile, (i + 1) * tile), slice(j * tile, (j + 1) * tile)
        both = target_ref[at_i, at_j].astype(f32) + target_ref[at_j, at_i].astype(f32).T
        both_ref[at_i, at_j] = both
        if i != j:
            both_ref[at_j, at_i] = both.T


def backward_kernel(
    shape, pixel_total, mine_ref, other_ref, both_ref, in_feat_ref, in_slope_ref, out_feat_ref, out_slope_ref,
    turned_ref, own_gram_ref, out_ref, gram_ref, full_ref, sym_ref, cat_ref,
):
    tile_rows, tile_cols, in_width, out_width, step = shape
    half = mine_ref.shape[0]
    side = side_of(0)
    gram_ref[rows_at(side, half), :] = mine_ref[...].astype(f32)
    gram_ref[rows_at(1 - side, half), :] = other_ref[...].astype(f32)
    for n, (i, j) in enumerate(tile_pairs(out_width)):
        at_i, at_j = slice(i * tile, (i + 1) * tile), slice(j * tile, (j + 1) * tile)
        gram = gram_ref[n * tile : (n + 1) * tile, :] * (1.0 / pixel_total)
        full_ref[at_i, at_j] = gram
        sym_ref[at_i, at_j] = (2.0 * gram - both_ref[at_i, at_j]).astype(bf16)
        if i != j:
            gram = gram.T
            full_ref[at_j, at_i] = gram
            sym_ref[at_j, at_i] = (2.0 * gram - both_ref[at_j, at_i]).astype(bf16)
    share = own_gram_ref.shape[0]
    start = device_index() * share
    if share % 8 == 0:
        own_gram_ref[...] = full_ref[pl.ds(pl.multiple_of(start, 8), share), :]
    else:
        group = full_ref[pl.ds(pl.multiple_of(start // 8 * 8, 8), 8), :]
        picked = group[0:share]
        for k in range(share, 8, share):
            picked = jnp.where(start % 8 == k, group[k : k + share], picked)
        own_gram_ref[...] = picked

    def grad_of(feat_ref, slope_ref, at):
        product = jnp.dot(feat_ref[at, :], sym_ref[...], preferred_element_type=f32)
        return product * slope_ref[at, :].astype(f32)

    main = 2 * tile_cols
    edges = grad_of(out_feat_ref, out_slope_ref, slice(2 * main, None))
    lines = [(out_feat_ref, out_slope_ref, 0)]
    lines += [(in_feat_ref, in_slope_ref, h * tile_cols) for h in range(0, tile_rows - 2, step)]
    lines += [(out_feat_ref, out_slope_ref, main)]
    grads = {}

    def upstream(c):
        feat_ref, slope_ref, begin = lines[c]
        grads[c] = grad_of(feat_ref, slope_ref, slice(begin, begin + step * tile_cols))

    def fill(c):
        for k in range(step):
            r = c * step + k
            fill_row(
                cat_ref, r, grads[c][k * tile_cols : (k + 1) * tile_cols],
                edges[r : r + 1], edges[edge + r : edge + r + 1],
            )

    span = 3 * out_width

    def convolve(begin, count):
        total = 0.0
        for a in range(3):
            total = total + jnp.dot(
                cat_ref[(begin + 2 - a) * tile_cols : (begin + 2 - a + count) * tile_cols, :],
                turned_ref[a * span : (a + 1) * span, :],
                preferred_element_type=f32,
            )
        out_ref[begin * tile_cols : (begin + count) * tile_cols, :] = total.astype(bf16)

    last = len(lines) - 1
    middle = last // 2
    half_rows = middle * step
    upstream(0)
    for c in range(last):
        upstream(c + 1)
        fill(c)
        if c == middle:
            convolve(0, half_rows)
    fill(last)
    convolve(half_rows, tile_rows - half_rows)


def on_device(canvas, conv_weight, conv_bias, target_gram):
    tile_rows, tile_cols, in_width = canvas.shape
    out_width = conv_weight.shape[3]
    pixel_total = tile_rows * tile_cols * lax.axis_size("rows") * lax.axis_size("cols")
    shape = (tile_rows, tile_cols, in_width, out_width, 2)
    kernel = conv_weight.reshape(9 * in_width, out_width)
    params = pltpu.CompilerParams(vmem_limit_bytes=24 * 1024 * 1024)
    vmem = pl.BlockSpec(memory_space=pltpu.VMEM)
    packed_shape = jax.ShapeDtypeStruct((len(tile_pairs(out_width)) * tile, tile), f32)

    rim_shape = jax.ShapeDtypeStruct((2, tile_rows, in_width), bf16)
    two = lax.axis_size("cols") == 2
    rims = local(
        rim_kernel,
        (rim_shape,) * (1 if two else 2),
        "column_rims",
        canvas,
        cost_estimate=pl.CostEstimate(flops=4_000_000_000, bytes_accessed=600_000, transcendentals=0),
    )
    if two:
        beyond = [lax.ppermute(rims[0], "cols", [(0, 1), (1, 0)])]
    else:
        beyond = shift_cols(rims[1], rims[0])
    payload_shape = jax.ShapeDtypeStruct((2 * tile_cols + edge, in_width), bf16)
    half_shape = jax.ShapeDtypeStruct((1, *target_gram.shape), bf16)
    even, odd, left, right, rows = local(
        payload_kernel,
        (payload_shape, payload_shape, rim_shape, rim_shape, half_shape),
        "row_payload",
        canvas,
        target_gram,
        *beyond,
    )
    count = lax.axis_size("rows")
    odd, even = swap_rows([range(1, count - 1, 2), range(0, count - 1, 2)], [odd, even])

    bits = (lax.axis_size("rows") * lax.axis_size("cols")).bit_length() - 1
    gather = Gather(rows)
    far = list(reversed(range(3, bits)))
    inner = (tile_rows - 2) * tile_cols
    in_feat, in_slope, in_gram, bias = pl.pallas_call(
        functools.partial(inner_kernel, shape),
        out_shape=(
            jax.ShapeDtypeStruct((inner, out_width), bf16),
            jax.ShapeDtypeStruct((inner, out_width), bf16),
            packed_shape,
            jax.ShapeDtypeStruct((1, out_width), f32),
        ),
        in_specs=[vmem] * 5,
        scratch_shapes=[pltpu.VMEM((tile_rows * tile_cols, 3 * in_width), bf16)],
        compiler_params=params,
        name="inner_rows",
        cost_estimate=pl.CostEstimate(
            flops=2 * inner * (9 * in_width + out_width) * out_width,
            bytes_accessed=6_000_000,
            transcendentals=inner * out_width,
        ),
    )(canvas, left, right, kernel, conv_bias)

    outer = 4 * tile_cols + 2 * edge
    half_gram = (packed_shape.shape[0] // 2, tile)
    out_feat, out_slope, send, keep = pl.pallas_call(
        functools.partial(outer_kernel, shape),
        out_shape=(
            jax.ShapeDtypeStruct((outer, out_width), bf16),
            jax.ShapeDtypeStruct((outer, out_width), bf16),
            jax.ShapeDtypeStruct(half_gram, bf16),
            jax.ShapeDtypeStruct(half_gram, f32),
        ),
        in_specs=[vmem] * 8,
        scratch_shapes=[
            pltpu.VMEM((outer, 9 * in_width), bf16),
            pltpu.VMEM(payload_shape.shape, bf16),
            pltpu.VMEM(payload_shape.shape, bf16),
            pltpu.VMEM(packed_shape.shape, f32),
        ],
        compiler_params=params,
        name="outer_rows",
    )(canvas, even, odd, left, right, kernel, bias, in_gram)

    exchanges = {"halve 1": far[:1], "halve 2": far[1:], "add 3": [2], "add 4": [1], "join 2": [0]}
    prepared = []

    def beside(name, sent, got):
        for bit in exchanges.get(name, []):
            gather.step(bit, sent)
        if name != "join 1":
            return got
        gather.settle(sent)
        prepared.extend(
            pl.pallas_call(
                prepare_kernel,
                out_shape=(
                    jax.ShapeDtypeStruct((9 * out_width, in_width), bf16),
                    jax.ShapeDtypeStruct((out_width, out_width), f32),
                ),
                in_specs=[vmem] * 2,
                compiler_params=params,
                name="prepare",
                cost_estimate=pl.CostEstimate(
                    flops=2_000_000_000, bytes_accessed=6_000_000, transcendentals=0
                ),
            )(kernel, gather.rows.reshape(out_width, out_width))
        )
        return lax.optimization_barrier((got, *prepared))[0]

    mine, other = sum_all(send, keep, beside)
    turned, both = prepared
    own_gram, grad = pl.pallas_call(
        functools.partial(backward_kernel, shape, pixel_total),
        out_shape=(
            jax.ShapeDtypeStruct(target_gram.shape, f32),
            jax.ShapeDtypeStruct((tile_rows * tile_cols, in_width), bf16),
        ),
        in_specs=[vmem] * 8,
        scratch_shapes=[
            pltpu.VMEM(packed_shape.shape, f32),
            pltpu.VMEM((out_width, out_width), f32),
            pltpu.VMEM((out_width, out_width), bf16),
            pltpu.VMEM(((tile_rows + 2) * tile_cols, 3 * out_width), bf16),
        ],
        compiler_params=params,
        name="grad_conv",
    )(mine, other, both, in_feat, in_slope, out_feat, out_slope, turned)
    return own_gram, grad.reshape(tile_rows, tile_cols, in_width)


def solution(mesh):
    return jax.shard_map(
        on_device,
        mesh=mesh,
        in_specs=(P("rows", "cols", None), P(), P(), P(("rows", "cols"), None)),
        out_specs=(P(("rows", "cols"), None), P("rows", "cols", None)),
        check_vma=False,
    )
```

```python
import functools
import math

import jax
import jax.numpy as jnp
from jax import lax
from jax.experimental import pallas as pl
from jax.experimental.pallas import tpu as pltpu
from jax.sharding import PartitionSpec as P

gelu_scale = math.sqrt(2.0 / math.pi)
tile = 128
edge = 16
f32, bf16 = jnp.float32, jnp.bfloat16


def tile_pairs(width):
    count = width // tile
    return [(i, j) for i in range(count) for j in range(i, count)]


def swap_rows(low, value):
    partner = {i: i for i in range(lax.axis_size("rows"))}
    partner.update({i: i + 1 for i in low})
    partner.update({i + 1: i for i in low})
    return lax.ppermute(value, "rows", list(partner.items()))


def shift_cols(last, first):
    count = lax.axis_size("cols")
    forward = [(i, i + 1) for i in range(count - 1)]
    backward = [(target, source) for source, target in forward]
    return lax.ppermute(last, "cols", forward), lax.ppermute(first, "cols", backward)


def device_index():
    return lax.axis_index("rows") * lax.axis_size("cols") + lax.axis_index("cols")


def swap(value, *bits):
    total = lax.axis_size("rows") * lax.axis_size("cols")
    flip = sum(1 << bit for bit in bits) | len(bits) % 2
    return lax.ppermute(value, ("rows", "cols"), [(i, i ^ flip) for i in range(total)])


def local(body, out_shape, name, *operands, **kwargs):
    return pl.pallas_call(
        body,
        out_shape=out_shape,
        in_specs=[pl.BlockSpec(memory_space=pltpu.VMEM)] * len(operands),
        compiler_params=pltpu.CompilerParams(vmem_limit_bytes=8 * 1024 * 1024),
        name=name,
        **kwargs,
    )(*operands)


def side_of(bit):
    index = device_index()
    if bit > 0:
        return lax.rem(index // (1 << bit), 2)
    bits = (lax.axis_size("rows") * lax.axis_size("cols")).bit_length() - 1
    return lax.rem(sum(lax.rem(index // (1 << k), 2) for k in range(bits)), 2)


def rows_at(index, count):
    return pl.ds(pl.multiple_of(index * count, count), count)


waiting = pl.CostEstimate(flops=1_500_000_000, bytes_accessed=100_000, transcendentals=0)
chained = pl.CostEstimate(flops=8_000_000_000, bytes_accessed=100_000, transcendentals=0)


def halve(keep, got, bit):
    half = keep.shape[0] // 2

    def body(keep_ref, got_ref, send_ref, stay_ref):
        side = side_of(bit)
        away, here = rows_at(1 - side, half), rows_at(side, half)
        send_ref[...] = (keep_ref[away, :] + got_ref[away, :].astype(f32)).astype(bf16)
        stay_ref[...] = keep_ref[here, :] + got_ref[here, :].astype(f32)

    shape = (half, keep.shape[1])
    return local(
        body,
        (jax.ShapeDtypeStruct(shape, bf16), jax.ShapeDtypeStruct(shape, f32)),
        "halve",
        keep,
        got,
        cost_estimate=chained,
    )


def add(*parts):
    def body(*refs):
        refs[-1][...] = sum(ref[...].astype(f32) for ref in refs[:-1]).astype(bf16)

    return local(body, jax.ShapeDtypeStruct(parts[0].shape, bf16), "add", *parts, cost_estimate=chained)


def join(mine, other, bit, **kwargs):
    def body(mine_ref, other_ref, both_ref):
        side = side_of(bit)
        both_ref[:, pl.ds(side, 1)] = mine_ref[...][:, None]
        both_ref[:, pl.ds(1 - side, 1)] = other_ref[...][:, None]

    shape = (mine.shape[0], 2, *mine.shape[1:])
    return local(body, jax.ShapeDtypeStruct(shape, mine.dtype), "join", mine, other, **kwargs)


def join_cores(mine, other, **kwargs):
    def body(mine_ref, other_ref, both_ref):
        side = side_of(0)
        for chip in range(mine.shape[0]):
            core = lax.rem(side + chip.bit_count(), 2)
            both_ref[chip, pl.ds(core, 1)] = mine_ref[chip][None]
            both_ref[chip, pl.ds(1 - core, 1)] = other_ref[chip][None]

    shape = (mine.shape[0], 2, *mine.shape[1:])
    return local(body, jax.ShapeDtypeStruct(shape, mine.dtype), "join_cores", mine, other, **kwargs)


class Gather:
    def __init__(self, rows):
        self.rows, self.got, self.done = rows, None, []

    def settle(self, after):
        if self.got is None:
            self.rows, _ = lax.optimization_barrier((self.rows, after))
            return
        share = self.rows.shape[-2:]
        got, _ = lax.optimization_barrier((self.got, after))
        bit = self.done[-1]
        if bit > 0:
            lead = 1 << sum(other > bit for other in self.done)
            mine, got = (part.reshape(lead, -1, *share) for part in (self.rows, got))
            both = join(mine, got, bit, cost_estimate=waiting)
        else:
            both = join_cores(self.rows, got, cost_estimate=waiting)
        self.rows, self.got = both.reshape(-1, *share), None

    def step(self, bit, after):
        self.settle(after)
        self.got = swap(self.rows, bit)
        self.done.append(bit)


def sum_all(send, keep, beside):
    bits = (lax.axis_size("rows") * lax.axis_size("cols")).bit_length() - 1
    halving = list(range(1, min(3, bits)))

    def step(value, bit, name):
        return beside(name, value, swap(value, bit))

    got = step(send, 0, "cores")
    for bit in halving:
        send, keep = halve(keep, got, bit)
        got = step(send, bit, f"halve {bit}")
    mine = add(keep, got)
    for bit in range(len(halving) + 1, bits, 2):
        if bit + 1 < bits:
            parts = [swap(mine, bit, bit + 1), swap(mine, bit), swap(mine, bit + 1)]
        else:
            parts = [swap(mine, bit)]
        parts[0] = beside(f"add {bit}", mine, parts[0])
        mine = add(mine, *parts)
    for bit in reversed(halving):
        got = step(mine, bit, f"join {bit}")
        mine = join(mine[None], got[None], bit, cost_estimate=chained).reshape(-1, mine.shape[1])
    return mine, step(mine, 0, "halves")


def gelu_pair(value):
    square = value * value
    tangent = jnp.tanh(value * (gelu_scale + gelu_scale * 0.044715 * square))
    half = 0.5 * value
    plus = 0.5 + 0.5 * tangent
    grad = plus + half * (1.0 - tangent * tangent) * (
        gelu_scale + gelu_scale * 3.0 * 0.044715 * square
    )
    return value * plus, grad


def column(value, c):
    return jnp.concatenate([value[r, c : c + 1] for r in range(value.shape[0])], axis=0)


def rim_kernel(canvas_ref, *out_refs):
    cols = canvas_ref.shape[1]
    begin = canvas_ref[:, 0:16, :].astype(f32)
    end = canvas_ref[:, cols - 16 :, :].astype(f32)
    for c in range(2):
        pair = column(begin, c), column(end, 14 + c)
        if len(out_refs) == 1:
            out_refs[0][c] = jnp.where(lax.axis_index("cols") == 0, pair[1], pair[0]).astype(bf16)
        else:
            out_refs[0][c], out_refs[1][c] = pair[0].astype(bf16), pair[1].astype(bf16)


def fill_payload(ref, canvas_ref, left_ref, right_ref, first, last):
    rows, cols, width = canvas_ref.shape

    def fill(r):
        for k in range(2):
            ref[k * cols : (k + 1) * cols, :] = canvas_ref[r + k]
        beyond = [part[c].astype(f32) for part in (left_ref, right_ref) for c in range(2)]
        rim = [part[r + k : r + k + 1] for k in range(2) for part in beyond]
        rim = jnp.concatenate([*rim, jnp.zeros((8, width), f32)], axis=0)
        ref[2 * cols :, :] = rim.astype(bf16)

    odd = lax.rem(lax.axis_index("rows"), 2)
    pl.when(odd == first)(lambda: fill(0))
    pl.when(odd == last)(lambda: fill(rows - 2))


def odd_payload_kernel(canvas_ref, target_ref, *refs):
    odd_ref, left_ref, right_ref, half_ref = refs[-4:]
    half_ref[0] = target_ref[...].astype(bf16)
    if len(refs) == 5:
        here = lax.axis_index("cols")
        other = refs[0][...].astype(f32)
        left_ref[...] = jnp.where(here == 0, 0.0, other).astype(bf16)
        right_ref[...] = jnp.where(here == 0, other, 0.0).astype(bf16)
    else:
        left_ref[...], right_ref[...] = refs[0][...], refs[1][...]
    fill_payload(odd_ref, canvas_ref, left_ref, right_ref, 0, 1)


def even_payload_kernel(canvas_ref, left_ref, right_ref, _, even_ref):
    fill_payload(even_ref, canvas_ref, left_ref, right_ref, 1, 0)


def moved_rows(row, before, after):
    cols, width = row.shape
    wide = row.astype(f32)
    place = lax.broadcasted_iota(jnp.int32, (cols, width), 0)
    right = jnp.where(place == 0, before, pltpu.roll(wide, 1, 0))
    left = jnp.where(place == cols - 1, after, pltpu.roll(wide, cols - 1, 0))
    return right.astype(bf16), row.astype(bf16), left.astype(bf16)


def fill_row(cat_ref, r, row, before, after):
    cols, width = row.shape
    for b, part in enumerate(moved_rows(row, before, after)):
        cat_ref[r * cols : (r + 1) * cols, b * width : (b + 1) * width] = part


def spread_kernel(own_ref, left_ref, right_ref, cat_ref, row_ref):
    lefts, rights = left_ref[1].astype(f32), right_ref[0].astype(f32)
    for r in range(own_ref.shape[0]):
        fill_row(cat_ref, r, own_ref[r], lefts[r : r + 1], rights[r : r + 1])
    row_ref[...] = cat_ref[0 : row_ref.shape[0], 0 : row_ref.shape[1]]


def gram_tiles(feat, gram_ref, base_ref=None):
    width = feat.shape[1]
    half = width // 2
    product = functools.partial(
        lax.dot_general,
        dimension_numbers=(((0,), (0,)), ((), ())),
        preferred_element_type=f32,
    )
    upper = product(feat[:, :half], feat)
    lower = product(feat[:, half:], feat[:, half:])
    for n, (i, j) in enumerate(tile_pairs(width)):
        at = slice(n * tile, (n + 1) * tile)
        if i * tile < half:
            part = upper[i * tile : (i + 1) * tile, j * tile : (j + 1) * tile]
        else:
            k, m = i * tile - half, j * tile - half
            part = lower[k : k + tile, m : m + tile]
        gram_ref[at, :] = part if base_ref is None else part + base_ref[at, :]


def inner_kernel(
    shape, cat_ref, kernel_ref, bias_ref, feat_ref, slope_ref, gram_ref, row_ref,
):
    row_ref[...] = bias_ref[...].astype(f32).reshape(row_ref.shape)
    tile_rows, tile_cols, in_width, out_width, step = shape
    bias = row_ref[...]
    root = 1.0 / math.sqrt(out_width)
    span = 3 * in_width
    for h in range(0, tile_rows - 2, step):
        total = bias
        for a in range(3):
            total = total + jnp.dot(
                cat_ref[(h + a) * tile_cols : (h + a + step) * tile_cols, :],
                kernel_ref[a * span : (a + 1) * span, :],
                preferred_element_type=f32,
            )
        features, slope = gelu_pair(total)
        at = slice(h * tile_cols, (h + step) * tile_cols)
        feat_ref[at, :] = features.astype(bf16)
        slope_ref[at, :] = (slope * root).astype(bf16)
    gram_tiles(feat_ref[...], gram_ref)


def outer_kernel(
    shape, own_ref, spread_ref, odd_ref, even_ref, left_ref, right_ref, kernel_ref, bias_ref, base_ref,
    feat_ref, slope_ref, send_ref, keep_ref, cat_ref, low_ref, high_ref, gram_ref,
):
    tile_rows, tile_cols, in_width, out_width, step = shape
    odd = lax.rem(lax.axis_index("rows"), 2)
    row = lax.axis_index("rows")
    low_ref[...] = jnp.where(odd == 0, odd_ref[...], even_ref[...])
    high_ref[...] = jnp.where(odd == 0, even_ref[...], odd_ref[...])

    @pl.when(row == 0)
    def _():
        low_ref[...] = jnp.zeros_like(low_ref)

    @pl.when(row == lax.axis_size("rows") - 1)
    def _():
        high_ref[...] = jnp.zeros_like(high_ref)

    first = (lax.axis_index("rows") > 0).astype(f32)
    last = (lax.axis_index("rows") < lax.axis_size("rows") - 1).astype(f32)
    left = (lax.axis_index("cols") > 0).astype(f32)
    right = (lax.axis_index("cols") < lax.axis_size("cols") - 1).astype(f32)
    main = 2 * tile_cols
    low_rim, high_rim = low_ref[main:, :].astype(f32), high_ref[main:, :].astype(f32)
    own_begin = column(own_ref[:, 0:16, :].astype(f32), 0)
    own_end = column(own_ref[:, tile_cols - 16 :, :].astype(f32), 15)

    def sides(c, own):
        return jnp.concatenate(
            [low_rim[c : c + 1], low_rim[4 + c : 5 + c], own, high_rim[c : c + 1], high_rim[4 + c : 5 + c]],
            axis=0,
        )

    def ends(c, own):
        c16 = c // 16 * 16
        piece = lambda ref, k: ref[k + c16 : k + c16 + 16, :].astype(f32)[c - c16 : c - c16 + 1]
        rows = [piece(low_ref, 0), piece(low_ref, tile_cols), own]
        return jnp.concatenate([*rows, piece(high_ref, 0), piece(high_ref, tile_cols)], axis=0)

    lefts = [
        sides(0, left_ref[0].astype(f32)), sides(1, left_ref[1].astype(f32)), ends(0, own_begin)
    ]
    rights = [
        ends(tile_cols - 1, own_end), sides(2, right_ref[0].astype(f32)), sides(3, right_ref[1].astype(f32))
    ]
    span = 3 * in_width
    for r, line in enumerate([0, 1, 2, 3, tile_rows, tile_rows + 1, tile_rows + 2, tile_rows + 3]):
        if line < 2:
            row = low_ref[line * tile_cols : (line + 1) * tile_cols, :]
        elif line < tile_rows + 2:
            row = None
        else:
            k = line - tile_rows - 2
            row = high_ref[k * tile_cols : (k + 1) * tile_cols, :]
        if row is None:
            parts = spread_ref[(line - 2) * tile_cols : (line - 1) * tile_cols, :]
        else:
            parts = jnp.concatenate(
                moved_rows(row, lefts[1][line : line + 1], rights[1][line : line + 1]), axis=1
            )
        for a in range(3):
            if 0 <= r % 4 - a < 2:
                to = 2 * (r // 4) + r % 4 - a
                cat_ref[to * tile_cols : (to + 1) * tile_cols, a * span : (a + 1) * span] = parts
    blank = jnp.zeros((edge - tile_rows - 2, in_width), f32)
    for a in range(3):
        for b in range(3):
            piece = jnp.concatenate(
                [lefts[b][a : a + tile_rows + 2], blank, rights[b][a : a + tile_rows + 2], blank],
                axis=0,
            )
            at = (3 * a + b) * in_width
            cat_ref[2 * main :, at : at + in_width] = piece.astype(bf16)
    root = 1.0 / math.sqrt(out_width)
    line = lax.broadcasted_iota(jnp.int32, (2 * edge, out_width // 2), 0)
    weight = jnp.where(line < edge, left, right)
    weight = jnp.where(line % edge == 0, weight * first, weight)
    weight = jnp.where(line % edge == tile_rows + 1, weight * last, weight)
    for at in (slice(0, out_width // 2), slice(out_width // 2, out_width)):
        total = bias_ref[:, at] + jnp.dot(
            cat_ref[...], kernel_ref[:, at], preferred_element_type=f32
        )
        features, slope = gelu_pair(total)
        slope = slope * root
        feat_ref[:, at] = features.astype(bf16)
        slope_ref[0:tile_cols, at] = (slope[:tile_cols] * first).astype(bf16)
        slope_ref[tile_cols : 3 * tile_cols, at] = slope[tile_cols : 3 * tile_cols].astype(bf16)
        slope_ref[3 * tile_cols : 2 * main, at] = (slope[3 * tile_cols : 2 * main] * last).astype(bf16)
        slope_ref[2 * main :, at] = (slope[2 * main :] * weight).astype(bf16)
    gram_tiles(feat_ref[tile_cols : 3 * tile_cols, :], gram_ref, base_ref)
    half = send_ref.shape[0]
    side = side_of(0)
    send_ref[...] = gram_ref[rows_at(1 - side, half), :].astype(bf16)
    keep_ref[...] = gram_ref[rows_at(side, half), :]


def prepare_kernel(kernel_ref, target_ref, turned_ref, both_ref):
    taps, in_width, out_width = 9, kernel_ref.shape[0] // 9, kernel_ref.shape[1]
    for n in range(taps):
        to = (n // 3 * 3 + 2 - n % 3) * out_width
        turned_ref[to : to + out_width, :] = kernel_ref[n * in_width : (n + 1) * in_width, :].T
    for i, j in tile_pairs(out_width):
        at_i, at_j = slice(i * tile, (i + 1) * tile), slice(j * tile, (j + 1) * tile)
        both = target_ref[at_i, at_j].astype(f32) + target_ref[at_j, at_i].astype(f32).T
        both_ref[at_i, at_j] = both
        if i != j:
            both_ref[at_j, at_i] = both.T


def backward_kernel(
    shape, pixel_total, mine_ref, other_ref, both_ref, in_feat_ref, in_slope_ref, out_feat_ref, out_slope_ref,
    turned_ref, own_gram_ref, out_ref, gram_ref, full_ref, sym_ref, cat_ref,
):
    tile_rows, tile_cols, in_width, out_width, step = shape
    half = mine_ref.shape[0]
    side = side_of(0)
    gram_ref[rows_at(side, half), :] = mine_ref[...].astype(f32)
    gram_ref[rows_at(1 - side, half), :] = other_ref[...].astype(f32)
    for n, (i, j) in enumerate(tile_pairs(out_width)):
        at_i, at_j = slice(i * tile, (i + 1) * tile), slice(j * tile, (j + 1) * tile)
        gram = gram_ref[n * tile : (n + 1) * tile, :] * (1.0 / pixel_total)
        full_ref[at_i, at_j] = gram
        sym_ref[at_i, at_j] = (2.0 * gram - both_ref[at_i, at_j]).astype(bf16)
        if i != j:
            gram = gram.T
            full_ref[at_j, at_i] = gram
            sym_ref[at_j, at_i] = (2.0 * gram - both_ref[at_j, at_i]).astype(bf16)
    share = own_gram_ref.shape[0]
    start = device_index() * share
    if share % 8 == 0:
        own_gram_ref[...] = full_ref[pl.ds(pl.multiple_of(start, 8), share), :]
    else:
        group = full_ref[pl.ds(pl.multiple_of(start // 8 * 8, 8), 8), :]
        picked = group[0:share]
        for k in range(share, 8, share):
            picked = jnp.where(start % 8 == k, group[k : k + share], picked)
        own_gram_ref[...] = picked

    def grad_of(feat_ref, slope_ref, at):
        product = jnp.dot(feat_ref[at, :], sym_ref[...], preferred_element_type=f32)
        return product * slope_ref[at, :].astype(f32)

    main = 2 * tile_cols
    edges = grad_of(out_feat_ref, out_slope_ref, slice(2 * main, None))
    lines = [(out_feat_ref, out_slope_ref, 0)]
    lines += [(in_feat_ref, in_slope_ref, h * tile_cols) for h in range(0, tile_rows - 2, step)]
    lines += [(out_feat_ref, out_slope_ref, main)]
    grads = {}

    def upstream(c):
        feat_ref, slope_ref, begin = lines[c]
        grads[c] = grad_of(feat_ref, slope_ref, slice(begin, begin + step * tile_cols))

    def fill(c):
        for k in range(step):
            r = c * step + k
            fill_row(
                cat_ref, r, grads[c][k * tile_cols : (k + 1) * tile_cols],
                edges[r : r + 1], edges[edge + r : edge + r + 1],
            )

    span = 3 * out_width

    def convolve(begin, count):
        total = 0.0
        for a in range(3):
            total = total + jnp.dot(
                cat_ref[(begin + 2 - a) * tile_cols : (begin + 2 - a + count) * tile_cols, :],
                turned_ref[a * span : (a + 1) * span, :],
                preferred_element_type=f32,
            )
        out_ref[begin * tile_cols : (begin + count) * tile_cols, :] = total.astype(bf16)

    last = len(lines) - 1
    middle = last // 2
    half_rows = middle * step
    upstream(0)
    for c in range(last):
        upstream(c + 1)
        fill(c)
        if c == middle:
            convolve(0, half_rows)
    fill(last)
    convolve(half_rows, tile_rows - half_rows)


def on_device(canvas, conv_weight, conv_bias, target_gram):
    tile_rows, tile_cols, in_width = canvas.shape
    out_width = conv_weight.shape[3]
    pixel_total = tile_rows * tile_cols * lax.axis_size("rows") * lax.axis_size("cols")
    shape = (tile_rows, tile_cols, in_width, out_width, 2)
    kernel = conv_weight.reshape(9 * in_width, out_width)
    params = pltpu.CompilerParams(vmem_limit_bytes=24 * 1024 * 1024)
    vmem = pl.BlockSpec(memory_space=pltpu.VMEM)
    packed_shape = jax.ShapeDtypeStruct((len(tile_pairs(out_width)) * tile, tile), f32)

    rim_shape = jax.ShapeDtypeStruct((2, tile_rows, in_width), bf16)
    two = lax.axis_size("cols") == 2
    rims = local(
        rim_kernel,
        (rim_shape,) * (1 if two else 2),
        "column_rims",
        canvas,
        cost_estimate=pl.CostEstimate(flops=4_000_000_000, bytes_accessed=600_000, transcendentals=0),
    )
    if two:
        beyond = [lax.ppermute(rims[0], "cols", [(0, 1), (1, 0)])]
    else:
        beyond = shift_cols(rims[1], rims[0])
    payload_shape = jax.ShapeDtypeStruct((2 * tile_cols + edge, in_width), bf16)
    half_shape = jax.ShapeDtypeStruct((1, *target_gram.shape), bf16)
    odd, left, right, rows = local(
        odd_payload_kernel,
        (payload_shape, rim_shape, rim_shape, half_shape),
        "odd_payload",
        canvas,
        target_gram,
        *beyond,
    )
    count = lax.axis_size("rows")
    odd = swap_rows(range(1, count - 1, 2), odd)
    spread, row = local(
        spread_kernel,
        (
            jax.ShapeDtypeStruct((tile_rows * tile_cols, 3 * in_width), bf16),
            jax.ShapeDtypeStruct((16, 128), bf16),
        ),
        "spread",
        canvas,
        left,
        right,
        cost_estimate=chained,
    )
    even = local(even_payload_kernel, payload_shape, "even_payload", canvas, left, right, row)
    even = swap_rows(range(0, count - 1, 2), even)
    bits = (lax.axis_size("rows") * lax.axis_size("cols")).bit_length() - 1
    gather = Gather(rows)
    far = list(reversed(range(3, bits)))
    inner = (tile_rows - 2) * tile_cols
    in_feat, in_slope, in_gram, bias = pl.pallas_call(
        functools.partial(inner_kernel, shape),
        out_shape=(
            jax.ShapeDtypeStruct((inner, out_width), bf16),
            jax.ShapeDtypeStruct((inner, out_width), bf16),
            packed_shape,
            jax.ShapeDtypeStruct((1, out_width), f32),
        ),
        in_specs=[vmem] * 3,
        compiler_params=params,
        name="inner_rows",
        cost_estimate=pl.CostEstimate(
            flops=2 * inner * (9 * in_width + out_width) * out_width,
            bytes_accessed=6_000_000,
            transcendentals=inner * out_width,
        ),
    )(spread, kernel, conv_bias)

    outer = 4 * tile_cols + 2 * edge
    half_gram = (packed_shape.shape[0] // 2, tile)
    out_feat, out_slope, send, keep = pl.pallas_call(
        functools.partial(outer_kernel, shape),
        out_shape=(
            jax.ShapeDtypeStruct((outer, out_width), bf16),
            jax.ShapeDtypeStruct((outer, out_width), bf16),
            jax.ShapeDtypeStruct(half_gram, bf16),
            jax.ShapeDtypeStruct(half_gram, f32),
        ),
        in_specs=[vmem] * 9,
        scratch_shapes=[
            pltpu.VMEM((outer, 9 * in_width), bf16),
            pltpu.VMEM(payload_shape.shape, bf16),
            pltpu.VMEM(payload_shape.shape, bf16),
            pltpu.VMEM(packed_shape.shape, f32),
        ],
        compiler_params=params,
        name="outer_rows",
    )(canvas, spread, odd, even, left, right, kernel, bias, in_gram)

    exchanges = {"halve 1": far[:1], "halve 2": far[1:], "add 3": [2], "join 2": [1], "join 1": [0]}
    prepared = []

    def beside(name, sent, got):
        for bit in exchanges.get(name, []):
            gather.step(bit, sent)
        if name != "halves":
            return got
        gather.settle(sent)
        prepared.extend(
            pl.pallas_call(
                prepare_kernel,
                out_shape=(
                    jax.ShapeDtypeStruct((9 * out_width, in_width), bf16),
                    jax.ShapeDtypeStruct((out_width, out_width), f32),
                ),
                in_specs=[vmem] * 2,
                compiler_params=params,
                name="prepare",
                cost_estimate=pl.CostEstimate(
                    flops=2_000_000_000, bytes_accessed=6_000_000, transcendentals=0
                ),
            )(kernel, gather.rows.reshape(out_width, out_width))
        )
        return lax.optimization_barrier((got, *prepared))[0]

    mine, other = sum_all(send, keep, beside)
    turned, both = prepared
    own_gram, grad = pl.pallas_call(
        functools.partial(backward_kernel, shape, pixel_total),
        out_shape=(
            jax.ShapeDtypeStruct(target_gram.shape, f32),
            jax.ShapeDtypeStruct((tile_rows * tile_cols, in_width), bf16),
        ),
        in_specs=[vmem] * 8,
        scratch_shapes=[
            pltpu.VMEM(packed_shape.shape, f32),
            pltpu.VMEM((out_width, out_width), f32),
            pltpu.VMEM((out_width, out_width), bf16),
            pltpu.VMEM(((tile_rows + 2) * tile_cols, 3 * out_width), bf16),
        ],
        compiler_params=params,
        name="grad_conv",
    )(mine, other, both, in_feat, in_slope, out_feat, out_slope, turned)
    return own_gram, grad.reshape(tile_rows, tile_cols, in_width)


def solution(mesh):
    return jax.shard_map(
        on_device,
        mesh=mesh,
        in_specs=(P("rows", "cols", None), P(), P(), P(("rows", "cols"), None)),
        out_specs=(P(("rows", "cols"), None), P("rows", "cols", None)),
        check_vma=False,
    )
```

```python
import functools
import math

import jax
import jax.numpy as jnp
from jax import lax
from jax.experimental import pallas as pl
from jax.experimental.pallas import tpu as pltpu
from jax.sharding import PartitionSpec as P

gelu_scale = math.sqrt(2.0 / math.pi)
tile = 128
edge = 16
f32, bf16 = jnp.float32, jnp.bfloat16


def tile_pairs(width):
    count = width // tile
    return [(i, j) for i in range(count) for j in range(i, count)]


def swap_rows(pairs, values):
    count = lax.axis_size("rows")

    def perm(low):
        partner = {i: i for i in range(count)}
        partner.update({i: i + 1 for i in low})
        partner.update({i + 1: i for i in low})
        return list(partner.items())

    return [lax.ppermute(value, "rows", perm(low)) for low, value in zip(pairs, values)]


def shift_cols(last, first):
    count = lax.axis_size("cols")
    forward = [(i, i + 1) for i in range(count - 1)]
    backward = [(target, source) for source, target in forward]
    return lax.ppermute(last, "cols", forward), lax.ppermute(first, "cols", backward)


def device_index():
    return lax.axis_index("rows") * lax.axis_size("cols") + lax.axis_index("cols")


def swap(value, bit):
    total = lax.axis_size("rows") * lax.axis_size("cols")
    return lax.ppermute(value, ("rows", "cols"), [(i, i ^ (1 << bit | 1)) for i in range(total)])


def local(body, out_shape, name, *operands, **kwargs):
    return pl.pallas_call(
        body,
        out_shape=out_shape,
        in_specs=[pl.BlockSpec(memory_space=pltpu.VMEM)] * len(operands),
        compiler_params=pltpu.CompilerParams(vmem_limit_bytes=8 * 1024 * 1024),
        name=name,
        **kwargs,
    )(*operands)


def side_of(bit):
    index = device_index()
    if bit > 0:
        return lax.rem(index // (1 << bit), 2)
    bits = (lax.axis_size("rows") * lax.axis_size("cols")).bit_length() - 1
    return lax.rem(sum(lax.rem(index // (1 << k), 2) for k in range(bits)), 2)


def rows_at(index, count):
    return pl.ds(pl.multiple_of(index * count, count), count)


waiting = pl.CostEstimate(flops=1_500_000_000, bytes_accessed=100_000, transcendentals=0)
chained = pl.CostEstimate(flops=8_000_000_000, bytes_accessed=100_000, transcendentals=0)


def halve(keep, got, bit):
    half = keep.shape[0] // 2

    def body(keep_ref, got_ref, send_ref, stay_ref):
        side = side_of(bit)
        away, here = rows_at(1 - side, half), rows_at(side, half)
        send_ref[...] = (keep_ref[away, :] + got_ref[away, :].astype(f32)).astype(bf16)
        stay_ref[...] = keep_ref[here, :] + got_ref[here, :].astype(f32)

    shape = (half, keep.shape[1])
    return local(
        body,
        (jax.ShapeDtypeStruct(shape, bf16), jax.ShapeDtypeStruct(shape, f32)),
        "halve",
        keep,
        got,
        cost_estimate=chained,
    )


def add(keep, got):
    def body(keep_ref, got_ref, sum_ref):
        sum_ref[...] = (keep_ref[...].astype(f32) + got_ref[...].astype(f32)).astype(bf16)

    return local(body, jax.ShapeDtypeStruct(got.shape, bf16), "add", keep, got, cost_estimate=chained)


def join(mine, other, bit, **kwargs):
    def body(mine_ref, other_ref, both_ref):
        side = side_of(bit)
        both_ref[:, pl.ds(side, 1)] = mine_ref[...][:, None]
        both_ref[:, pl.ds(1 - side, 1)] = other_ref[...][:, None]

    shape = (mine.shape[0], 2, *mine.shape[1:])
    return local(body, jax.ShapeDtypeStruct(shape, mine.dtype), "join", mine, other, **kwargs)


def join_cores(mine, other, **kwargs):
    def body(mine_ref, other_ref, both_ref):
        side = side_of(0)
        for chip in range(mine.shape[0]):
            core = lax.rem(side + chip.bit_count(), 2)
            both_ref[chip, pl.ds(core, 1)] = mine_ref[chip][None]
            both_ref[chip, pl.ds(1 - core, 1)] = other_ref[chip][None]

    shape = (mine.shape[0], 2, *mine.shape[1:])
    return local(body, jax.ShapeDtypeStruct(shape, mine.dtype), "join_cores", mine, other, **kwargs)


class Gather:
    def __init__(self, rows):
        self.rows, self.got, self.done = rows, None, []

    def settle(self, after):
        if self.got is None:
            self.rows, _ = lax.optimization_barrier((self.rows, after))
            return
        share = self.rows.shape[-2:]
        got, _ = lax.optimization_barrier((self.got, after))
        bit = self.done[-1]
        if bit > 0:
            lead = 1 << sum(other > bit for other in self.done)
            mine, got = (part.reshape(lead, -1, *share) for part in (self.rows, got))
            both = join(mine, got, bit, cost_estimate=waiting)
        else:
            both = join_cores(self.rows, got, cost_estimate=waiting)
        self.rows, self.got = both.reshape(-1, *share), None

    def step(self, bit, after):
        self.settle(after)
        self.got = swap(self.rows, bit)
        self.done.append(bit)


def sum_all(send, keep, beside):
    bits = (lax.axis_size("rows") * lax.axis_size("cols")).bit_length() - 1
    halving = list(range(1, min(3, bits)))

    def step(value, bit, name):
        got = swap(value, bit)
        return beside(name, value, got)

    got = step(send, 0, "cores")
    for bit in halving:
        send, keep = halve(keep, got, bit)
        got = step(send, bit, f"halve {bit}")
    mine = add(keep, got)
    for bit in range(len(halving) + 1, bits):
        mine = add(mine, step(mine, bit, f"add {bit}"))
    for bit in reversed(halving):
        got = step(mine, bit, f"join {bit}")
        mine = join(mine[None], got[None], bit, cost_estimate=chained).reshape(-1, mine.shape[1])
    return mine, step(mine, 0, "halves")


def gelu_pair(value):
    square = value * value
    tangent = jnp.tanh(value * (gelu_scale + gelu_scale * 0.044715 * square))
    half = 0.5 * value
    plus = 0.5 + 0.5 * tangent
    grad = plus + half * (1.0 - tangent * tangent) * (
        gelu_scale + gelu_scale * 3.0 * 0.044715 * square
    )
    return value * plus, grad


def column(value, c):
    return jnp.concatenate([value[r, c : c + 1] for r in range(value.shape[0])], axis=0)


def rim_kernel(canvas_ref, *out_refs):
    cols = canvas_ref.shape[1]
    begin = canvas_ref[:, 0:16, :].astype(f32)
    end = canvas_ref[:, cols - 16 :, :].astype(f32)
    for c in range(2):
        pair = column(begin, c), column(end, 14 + c)
        if len(out_refs) == 1:
            out_refs[0][c] = jnp.where(lax.axis_index("cols") == 0, pair[1], pair[0]).astype(bf16)
        else:
            out_refs[0][c], out_refs[1][c] = pair[0].astype(bf16), pair[1].astype(bf16)


def payload_kernel(canvas_ref, target_ref, *refs):
    even_ref, odd_ref, left_ref, right_ref, half_ref = refs[-5:]
    rows, cols, width = canvas_ref.shape
    half_ref[0] = target_ref[...].astype(bf16)
    if len(refs) == 6:
        here = lax.axis_index("cols")
        other = refs[0][...].astype(f32)
        left_ref[...] = jnp.where(here == 0, 0.0, other).astype(bf16)
        right_ref[...] = jnp.where(here == 0, other, 0.0).astype(bf16)
    else:
        left_ref[...], right_ref[...] = refs[0][...], refs[1][...]
    beyond = [ref[c].astype(f32) for ref in (left_ref, right_ref) for c in range(2)]

    def fill(ref, r):
        for k in range(2):
            ref[k * cols : (k + 1) * cols, :] = canvas_ref[r + k]
        rim = [part[r + k : r + k + 1] for k in range(2) for part in beyond]
        rim = jnp.concatenate([*rim, jnp.zeros((8, width), f32)], axis=0)
        ref[2 * cols :, :] = rim.astype(bf16)

    odd = lax.rem(lax.axis_index("rows"), 2)

    @pl.when(odd == 0)
    def _():
        fill(even_ref, rows - 2)
        fill(odd_ref, 0)

    @pl.when(odd == 1)
    def _():
        fill(even_ref, 0)
        fill(odd_ref, rows - 2)


def moved_rows(row, before, after):
    cols = row.shape[0]
    wide = row.astype(f32)
    place = lax.broadcasted_iota(jnp.int32, (8, row.shape[1]), 0)
    right, left = pltpu.roll(wide, 1, 0), pltpu.roll(wide, cols - 1, 0)
    right = jnp.concatenate([jnp.where(place == 0, before, right[:8]), right[8:]], axis=0)
    left = jnp.concatenate([left[:-8], jnp.where(place == 7, after, left[-8:])], axis=0)
    return right.astype(bf16), row.astype(bf16), left.astype(bf16)


def fill_row(cat_ref, r, row, before, after):
    cols, width = row.shape
    for b, part in enumerate(moved_rows(row, before, after)):
        cat_ref[r * cols : (r + 1) * cols, b * width : (b + 1) * width] = part


def gram_tiles(feat, gram_ref, base_ref=None):
    width = feat.shape[1]
    half = width // 2
    product = functools.partial(
        lax.dot_general,
        dimension_numbers=(((0,), (0,)), ((), ())),
        preferred_element_type=f32,
    )
    upper = product(feat[:, :half], feat)
    lower = product(feat[:, half:], feat[:, half:])
    for n, (i, j) in enumerate(tile_pairs(width)):
        at = slice(n * tile, (n + 1) * tile)
        if i * tile < half:
            part = upper[i * tile : (i + 1) * tile, j * tile : (j + 1) * tile]
        else:
            k, m = i * tile - half, j * tile - half
            part = lower[k : k + tile, m : m + tile]
        gram_ref[at, :] = part if base_ref is None else part + base_ref[at, :]


def inner_kernel(
    shape, own_ref, left_ref, right_ref, kernel_ref, bias_ref,
    feat_ref, slope_ref, gram_ref, row_ref, part_ref, cat_ref,
):
    row_ref[...] = bias_ref[...].astype(f32).reshape(row_ref.shape)
    tile_rows, tile_cols, in_width, out_width, step = shape
    lefts, rights = left_ref[1].astype(f32), right_ref[0].astype(f32)
    for r in range(tile_rows):
        fill_row(cat_ref, r, own_ref[r], lefts[r : r + 1], rights[r : r + 1])
    bias = row_ref[...]
    root = 1.0 / math.sqrt(out_width)
    span = 3 * in_width

    def product(begin, count, a):
        return jnp.dot(
            cat_ref[begin * tile_cols : (begin + count) * tile_cols, :],
            kernel_ref[a * span : (a + 1) * span, :],
            preferred_element_type=f32,
        )

    for h in range(0, tile_rows - 2, step):
        total = bias
        for a in range(3):
            total = total + product(h + a, step, a)
        features, slope = gelu_pair(total)
        at = slice(h * tile_cols, (h + step) * tile_cols)
        feat_ref[at, :] = features.astype(bf16)
        slope_ref[at, :] = (slope * root).astype(bf16)
    low, high = product(0, 2, 2), product(tile_rows - 2, 2, 0)
    ends = product(0, 1, 1), product(tile_rows - 1, 1, 1)
    part_ref[0:tile_cols, :] = low[:tile_cols] + bias
    part_ref[tile_cols : 2 * tile_cols, :] = low[tile_cols:] + ends[0] + bias
    part_ref[2 * tile_cols : 3 * tile_cols, :] = high[:tile_cols] + ends[1] + bias
    part_ref[3 * tile_cols :, :] = high[tile_cols:] + bias
    gram_tiles(feat_ref[...], gram_ref)


def outer_kernel(
    shape, own_ref, even_ref, odd_ref, left_ref, right_ref, kernel_ref, bias_ref, base_ref, part_ref,
    feat_ref, slope_ref, send_ref, keep_ref, cat_ref, edge_ref, low_ref, high_ref, gram_ref,
):
    tile_rows, tile_cols, in_width, out_width, step = shape
    odd = lax.rem(lax.axis_index("rows"), 2)
    row = lax.axis_index("rows")
    low_ref[...] = jnp.where(odd == 0, odd_ref[...], even_ref[...])
    high_ref[...] = jnp.where(odd == 0, even_ref[...], odd_ref[...])

    @pl.when(row == 0)
    def _():
        low_ref[...] = jnp.zeros_like(low_ref)

    @pl.when(row == lax.axis_size("rows") - 1)
    def _():
        high_ref[...] = jnp.zeros_like(high_ref)

    first = (lax.axis_index("rows") > 0).astype(f32)
    last = (lax.axis_index("rows") < lax.axis_size("rows") - 1).astype(f32)
    left = (lax.axis_index("cols") > 0).astype(f32)
    right = (lax.axis_index("cols") < lax.axis_size("cols") - 1).astype(f32)
    main = 2 * tile_cols
    low_rim, high_rim = low_ref[main:, :].astype(f32), high_ref[main:, :].astype(f32)
    own_begin = column(own_ref[:, 0:16, :].astype(f32), 0)
    own_end = column(own_ref[:, tile_cols - 16 :, :].astype(f32), 15)

    def sides(c, own):
        return jnp.concatenate(
            [low_rim[c : c + 1], low_rim[4 + c : 5 + c], own, high_rim[c : c + 1], high_rim[4 + c : 5 + c]],
            axis=0,
        )

    def ends(c, own):
        c16 = c // 16 * 16
        piece = lambda ref, k: ref[k + c16 : k + c16 + 16, :].astype(f32)[c - c16 : c - c16 + 1]
        rows = [piece(low_ref, 0), piece(low_ref, tile_cols), own]
        return jnp.concatenate([*rows, piece(high_ref, 0), piece(high_ref, tile_cols)], axis=0)

    lefts = [
        sides(0, left_ref[0].astype(f32)), sides(1, left_ref[1].astype(f32)), ends(0, own_begin)
    ]
    rights = [
        ends(tile_cols - 1, own_end), sides(2, right_ref[0].astype(f32)), sides(3, right_ref[1].astype(f32))
    ]
    span = 3 * in_width
    for r, line in enumerate([0, 1, tile_rows + 2, tile_rows + 3]):
        source = low_ref if r < 2 else high_ref
        row = source[r % 2 * tile_cols : (r % 2 + 1) * tile_cols, :]
        fill_row(cat_ref, r, row, lefts[1][line : line + 1], rights[1][line : line + 1])
    blank = jnp.zeros((edge - tile_rows - 2, in_width), f32)
    for a in range(3):
        for b in range(3):
            piece = jnp.concatenate(
                [lefts[b][a : a + tile_rows + 2], blank, rights[b][a : a + tile_rows + 2], blank],
                axis=0,
            )
            at = (3 * a + b) * in_width
            edge_ref[:, at : at + in_width] = piece.astype(bf16)
    root = 1.0 / math.sqrt(out_width)
    line = lax.broadcasted_iota(jnp.int32, (2 * edge, out_width // 2), 0)
    weight = jnp.where(line < edge, left, right)
    weight = jnp.where(line % edge == 0, weight * first, weight)
    weight = jnp.where(line % edge == tile_rows + 1, weight * last, weight)
    for at in (slice(0, out_width // 2), slice(out_width // 2, out_width)):
        taps = [
            jnp.dot(
                cat_ref[a * tile_cols : (a + 2) * tile_cols, :],
                kernel_ref[a * span : (a + 1) * span, at],
                preferred_element_type=f32,
            )
            for a in range(3)
        ]
        totals = [
            part_ref[0:tile_cols, at] + taps[0][:tile_cols] + taps[1][:tile_cols],
            part_ref[tile_cols : 2 * tile_cols, at] + taps[0][tile_cols:],
            part_ref[2 * tile_cols : 3 * tile_cols, at] + taps[2][:tile_cols],
            part_ref[3 * tile_cols :, at] + taps[1][tile_cols:] + taps[2][tile_cols:],
            bias_ref[:, at]
            + jnp.dot(edge_ref[...], kernel_ref[:, at], preferred_element_type=f32),
        ]
        scales = [first * root, root, root, last * root, weight * root]
        for n, (total, scale) in enumerate(zip(totals, scales)):
            features, slope = gelu_pair(total)
            rows = slice(n * tile_cols, n * tile_cols + total.shape[0])
            feat_ref[rows, at] = features.astype(bf16)
            slope_ref[rows, at] = (slope * scale).astype(bf16)
    gram_tiles(feat_ref[tile_cols : 3 * tile_cols, :], gram_ref, base_ref)
    half = send_ref.shape[0]
    side = side_of(0)
    send_ref[...] = gram_ref[rows_at(1 - side, half), :].astype(bf16)
    keep_ref[...] = gram_ref[rows_at(side, half), :]


def prepare_kernel(kernel_ref, target_ref, turned_ref, both_ref):
    taps, in_width, out_width = 9, kernel_ref.shape[0] // 9, kernel_ref.shape[1]
    for n in range(taps):
        to = (n // 3 * 3 + 2 - n % 3) * out_width
        turned_ref[to : to + out_width, :] = kernel_ref[n * in_width : (n + 1) * in_width, :].T
    for i, j in tile_pairs(out_width):
        at_i, at_j = slice(i * tile, (i + 1) * tile), slice(j * tile, (j + 1) * tile)
        both = target_ref[at_i, at_j].astype(f32) + target_ref[at_j, at_i].astype(f32).T
        both_ref[at_i, at_j] = both
        if i != j:
            both_ref[at_j, at_i] = both.T


def backward_kernel(
    shape, pixel_total, mine_ref, other_ref, both_ref, in_feat_ref, in_slope_ref, out_feat_ref, out_slope_ref,
    turned_ref, own_gram_ref, out_ref, gram_ref, full_ref, sym_ref, cat_ref,
):
    tile_rows, tile_cols, in_width, out_width, step = shape
    half = mine_ref.shape[0]
    side = side_of(0)
    gram_ref[rows_at(side, half), :] = mine_ref[...].astype(f32)
    gram_ref[rows_at(1 - side, half), :] = other_ref[...].astype(f32)
    for n, (i, j) in enumerate(tile_pairs(out_width)):
        at_i, at_j = slice(i * tile, (i + 1) * tile), slice(j * tile, (j + 1) * tile)
        gram = gram_ref[n * tile : (n + 1) * tile, :] * (1.0 / pixel_total)
        full_ref[at_i, at_j] = gram
        sym_ref[at_i, at_j] = (2.0 * gram - both_ref[at_i, at_j]).astype(bf16)
        if i != j:
            gram = gram.T
            full_ref[at_j, at_i] = gram
            sym_ref[at_j, at_i] = (2.0 * gram - both_ref[at_j, at_i]).astype(bf16)
    share = own_gram_ref.shape[0]
    start = device_index() * share
    if share % 8 == 0:
        own_gram_ref[...] = full_ref[pl.ds(pl.multiple_of(start, 8), share), :]
    else:
        group = full_ref[pl.ds(pl.multiple_of(start // 8 * 8, 8), 8), :]
        picked = group[0:share]
        for k in range(share, 8, share):
            picked = jnp.where(start % 8 == k, group[k : k + share], picked)
        own_gram_ref[...] = picked

    def grad_of(feat_ref, slope_ref, at):
        product = jnp.dot(feat_ref[at, :], sym_ref[...], preferred_element_type=f32)
        return product * slope_ref[at, :].astype(f32)

    main = 2 * tile_cols
    edges = grad_of(out_feat_ref, out_slope_ref, slice(2 * main, None))
    lines = [(out_feat_ref, out_slope_ref, 0)]
    lines += [(in_feat_ref, in_slope_ref, h * tile_cols) for h in range(0, tile_rows - 2, step)]
    lines += [(out_feat_ref, out_slope_ref, main)]
    grads = {}

    def upstream(c):
        feat_ref, slope_ref, begin = lines[c]
        grads[c] = grad_of(feat_ref, slope_ref, slice(begin, begin + step * tile_cols))

    def fill(c):
        for k in range(step):
            r = c * step + k
            fill_row(
                cat_ref, r, grads[c][k * tile_cols : (k + 1) * tile_cols],
                edges[r : r + 1], edges[edge + r : edge + r + 1],
            )

    span = 3 * out_width

    def convolve(begin, count):
        total = 0.0
        for a in range(3):
            total = total + jnp.dot(
                cat_ref[(begin + 2 - a) * tile_cols : (begin + 2 - a + count) * tile_cols, :],
                turned_ref[a * span : (a + 1) * span, :],
                preferred_element_type=f32,
            )
        out_ref[begin * tile_cols : (begin + count) * tile_cols, :] = total.astype(bf16)

    last = len(lines) - 1
    middle = last // 2
    half_rows = middle * step
    upstream(0)
    for c in range(last):
        upstream(c + 1)
        fill(c)
        if c == middle:
            convolve(0, half_rows)
    fill(last)
    convolve(half_rows, tile_rows - half_rows)


def on_device(canvas, conv_weight, conv_bias, target_gram):
    tile_rows, tile_cols, in_width = canvas.shape
    out_width = conv_weight.shape[3]
    pixel_total = tile_rows * tile_cols * lax.axis_size("rows") * lax.axis_size("cols")
    shape = (tile_rows, tile_cols, in_width, out_width, 2)
    kernel = conv_weight.reshape(9 * in_width, out_width)
    params = pltpu.CompilerParams(vmem_limit_bytes=24 * 1024 * 1024)
    vmem = pl.BlockSpec(memory_space=pltpu.VMEM)
    packed_shape = jax.ShapeDtypeStruct((len(tile_pairs(out_width)) * tile, tile), f32)

    rim_shape = jax.ShapeDtypeStruct((2, tile_rows, in_width), bf16)
    two = lax.axis_size("cols") == 2
    rims = local(
        rim_kernel,
        (rim_shape,) * (1 if two else 2),
        "column_rims",
        canvas,
        cost_estimate=pl.CostEstimate(flops=4_000_000_000, bytes_accessed=600_000, transcendentals=0),
    )
    if two:
        beyond = [lax.ppermute(rims[0], "cols", [(0, 1), (1, 0)])]
    else:
        beyond = shift_cols(rims[1], rims[0])
    payload_shape = jax.ShapeDtypeStruct((2 * tile_cols + edge, in_width), bf16)
    half_shape = jax.ShapeDtypeStruct((1, *target_gram.shape), bf16)
    even, odd, left, right, rows = local(
        payload_kernel,
        (payload_shape, payload_shape, rim_shape, rim_shape, half_shape),
        "row_payload",
        canvas,
        target_gram,
        *beyond,
    )
    count = lax.axis_size("rows")
    odd, even = swap_rows([range(1, count - 1, 2), range(0, count - 1, 2)], [odd, even])

    bits = (lax.axis_size("rows") * lax.axis_size("cols")).bit_length() - 1
    gather = Gather(rows)
    far = list(reversed(range(3, bits)))
    inner = (tile_rows - 2) * tile_cols
    in_feat, in_slope, in_gram, bias, part = pl.pallas_call(
        functools.partial(inner_kernel, shape),
        out_shape=(
            jax.ShapeDtypeStruct((inner, out_width), bf16),
            jax.ShapeDtypeStruct((inner, out_width), bf16),
            packed_shape,
            jax.ShapeDtypeStruct((1, out_width), f32),
            jax.ShapeDtypeStruct((4 * tile_cols, out_width), f32),
        ),
        in_specs=[vmem] * 5,
        scratch_shapes=[pltpu.VMEM((tile_rows * tile_cols, 3 * in_width), bf16)],
        compiler_params=params,
        name="inner_rows",
        cost_estimate=pl.CostEstimate(
            flops=2 * inner * (9 * in_width + out_width) * out_width,
            bytes_accessed=6_000_000,
            transcendentals=inner * out_width,
        ),
    )(canvas, left, right, kernel, conv_bias)

    outer = 4 * tile_cols + 2 * edge
    half_gram = (packed_shape.shape[0] // 2, tile)
    out_feat, out_slope, send, keep = pl.pallas_call(
        functools.partial(outer_kernel, shape),
        out_shape=(
            jax.ShapeDtypeStruct((outer, out_width), bf16),
            jax.ShapeDtypeStruct((outer, out_width), bf16),
            jax.ShapeDtypeStruct(half_gram, bf16),
            jax.ShapeDtypeStruct(half_gram, f32),
        ),
        in_specs=[vmem] * 9,
        scratch_shapes=[
            pltpu.VMEM((4 * tile_cols, 3 * in_width), bf16),
            pltpu.VMEM((2 * edge, 9 * in_width), bf16),
            pltpu.VMEM(payload_shape.shape, bf16),
            pltpu.VMEM(payload_shape.shape, bf16),
            pltpu.VMEM(packed_shape.shape, f32),
        ],
        compiler_params=params,
        name="outer_rows",
    )(canvas, even, odd, left, right, kernel, bias, in_gram, part)

    exchanges = {"cores": far[:1], "halve 1": far[1:], "halve 2": [1], "add 3": [2], "add 4": [0]}
    prepared = []

    def beside(name, sent, got):
        for bit in exchanges.get(name, []):
            gather.step(bit, sent)
        if name != "join 2":
            return got
        gather.settle(sent)
        prepared.extend(
            pl.pallas_call(
                prepare_kernel,
                out_shape=(
                    jax.ShapeDtypeStruct((9 * out_width, in_width), bf16),
                    jax.ShapeDtypeStruct((out_width, out_width), f32),
                ),
                in_specs=[vmem] * 2,
                compiler_params=params,
                name="prepare",
                cost_estimate=pl.CostEstimate(
                    flops=2_000_000_000, bytes_accessed=6_000_000, transcendentals=0
                ),
            )(kernel, gather.rows.reshape(out_width, out_width))
        )
        return lax.optimization_barrier((got, *prepared))[0]

    mine, other = sum_all(send, keep, beside)
    turned, both = prepared
    own_gram, grad = pl.pallas_call(
        functools.partial(backward_kernel, shape, pixel_total),
        out_shape=(
            jax.ShapeDtypeStruct(target_gram.shape, f32),
            jax.ShapeDtypeStruct((tile_rows * tile_cols, in_width), bf16),
        ),
        in_specs=[vmem] * 8,
        scratch_shapes=[
            pltpu.VMEM(packed_shape.shape, f32),
            pltpu.VMEM((out_width, out_width), f32),
            pltpu.VMEM((out_width, out_width), bf16),
            pltpu.VMEM(((tile_rows + 2) * tile_cols, 3 * out_width), bf16),
        ],
        compiler_params=params,
        name="grad_conv",
    )(mine, other, both, in_feat, in_slope, out_feat, out_slope, turned)
    return own_gram, grad.reshape(tile_rows, tile_cols, in_width)


def solution(mesh):
    return jax.shard_map(
        on_device,
        mesh=mesh,
        in_specs=(P("rows", "cols", None), P(), P(), P(("rows", "cols"), None)),
        out_specs=(P(("rows", "cols"), None), P("rows", "cols", None)),
        check_vma=False,
    )
```

```python
import functools
import math

import jax
import jax.numpy as jnp
from jax import lax
from jax.experimental import pallas as pl
from jax.experimental.pallas import tpu as pltpu
from jax.sharding import PartitionSpec as P

gelu_scale = math.sqrt(2.0 / math.pi)
tile = 128
edge = 16
f32, bf16 = jnp.float32, jnp.bfloat16


def tile_pairs(width):
    count = width // tile
    return [(i, j) for i in range(count) for j in range(i, count)]


def swap_rows(low, value):
    count = lax.axis_size("rows")
    pairs = [(i, (i + 1) % count) for i in low]
    return lax.ppermute(value, "rows", pairs + [(target, source) for source, target in pairs])


def shift_cols(last, first):
    count = lax.axis_size("cols")
    forward = [(i, i + 1) for i in range(count - 1)]
    backward = [(target, source) for source, target in forward]
    return lax.ppermute(last, "cols", forward), lax.ppermute(first, "cols", backward)


def device_index():
    return lax.axis_index("rows") * lax.axis_size("cols") + lax.axis_index("cols")


def swap(value, bit):
    total = lax.axis_size("rows") * lax.axis_size("cols")
    return lax.ppermute(value, ("rows", "cols"), [(i, i ^ (1 << bit | 1)) for i in range(total)])


def local(body, out_shape, name, *operands, **kwargs):
    return pl.pallas_call(
        body,
        out_shape=out_shape,
        in_specs=[pl.BlockSpec(memory_space=pltpu.VMEM)] * len(operands),
        compiler_params=pltpu.CompilerParams(vmem_limit_bytes=8 * 1024 * 1024),
        name=name,
        **kwargs,
    )(*operands)


def side_of(bit):
    index = device_index()
    if bit > 0:
        return lax.rem(index // (1 << bit), 2)
    bits = (lax.axis_size("rows") * lax.axis_size("cols")).bit_length() - 1
    return lax.rem(sum(lax.rem(index // (1 << k), 2) for k in range(bits)), 2)


def rows_at(index, count):
    return pl.ds(pl.multiple_of(index * count, count), count)


waiting = pl.CostEstimate(flops=1_500_000_000, bytes_accessed=100_000, transcendentals=0)
chained = pl.CostEstimate(flops=8_000_000_000, bytes_accessed=100_000, transcendentals=0)


def halve(keep, got, bit):
    half = keep.shape[0] // 2

    def body(keep_ref, got_ref, send_ref, stay_ref):
        side = side_of(bit)
        away, here = rows_at(1 - side, half), rows_at(side, half)
        send_ref[...] = (keep_ref[away, :] + got_ref[away, :].astype(f32)).astype(bf16)
        stay_ref[...] = keep_ref[here, :] + got_ref[here, :].astype(f32)

    shape = (half, keep.shape[1])
    return local(
        body,
        (jax.ShapeDtypeStruct(shape, bf16), jax.ShapeDtypeStruct(shape, f32)),
        "halve",
        keep,
        got,
        cost_estimate=chained,
    )


def add(keep, got):
    def body(keep_ref, got_ref, sum_ref):
        sum_ref[...] = (keep_ref[...].astype(f32) + got_ref[...].astype(f32)).astype(bf16)

    return local(body, jax.ShapeDtypeStruct(got.shape, bf16), "add", keep, got, cost_estimate=chained)


def join(mine, other, bit, **kwargs):
    def body(mine_ref, other_ref, both_ref):
        side = side_of(bit)
        both_ref[:, pl.ds(side, 1)] = mine_ref[...][:, None]
        both_ref[:, pl.ds(1 - side, 1)] = other_ref[...][:, None]

    shape = (mine.shape[0], 2, *mine.shape[1:])
    return local(body, jax.ShapeDtypeStruct(shape, mine.dtype), "join", mine, other, **kwargs)


def join_cores(mine, other, **kwargs):
    def body(mine_ref, other_ref, both_ref):
        side = side_of(0)
        for chip in range(mine.shape[0]):
            core = lax.rem(side + chip.bit_count(), 2)
            both_ref[chip, pl.ds(core, 1)] = mine_ref[chip][None]
            both_ref[chip, pl.ds(1 - core, 1)] = other_ref[chip][None]

    shape = (mine.shape[0], 2, *mine.shape[1:])
    return local(body, jax.ShapeDtypeStruct(shape, mine.dtype), "join_cores", mine, other, **kwargs)


class Gather:
    def __init__(self, rows):
        self.rows, self.got, self.done = rows, None, []

    def settle(self, after):
        if self.got is None:
            self.rows, _ = lax.optimization_barrier((self.rows, after))
            return
        share = self.rows.shape[-2:]
        got, _ = lax.optimization_barrier((self.got, after))
        bit = self.done[-1]
        if bit > 0:
            lead = 1 << sum(other > bit for other in self.done)
            mine, got = (part.reshape(lead, -1, *share) for part in (self.rows, got))
            both = join(mine, got, bit, cost_estimate=waiting)
        else:
            both = join_cores(self.rows, got, cost_estimate=waiting)
        self.rows, self.got = both.reshape(-1, *share), None

    def step(self, bit, after):
        self.settle(after)
        self.got = swap(self.rows, bit)
        self.done.append(bit)


def sum_all(send, keep, beside):
    bits = (lax.axis_size("rows") * lax.axis_size("cols")).bit_length() - 1
    halving = list(range(1, min(3, bits)))

    def step(value, bit, name):
        got = swap(value, bit)
        return beside(name, value, got)

    got = step(send, 0, "cores")
    for bit in halving:
        send, keep = halve(keep, got, bit)
        got = step(send, bit, f"halve {bit}")
    mine = add(keep, got)
    for bit in range(len(halving) + 1, bits):
        mine = add(mine, step(mine, bit, f"add {bit}"))
    for bit in reversed(halving):
        got = step(mine, bit, f"join {bit}")
        mine = join(mine[None], got[None], bit, cost_estimate=chained).reshape(-1, mine.shape[1])
    return mine, step(mine, 0, "halves")


def gelu_pair(value):
    square = value * value
    tangent = jnp.tanh(value * (gelu_scale + gelu_scale * 0.044715 * square))
    half = 0.5 * value
    plus = 0.5 + 0.5 * tangent
    grad = plus + half * (1.0 - tangent * tangent) * (
        gelu_scale + gelu_scale * 3.0 * 0.044715 * square
    )
    return value * plus, grad


def column(value, c):
    return jnp.concatenate([value[r, c : c + 1] for r in range(value.shape[0])], axis=0)


def rim_kernel(canvas_ref, *out_refs):
    cols = canvas_ref.shape[1]
    begin = canvas_ref[:, 0:16, :].astype(f32)
    end = canvas_ref[:, cols - 16 :, :].astype(f32)
    for c in range(2):
        pair = column(begin, c), column(end, 14 + c)
        if len(out_refs) == 1:
            out_refs[0][c] = jnp.where(lax.axis_index("cols") == 0, pair[1], pair[0]).astype(bf16)
        else:
            out_refs[0][c], out_refs[1][c] = pair[0].astype(bf16), pair[1].astype(bf16)


def payload_kernel(canvas_ref, target_ref, *refs):
    even_ref, odd_ref, left_ref, right_ref, half_ref = refs[-5:]
    rows, cols, width = canvas_ref.shape
    half_ref[0] = target_ref[...].astype(bf16)
    if len(refs) == 6:
        here = lax.axis_index("cols")
        other = refs[0][...].astype(f32)
        left_ref[...] = jnp.where(here == 0, 0.0, other).astype(bf16)
        right_ref[...] = jnp.where(here == 0, other, 0.0).astype(bf16)
    else:
        left_ref[...], right_ref[...] = refs[0][...], refs[1][...]
    beyond = [ref[c].astype(f32) for ref in (left_ref, right_ref) for c in range(2)]

    def fill(ref, r):
        for k in range(2):
            ref[k * cols : (k + 1) * cols, :] = canvas_ref[r + k]
        rim = [part[r + k : r + k + 1] for k in range(2) for part in beyond]
        rim = jnp.concatenate([*rim, jnp.zeros((8, width), f32)], axis=0)
        ref[2 * cols :, :] = rim.astype(bf16)

    odd = lax.rem(lax.axis_index("rows"), 2)

    @pl.when(odd == 0)
    def _():
        fill(even_ref, rows - 2)
        fill(odd_ref, 0)

    @pl.when(odd == 1)
    def _():
        fill(even_ref, 0)
        fill(odd_ref, rows - 2)


def moved_rows(row, before, after):
    cols = row.shape[0]
    wide = row.astype(f32)
    place = lax.broadcasted_iota(jnp.int32, (8, row.shape[1]), 0)
    right, left = pltpu.roll(wide, 1, 0), pltpu.roll(wide, cols - 1, 0)
    right = jnp.concatenate([jnp.where(place == 0, before, right[:8]), right[8:]], axis=0)
    left = jnp.concatenate([left[:-8], jnp.where(place == 7, after, left[-8:])], axis=0)
    return right.astype(bf16), row.astype(bf16), left.astype(bf16)


def fill_row(cat_ref, r, row, before, after):
    cols, width = row.shape
    for b, part in enumerate(moved_rows(row, before, after)):
        cat_ref[r * cols : (r + 1) * cols, b * width : (b + 1) * width] = part


def gram_tiles(feat, gram_ref, base_ref=None):
    width = feat.shape[1]
    half = width // 2
    product = functools.partial(
        lax.dot_general,
        dimension_numbers=(((0,), (0,)), ((), ())),
        preferred_element_type=f32,
    )
    upper = product(feat[:, :half], feat)
    lower = product(feat[:, half:], feat[:, half:])
    for n, (i, j) in enumerate(tile_pairs(width)):
        at = slice(n * tile, (n + 1) * tile)
        if i * tile < half:
            part = upper[i * tile : (i + 1) * tile, j * tile : (j + 1) * tile]
        else:
            k, m = i * tile - half, j * tile - half
            part = lower[k : k + tile, m : m + tile]
        gram_ref[at, :] = part if base_ref is None else part + base_ref[at, :]


def inner_kernel(
    shape, own_ref, left_ref, right_ref, kernel_ref, bias_ref,
    feat_ref, slope_ref, gram_ref, row_ref, part_ref, cat_ref,
):
    row_ref[...] = bias_ref[...].astype(f32).reshape(row_ref.shape)
    tile_rows, tile_cols, in_width, out_width, step = shape
    lefts, rights = left_ref[1].astype(f32), right_ref[0].astype(f32)
    for r in range(tile_rows):
        fill_row(cat_ref, r, own_ref[r], lefts[r : r + 1], rights[r : r + 1])
    bias = row_ref[...]
    root = 1.0 / math.sqrt(out_width)
    span = 3 * in_width

    def product(begin, count, a):
        return jnp.dot(
            cat_ref[begin * tile_cols : (begin + count) * tile_cols, :],
            kernel_ref[a * span : (a + 1) * span, :],
            preferred_element_type=f32,
        )

    for h in range(0, tile_rows - 2, step):
        total = bias
        for a in range(3):
            total = total + product(h + a, step, a)
        features, slope = gelu_pair(total)
        at = slice(h * tile_cols, (h + step) * tile_cols)
        feat_ref[at, :] = features.astype(bf16)
        slope_ref[at, :] = (slope * root).astype(bf16)
    low, high = product(0, 2, 2), product(tile_rows - 2, 2, 0)
    ends = product(0, 1, 1), product(tile_rows - 1, 1, 1)
    part_ref[0:tile_cols, :] = low[:tile_cols] + bias
    part_ref[tile_cols : 2 * tile_cols, :] = low[tile_cols:] + ends[0] + bias
    part_ref[2 * tile_cols : 3 * tile_cols, :] = high[:tile_cols] + ends[1] + bias
    part_ref[3 * tile_cols :, :] = high[tile_cols:] + bias
    gram_tiles(feat_ref[...], gram_ref)


def halo_rows(even_ref, odd_ref, low_ref, high_ref):
    row = lax.axis_index("rows")
    odd = lax.rem(row, 2)
    low_ref[...] = jnp.where(odd == 0, odd_ref[...], even_ref[...])
    high_ref[...] = jnp.where(odd == 0, even_ref[...], odd_ref[...])

    @pl.when(row == 0)
    def _():
        low_ref[...] = jnp.zeros_like(low_ref)

    @pl.when(row == lax.axis_size("rows") - 1)
    def _():
        high_ref[...] = jnp.zeros_like(high_ref)


def halves(width):
    return slice(0, width // 2), slice(width // 2, width)


def outer_kernel(
    shape, even_ref, odd_ref, kernel_ref, base_ref, part_ref,
    feat_ref, slope_ref, send_ref, keep_ref, low_ref, high_ref, cat_ref, gram_ref,
):
    tile_rows, tile_cols, in_width, out_width, step = shape
    span, main = 3 * in_width, 2 * tile_cols
    halo_rows(even_ref, odd_ref, low_ref, high_ref)
    for n, (source, at) in enumerate([(low_ref, tile_cols), (high_ref, 0)]):
        rim = source[main:, :].astype(f32)
        k = 4 * (1 - n)
        fill_row(cat_ref, n, source[at : at + tile_cols, :], rim[k + 1 : k + 2], rim[k + 2 : k + 3])
    root = 1.0 / math.sqrt(out_width)
    for at in halves(out_width):
        for n, a in enumerate([0, 2]):
            rows = slice(n * tile_cols, (n + 1) * tile_cols)
            features, slope = gelu_pair(
                part_ref[(n + 1) * tile_cols : (n + 2) * tile_cols, at]
                + jnp.dot(
                    cat_ref[rows, :],
                    kernel_ref[a * span : (a + 1) * span, at],
                    preferred_element_type=f32,
                )
            )
            feat_ref[rows, at] = features.astype(bf16)
            slope_ref[rows, at] = (slope * root).astype(bf16)
    gram_tiles(feat_ref[...], gram_ref, base_ref)
    half = send_ref.shape[0]
    side = side_of(0)
    send_ref[...] = gram_ref[rows_at(1 - side, half), :].astype(bf16)
    keep_ref[...] = gram_ref[rows_at(side, half), :]


def beyond_kernel(
    shape, own_ref, even_ref, odd_ref, left_ref, right_ref, kernel_ref, bias_ref, part_ref,
    feat_ref, slope_ref, low_ref, high_ref, cat_ref, edge_ref,
):
    tile_rows, tile_cols, in_width, out_width, step = shape
    halo_rows(even_ref, odd_ref, low_ref, high_ref)
    first = (lax.axis_index("rows") > 0).astype(f32)
    last = (lax.axis_index("rows") < lax.axis_size("rows") - 1).astype(f32)
    left = (lax.axis_index("cols") > 0).astype(f32)
    right = (lax.axis_index("cols") < lax.axis_size("cols") - 1).astype(f32)
    main = 2 * tile_cols
    low_rim, high_rim = low_ref[main:, :].astype(f32), high_ref[main:, :].astype(f32)
    own_begin = column(own_ref[:, 0:16, :].astype(f32), 0)
    own_end = column(own_ref[:, tile_cols - 16 :, :].astype(f32), 15)

    def sides(c, own):
        return jnp.concatenate(
            [low_rim[c : c + 1], low_rim[4 + c : 5 + c], own, high_rim[c : c + 1], high_rim[4 + c : 5 + c]],
            axis=0,
        )

    def ends(c, own):
        c16 = c // 16 * 16
        piece = lambda ref, k: ref[k + c16 : k + c16 + 16, :].astype(f32)[c - c16 : c - c16 + 1]
        rows = [piece(low_ref, 0), piece(low_ref, tile_cols), own]
        return jnp.concatenate([*rows, piece(high_ref, 0), piece(high_ref, tile_cols)], axis=0)

    lefts = [
        sides(0, left_ref[0].astype(f32)), sides(1, left_ref[1].astype(f32)), ends(0, own_begin)
    ]
    rights = [
        ends(tile_cols - 1, own_end), sides(2, right_ref[0].astype(f32)), sides(3, right_ref[1].astype(f32))
    ]
    span = 3 * in_width
    for r, line in enumerate([0, 1, tile_rows + 2, tile_rows + 3]):
        source = low_ref if r < 2 else high_ref
        row = source[r % 2 * tile_cols : (r % 2 + 1) * tile_cols, :]
        fill_row(cat_ref, r, row, lefts[1][line : line + 1], rights[1][line : line + 1])
    blank = jnp.zeros((edge - tile_rows - 2, in_width), f32)
    for a in range(3):
        for b in range(3):
            piece = jnp.concatenate(
                [lefts[b][a : a + tile_rows + 2], blank, rights[b][a : a + tile_rows + 2], blank],
                axis=0,
            )
            at = (3 * a + b) * in_width
            edge_ref[:, at : at + in_width] = piece.astype(bf16)
    root = 1.0 / math.sqrt(out_width)
    line = lax.broadcasted_iota(jnp.int32, (2 * edge, out_width // 2), 0)
    weight = jnp.where(line < edge, left, right)
    weight = jnp.where(line % edge == 0, weight * first, weight)
    weight = jnp.where(line % edge == tile_rows + 1, weight * last, weight)
    for at in halves(out_width):

        def product(begin, a):
            return jnp.dot(
                cat_ref[begin * tile_cols : (begin + 1) * tile_cols, :],
                kernel_ref[a * span : (a + 1) * span, at],
                preferred_element_type=f32,
            )

        totals = [
            part_ref[0:tile_cols, at] + product(0, 0) + product(1, 1),
            part_ref[3 * tile_cols :, at] + product(2, 1) + product(3, 2),
            bias_ref[:, at] + jnp.dot(edge_ref[...], kernel_ref[:, at], preferred_element_type=f32),
        ]
        scales = [first * root, last * root, weight * root]
        for n, (total, scale) in enumerate(zip(totals, scales)):
            features, slope = gelu_pair(total)
            rows = slice(n * tile_cols, n * tile_cols + total.shape[0])
            feat_ref[rows, at] = features.astype(bf16)
            slope_ref[rows, at] = (slope * scale).astype(bf16)


def prepare_kernel(kernel_ref, target_ref, turned_ref, both_ref):
    taps, in_width, out_width = 9, kernel_ref.shape[0] // 9, kernel_ref.shape[1]
    for n in range(taps):
        to = (n // 3 * 3 + 2 - n % 3) * out_width
        turned_ref[to : to + out_width, :] = kernel_ref[n * in_width : (n + 1) * in_width, :].T
    for i, j in tile_pairs(out_width):
        at_i, at_j = slice(i * tile, (i + 1) * tile), slice(j * tile, (j + 1) * tile)
        both = target_ref[at_i, at_j].astype(f32) + target_ref[at_j, at_i].astype(f32).T
        both_ref[at_i, at_j] = both
        if i != j:
            both_ref[at_j, at_i] = both.T


def backward_kernel(
    shape, pixel_total, mine_ref, other_ref, both_ref, in_feat_ref, in_slope_ref, out_feat_ref, out_slope_ref,
    far_feat_ref, far_slope_ref, turned_ref, own_gram_ref, out_ref, gram_ref, full_ref, sym_ref, cat_ref,
):
    tile_rows, tile_cols, in_width, out_width, step = shape
    half = mine_ref.shape[0]
    side = side_of(0)
    gram_ref[rows_at(side, half), :] = mine_ref[...].astype(f32)
    gram_ref[rows_at(1 - side, half), :] = other_ref[...].astype(f32)
    for n, (i, j) in enumerate(tile_pairs(out_width)):
        at_i, at_j = slice(i * tile, (i + 1) * tile), slice(j * tile, (j + 1) * tile)
        gram = gram_ref[n * tile : (n + 1) * tile, :] * (1.0 / pixel_total)
        full_ref[at_i, at_j] = gram
        sym_ref[at_i, at_j] = (2.0 * gram - both_ref[at_i, at_j]).astype(bf16)
        if i != j:
            gram = gram.T
            full_ref[at_j, at_i] = gram
            sym_ref[at_j, at_i] = (2.0 * gram - both_ref[at_j, at_i]).astype(bf16)
    share = own_gram_ref.shape[0]
    start = device_index() * share
    if share % 8 == 0:
        own_gram_ref[...] = full_ref[pl.ds(pl.multiple_of(start, 8), share), :]
    else:
        group = full_ref[pl.ds(pl.multiple_of(start // 8 * 8, 8), 8), :]
        picked = group[0:share]
        for k in range(share, 8, share):
            picked = jnp.where(start % 8 == k, group[k : k + share], picked)
        own_gram_ref[...] = picked

    def grad_of(feat_ref, slope_ref, at):
        product = jnp.dot(feat_ref[at, :], sym_ref[...], preferred_element_type=f32)
        return product * slope_ref[at, :].astype(f32)

    main = 2 * tile_cols
    edges = grad_of(far_feat_ref, far_slope_ref, slice(main, None))
    near, far = (out_feat_ref, out_slope_ref), (far_feat_ref, far_slope_ref)
    lines = [[(*far, 0), (*near, 0)]]
    lines += [
        [(in_feat_ref, in_slope_ref, k * tile_cols) for k in range(h, h + step)]
        for h in range(0, tile_rows - 2, step)
    ]
    lines += [[(*near, tile_cols), (*far, tile_cols)]]
    grads = {}

    def upstream(c):
        pieces = lines[c]
        if pieces[0][0] is pieces[1][0]:
            feat_ref, slope_ref, begin = pieces[0]
            grads[c] = grad_of(feat_ref, slope_ref, slice(begin, begin + step * tile_cols))
        else:
            parts = [grad_of(feat, slope, slice(begin, begin + tile_cols)) for feat, slope, begin in pieces]
            grads[c] = jnp.concatenate(parts, axis=0)

    def fill(c):
        for k in range(step):
            r = c * step + k
            fill_row(
                cat_ref, r, grads[c][k * tile_cols : (k + 1) * tile_cols],
                edges[r : r + 1], edges[edge + r : edge + r + 1],
            )

    span = 3 * out_width

    def convolve(begin, count):
        total = 0.0
        for a in range(3):
            total = total + jnp.dot(
                cat_ref[(begin + 2 - a) * tile_cols : (begin + 2 - a + count) * tile_cols, :],
                turned_ref[a * span : (a + 1) * span, :],
                preferred_element_type=f32,
            )
        out_ref[begin * tile_cols : (begin + count) * tile_cols, :] = total.astype(bf16)

    last = len(lines) - 1
    middle = last // 2
    half_rows = middle * step
    upstream(0)
    for c in range(last):
        upstream(c + 1)
        fill(c)
        if c == middle:
            convolve(0, half_rows)
    fill(last)
    convolve(half_rows, tile_rows - half_rows)


def on_device(canvas, conv_weight, conv_bias, target_gram):
    tile_rows, tile_cols, in_width = canvas.shape
    out_width = conv_weight.shape[3]
    pixel_total = tile_rows * tile_cols * lax.axis_size("rows") * lax.axis_size("cols")
    shape = (tile_rows, tile_cols, in_width, out_width, 2)
    kernel = conv_weight.reshape(9 * in_width, out_width)
    params = pltpu.CompilerParams(vmem_limit_bytes=24 * 1024 * 1024)
    vmem = pl.BlockSpec(memory_space=pltpu.VMEM)
    packed_shape = jax.ShapeDtypeStruct((len(tile_pairs(out_width)) * tile, tile), f32)

    rim_shape = jax.ShapeDtypeStruct((2, tile_rows, in_width), bf16)
    two = lax.axis_size("cols") == 2
    rims = local(
        rim_kernel,
        (rim_shape,) * (1 if two else 2),
        "column_rims",
        canvas,
        cost_estimate=pl.CostEstimate(flops=4_000_000_000, bytes_accessed=600_000, transcendentals=0),
    )
    if two:
        beyond = [lax.ppermute(rims[0], "cols", [(0, 1), (1, 0)])]
    else:
        beyond = shift_cols(rims[1], rims[0])
    payload_shape = jax.ShapeDtypeStruct((2 * tile_cols + edge, in_width), bf16)
    half_shape = jax.ShapeDtypeStruct((1, *target_gram.shape), bf16)
    even, odd, left, right, rows = local(
        payload_kernel,
        (payload_shape, payload_shape, rim_shape, rim_shape, half_shape),
        "row_payload",
        canvas,
        target_gram,
        *beyond,
    )
    count = lax.axis_size("rows")
    even, odd = swap_rows(range(0, count, 2), even), swap_rows(range(1, count, 2), odd)

    bits = (lax.axis_size("rows") * lax.axis_size("cols")).bit_length() - 1
    gather = Gather(rows)
    far = list(reversed(range(3, bits)))
    inner = (tile_rows - 2) * tile_cols
    in_feat, in_slope, in_gram, bias, part = pl.pallas_call(
        functools.partial(inner_kernel, shape),
        out_shape=(
            jax.ShapeDtypeStruct((inner, out_width), bf16),
            jax.ShapeDtypeStruct((inner, out_width), bf16),
            packed_shape,
            jax.ShapeDtypeStruct((1, out_width), f32),
            jax.ShapeDtypeStruct((4 * tile_cols, out_width), f32),
        ),
        in_specs=[vmem] * 5,
        scratch_shapes=[pltpu.VMEM((tile_rows * tile_cols, 3 * in_width), bf16)],
        compiler_params=params,
        name="inner_rows",
        cost_estimate=pl.CostEstimate(
            flops=2 * inner * (9 * in_width + out_width) * out_width,
            bytes_accessed=6_000_000,
            transcendentals=inner * out_width,
        ),
    )(canvas, left, right, kernel, conv_bias)

    half_gram = (packed_shape.shape[0] // 2, tile)
    halo_scratch = [pltpu.VMEM(payload_shape.shape, bf16), pltpu.VMEM(payload_shape.shape, bf16)]
    out_feat, out_slope, send, keep = pl.pallas_call(
        functools.partial(outer_kernel, shape),
        out_shape=(
            jax.ShapeDtypeStruct((2 * tile_cols, out_width), bf16),
            jax.ShapeDtypeStruct((2 * tile_cols, out_width), bf16),
            jax.ShapeDtypeStruct(half_gram, bf16),
            jax.ShapeDtypeStruct(half_gram, f32),
        ),
        in_specs=[vmem] * 5,
        scratch_shapes=[
            *halo_scratch,
            pltpu.VMEM((2 * tile_cols, 3 * in_width), bf16),
            pltpu.VMEM(packed_shape.shape, f32),
        ],
        compiler_params=params,
        name="outer_rows",
    )(even, odd, kernel, in_gram, part)

    exchanges = {"cores": far[:1], "halve 1": far[1:], "halve 2": [1], "add 3": [2], "add 4": [0]}
    prepared, far_pixels = [], []

    def beside(name, sent, got):
        if name == "join 1":
            outer = 2 * tile_cols + 2 * edge
            rim_sums, _ = lax.optimization_barrier((part, sent))
            far_pixels.extend(
                pl.pallas_call(
                    functools.partial(beyond_kernel, shape),
                    out_shape=(jax.ShapeDtypeStruct((outer, out_width), bf16),) * 2,
                    in_specs=[vmem] * 8,
                    scratch_shapes=[
                        *halo_scratch,
                        pltpu.VMEM((4 * tile_cols, 3 * in_width), bf16),
                        pltpu.VMEM((2 * edge, 9 * in_width), bf16),
                    ],
                    compiler_params=params,
                    name="beyond",
                    cost_estimate=chained,
                )(canvas, even, odd, left, right, kernel, bias, rim_sums)
            )
            return lax.optimization_barrier((got, *far_pixels))[0]
        for bit in exchanges.get(name, []):
            gather.step(bit, sent)
        if name != "join 2":
            return got
        gather.settle(sent)
        prepared.extend(
            pl.pallas_call(
                prepare_kernel,
                out_shape=(
                    jax.ShapeDtypeStruct((9 * out_width, in_width), bf16),
                    jax.ShapeDtypeStruct((out_width, out_width), f32),
                ),
                in_specs=[vmem] * 2,
                compiler_params=params,
                name="prepare",
                cost_estimate=pl.CostEstimate(
                    flops=2_000_000_000, bytes_accessed=6_000_000, transcendentals=0
                ),
            )(kernel, gather.rows.reshape(out_width, out_width))
        )
        return lax.optimization_barrier((got, *prepared))[0]

    mine, other = sum_all(send, keep, beside)
    turned, both = prepared
    far_feat, far_slope = far_pixels
    own_gram, grad = pl.pallas_call(
        functools.partial(backward_kernel, shape, pixel_total),
        out_shape=(
            jax.ShapeDtypeStruct(target_gram.shape, f32),
            jax.ShapeDtypeStruct((tile_rows * tile_cols, in_width), bf16),
        ),
        in_specs=[vmem] * 10,
        scratch_shapes=[
            pltpu.VMEM(packed_shape.shape, f32),
            pltpu.VMEM((out_width, out_width), f32),
            pltpu.VMEM((out_width, out_width), bf16),
            pltpu.VMEM(((tile_rows + 2) * tile_cols, 3 * out_width), bf16),
        ],
        compiler_params=params,
        name="grad_conv",
    )(mine, other, both, in_feat, in_slope, out_feat, out_slope, far_feat, far_slope, turned)
    return own_gram, grad.reshape(tile_rows, tile_cols, in_width)


def solution(mesh):
    return jax.shard_map(
        on_device,
        mesh=mesh,
        in_specs=(P("rows", "cols", None), P(), P(), P(("rows", "cols"), None)),
        out_specs=(P(("rows", "cols"), None), P("rows", "cols", None)),
        check_vma=False,
    )
```

```python
import functools
import math

import jax
import jax.numpy as jnp
from jax import lax
from jax.experimental import pallas as pl
from jax.experimental.pallas import tpu as pltpu
from jax.sharding import PartitionSpec as P

gelu_scale = math.sqrt(2.0 / math.pi)
tile = 128
edge = 16
f32, bf16 = jnp.float32, jnp.bfloat16


def tile_pairs(width):
    count = width // tile
    return [(i, j) for i in range(count) for j in range(i, count)]


def swap_rows(low, value):
    count = lax.axis_size("rows")
    pairs = [(i, (i + 1) % count) for i in low]
    return lax.ppermute(value, "rows", pairs + [(target, source) for source, target in pairs])


def shift_cols(last, first):
    count = lax.axis_size("cols")
    forward = [(i, i + 1) for i in range(count - 1)]
    backward = [(target, source) for source, target in forward]
    return lax.ppermute(last, "cols", forward), lax.ppermute(first, "cols", backward)


def device_index():
    return lax.axis_index("rows") * lax.axis_size("cols") + lax.axis_index("cols")


def swap(value, bit, other=None):
    total = lax.axis_size("rows") * lax.axis_size("cols")
    flip = lambda i: 1 << (other if other is not None and i.bit_count() % 2 else bit) | 1
    return lax.ppermute(value, ("rows", "cols"), [(i, i ^ flip(i)) for i in range(total)])


def local(body, out_shape, name, *operands, **kwargs):
    return pl.pallas_call(
        body,
        out_shape=out_shape,
        in_specs=[pl.BlockSpec(memory_space=pltpu.VMEM)] * len(operands),
        compiler_params=pltpu.CompilerParams(vmem_limit_bytes=8 * 1024 * 1024),
        name=name,
        **kwargs,
    )(*operands)


def side_of(bit, other=None):
    index = device_index()
    if bit > 0:
        side = lax.rem(index // (1 << bit), 2)
        if other is None:
            return side
        return jnp.where(side_of(0) == 0, side, lax.rem(index // (1 << other), 2))
    bits = (lax.axis_size("rows") * lax.axis_size("cols")).bit_length() - 1
    return lax.rem(sum(lax.rem(index // (1 << k), 2) for k in range(bits)), 2)


def rows_at(index, count):
    return pl.ds(pl.multiple_of(index * count, count), count)


waiting = pl.CostEstimate(flops=1_500_000_000, bytes_accessed=100_000, transcendentals=0)
chained = pl.CostEstimate(flops=8_000_000_000, bytes_accessed=100_000, transcendentals=0)


def halve(keep, got, bit, other=None):
    half = keep.shape[0] // 2

    def body(keep_ref, got_ref, send_ref, stay_ref):
        side = side_of(bit, other)
        away, here = rows_at(1 - side, half), rows_at(side, half)
        send_ref[...] = (keep_ref[away, :] + got_ref[away, :].astype(f32)).astype(bf16)
        stay_ref[...] = keep_ref[here, :] + got_ref[here, :].astype(f32)

    shape = (half, keep.shape[1])
    return local(
        body,
        (jax.ShapeDtypeStruct(shape, bf16), jax.ShapeDtypeStruct(shape, f32)),
        "halve",
        keep,
        got,
        cost_estimate=chained,
    )


def add(keep, got):
    def body(keep_ref, got_ref, sum_ref):
        sum_ref[...] = (keep_ref[...].astype(f32) + got_ref[...].astype(f32)).astype(bf16)

    return local(body, jax.ShapeDtypeStruct(got.shape, bf16), "add", keep, got, cost_estimate=chained)


def join(mine, got, bit, other=None, **kwargs):
    def body(mine_ref, got_ref, both_ref):
        side = side_of(bit, other)
        both_ref[:, pl.ds(side, 1)] = mine_ref[...][:, None]
        both_ref[:, pl.ds(1 - side, 1)] = got_ref[...][:, None]

    shape = (mine.shape[0], 2, *mine.shape[1:])
    return local(body, jax.ShapeDtypeStruct(shape, mine.dtype), "join", mine, got, **kwargs)


def join_second(mine, got, bit, other, **kwargs):
    def body(mine_ref, got_ref, both_ref):
        parity, side = side_of(0), side_of(bit, other)

        @pl.when(parity == 0)
        def _():
            both_ref[:, pl.ds(side, 1)] = mine_ref[...][:, None]
            both_ref[:, pl.ds(1 - side, 1)] = got_ref[...][:, None]

        @pl.when(parity == 1)
        def _():
            both_ref[:, :, pl.ds(side, 1)] = mine_ref[...][:, :, None]
            both_ref[:, :, pl.ds(1 - side, 1)] = got_ref[...][:, :, None]

    shape = (mine.shape[0], 2, *mine.shape[1:])
    return local(body, jax.ShapeDtypeStruct(shape, mine.dtype), "join_second", mine, got, **kwargs)


def join_cores(mine, other, **kwargs):
    def body(mine_ref, other_ref, both_ref):
        side = side_of(0)
        for chip in range(mine.shape[0]):
            core = lax.rem(side + chip.bit_count(), 2)
            both_ref[chip, pl.ds(core, 1)] = mine_ref[chip][None]
            both_ref[chip, pl.ds(1 - core, 1)] = other_ref[chip][None]

    shape = (mine.shape[0], 2, *mine.shape[1:])
    return local(body, jax.ShapeDtypeStruct(shape, mine.dtype), "join_cores", mine, other, **kwargs)


class Gather:
    def __init__(self, rows):
        self.rows, self.got, self.last = rows, None, None

    def settle(self, after):
        if self.got is None:
            self.rows, _ = lax.optimization_barrier((self.rows, after))
            return
        share = self.rows.shape[-2:]
        got, _ = lax.optimization_barrier((self.got, after))
        bit, other = self.last
        if bit == 0:
            both = join_cores(self.rows, got, cost_estimate=waiting)
        elif other is None or bit < other:
            mine, got = (part.reshape(-1, 1, *share) for part in (self.rows, got))
            both = join(mine, got, bit, other, cost_estimate=waiting)
        else:
            mine, got = (part.reshape(-1, 2, *share) for part in (self.rows, got))
            both = join_second(mine, got, bit, other, cost_estimate=waiting)
        self.rows, self.got = both.reshape(-1, *share), None

    def step(self, after, bit, other=None):
        self.settle(after)
        self.got, self.last = swap(self.rows, bit, other), (bit, other)


def sum_all(send, keep, beside):
    bits = (lax.axis_size("rows") * lax.axis_size("cols")).bit_length() - 1
    halving = [(1, 2), (2, 1)]
    adding = []
    for bit in range(3, bits, 2):
        adding += [(bit, bit + 1), (bit + 1, bit)] if bit + 1 < bits else [(bit, None)]

    got = beside("cores", send, swap(send, 0))
    for n, pair in enumerate(halving):
        send, keep = halve(keep, got, *pair)
        got = beside(f"halve {n}", send, swap(send, *pair))
    mine = add(keep, got)
    for n, pair in enumerate(adding):
        mine = add(mine, beside(f"add {n}", mine, swap(mine, *pair)))
    for n, pair in enumerate(reversed(halving)):
        got = beside(f"join {n}", mine, swap(mine, *pair))
        mine = join(mine[None], got[None], *pair, cost_estimate=chained).reshape(-1, mine.shape[1])
    return mine, beside("halves", mine, swap(mine, 0))


def gelu_pair(value):
    square = value * value
    tangent = jnp.tanh(value * (gelu_scale + gelu_scale * 0.044715 * square))
    half = 0.5 * value
    plus = 0.5 + 0.5 * tangent
    grad = plus + half * (1.0 - tangent * tangent) * (
        gelu_scale + gelu_scale * 3.0 * 0.044715 * square
    )
    return value * plus, grad


def column(value, c):
    return jnp.concatenate([value[r, c : c + 1] for r in range(value.shape[0])], axis=0)


def rim_kernel(canvas_ref, *out_refs):
    cols = canvas_ref.shape[1]
    begin = canvas_ref[:, 0:16, :].astype(f32)
    end = canvas_ref[:, cols - 16 :, :].astype(f32)
    for c in range(2):
        pair = column(begin, c), column(end, 14 + c)
        if len(out_refs) == 1:
            out_refs[0][c] = jnp.where(lax.axis_index("cols") == 0, pair[1], pair[0]).astype(bf16)
        else:
            out_refs[0][c], out_refs[1][c] = pair[0].astype(bf16), pair[1].astype(bf16)


def payload_kernel(canvas_ref, target_ref, *refs):
    even_ref, odd_ref, left_ref, right_ref, half_ref = refs[-5:]
    rows, cols, width = canvas_ref.shape
    half_ref[0] = target_ref[...].astype(bf16)
    if len(refs) == 6:
        here = lax.axis_index("cols")
        other = refs[0][...].astype(f32)
        left_ref[...] = jnp.where(here == 0, 0.0, other).astype(bf16)
        right_ref[...] = jnp.where(here == 0, other, 0.0).astype(bf16)
    else:
        left_ref[...], right_ref[...] = refs[0][...], refs[1][...]
    beyond = [ref[c].astype(f32) for ref in (left_ref, right_ref) for c in range(2)]

    def fill(ref, r):
        for k in range(2):
            ref[k * cols : (k + 1) * cols, :] = canvas_ref[r + k]
        rim = [part[r + k : r + k + 1] for k in range(2) for part in beyond]
        rim = jnp.concatenate([*rim, jnp.zeros((8, width), f32)], axis=0)
        ref[2 * cols :, :] = rim.astype(bf16)

    odd = lax.rem(lax.axis_index("rows"), 2)

    @pl.when(odd == 0)
    def _():
        fill(even_ref, rows - 2)
        fill(odd_ref, 0)

    @pl.when(odd == 1)
    def _():
        fill(even_ref, 0)
        fill(odd_ref, rows - 2)


def moved_rows(row, before, after):
    cols = row.shape[0]
    wide = row.astype(f32)
    place = lax.broadcasted_iota(jnp.int32, (8, row.shape[1]), 0)
    right, left = pltpu.roll(wide, 1, 0), pltpu.roll(wide, cols - 1, 0)
    right = jnp.concatenate([jnp.where(place == 0, before, right[:8]), right[8:]], axis=0)
    left = jnp.concatenate([left[:-8], jnp.where(place == 7, after, left[-8:])], axis=0)
    return right.astype(bf16), row.astype(bf16), left.astype(bf16)


def fill_row(cat_ref, r, row, before, after):
    cols, width = row.shape
    for b, part in enumerate(moved_rows(row, before, after)):
        cat_ref[r * cols : (r + 1) * cols, b * width : (b + 1) * width] = part


def gram_tiles(feat, gram_ref, base_ref=None):
    width = feat.shape[1]
    half = width // 2
    product = functools.partial(
        lax.dot_general,
        dimension_numbers=(((0,), (0,)), ((), ())),
        preferred_element_type=f32,
    )
    upper = product(feat[:, :half], feat)
    lower = product(feat[:, half:], feat[:, half:])
    for n, (i, j) in enumerate(tile_pairs(width)):
        at = slice(n * tile, (n + 1) * tile)
        if i * tile < half:
            part = upper[i * tile : (i + 1) * tile, j * tile : (j + 1) * tile]
        else:
            k, m = i * tile - half, j * tile - half
            part = lower[k : k + tile, m : m + tile]
        gram_ref[at, :] = part if base_ref is None else part + base_ref[at, :]


def inner_kernel(
    shape, own_ref, left_ref, right_ref, kernel_ref, bias_ref,
    feat_ref, slope_ref, gram_ref, row_ref, part_ref, cat_ref,
):
    row_ref[...] = bias_ref[...].astype(f32).reshape(row_ref.shape)
    tile_rows, tile_cols, in_width, out_width, step = shape
    lefts, rights = left_ref[1].astype(f32), right_ref[0].astype(f32)
    for r in range(tile_rows):
        fill_row(cat_ref, r, own_ref[r], lefts[r : r + 1], rights[r : r + 1])
    bias = row_ref[...]
    root = 1.0 / math.sqrt(out_width)
    span = 3 * in_width

    def product(begin, count, a):
        return jnp.dot(
            cat_ref[begin * tile_cols : (begin + count) * tile_cols, :],
            kernel_ref[a * span : (a + 1) * span, :],
            preferred_element_type=f32,
        )

    for h in range(0, tile_rows - 2, step):
        total = bias
        for a in range(3):
            total = total + product(h + a, step, a)
        features, slope = gelu_pair(total)
        at = slice(h * tile_cols, (h + step) * tile_cols)
        feat_ref[at, :] = features.astype(bf16)
        slope_ref[at, :] = (slope * root).astype(bf16)
    low, high = product(0, 2, 2), product(tile_rows - 2, 2, 0)
    ends = product(0, 1, 1), product(tile_rows - 1, 1, 1)
    part_ref[0:tile_cols, :] = low[:tile_cols] + bias
    part_ref[tile_cols : 2 * tile_cols, :] = low[tile_cols:] + ends[0] + bias
    part_ref[2 * tile_cols : 3 * tile_cols, :] = high[:tile_cols] + ends[1] + bias
    part_ref[3 * tile_cols :, :] = high[tile_cols:] + bias
    gram_tiles(feat_ref[...], gram_ref)


def halo_rows(even_ref, odd_ref, low_ref, high_ref):
    row = lax.axis_index("rows")
    odd = lax.rem(row, 2)
    low_ref[...] = jnp.where(odd == 0, odd_ref[...], even_ref[...])
    high_ref[...] = jnp.where(odd == 0, even_ref[...], odd_ref[...])

    @pl.when(row == 0)
    def _():
        low_ref[...] = jnp.zeros_like(low_ref)

    @pl.when(row == lax.axis_size("rows") - 1)
    def _():
        high_ref[...] = jnp.zeros_like(high_ref)


def halves(width):
    return slice(0, width // 2), slice(width // 2, width)


def outer_kernel(
    shape, even_ref, odd_ref, kernel_ref, base_ref, part_ref,
    feat_ref, slope_ref, send_ref, keep_ref, low_ref, high_ref, cat_ref, gram_ref,
):
    tile_rows, tile_cols, in_width, out_width, step = shape
    span, main = 3 * in_width, 2 * tile_cols
    halo_rows(even_ref, odd_ref, low_ref, high_ref)
    for n, (source, at) in enumerate([(low_ref, tile_cols), (high_ref, 0)]):
        rim = source[main:, :].astype(f32)
        k = 4 * (1 - n)
        fill_row(cat_ref, n, source[at : at + tile_cols, :], rim[k + 1 : k + 2], rim[k + 2 : k + 3])
    root = 1.0 / math.sqrt(out_width)
    for at in halves(out_width):
        for n, a in enumerate([0, 2]):
            rows = slice(n * tile_cols, (n + 1) * tile_cols)
            features, slope = gelu_pair(
                part_ref[(n + 1) * tile_cols : (n + 2) * tile_cols, at]
                + jnp.dot(
                    cat_ref[rows, :],
                    kernel_ref[a * span : (a + 1) * span, at],
                    preferred_element_type=f32,
                )
            )
            feat_ref[rows, at] = features.astype(bf16)
            slope_ref[rows, at] = (slope * root).astype(bf16)
    gram_tiles(feat_ref[...], gram_ref, base_ref)
    half = send_ref.shape[0]
    side = side_of(0)
    send_ref[...] = gram_ref[rows_at(1 - side, half), :].astype(bf16)
    keep_ref[...] = gram_ref[rows_at(side, half), :]


def beyond_kernel(
    shape, own_ref, even_ref, odd_ref, left_ref, right_ref, kernel_ref, bias_ref, part_ref,
    feat_ref, slope_ref, low_ref, high_ref, cat_ref, edge_ref,
):
    tile_rows, tile_cols, in_width, out_width, step = shape
    halo_rows(even_ref, odd_ref, low_ref, high_ref)
    first = (lax.axis_index("rows") > 0).astype(f32)
    last = (lax.axis_index("rows") < lax.axis_size("rows") - 1).astype(f32)
    left = (lax.axis_index("cols") > 0).astype(f32)
    right = (lax.axis_index("cols") < lax.axis_size("cols") - 1).astype(f32)
    main = 2 * tile_cols
    low_rim, high_rim = low_ref[main:, :].astype(f32), high_ref[main:, :].astype(f32)
    own_begin = column(own_ref[:, 0:16, :].astype(f32), 0)
    own_end = column(own_ref[:, tile_cols - 16 :, :].astype(f32), 15)

    def sides(c, own):
        return jnp.concatenate(
            [low_rim[c : c + 1], low_rim[4 + c : 5 + c], own, high_rim[c : c + 1], high_rim[4 + c : 5 + c]],
            axis=0,
        )

    def ends(c, own):
        c16 = c // 16 * 16
        piece = lambda ref, k: ref[k + c16 : k + c16 + 16, :].astype(f32)[c - c16 : c - c16 + 1]
        rows = [piece(low_ref, 0), piece(low_ref, tile_cols), own]
        return jnp.concatenate([*rows, piece(high_ref, 0), piece(high_ref, tile_cols)], axis=0)

    lefts = [
        sides(0, left_ref[0].astype(f32)), sides(1, left_ref[1].astype(f32)), ends(0, own_begin)
    ]
    rights = [
        ends(tile_cols - 1, own_end), sides(2, right_ref[0].astype(f32)), sides(3, right_ref[1].astype(f32))
    ]
    span = 3 * in_width
    for r, line in enumerate([0, 1, tile_rows + 2, tile_rows + 3]):
        source = low_ref if r < 2 else high_ref
        row = source[r % 2 * tile_cols : (r % 2 + 1) * tile_cols, :]
        fill_row(cat_ref, r, row, lefts[1][line : line + 1], rights[1][line : line + 1])
    blank = jnp.zeros((edge - tile_rows - 2, in_width), f32)
    for a in range(3):
        for b in range(3):
            piece = jnp.concatenate(
                [lefts[b][a : a + tile_rows + 2], blank, rights[b][a : a + tile_rows + 2], blank],
                axis=0,
            )
            at = (3 * a + b) * in_width
            edge_ref[:, at : at + in_width] = piece.astype(bf16)
    root = 1.0 / math.sqrt(out_width)
    line = lax.broadcasted_iota(jnp.int32, (2 * edge, out_width // 2), 0)
    weight = jnp.where(line < edge, left, right)
    weight = jnp.where(line % edge == 0, weight * first, weight)
    weight = jnp.where(line % edge == tile_rows + 1, weight * last, weight)
    for at in halves(out_width):

        def product(begin, a):
            return jnp.dot(
                cat_ref[begin * tile_cols : (begin + 1) * tile_cols, :],
                kernel_ref[a * span : (a + 1) * span, at],
                preferred_element_type=f32,
            )

        totals = [
            part_ref[0:tile_cols, at] + product(0, 0) + product(1, 1),
            part_ref[3 * tile_cols :, at] + product(2, 1) + product(3, 2),
            bias_ref[:, at] + jnp.dot(edge_ref[...], kernel_ref[:, at], preferred_element_type=f32),
        ]
        scales = [first * root, last * root, weight * root]
        for n, (total, scale) in enumerate(zip(totals, scales)):
            features, slope = gelu_pair(total)
            rows = slice(n * tile_cols, n * tile_cols + total.shape[0])
            feat_ref[rows, at] = features.astype(bf16)
            slope_ref[rows, at] = (slope * scale).astype(bf16)


def prepare_kernel(kernel_ref, target_ref, turned_ref, both_ref):
    taps, in_width, out_width = 9, kernel_ref.shape[0] // 9, kernel_ref.shape[1]
    for n in range(taps):
        to = (n // 3 * 3 + 2 - n % 3) * out_width
        turned_ref[to : to + out_width, :] = kernel_ref[n * in_width : (n + 1) * in_width, :].T
    for i, j in tile_pairs(out_width):
        at_i, at_j = slice(i * tile, (i + 1) * tile), slice(j * tile, (j + 1) * tile)
        both = target_ref[at_i, at_j].astype(f32) + target_ref[at_j, at_i].astype(f32).T
        both_ref[at_i, at_j] = both
        if i != j:
            both_ref[at_j, at_i] = both.T


def backward_kernel(
    shape, pixel_total, mine_ref, other_ref, both_ref, in_feat_ref, in_slope_ref, out_feat_ref, out_slope_ref,
    far_feat_ref, far_slope_ref, turned_ref, own_gram_ref, out_ref, gram_ref, full_ref, sym_ref, cat_ref,
):
    tile_rows, tile_cols, in_width, out_width, step = shape
    half = mine_ref.shape[0]
    side = side_of(0)
    gram_ref[rows_at(side, half), :] = mine_ref[...].astype(f32)
    gram_ref[rows_at(1 - side, half), :] = other_ref[...].astype(f32)
    for n, (i, j) in enumerate(tile_pairs(out_width)):
        at_i, at_j = slice(i * tile, (i + 1) * tile), slice(j * tile, (j + 1) * tile)
        gram = gram_ref[n * tile : (n + 1) * tile, :] * (1.0 / pixel_total)
        full_ref[at_i, at_j] = gram
        sym_ref[at_i, at_j] = (2.0 * gram - both_ref[at_i, at_j]).astype(bf16)
        if i != j:
            gram = gram.T
            full_ref[at_j, at_i] = gram
            sym_ref[at_j, at_i] = (2.0 * gram - both_ref[at_j, at_i]).astype(bf16)
    share = own_gram_ref.shape[0]
    start = device_index() * share
    if share % 8 == 0:
        own_gram_ref[...] = full_ref[pl.ds(pl.multiple_of(start, 8), share), :]
    else:
        group = full_ref[pl.ds(pl.multiple_of(start // 8 * 8, 8), 8), :]
        picked = group[0:share]
        for k in range(share, 8, share):
            picked = jnp.where(start % 8 == k, group[k : k + share], picked)
        own_gram_ref[...] = picked

    def grad_of(feat_ref, slope_ref, at):
        product = jnp.dot(feat_ref[at, :], sym_ref[...], preferred_element_type=f32)
        return product * slope_ref[at, :].astype(f32)

    main = 2 * tile_cols
    edges = grad_of(far_feat_ref, far_slope_ref, slice(main, None))
    near, far = (out_feat_ref, out_slope_ref), (far_feat_ref, far_slope_ref)
    lines = [[(*far, 0), (*near, 0)]]
    lines += [
        [(in_feat_ref, in_slope_ref, k * tile_cols) for k in range(h, h + step)]
        for h in range(0, tile_rows - 2, step)
    ]
    lines += [[(*near, tile_cols), (*far, tile_cols)]]
    grads = {}

    def upstream(c):
        pieces = lines[c]
        if pieces[0][0] is pieces[1][0]:
            feat_ref, slope_ref, begin = pieces[0]
            grads[c] = grad_of(feat_ref, slope_ref, slice(begin, begin + step * tile_cols))
        else:
            parts = [grad_of(feat, slope, slice(begin, begin + tile_cols)) for feat, slope, begin in pieces]
            grads[c] = jnp.concatenate(parts, axis=0)

    def fill(c):
        for k in range(step):
            r = c * step + k
            fill_row(
                cat_ref, r, grads[c][k * tile_cols : (k + 1) * tile_cols],
                edges[r : r + 1], edges[edge + r : edge + r + 1],
            )

    span = 3 * out_width

    def convolve(begin, count):
        total = 0.0
        for a in range(3):
            total = total + jnp.dot(
                cat_ref[(begin + 2 - a) * tile_cols : (begin + 2 - a + count) * tile_cols, :],
                turned_ref[a * span : (a + 1) * span, :],
                preferred_element_type=f32,
            )
        out_ref[begin * tile_cols : (begin + count) * tile_cols, :] = total.astype(bf16)

    last = len(lines) - 1
    middle = last // 2
    half_rows = middle * step
    upstream(0)
    for c in range(last):
        upstream(c + 1)
        fill(c)
        if c == middle:
            convolve(0, half_rows)
    fill(last)
    convolve(half_rows, tile_rows - half_rows)


def on_device(canvas, conv_weight, conv_bias, target_gram):
    tile_rows, tile_cols, in_width = canvas.shape
    out_width = conv_weight.shape[3]
    pixel_total = tile_rows * tile_cols * lax.axis_size("rows") * lax.axis_size("cols")
    shape = (tile_rows, tile_cols, in_width, out_width, 2)
    kernel = conv_weight.reshape(9 * in_width, out_width)
    params = pltpu.CompilerParams(vmem_limit_bytes=24 * 1024 * 1024)
    vmem = pl.BlockSpec(memory_space=pltpu.VMEM)
    packed_shape = jax.ShapeDtypeStruct((len(tile_pairs(out_width)) * tile, tile), f32)

    rim_shape = jax.ShapeDtypeStruct((2, tile_rows, in_width), bf16)
    two = lax.axis_size("cols") == 2
    rims = local(
        rim_kernel,
        (rim_shape,) * (1 if two else 2),
        "column_rims",
        canvas,
        cost_estimate=pl.CostEstimate(flops=4_000_000_000, bytes_accessed=600_000, transcendentals=0),
    )
    if two:
        beyond = [lax.ppermute(rims[0], "cols", [(0, 1), (1, 0)])]
    else:
        beyond = shift_cols(rims[1], rims[0])
    payload_shape = jax.ShapeDtypeStruct((2 * tile_cols + edge, in_width), bf16)
    half_shape = jax.ShapeDtypeStruct((1, *target_gram.shape), bf16)
    even, odd, left, right, rows = local(
        payload_kernel,
        (payload_shape, payload_shape, rim_shape, rim_shape, half_shape),
        "row_payload",
        canvas,
        target_gram,
        *beyond,
    )
    count = lax.axis_size("rows")
    even, odd = swap_rows(range(0, count, 2), even), swap_rows(range(1, count, 2), odd)

    bits = (lax.axis_size("rows") * lax.axis_size("cols")).bit_length() - 1
    gather = Gather(rows)
    far = list(reversed(range(3, bits)))
    inner = (tile_rows - 2) * tile_cols
    in_feat, in_slope, in_gram, bias, part = pl.pallas_call(
        functools.partial(inner_kernel, shape),
        out_shape=(
            jax.ShapeDtypeStruct((inner, out_width), bf16),
            jax.ShapeDtypeStruct((inner, out_width), bf16),
            packed_shape,
            jax.ShapeDtypeStruct((1, out_width), f32),
            jax.ShapeDtypeStruct((4 * tile_cols, out_width), f32),
        ),
        in_specs=[vmem] * 5,
        scratch_shapes=[pltpu.VMEM((tile_rows * tile_cols, 3 * in_width), bf16)],
        compiler_params=params,
        name="inner_rows",
        cost_estimate=pl.CostEstimate(
            flops=2 * inner * (9 * in_width + out_width) * out_width,
            bytes_accessed=6_000_000,
            transcendentals=inner * out_width,
        ),
    )(canvas, left, right, kernel, conv_bias)

    half_gram = (packed_shape.shape[0] // 2, tile)
    halo_scratch = [pltpu.VMEM(payload_shape.shape, bf16), pltpu.VMEM(payload_shape.shape, bf16)]
    out_feat, out_slope, send, keep = pl.pallas_call(
        functools.partial(outer_kernel, shape),
        out_shape=(
            jax.ShapeDtypeStruct((2 * tile_cols, out_width), bf16),
            jax.ShapeDtypeStruct((2 * tile_cols, out_width), bf16),
            jax.ShapeDtypeStruct(half_gram, bf16),
            jax.ShapeDtypeStruct(half_gram, f32),
        ),
        in_specs=[vmem] * 5,
        scratch_shapes=[
            *halo_scratch,
            pltpu.VMEM((2 * tile_cols, 3 * in_width), bf16),
            pltpu.VMEM(packed_shape.shape, f32),
        ],
        compiler_params=params,
        name="outer_rows",
    )(even, odd, kernel, in_gram, part)

    exchanges = {
        "cores": [(bit,) for bit in far[:1]],
        "halve 0": [(bit,) for bit in far[1:]],
        "halve 1": [(1, 2)],
        "add 0": [(2, 1)],
        "add 1": [(0,)],
    }
    prepared, far_pixels = [], []

    def beside(name, sent, got):
        if name == "join 1":
            outer = 2 * tile_cols + 2 * edge
            rim_sums, _ = lax.optimization_barrier((part, sent))
            far_pixels.extend(
                pl.pallas_call(
                    functools.partial(beyond_kernel, shape),
                    out_shape=(jax.ShapeDtypeStruct((outer, out_width), bf16),) * 2,
                    in_specs=[vmem] * 8,
                    scratch_shapes=[
                        *halo_scratch,
                        pltpu.VMEM((4 * tile_cols, 3 * in_width), bf16),
                        pltpu.VMEM((2 * edge, 9 * in_width), bf16),
                    ],
                    compiler_params=params,
                    name="beyond",
                    cost_estimate=chained,
                )(canvas, even, odd, left, right, kernel, bias, rim_sums)
            )
            return lax.optimization_barrier((got, *far_pixels))[0]
        for bit in exchanges.get(name, []):
            gather.step(sent, *bit)
        if name != "join 0":
            return got
        gather.settle(sent)
        prepared.extend(
            pl.pallas_call(
                prepare_kernel,
                out_shape=(
                    jax.ShapeDtypeStruct((9 * out_width, in_width), bf16),
                    jax.ShapeDtypeStruct((out_width, out_width), f32),
                ),
                in_specs=[vmem] * 2,
                compiler_params=params,
                name="prepare",
                cost_estimate=pl.CostEstimate(
                    flops=2_000_000_000, bytes_accessed=6_000_000, transcendentals=0
                ),
            )(kernel, gather.rows.reshape(out_width, out_width))
        )
        return lax.optimization_barrier((got, *prepared))[0]

    mine, other = sum_all(send, keep, beside)
    turned, both = prepared
    far_feat, far_slope = far_pixels
    own_gram, grad = pl.pallas_call(
        functools.partial(backward_kernel, shape, pixel_total),
        out_shape=(
            jax.ShapeDtypeStruct(target_gram.shape, f32),
            jax.ShapeDtypeStruct((tile_rows * tile_cols, in_width), bf16),
        ),
        in_specs=[vmem] * 10,
        scratch_shapes=[
            pltpu.VMEM(packed_shape.shape, f32),
            pltpu.VMEM((out_width, out_width), f32),
            pltpu.VMEM((out_width, out_width), bf16),
            pltpu.VMEM(((tile_rows + 2) * tile_cols, 3 * out_width), bf16),
        ],
        compiler_params=params,
        name="grad_conv",
    )(mine, other, both, in_feat, in_slope, out_feat, out_slope, far_feat, far_slope, turned)
    return own_gram, grad.reshape(tile_rows, tile_cols, in_width)


def solution(mesh):
    return jax.shard_map(
        on_device,
        mesh=mesh,
        in_specs=(P("rows", "cols", None), P(), P(), P(("rows", "cols"), None)),
        out_specs=(P(("rows", "cols"), None), P("rows", "cols", None)),
        check_vma=False,
    )
```

```python
import functools
import math

import jax
import jax.numpy as jnp
from jax import lax
from jax.experimental import pallas as pl
from jax.experimental.pallas import tpu as pltpu
from jax.sharding import PartitionSpec as P

gelu_scale = math.sqrt(2.0 / math.pi)
tile = 128
edge = 16
f32, bf16 = jnp.float32, jnp.bfloat16


def tile_pairs(width):
    count = width // tile
    return [(i, j) for i in range(count) for j in range(i, count)]


def swap_rows(low, value):
    count = lax.axis_size("rows")
    pairs = [(i, (i + 1) % count) for i in low]
    return lax.ppermute(value, "rows", pairs + [(target, source) for source, target in pairs])


def shift_cols(last, first):
    count = lax.axis_size("cols")
    forward = [(i, i + 1) for i in range(count - 1)]
    backward = [(target, source) for source, target in forward]
    return lax.ppermute(last, "cols", forward), lax.ppermute(first, "cols", backward)


def device_index():
    return lax.axis_index("rows") * lax.axis_size("cols") + lax.axis_index("cols")


def swap(value, bit, other=None):
    total = lax.axis_size("rows") * lax.axis_size("cols")
    flip = lambda i: 1 << (other if other is not None and i.bit_count() % 2 else bit) | 1
    return lax.ppermute(value, ("rows", "cols"), [(i, i ^ flip(i)) for i in range(total)])


def local(body, out_shape, name, *operands, **kwargs):
    return pl.pallas_call(
        body,
        out_shape=out_shape,
        in_specs=[pl.BlockSpec(memory_space=pltpu.VMEM)] * len(operands),
        compiler_params=pltpu.CompilerParams(vmem_limit_bytes=8 * 1024 * 1024),
        name=name,
        **kwargs,
    )(*operands)


def side_of(bit, other=None):
    index = device_index()
    if bit > 0:
        side = lax.rem(index // (1 << bit), 2)
        if other is None:
            return side
        return jnp.where(side_of(0) == 0, side, lax.rem(index // (1 << other), 2))
    bits = (lax.axis_size("rows") * lax.axis_size("cols")).bit_length() - 1
    return lax.rem(sum(lax.rem(index // (1 << k), 2) for k in range(bits)), 2)


def rows_at(index, count):
    return pl.ds(pl.multiple_of(index * count, count), count)


waiting = pl.CostEstimate(flops=1_500_000_000, bytes_accessed=100_000, transcendentals=0)
chained = pl.CostEstimate(flops=8_000_000_000, bytes_accessed=100_000, transcendentals=0)


def halve(keep, got, bit, other=None):
    half = keep.shape[0] // 2

    def body(keep_ref, got_ref, send_ref, stay_ref):
        side = side_of(bit, other)
        away, here = rows_at(1 - side, half), rows_at(side, half)
        send_ref[...] = (keep_ref[away, :] + got_ref[away, :].astype(f32)).astype(bf16)
        stay_ref[...] = keep_ref[here, :] + got_ref[here, :].astype(f32)

    shape = (half, keep.shape[1])
    return local(
        body,
        (jax.ShapeDtypeStruct(shape, bf16), jax.ShapeDtypeStruct(shape, f32)),
        "halve",
        keep,
        got,
        cost_estimate=chained,
    )


def add(keep, got):
    def body(keep_ref, got_ref, sum_ref):
        sum_ref[...] = (keep_ref[...].astype(f32) + got_ref[...].astype(f32)).astype(bf16)

    return local(body, jax.ShapeDtypeStruct(got.shape, bf16), "add", keep, got, cost_estimate=chained)


def join(mine, got, bit, other=None, **kwargs):
    def body(mine_ref, got_ref, both_ref):
        side = side_of(bit, other)
        both_ref[:, pl.ds(side, 1)] = mine_ref[...][:, None]
        both_ref[:, pl.ds(1 - side, 1)] = got_ref[...][:, None]

    shape = (mine.shape[0], 2, *mine.shape[1:])
    return local(body, jax.ShapeDtypeStruct(shape, mine.dtype), "join", mine, got, **kwargs)


def join_second(mine, got, bit, other, **kwargs):
    def body(mine_ref, got_ref, both_ref):
        parity, side = side_of(0), side_of(bit, other)

        @pl.when(parity == 0)
        def _():
            both_ref[:, pl.ds(side, 1)] = mine_ref[...][:, None]
            both_ref[:, pl.ds(1 - side, 1)] = got_ref[...][:, None]

        @pl.when(parity == 1)
        def _():
            both_ref[:, :, pl.ds(side, 1)] = mine_ref[...][:, :, None]
            both_ref[:, :, pl.ds(1 - side, 1)] = got_ref[...][:, :, None]

    shape = (mine.shape[0], 2, *mine.shape[1:])
    return local(body, jax.ShapeDtypeStruct(shape, mine.dtype), "join_second", mine, got, **kwargs)


def join_cores(mine, other, **kwargs):
    def body(mine_ref, other_ref, both_ref):
        side = side_of(0)
        for chip in range(mine.shape[0]):
            core = lax.rem(side + chip.bit_count(), 2)
            both_ref[chip, pl.ds(core, 1)] = mine_ref[chip][None]
            both_ref[chip, pl.ds(1 - core, 1)] = other_ref[chip][None]

    shape = (mine.shape[0], 2, *mine.shape[1:])
    return local(body, jax.ShapeDtypeStruct(shape, mine.dtype), "join_cores", mine, other, **kwargs)


class Gather:
    def __init__(self, rows):
        self.rows, self.got, self.last = rows, None, None

    def settle(self, after):
        if self.got is None:
            self.rows, _ = lax.optimization_barrier((self.rows, after))
            return
        share = self.rows.shape[-2:]
        got, _ = lax.optimization_barrier((self.got, after))
        bit, other = self.last
        if bit == 0:
            both = join_cores(self.rows, got, cost_estimate=waiting)
        elif other is None or bit < other:
            mine, got = (part.reshape(-1, 1, *share) for part in (self.rows, got))
            both = join(mine, got, bit, other, cost_estimate=waiting)
        else:
            mine, got = (part.reshape(-1, 2, *share) for part in (self.rows, got))
            both = join_second(mine, got, bit, other, cost_estimate=waiting)
        self.rows, self.got = both.reshape(-1, *share), None

    def step(self, after, bit, other=None):
        self.settle(after)
        self.got, self.last = swap(self.rows, bit, other), (bit, other)


def sum_all(send, keep, beside):
    bits = (lax.axis_size("rows") * lax.axis_size("cols")).bit_length() - 1
    halving = [(1, 2), (2, 1)]
    adding = []
    for bit in range(3, bits, 2):
        adding += [(bit, bit + 1), (bit + 1, bit)] if bit + 1 < bits else [(bit, None)]

    got = beside("cores", send, swap(send, 0))
    for n, pair in enumerate(halving):
        send, keep = halve(keep, got, *pair)
        got = beside(f"halve {n}", send, swap(send, *pair))
    mine = add(keep, got)
    for n, pair in enumerate(adding):
        mine = add(mine, beside(f"add {n}", mine, swap(mine, *pair)))
    for n, pair in enumerate(reversed(halving)):
        got = beside(f"join {n}", mine, swap(mine, *pair))
        mine = join(mine[None], got[None], *pair, cost_estimate=chained).reshape(-1, mine.shape[1])
    return mine, beside("halves", mine, swap(mine, 0))


def gelu_pair(value):
    square = value * value
    tangent = jnp.tanh(value * (gelu_scale + gelu_scale * 0.044715 * square))
    half = 0.5 * value
    plus = 0.5 + 0.5 * tangent
    grad = plus + half * (1.0 - tangent * tangent) * (
        gelu_scale + gelu_scale * 3.0 * 0.044715 * square
    )
    return value * plus, grad


def column(value, c):
    return jnp.concatenate([value[r, c : c + 1] for r in range(value.shape[0])], axis=0)


def rim_kernel(canvas_ref, *out_refs):
    cols = canvas_ref.shape[1]
    begin = canvas_ref[:, 0:16, :].astype(f32)
    end = canvas_ref[:, cols - 16 :, :].astype(f32)
    for c in range(2):
        pair = column(begin, c), column(end, 14 + c)
        if len(out_refs) == 1:
            out_refs[0][c] = jnp.where(lax.axis_index("cols") == 0, pair[1], pair[0]).astype(bf16)
        else:
            out_refs[0][c], out_refs[1][c] = pair[0].astype(bf16), pair[1].astype(bf16)


def payload_kernel(canvas_ref, target_ref, *refs):
    payload_refs, (left_ref, right_ref, half_ref) = refs[-7:-3], refs[-3:]
    rows, cols, width = canvas_ref.shape
    half_ref[0] = target_ref[...].astype(bf16)
    if len(refs) == 8:
        here = lax.axis_index("cols")
        other = refs[0][...].astype(f32)
        left_ref[...] = jnp.where(here == 0, 0.0, other).astype(bf16)
        right_ref[...] = jnp.where(here == 0, other, 0.0).astype(bf16)
    else:
        left_ref[...], right_ref[...] = refs[0][...], refs[1][...]
    beyond = [ref[c].astype(f32) for ref in (left_ref, right_ref) for c in range(2)]

    def fill(ref, r):
        ref[0:cols, :] = canvas_ref[r]
        rim = jnp.concatenate([*(part[r : r + 1] for part in beyond), jnp.zeros((12, width), f32)], axis=0)
        ref[cols:, :] = rim.astype(bf16)

    odd = lax.rem(lax.axis_index("rows"), 2)
    for case, order in ((0, [rows - 1, 0, rows - 2, 1]), (1, [0, rows - 1, 1, rows - 2])):

        @pl.when(odd == case)
        def _():
            for ref, r in zip(payload_refs, order):
                fill(ref, r)


def moved_rows(row, before, after):
    cols = row.shape[0]
    wide = row.astype(f32)
    place = lax.broadcasted_iota(jnp.int32, (8, row.shape[1]), 0)
    right, left = pltpu.roll(wide, 1, 0), pltpu.roll(wide, cols - 1, 0)
    right = jnp.concatenate([jnp.where(place == 0, before, right[:8]), right[8:]], axis=0)
    left = jnp.concatenate([left[:-8], jnp.where(place == 7, after, left[-8:])], axis=0)
    return right.astype(bf16), row.astype(bf16), left.astype(bf16)


def fill_row(cat_ref, r, row, before, after):
    cols, width = row.shape
    for b, part in enumerate(moved_rows(row, before, after)):
        cat_ref[r * cols : (r + 1) * cols, b * width : (b + 1) * width] = part


def gram_tiles(feat, gram_ref, base_ref=None):
    width = feat.shape[1]
    half = width // 2
    product = functools.partial(
        lax.dot_general,
        dimension_numbers=(((0,), (0,)), ((), ())),
        preferred_element_type=f32,
    )
    upper = product(feat[:, :half], feat)
    lower = product(feat[:, half:], feat[:, half:])
    for n, (i, j) in enumerate(tile_pairs(width)):
        at = slice(n * tile, (n + 1) * tile)
        if i * tile < half:
            part = upper[i * tile : (i + 1) * tile, j * tile : (j + 1) * tile]
        else:
            k, m = i * tile - half, j * tile - half
            part = lower[k : k + tile, m : m + tile]
        gram_ref[at, :] = part if base_ref is None else part + base_ref[at, :]


def inner_kernel(
    shape, own_ref, left_ref, right_ref, kernel_ref, bias_ref,
    feat_ref, slope_ref, gram_ref, row_ref, part_ref, cat_ref,
):
    row_ref[...] = bias_ref[...].astype(f32).reshape(row_ref.shape)
    tile_rows, tile_cols, in_width, out_width, step = shape
    lefts, rights = left_ref[1].astype(f32), right_ref[0].astype(f32)
    for r in range(tile_rows):
        fill_row(cat_ref, r, own_ref[r], lefts[r : r + 1], rights[r : r + 1])
    bias = row_ref[...]
    root = 1.0 / math.sqrt(out_width)
    span = 3 * in_width

    def product(begin, count, a):
        return jnp.dot(
            cat_ref[begin * tile_cols : (begin + count) * tile_cols, :],
            kernel_ref[a * span : (a + 1) * span, :],
            preferred_element_type=f32,
        )

    for h in range(0, tile_rows - 2, step):
        total = bias
        for a in range(3):
            total = total + product(h + a, step, a)
        features, slope = gelu_pair(total)
        at = slice(h * tile_cols, (h + step) * tile_cols)
        feat_ref[at, :] = features.astype(bf16)
        slope_ref[at, :] = (slope * root).astype(bf16)
    low, high = product(0, 2, 2), product(tile_rows - 2, 2, 0)
    ends = product(0, 1, 1), product(tile_rows - 1, 1, 1)
    part_ref[0:tile_cols, :] = low[:tile_cols] + bias
    part_ref[tile_cols : 2 * tile_cols, :] = low[tile_cols:] + ends[0] + bias
    part_ref[2 * tile_cols : 3 * tile_cols, :] = high[:tile_cols] + ends[1] + bias
    part_ref[3 * tile_cols :, :] = high[tile_cols:] + bias
    gram_tiles(feat_ref[...], gram_ref)


def halo_rows(even_ref, odd_ref, low_ref, high_ref):
    row = lax.axis_index("rows")
    odd = lax.rem(row, 2)
    low_ref[...] = jnp.where(odd == 0, odd_ref[...], even_ref[...])
    high_ref[...] = jnp.where(odd == 0, even_ref[...], odd_ref[...])

    @pl.when(row == 0)
    def _():
        low_ref[...] = jnp.zeros_like(low_ref)

    @pl.when(row == lax.axis_size("rows") - 1)
    def _():
        high_ref[...] = jnp.zeros_like(high_ref)


def halves(width):
    return slice(0, width // 2), slice(width // 2, width)


def outer_kernel(
    shape, even_ref, odd_ref, kernel_ref, base_ref, part_ref,
    feat_ref, slope_ref, send_ref, keep_ref, low_ref, high_ref, cat_ref, gram_ref,
):
    tile_rows, tile_cols, in_width, out_width, step = shape
    span = 3 * in_width
    halo_rows(even_ref, odd_ref, low_ref, high_ref)
    for n, source in enumerate([low_ref, high_ref]):
        rim = source[tile_cols:, :].astype(f32)
        fill_row(cat_ref, n, source[0:tile_cols, :], rim[1:2], rim[2:3])
    root = 1.0 / math.sqrt(out_width)
    for at in halves(out_width):
        for n, a in enumerate([0, 2]):
            rows = slice(n * tile_cols, (n + 1) * tile_cols)
            features, slope = gelu_pair(
                part_ref[(n + 1) * tile_cols : (n + 2) * tile_cols, at]
                + jnp.dot(
                    cat_ref[rows, :],
                    kernel_ref[a * span : (a + 1) * span, at],
                    preferred_element_type=f32,
                )
            )
            feat_ref[rows, at] = features.astype(bf16)
            slope_ref[rows, at] = (slope * root).astype(bf16)
    gram_tiles(feat_ref[...], gram_ref, base_ref)
    half = send_ref.shape[0]
    side = side_of(0)
    send_ref[...] = gram_ref[rows_at(1 - side, half), :].astype(bf16)
    keep_ref[...] = gram_ref[rows_at(side, half), :]


def beyond_kernel(
    shape, own_ref, even_ref, odd_ref, far_even_ref, far_odd_ref, left_ref, right_ref, kernel_ref, bias_ref,
    part_ref, feat_ref, slope_ref, low_ref, high_ref, far_low_ref, far_high_ref, cat_ref, edge_ref,
):
    tile_rows, tile_cols, in_width, out_width, step = shape
    halo_rows(even_ref, odd_ref, low_ref, high_ref)
    halo_rows(far_even_ref, far_odd_ref, far_low_ref, far_high_ref)
    first = (lax.axis_index("rows") > 0).astype(f32)
    last = (lax.axis_index("rows") < lax.axis_size("rows") - 1).astype(f32)
    left = (lax.axis_index("cols") > 0).astype(f32)
    right = (lax.axis_index("cols") < lax.axis_size("cols") - 1).astype(f32)
    around = [far_low_ref, low_ref, high_ref, far_high_ref]
    rims = [ref[tile_cols:, :].astype(f32) for ref in around]
    own_begin = column(own_ref[:, 0:16, :].astype(f32), 0)
    own_end = column(own_ref[:, tile_cols - 16 :, :].astype(f32), 15)

    def sides(c, own):
        parts = [rim[c : c + 1] for rim in rims]
        return jnp.concatenate([*parts[:2], own, *parts[2:]], axis=0)

    def ends(c, own):
        c16 = c // 16 * 16
        parts = [ref[c16 : c16 + 16, :].astype(f32)[c - c16 : c - c16 + 1] for ref in around]
        return jnp.concatenate([*parts[:2], own, *parts[2:]], axis=0)

    lefts = [
        sides(0, left_ref[0].astype(f32)), sides(1, left_ref[1].astype(f32)), ends(0, own_begin)
    ]
    rights = [
        ends(tile_cols - 1, own_end), sides(2, right_ref[0].astype(f32)), sides(3, right_ref[1].astype(f32))
    ]
    span = 3 * in_width
    for r, (source, line) in enumerate(zip(around, [0, 1, tile_rows + 2, tile_rows + 3])):
        row = source[0:tile_cols, :]
        fill_row(cat_ref, r, row, lefts[1][line : line + 1], rights[1][line : line + 1])
    blank = jnp.zeros((edge - tile_rows - 2, in_width), f32)
    for a in range(3):
        for b in range(3):
            piece = jnp.concatenate(
                [lefts[b][a : a + tile_rows + 2], blank, rights[b][a : a + tile_rows + 2], blank],
                axis=0,
            )
            at = (3 * a + b) * in_width
            edge_ref[:, at : at + in_width] = piece.astype(bf16)
    root = 1.0 / math.sqrt(out_width)
    line = lax.broadcasted_iota(jnp.int32, (2 * edge, out_width // 2), 0)
    weight = jnp.where(line < edge, left, right)
    weight = jnp.where(line % edge == 0, weight * first, weight)
    weight = jnp.where(line % edge == tile_rows + 1, weight * last, weight)
    for at in halves(out_width):

        def product(begin, a):
            return jnp.dot(
                cat_ref[begin * tile_cols : (begin + 1) * tile_cols, :],
                kernel_ref[a * span : (a + 1) * span, at],
                preferred_element_type=f32,
            )

        totals = [
            part_ref[0:tile_cols, at] + product(0, 0) + product(1, 1),
            part_ref[3 * tile_cols :, at] + product(2, 1) + product(3, 2),
            bias_ref[:, at] + jnp.dot(edge_ref[...], kernel_ref[:, at], preferred_element_type=f32),
        ]
        scales = [first * root, last * root, weight * root]
        for n, (total, scale) in enumerate(zip(totals, scales)):
            features, slope = gelu_pair(total)
            rows = slice(n * tile_cols, n * tile_cols + total.shape[0])
            feat_ref[rows, at] = features.astype(bf16)
            slope_ref[rows, at] = (slope * scale).astype(bf16)


def prepare_kernel(kernel_ref, target_ref, turned_ref, both_ref):
    taps, in_width, out_width = 9, kernel_ref.shape[0] // 9, kernel_ref.shape[1]
    for n in range(taps):
        to = (n // 3 * 3 + 2 - n % 3) * out_width
        turned_ref[to : to + out_width, :] = kernel_ref[n * in_width : (n + 1) * in_width, :].T
    for i, j in tile_pairs(out_width):
        at_i, at_j = slice(i * tile, (i + 1) * tile), slice(j * tile, (j + 1) * tile)
        both = target_ref[at_i, at_j].astype(f32) + target_ref[at_j, at_i].astype(f32).T
        both_ref[at_i, at_j] = both
        if i != j:
            both_ref[at_j, at_i] = both.T


def backward_kernel(
    shape, pixel_total, mine_ref, other_ref, both_ref, in_feat_ref, in_slope_ref, out_feat_ref, out_slope_ref,
    far_feat_ref, far_slope_ref, turned_ref, own_gram_ref, out_ref, gram_ref, full_ref, sym_ref, cat_ref,
):
    tile_rows, tile_cols, in_width, out_width, step = shape
    half = mine_ref.shape[0]
    side = side_of(0)
    gram_ref[rows_at(side, half), :] = mine_ref[...].astype(f32)
    gram_ref[rows_at(1 - side, half), :] = other_ref[...].astype(f32)
    for n, (i, j) in enumerate(tile_pairs(out_width)):
        at_i, at_j = slice(i * tile, (i + 1) * tile), slice(j * tile, (j + 1) * tile)
        gram = gram_ref[n * tile : (n + 1) * tile, :] * (1.0 / pixel_total)
        full_ref[at_i, at_j] = gram
        sym_ref[at_i, at_j] = (2.0 * gram - both_ref[at_i, at_j]).astype(bf16)
        if i != j:
            gram = gram.T
            full_ref[at_j, at_i] = gram
            sym_ref[at_j, at_i] = (2.0 * gram - both_ref[at_j, at_i]).astype(bf16)
    share = own_gram_ref.shape[0]
    start = device_index() * share
    if share % 8 == 0:
        own_gram_ref[...] = full_ref[pl.ds(pl.multiple_of(start, 8), share), :]
    else:
        group = full_ref[pl.ds(pl.multiple_of(start // 8 * 8, 8), 8), :]
        picked = group[0:share]
        for k in range(share, 8, share):
            picked = jnp.where(start % 8 == k, group[k : k + share], picked)
        own_gram_ref[...] = picked

    def grad_of(feat_ref, slope_ref, at):
        product = jnp.dot(feat_ref[at, :], sym_ref[...], preferred_element_type=f32)
        return product * slope_ref[at, :].astype(f32)

    main = 2 * tile_cols
    edges = grad_of(far_feat_ref, far_slope_ref, slice(main, None))
    near, far = (out_feat_ref, out_slope_ref), (far_feat_ref, far_slope_ref)
    lines = [[(*far, 0), (*near, 0)]]
    lines += [
        [(in_feat_ref, in_slope_ref, k * tile_cols) for k in range(h, h + step)]
        for h in range(0, tile_rows - 2, step)
    ]
    lines += [[(*near, tile_cols), (*far, tile_cols)]]
    grads = {}

    def upstream(c):
        pieces = lines[c]
        if pieces[0][0] is pieces[1][0]:
            feat_ref, slope_ref, begin = pieces[0]
            grads[c] = grad_of(feat_ref, slope_ref, slice(begin, begin + step * tile_cols))
        else:
            parts = [grad_of(feat, slope, slice(begin, begin + tile_cols)) for feat, slope, begin in pieces]
            grads[c] = jnp.concatenate(parts, axis=0)

    def fill(c):
        for k in range(step):
            r = c * step + k
            fill_row(
                cat_ref, r, grads[c][k * tile_cols : (k + 1) * tile_cols],
                edges[r : r + 1], edges[edge + r : edge + r + 1],
            )

    span = 3 * out_width

    def convolve(begin, count):
        total = 0.0
        for a in range(3):
            total = total + jnp.dot(
                cat_ref[(begin + 2 - a) * tile_cols : (begin + 2 - a + count) * tile_cols, :],
                turned_ref[a * span : (a + 1) * span, :],
                preferred_element_type=f32,
            )
        out_ref[begin * tile_cols : (begin + count) * tile_cols, :] = total.astype(bf16)

    last = len(lines) - 1
    middle = last // 2
    half_rows = middle * step
    upstream(0)
    for c in range(last):
        upstream(c + 1)
        fill(c)
        if c == middle:
            convolve(0, half_rows)
    fill(last)
    convolve(half_rows, tile_rows - half_rows)


def on_device(canvas, conv_weight, conv_bias, target_gram):
    tile_rows, tile_cols, in_width = canvas.shape
    out_width = conv_weight.shape[3]
    pixel_total = tile_rows * tile_cols * lax.axis_size("rows") * lax.axis_size("cols")
    shape = (tile_rows, tile_cols, in_width, out_width, 2)
    kernel = conv_weight.reshape(9 * in_width, out_width)
    params = pltpu.CompilerParams(vmem_limit_bytes=24 * 1024 * 1024)
    vmem = pl.BlockSpec(memory_space=pltpu.VMEM)
    packed_shape = jax.ShapeDtypeStruct((len(tile_pairs(out_width)) * tile, tile), f32)

    rim_shape = jax.ShapeDtypeStruct((2, tile_rows, in_width), bf16)
    two = lax.axis_size("cols") == 2
    rims = local(
        rim_kernel,
        (rim_shape,) * (1 if two else 2),
        "column_rims",
        canvas,
        cost_estimate=pl.CostEstimate(flops=4_000_000_000, bytes_accessed=600_000, transcendentals=0),
    )
    if two:
        beyond = [lax.ppermute(rims[0], "cols", [(0, 1), (1, 0)])]
    else:
        beyond = shift_cols(rims[1], rims[0])
    payload_shape = jax.ShapeDtypeStruct((tile_cols + edge, in_width), bf16)
    half_shape = jax.ShapeDtypeStruct((1, *target_gram.shape), bf16)
    even, odd, far_even, far_odd, left, right, rows = local(
        payload_kernel,
        (*(payload_shape,) * 4, rim_shape, rim_shape, half_shape),
        "row_payload",
        canvas,
        target_gram,
        *beyond,
    )
    count = lax.axis_size("rows")
    even, odd = swap_rows(range(0, count, 2), even), swap_rows(range(1, count, 2), odd)

    bits = (lax.axis_size("rows") * lax.axis_size("cols")).bit_length() - 1
    gather = Gather(rows)
    far = list(reversed(range(3, bits)))
    inner = (tile_rows - 2) * tile_cols
    in_feat, in_slope, in_gram, bias, part = pl.pallas_call(
        functools.partial(inner_kernel, shape),
        out_shape=(
            jax.ShapeDtypeStruct((inner, out_width), bf16),
            jax.ShapeDtypeStruct((inner, out_width), bf16),
            packed_shape,
            jax.ShapeDtypeStruct((1, out_width), f32),
            jax.ShapeDtypeStruct((4 * tile_cols, out_width), f32),
        ),
        in_specs=[vmem] * 5,
        scratch_shapes=[pltpu.VMEM((tile_rows * tile_cols, 3 * in_width), bf16)],
        compiler_params=params,
        name="inner_rows",
        cost_estimate=pl.CostEstimate(
            flops=2 * inner * (9 * in_width + out_width) * out_width,
            bytes_accessed=6_000_000,
            transcendentals=inner * out_width,
        ),
    )(canvas, left, right, kernel, conv_bias)

    half_gram = (packed_shape.shape[0] // 2, tile)
    halo_scratch = [pltpu.VMEM(payload_shape.shape, bf16), pltpu.VMEM(payload_shape.shape, bf16)]
    out_feat, out_slope, send, keep = pl.pallas_call(
        functools.partial(outer_kernel, shape),
        out_shape=(
            jax.ShapeDtypeStruct((2 * tile_cols, out_width), bf16),
            jax.ShapeDtypeStruct((2 * tile_cols, out_width), bf16),
            jax.ShapeDtypeStruct(half_gram, bf16),
            jax.ShapeDtypeStruct(half_gram, f32),
        ),
        in_specs=[vmem] * 5,
        scratch_shapes=[
            *halo_scratch,
            pltpu.VMEM((2 * tile_cols, 3 * in_width), bf16),
            pltpu.VMEM(packed_shape.shape, f32),
        ],
        compiler_params=params,
        name="outer_rows",
    )(even, odd, kernel, in_gram, part)

    exchanges = {
        "cores": [(bit,) for bit in far[:1]],
        "halve 0": [(bit,) for bit in far[1:]],
        "halve 1": [(1, 2)],
        "add 0": [(2, 1)],
        "add 1": [(0,)],
    }
    prepared, far_pixels, second_rows = [], [], []

    def beside(name, sent, got):
        for bits in exchanges.get(name, []):
            gather.step(sent, *bits)
        if name == "join 0":
            sends = lax.optimization_barrier((far_even, far_odd, sent))
            second_rows.extend(swap_rows(range(k, count, 2), sends[k]) for k in range(2))
            gather.settle(sent)
            got, gather.rows = lax.optimization_barrier((got, gather.rows))
        if name == "join 1":
            outer = 2 * tile_cols + 2 * edge
            rim_sums, _ = lax.optimization_barrier((part, sent))
            far_pixels.extend(
                pl.pallas_call(
                    functools.partial(beyond_kernel, shape),
                    out_shape=(jax.ShapeDtypeStruct((outer, out_width), bf16),) * 2,
                    in_specs=[vmem] * 10,
                    scratch_shapes=[
                        *halo_scratch,
                        *halo_scratch,
                        pltpu.VMEM((4 * tile_cols, 3 * in_width), bf16),
                        pltpu.VMEM((2 * edge, 9 * in_width), bf16),
                    ],
                    compiler_params=params,
                    name="beyond",
                    cost_estimate=chained,
                )(canvas, even, odd, *second_rows, left, right, kernel, bias, rim_sums)
            )
            return lax.optimization_barrier((got, *far_pixels))[0]
        if name != "halves":
            return got
        rows, _ = lax.optimization_barrier((gather.rows, sent))
        prepared.extend(
            pl.pallas_call(
                prepare_kernel,
                out_shape=(
                    jax.ShapeDtypeStruct((9 * out_width, in_width), bf16),
                    jax.ShapeDtypeStruct((out_width, out_width), f32),
                ),
                in_specs=[vmem] * 2,
                compiler_params=params,
                name="prepare",
                cost_estimate=pl.CostEstimate(
                    flops=2_000_000_000, bytes_accessed=6_000_000, transcendentals=0
                ),
            )(kernel, rows.reshape(out_width, out_width))
        )
        return lax.optimization_barrier((got, *prepared))[0]

    mine, other = sum_all(send, keep, beside)
    turned, both = prepared
    far_feat, far_slope = far_pixels
    own_gram, grad = pl.pallas_call(
        functools.partial(backward_kernel, shape, pixel_total),
        out_shape=(
            jax.ShapeDtypeStruct(target_gram.shape, f32),
            jax.ShapeDtypeStruct((tile_rows * tile_cols, in_width), bf16),
        ),
        in_specs=[vmem] * 10,
        scratch_shapes=[
            pltpu.VMEM(packed_shape.shape, f32),
            pltpu.VMEM((out_width, out_width), f32),
            pltpu.VMEM((out_width, out_width), bf16),
            pltpu.VMEM(((tile_rows + 2) * tile_cols, 3 * out_width), bf16),
        ],
        compiler_params=params,
        name="grad_conv",
    )(mine, other, both, in_feat, in_slope, out_feat, out_slope, far_feat, far_slope, turned)
    return own_gram, grad.reshape(tile_rows, tile_cols, in_width)


def solution(mesh):
    return jax.shard_map(
        on_device,
        mesh=mesh,
        in_specs=(P("rows", "cols", None), P(), P(), P(("rows", "cols"), None)),
        out_specs=(P(("rows", "cols"), None), P("rows", "cols", None)),
        check_vma=False,
    )
```

```python
import functools
import math

import jax
import jax.numpy as jnp
from jax import lax
from jax.experimental import pallas as pl
from jax.experimental.pallas import tpu as pltpu
from jax.sharding import PartitionSpec as P

gelu_scale = math.sqrt(2.0 / math.pi)
tile = 128
edge = 16
f32, bf16 = jnp.float32, jnp.bfloat16


def tile_pairs(width):
    count = width // tile
    return [(i, j) for i in range(count) for j in range(i, count)]


def swap_rows(low, value):
    count = lax.axis_size("rows")
    pairs = [(i, (i + 1) % count) for i in low]
    return lax.ppermute(value, "rows", pairs + [(target, source) for source, target in pairs])


def shift_cols(last, first):
    count = lax.axis_size("cols")
    forward = [(i, i + 1) for i in range(count - 1)]
    backward = [(target, source) for source, target in forward]
    return lax.ppermute(last, "cols", forward), lax.ppermute(first, "cols", backward)


def device_index():
    return lax.axis_index("rows") * lax.axis_size("cols") + lax.axis_index("cols")


def swap(value, bit, other=None):
    total = lax.axis_size("rows") * lax.axis_size("cols")
    flip = lambda i: 1 << (other if other is not None and i.bit_count() % 2 else bit) | 1
    return lax.ppermute(value, ("rows", "cols"), [(i, i ^ flip(i)) for i in range(total)])


def local(body, out_shape, name, *operands, **kwargs):
    return pl.pallas_call(
        body,
        out_shape=out_shape,
        in_specs=[pl.BlockSpec(memory_space=pltpu.VMEM)] * len(operands),
        compiler_params=pltpu.CompilerParams(vmem_limit_bytes=8 * 1024 * 1024),
        name=name,
        **kwargs,
    )(*operands)


def side_of(bit, other=None):
    index = device_index()
    if bit > 0:
        side = lax.rem(index // (1 << bit), 2)
        if other is None:
            return side
        return jnp.where(side_of(0) == 0, side, lax.rem(index // (1 << other), 2))
    bits = (lax.axis_size("rows") * lax.axis_size("cols")).bit_length() - 1
    return lax.rem(sum(lax.rem(index // (1 << k), 2) for k in range(bits)), 2)


def rows_at(index, count):
    return pl.ds(pl.multiple_of(index * count, count), count)


waiting = pl.CostEstimate(flops=1_500_000_000, bytes_accessed=100_000, transcendentals=0)
chained = pl.CostEstimate(flops=8_000_000_000, bytes_accessed=100_000, transcendentals=0)


def halve(keep, got, bit, other=None):
    half = keep.shape[0] // 2

    def body(keep_ref, got_ref, send_ref, stay_ref):
        side = side_of(bit, other)
        away, here = rows_at(1 - side, half), rows_at(side, half)
        send_ref[...] = (keep_ref[away, :] + got_ref[away, :].astype(f32)).astype(bf16)
        stay_ref[...] = keep_ref[here, :] + got_ref[here, :].astype(f32)

    shape = (half, keep.shape[1])
    return local(
        body,
        (jax.ShapeDtypeStruct(shape, bf16), jax.ShapeDtypeStruct(shape, f32)),
        "halve",
        keep,
        got,
        cost_estimate=chained,
    )


def add(keep, got):
    def body(keep_ref, got_ref, sum_ref):
        sum_ref[...] = (keep_ref[...].astype(f32) + got_ref[...].astype(f32)).astype(bf16)

    return local(body, jax.ShapeDtypeStruct(got.shape, bf16), "add", keep, got, cost_estimate=chained)


def join(mine, got, bit, other=None, **kwargs):
    def body(mine_ref, got_ref, both_ref):
        side = side_of(bit, other)
        both_ref[:, pl.ds(side, 1)] = mine_ref[...][:, None]
        both_ref[:, pl.ds(1 - side, 1)] = got_ref[...][:, None]

    shape = (mine.shape[0], 2, *mine.shape[1:])
    return local(body, jax.ShapeDtypeStruct(shape, mine.dtype), "join", mine, got, **kwargs)


def join_second(mine, got, bit, other, **kwargs):
    def body(mine_ref, got_ref, both_ref):
        parity, side = side_of(0), side_of(bit, other)

        @pl.when(parity == 0)
        def _():
            both_ref[:, pl.ds(side, 1)] = mine_ref[...][:, None]
            both_ref[:, pl.ds(1 - side, 1)] = got_ref[...][:, None]

        @pl.when(parity == 1)
        def _():
            both_ref[:, :, pl.ds(side, 1)] = mine_ref[...][:, :, None]
            both_ref[:, :, pl.ds(1 - side, 1)] = got_ref[...][:, :, None]

    shape = (mine.shape[0], 2, *mine.shape[1:])
    return local(body, jax.ShapeDtypeStruct(shape, mine.dtype), "join_second", mine, got, **kwargs)


def join_cores(mine, other, **kwargs):
    def body(mine_ref, other_ref, both_ref):
        side = side_of(0)
        for chip in range(mine.shape[0]):
            core = lax.rem(side + chip.bit_count(), 2)
            both_ref[chip, pl.ds(core, 1)] = mine_ref[chip][None]
            both_ref[chip, pl.ds(1 - core, 1)] = other_ref[chip][None]

    shape = (mine.shape[0], 2, *mine.shape[1:])
    return local(body, jax.ShapeDtypeStruct(shape, mine.dtype), "join_cores", mine, other, **kwargs)


class Gather:
    def __init__(self, rows):
        self.rows, self.got, self.last = rows, None, None

    def settle(self, after):
        if self.got is None:
            self.rows, _ = lax.optimization_barrier((self.rows, after))
            return
        share = self.rows.shape[-2:]
        got, _ = lax.optimization_barrier((self.got, after))
        bit, other = self.last
        if bit == 0:
            both = join_cores(self.rows, got, cost_estimate=waiting)
        elif other is None or bit < other:
            mine, got = (part.reshape(-1, 1, *share) for part in (self.rows, got))
            both = join(mine, got, bit, other, cost_estimate=waiting)
        else:
            mine, got = (part.reshape(-1, 2, *share) for part in (self.rows, got))
            both = join_second(mine, got, bit, other, cost_estimate=waiting)
        self.rows, self.got = both.reshape(-1, *share), None

    def step(self, after, bit, other=None):
        self.settle(after)
        self.got, self.last = swap(self.rows, bit, other), (bit, other)


def sum_all(send, keep, beside):
    bits = (lax.axis_size("rows") * lax.axis_size("cols")).bit_length() - 1
    halving = [(1, 2), (2, 1)]
    adding = []
    for bit in range(3, bits, 2):
        adding += [(bit, bit + 1), (bit + 1, bit)] if bit + 1 < bits else [(bit, None)]

    got = beside("cores", send, swap(send, 0))
    for n, pair in enumerate(halving):
        send, keep = halve(keep, got, *pair)
        got = beside(f"halve {n}", send, swap(send, *pair))
    mine = add(keep, got)
    for n, pair in enumerate(adding):
        mine = add(mine, beside(f"add {n}", mine, swap(mine, *pair)))
    for n, pair in enumerate(reversed(halving)):
        got = beside(f"join {n}", mine, swap(mine, *pair))
        mine = join(mine[None], got[None], *pair, cost_estimate=chained).reshape(-1, mine.shape[1])
    return mine, beside("halves", mine, swap(mine, 0))


def gelu_pair(value):
    square = value * value
    tangent = jnp.tanh(value * (gelu_scale + gelu_scale * 0.044715 * square))
    half = 0.5 * value
    plus = 0.5 + 0.5 * tangent
    grad = plus + half * (1.0 - tangent * tangent) * (
        gelu_scale + gelu_scale * 3.0 * 0.044715 * square
    )
    return value * plus, grad


def column(value, c):
    return jnp.concatenate([value[r, c : c + 1] for r in range(value.shape[0])], axis=0)


def rim_kernel(canvas_ref, *out_refs):
    cols = canvas_ref.shape[1]
    begin = canvas_ref[:, 0:16, :].astype(f32)
    end = canvas_ref[:, cols - 16 :, :].astype(f32)
    for c in range(2):
        pair = column(begin, c), column(end, 14 + c)
        if len(out_refs) == 1:
            out_refs[0][c] = jnp.where(lax.axis_index("cols") == 0, pair[1], pair[0]).astype(bf16)
        else:
            out_refs[0][c], out_refs[1][c] = pair[0].astype(bf16), pair[1].astype(bf16)


def payload_kernel(canvas_ref, target_ref, *refs):
    even_ref, odd_ref, left_ref, right_ref, half_ref = refs[-5:]
    rows, cols, width = canvas_ref.shape
    half_ref[0] = target_ref[...].astype(bf16)
    if len(refs) == 6:
        here = lax.axis_index("cols")
        other = refs[0][...].astype(f32)
        left_ref[...] = jnp.where(here == 0, 0.0, other).astype(bf16)
        right_ref[...] = jnp.where(here == 0, other, 0.0).astype(bf16)
    else:
        left_ref[...], right_ref[...] = refs[0][...], refs[1][...]
    beyond = [ref[c].astype(f32) for ref in (left_ref, right_ref) for c in range(2)]

    def fill(ref, r):
        for k in range(2):
            ref[k * cols : (k + 1) * cols, :] = canvas_ref[r + k]
        rim = [part[r + k : r + k + 1] for k in range(2) for part in beyond]
        rim = jnp.concatenate([*rim, jnp.zeros((8, width), f32)], axis=0)
        ref[2 * cols :, :] = rim.astype(bf16)

    odd = lax.rem(lax.axis_index("rows"), 2)

    @pl.when(odd == 0)
    def _():
        fill(even_ref, rows - 2)
        fill(odd_ref, 0)

    @pl.when(odd == 1)
    def _():
        fill(even_ref, 0)
        fill(odd_ref, rows - 2)


def moved_rows(row, before, after):
    cols = row.shape[0]
    wide = row.astype(f32)
    place = lax.broadcasted_iota(jnp.int32, (8, row.shape[1]), 0)
    right, left = pltpu.roll(wide, 1, 0), pltpu.roll(wide, cols - 1, 0)
    right = jnp.concatenate([jnp.where(place == 0, before, right[:8]), right[8:]], axis=0)
    left = jnp.concatenate([left[:-8], jnp.where(place == 7, after, left[-8:])], axis=0)
    return right.astype(bf16), row.astype(bf16), left.astype(bf16)


def fill_row(cat_ref, r, row, before, after):
    cols, width = row.shape
    for b, part in enumerate(moved_rows(row, before, after)):
        cat_ref[r * cols : (r + 1) * cols, b * width : (b + 1) * width] = part


def gram_tiles(feat, gram_ref, base_ref=None):
    width = feat.shape[1]
    half = width // 2
    product = functools.partial(
        lax.dot_general,
        dimension_numbers=(((0,), (0,)), ((), ())),
        preferred_element_type=f32,
    )
    upper = product(feat[:, :half], feat)
    lower = product(feat[:, half:], feat[:, half:])
    for n, (i, j) in enumerate(tile_pairs(width)):
        at = slice(n * tile, (n + 1) * tile)
        if i * tile < half:
            part = upper[i * tile : (i + 1) * tile, j * tile : (j + 1) * tile]
        else:
            k, m = i * tile - half, j * tile - half
            part = lower[k : k + tile, m : m + tile]
        gram_ref[at, :] = part if base_ref is None else part + base_ref[at, :]


def inner_kernel(
    shape, own_ref, left_ref, right_ref, kernel_ref, bias_ref,
    feat_ref, slope_ref, gram_ref, row_ref, part_ref, cat_ref,
):
    row_ref[...] = bias_ref[...].astype(f32).reshape(row_ref.shape)
    tile_rows, tile_cols, in_width, out_width, step = shape
    lefts, rights = left_ref[1].astype(f32), right_ref[0].astype(f32)
    for r in range(tile_rows):
        fill_row(cat_ref, r, own_ref[r], lefts[r : r + 1], rights[r : r + 1])
    bias = row_ref[...]
    root = 1.0 / math.sqrt(out_width)
    span = 3 * in_width

    def product(begin, count, a):
        return jnp.dot(
            cat_ref[begin * tile_cols : (begin + count) * tile_cols, :],
            kernel_ref[a * span : (a + 1) * span, :],
            preferred_element_type=f32,
        )

    for h in range(0, tile_rows - 2, step):
        total = bias
        for a in range(3):
            total = total + product(h + a, step, a)
        features, slope = gelu_pair(total)
        at = slice(h * tile_cols, (h + step) * tile_cols)
        feat_ref[at, :] = features.astype(bf16)
        slope_ref[at, :] = (slope * root).astype(bf16)
    low, high = product(0, 2, 2), product(tile_rows - 2, 2, 0)
    ends = product(0, 1, 1), product(tile_rows - 1, 1, 1)
    part_ref[0:tile_cols, :] = low[:tile_cols] + bias
    part_ref[tile_cols : 2 * tile_cols, :] = low[tile_cols:] + ends[0] + bias
    part_ref[2 * tile_cols : 3 * tile_cols, :] = high[:tile_cols] + ends[1] + bias
    part_ref[3 * tile_cols :, :] = high[tile_cols:] + bias
    gram_tiles(feat_ref[...], gram_ref)


def halo_rows(even_ref, odd_ref, low_ref, high_ref):
    row = lax.axis_index("rows")
    odd = lax.rem(row, 2)
    low_ref[...] = jnp.where(odd == 0, odd_ref[...], even_ref[...])
    high_ref[...] = jnp.where(odd == 0, even_ref[...], odd_ref[...])

    @pl.when(row == 0)
    def _():
        low_ref[...] = jnp.zeros_like(low_ref)

    @pl.when(row == lax.axis_size("rows") - 1)
    def _():
        high_ref[...] = jnp.zeros_like(high_ref)


def halves(width):
    return slice(0, width // 2), slice(width // 2, width)


def outer_kernel(
    shape, even_ref, odd_ref, kernel_ref, base_ref, part_ref,
    feat_ref, slope_ref, send_ref, keep_ref, low_ref, high_ref, cat_ref, gram_ref,
):
    tile_rows, tile_cols, in_width, out_width, step = shape
    span, main = 3 * in_width, 2 * tile_cols
    halo_rows(even_ref, odd_ref, low_ref, high_ref)
    for n, (source, at) in enumerate([(low_ref, tile_cols), (high_ref, 0)]):
        rim = source[main:, :].astype(f32)
        k = 4 * (1 - n)
        fill_row(cat_ref, n, source[at : at + tile_cols, :], rim[k + 1 : k + 2], rim[k + 2 : k + 3])
    root = 1.0 / math.sqrt(out_width)
    for at in halves(out_width):
        for n, a in enumerate([0, 2]):
            rows = slice(n * tile_cols, (n + 1) * tile_cols)
            features, slope = gelu_pair(
                part_ref[(n + 1) * tile_cols : (n + 2) * tile_cols, at]
                + jnp.dot(
                    cat_ref[rows, :],
                    kernel_ref[a * span : (a + 1) * span, at],
                    preferred_element_type=f32,
                )
            )
            feat_ref[rows, at] = features.astype(bf16)
            slope_ref[rows, at] = (slope * root).astype(bf16)
    gram_tiles(feat_ref[...], gram_ref, base_ref)
    half = send_ref.shape[0]
    side = side_of(0)
    send_ref[...] = gram_ref[rows_at(1 - side, half), :].astype(bf16)
    keep_ref[...] = gram_ref[rows_at(side, half), :]


def beyond_kernel(
    shape, own_ref, even_ref, odd_ref, left_ref, right_ref, kernel_ref, bias_ref, part_ref,
    feat_ref, slope_ref, low_ref, high_ref, cat_ref, edge_ref,
):
    tile_rows, tile_cols, in_width, out_width, step = shape
    halo_rows(even_ref, odd_ref, low_ref, high_ref)
    first = (lax.axis_index("rows") > 0).astype(f32)
    last = (lax.axis_index("rows") < lax.axis_size("rows") - 1).astype(f32)
    left = (lax.axis_index("cols") > 0).astype(f32)
    right = (lax.axis_index("cols") < lax.axis_size("cols") - 1).astype(f32)
    main = 2 * tile_cols
    low_rim, high_rim = low_ref[main:, :].astype(f32), high_ref[main:, :].astype(f32)
    own_begin = column(own_ref[:, 0:16, :].astype(f32), 0)
    own_end = column(own_ref[:, tile_cols - 16 :, :].astype(f32), 15)

    def sides(c, own):
        return jnp.concatenate(
            [low_rim[c : c + 1], low_rim[4 + c : 5 + c], own, high_rim[c : c + 1], high_rim[4 + c : 5 + c]],
            axis=0,
        )

    def ends(c, own):
        c16 = c // 16 * 16
        piece = lambda ref, k: ref[k + c16 : k + c16 + 16, :].astype(f32)[c - c16 : c - c16 + 1]
        rows = [piece(low_ref, 0), piece(low_ref, tile_cols), own]
        return jnp.concatenate([*rows, piece(high_ref, 0), piece(high_ref, tile_cols)], axis=0)

    lefts = [
        sides(0, left_ref[0].astype(f32)), sides(1, left_ref[1].astype(f32)), ends(0, own_begin)
    ]
    rights = [
        ends(tile_cols - 1, own_end), sides(2, right_ref[0].astype(f32)), sides(3, right_ref[1].astype(f32))
    ]
    span = 3 * in_width
    for r, line in enumerate([0, 1, tile_rows + 2, tile_rows + 3]):
        source = low_ref if r < 2 else high_ref
        row = source[r % 2 * tile_cols : (r % 2 + 1) * tile_cols, :]
        fill_row(cat_ref, r, row, lefts[1][line : line + 1], rights[1][line : line + 1])
    blank = jnp.zeros((edge - tile_rows - 2, in_width), f32)
    for a in range(3):
        for b in range(3):
            piece = jnp.concatenate(
                [lefts[b][a : a + tile_rows + 2], blank, rights[b][a : a + tile_rows + 2], blank],
                axis=0,
            )
            at = (3 * a + b) * in_width
            edge_ref[:, at : at + in_width] = piece.astype(bf16)
    root = 1.0 / math.sqrt(out_width)
    line = lax.broadcasted_iota(jnp.int32, (2 * edge, out_width // 2), 0)
    weight = jnp.where(line < edge, left, right)
    weight = jnp.where(line % edge == 0, weight * first, weight)
    weight = jnp.where(line % edge == tile_rows + 1, weight * last, weight)
    for at in halves(out_width):

        def product(begin, a):
            return jnp.dot(
                cat_ref[begin * tile_cols : (begin + 1) * tile_cols, :],
                kernel_ref[a * span : (a + 1) * span, at],
                preferred_element_type=f32,
            )

        totals = [
            part_ref[0:tile_cols, at] + product(0, 0) + product(1, 1),
            part_ref[3 * tile_cols :, at] + product(2, 1) + product(3, 2),
            bias_ref[:, at] + jnp.dot(edge_ref[...], kernel_ref[:, at], preferred_element_type=f32),
        ]
        scales = [first * root, last * root, weight * root]
        for n, (total, scale) in enumerate(zip(totals, scales)):
            features, slope = gelu_pair(total)
            rows = slice(n * tile_cols, n * tile_cols + total.shape[0])
            feat_ref[rows, at] = features.astype(bf16)
            slope_ref[rows, at] = (slope * scale).astype(bf16)


def prepare_kernel(kernel_ref, target_ref, turned_ref, both_ref):
    taps, in_width, out_width = 9, kernel_ref.shape[0] // 9, kernel_ref.shape[1]
    for n in range(taps):
        to = (n // 3 * 3 + 2 - n % 3) * out_width
        turned_ref[to : to + out_width, :] = kernel_ref[n * in_width : (n + 1) * in_width, :].T
    for i, j in tile_pairs(out_width):
        at_i, at_j = slice(i * tile, (i + 1) * tile), slice(j * tile, (j + 1) * tile)
        both = target_ref[at_i, at_j].astype(f32) + target_ref[at_j, at_i].astype(f32).T
        both_ref[at_i, at_j] = both
        if i != j:
            both_ref[at_j, at_i] = both.T


def backward_kernel(
    shape, pixel_total, mine_ref, other_ref, both_ref, in_feat_ref, in_slope_ref, out_feat_ref, out_slope_ref,
    far_feat_ref, far_slope_ref, turned_ref, own_gram_ref, out_ref, gram_ref, full_ref, sym_ref, cat_ref,
):
    tile_rows, tile_cols, in_width, out_width, step = shape
    half = mine_ref.shape[0]
    side = side_of(0)
    gram_ref[rows_at(side, half), :] = mine_ref[...].astype(f32)
    gram_ref[rows_at(1 - side, half), :] = other_ref[...].astype(f32)
    for n, (i, j) in enumerate(tile_pairs(out_width)):
        at_i, at_j = slice(i * tile, (i + 1) * tile), slice(j * tile, (j + 1) * tile)
        gram = gram_ref[n * tile : (n + 1) * tile, :] * (1.0 / pixel_total)
        full_ref[at_i, at_j] = gram
        sym_ref[at_i, at_j] = (2.0 * gram - both_ref[at_i, at_j]).astype(bf16)
        if i != j:
            gram = gram.T
            full_ref[at_j, at_i] = gram
            sym_ref[at_j, at_i] = (2.0 * gram - both_ref[at_j, at_i]).astype(bf16)
    share = own_gram_ref.shape[0]
    start = device_index() * share
    if share % 8 == 0:
        own_gram_ref[...] = full_ref[pl.ds(pl.multiple_of(start, 8), share), :]
    else:
        group = full_ref[pl.ds(pl.multiple_of(start // 8 * 8, 8), 8), :]
        picked = group[0:share]
        for k in range(share, 8, share):
            picked = jnp.where(start % 8 == k, group[k : k + share], picked)
        own_gram_ref[...] = picked

    def grad_of(feat_ref, slope_ref, at):
        product = jnp.dot(feat_ref[at, :], sym_ref[...], preferred_element_type=f32)
        return product * slope_ref[at, :].astype(f32)

    main = 2 * tile_cols
    edges = grad_of(far_feat_ref, far_slope_ref, slice(main, None))
    near, far = (out_feat_ref, out_slope_ref), (far_feat_ref, far_slope_ref)
    lines = [[(*far, 0), (*near, 0)]]
    lines += [
        [(in_feat_ref, in_slope_ref, k * tile_cols) for k in range(h, h + step)]
        for h in range(0, tile_rows - 2, step)
    ]
    lines += [[(*near, tile_cols), (*far, tile_cols)]]
    grads = {}

    def upstream(c):
        pieces = lines[c]
        if pieces[0][0] is pieces[1][0]:
            feat_ref, slope_ref, begin = pieces[0]
            grads[c] = grad_of(feat_ref, slope_ref, slice(begin, begin + step * tile_cols))
        else:
            parts = [grad_of(feat, slope, slice(begin, begin + tile_cols)) for feat, slope, begin in pieces]
            grads[c] = jnp.concatenate(parts, axis=0)

    def fill(c):
        for k in range(step):
            r = c * step + k
            fill_row(
                cat_ref, r, grads[c][k * tile_cols : (k + 1) * tile_cols],
                edges[r : r + 1], edges[edge + r : edge + r + 1],
            )

    span = 3 * out_width

    def convolve(begin, count):
        total = 0.0
        for a in range(3):
            total = total + jnp.dot(
                cat_ref[(begin + 2 - a) * tile_cols : (begin + 2 - a + count) * tile_cols, :],
                turned_ref[a * span : (a + 1) * span, :],
                preferred_element_type=f32,
            )
        out_ref[begin * tile_cols : (begin + count) * tile_cols, :] = total.astype(bf16)

    last = len(lines) - 1
    middle = last // 2
    half_rows = middle * step
    upstream(0)
    for c in range(last):
        upstream(c + 1)
        fill(c)
        if c == middle:
            convolve(0, half_rows)
    fill(last)
    convolve(half_rows, tile_rows - half_rows)


def on_device(canvas, conv_weight, conv_bias, target_gram):
    tile_rows, tile_cols, in_width = canvas.shape
    out_width = conv_weight.shape[3]
    pixel_total = tile_rows * tile_cols * lax.axis_size("rows") * lax.axis_size("cols")
    shape = (tile_rows, tile_cols, in_width, out_width, 2)
    kernel = conv_weight.reshape(9 * in_width, out_width)
    params = pltpu.CompilerParams(vmem_limit_bytes=24 * 1024 * 1024)
    vmem = pl.BlockSpec(memory_space=pltpu.VMEM)
    packed_shape = jax.ShapeDtypeStruct((len(tile_pairs(out_width)) * tile, tile), f32)

    rim_shape = jax.ShapeDtypeStruct((2, tile_rows, in_width), bf16)
    two = lax.axis_size("cols") == 2
    rims = local(
        rim_kernel,
        (rim_shape,) * (1 if two else 2),
        "column_rims",
        canvas,
        cost_estimate=pl.CostEstimate(flops=4_000_000_000, bytes_accessed=600_000, transcendentals=0),
    )
    if two:
        beyond = [lax.ppermute(rims[0], "cols", [(0, 1), (1, 0)])]
    else:
        beyond = shift_cols(rims[1], rims[0])
    payload_shape = jax.ShapeDtypeStruct((2 * tile_cols + edge, in_width), bf16)
    half_shape = jax.ShapeDtypeStruct((1, *target_gram.shape), bf16)
    even, odd, left, right, rows = local(
        payload_kernel,
        (payload_shape, payload_shape, rim_shape, rim_shape, half_shape),
        "row_payload",
        canvas,
        target_gram,
        *beyond,
    )
    count = lax.axis_size("rows")
    even, odd = swap_rows(range(0, count, 2), even), swap_rows(range(1, count, 2), odd)

    bits = (lax.axis_size("rows") * lax.axis_size("cols")).bit_length() - 1
    gather = Gather(rows)
    far = list(reversed(range(3, bits)))
    inner = (tile_rows - 2) * tile_cols
    in_feat, in_slope, in_gram, bias, part = pl.pallas_call(
        functools.partial(inner_kernel, shape),
        out_shape=(
            jax.ShapeDtypeStruct((inner, out_width), bf16),
            jax.ShapeDtypeStruct((inner, out_width), bf16),
            packed_shape,
            jax.ShapeDtypeStruct((1, out_width), f32),
            jax.ShapeDtypeStruct((4 * tile_cols, out_width), f32),
        ),
        in_specs=[vmem] * 5,
        scratch_shapes=[pltpu.VMEM((tile_rows * tile_cols, 3 * in_width), bf16)],
        compiler_params=params,
        name="inner_rows",
        cost_estimate=pl.CostEstimate(
            flops=2 * inner * (9 * in_width + out_width) * out_width,
            bytes_accessed=6_000_000,
            transcendentals=inner * out_width,
        ),
    )(canvas, left, right, kernel, conv_bias)

    half_gram = (packed_shape.shape[0] // 2, tile)
    halo_scratch = [pltpu.VMEM(payload_shape.shape, bf16), pltpu.VMEM(payload_shape.shape, bf16)]
    out_feat, out_slope, send, keep = pl.pallas_call(
        functools.partial(outer_kernel, shape),
        out_shape=(
            jax.ShapeDtypeStruct((2 * tile_cols, out_width), bf16),
            jax.ShapeDtypeStruct((2 * tile_cols, out_width), bf16),
            jax.ShapeDtypeStruct(half_gram, bf16),
            jax.ShapeDtypeStruct(half_gram, f32),
        ),
        in_specs=[vmem] * 5,
        scratch_shapes=[
            *halo_scratch,
            pltpu.VMEM((2 * tile_cols, 3 * in_width), bf16),
            pltpu.VMEM(packed_shape.shape, f32),
        ],
        compiler_params=params,
        name="outer_rows",
    )(even, odd, kernel, in_gram, part)

    exchanges = {
        "halve 0": [(bit,) for bit in far[:1]],
        "halve 1": [(bit,) for bit in far[1:]],
        "add 0": [(1, 2)],
        "add 1": [(2, 1)],
        "join 0": [(0,)],
    }
    prepared, far_pixels = [], []

    def beside(name, sent, got):
        if name == "join 1":
            outer = 2 * tile_cols + 2 * edge
            rim_sums, _ = lax.optimization_barrier((part, sent))
            far_pixels.extend(
                pl.pallas_call(
                    functools.partial(beyond_kernel, shape),
                    out_shape=(jax.ShapeDtypeStruct((outer, out_width), bf16),) * 2,
                    in_specs=[vmem] * 8,
                    scratch_shapes=[
                        *halo_scratch,
                        pltpu.VMEM((4 * tile_cols, 3 * in_width), bf16),
                        pltpu.VMEM((2 * edge, 9 * in_width), bf16),
                    ],
                    compiler_params=params,
                    name="beyond",
                    cost_estimate=chained,
                )(canvas, even, odd, left, right, kernel, bias, rim_sums)
            )
            gather.settle(sent)
            got, gather.rows, *_ = lax.optimization_barrier((got, gather.rows, *far_pixels))
            return got
        for bit in exchanges.get(name, []):
            gather.step(sent, *bit)
        if name == "join 0":
            got, gather.rows = lax.optimization_barrier((got, gather.rows))
        if name != "halves":
            return got
        gather.settle(sent)
        prepared.extend(
            pl.pallas_call(
                prepare_kernel,
                out_shape=(
                    jax.ShapeDtypeStruct((9 * out_width, in_width), bf16),
                    jax.ShapeDtypeStruct((out_width, out_width), f32),
                ),
                in_specs=[vmem] * 2,
                compiler_params=params,
                name="prepare",
                cost_estimate=pl.CostEstimate(
                    flops=2_000_000_000, bytes_accessed=6_000_000, transcendentals=0
                ),
            )(kernel, gather.rows.reshape(out_width, out_width))
        )
        return lax.optimization_barrier((got, *prepared))[0]

    mine, other = sum_all(send, keep, beside)
    turned, both = prepared
    far_feat, far_slope = far_pixels
    own_gram, grad = pl.pallas_call(
        functools.partial(backward_kernel, shape, pixel_total),
        out_shape=(
            jax.ShapeDtypeStruct(target_gram.shape, f32),
            jax.ShapeDtypeStruct((tile_rows * tile_cols, in_width), bf16),
        ),
        in_specs=[vmem] * 10,
        scratch_shapes=[
            pltpu.VMEM(packed_shape.shape, f32),
            pltpu.VMEM((out_width, out_width), f32),
            pltpu.VMEM((out_width, out_width), bf16),
            pltpu.VMEM(((tile_rows + 2) * tile_cols, 3 * out_width), bf16),
        ],
        compiler_params=params,
        name="grad_conv",
    )(mine, other, both, in_feat, in_slope, out_feat, out_slope, far_feat, far_slope, turned)
    return own_gram, grad.reshape(tile_rows, tile_cols, in_width)


def solution(mesh):
    return jax.shard_map(
        on_device,
        mesh=mesh,
        in_specs=(P("rows", "cols", None), P(), P(), P(("rows", "cols"), None)),
        out_specs=(P(("rows", "cols"), None), P("rows", "cols", None)),
        check_vma=False,
    )
```

```python
import functools
import math

import jax
import jax.numpy as jnp
from jax import lax
from jax.experimental import pallas as pl
from jax.experimental.pallas import tpu as pltpu
from jax.sharding import PartitionSpec as P

gelu_scale = math.sqrt(2.0 / math.pi)
tile = 128
edge = 16
f32, bf16 = jnp.float32, jnp.bfloat16


def tile_pairs(width):
    count = width // tile
    return [(i, j) for i in range(count) for j in range(i, count)]


def swap_rows(low, value):
    count = lax.axis_size("rows")
    pairs = [(i, (i + 1) % count) for i in low]
    return lax.ppermute(value, "rows", pairs + [(target, source) for source, target in pairs])


def shift_cols(last, first):
    count = lax.axis_size("cols")
    forward = [(i, i + 1) for i in range(count - 1)]
    backward = [(target, source) for source, target in forward]
    return lax.ppermute(last, "cols", forward), lax.ppermute(first, "cols", backward)


def device_index():
    return lax.axis_index("rows") * lax.axis_size("cols") + lax.axis_index("cols")


def swap(value, bit, other=None):
    total = lax.axis_size("rows") * lax.axis_size("cols")
    flip = lambda i: 1 << (other if other is not None and i.bit_count() % 2 else bit) | 1
    return lax.ppermute(value, ("rows", "cols"), [(i, i ^ flip(i)) for i in range(total)])


def local(body, out_shape, name, *operands, **kwargs):
    return pl.pallas_call(
        body,
        out_shape=out_shape,
        in_specs=[pl.BlockSpec(memory_space=pltpu.VMEM)] * len(operands),
        compiler_params=pltpu.CompilerParams(vmem_limit_bytes=8 * 1024 * 1024),
        name=name,
        **kwargs,
    )(*operands)


def side_of(bit, other=None):
    index = device_index()
    if bit > 0:
        side = lax.rem(index // (1 << bit), 2)
        if other is None:
            return side
        return jnp.where(side_of(0) == 0, side, lax.rem(index // (1 << other), 2))
    bits = (lax.axis_size("rows") * lax.axis_size("cols")).bit_length() - 1
    return lax.rem(sum(lax.rem(index // (1 << k), 2) for k in range(bits)), 2)


def rows_at(index, count):
    return pl.ds(pl.multiple_of(index * count, count), count)


waiting = pl.CostEstimate(flops=1_500_000_000, bytes_accessed=100_000, transcendentals=0)
chained = pl.CostEstimate(flops=8_000_000_000, bytes_accessed=100_000, transcendentals=0)


def halve(keep, got, bit, other=None):
    half = keep.shape[0] // 2

    def body(keep_ref, got_ref, send_ref, stay_ref):
        side = side_of(bit, other)
        away, here = rows_at(1 - side, half), rows_at(side, half)
        send_ref[...] = (keep_ref[away, :] + got_ref[away, :].astype(f32)).astype(bf16)
        stay_ref[...] = keep_ref[here, :] + got_ref[here, :].astype(f32)

    shape = (half, keep.shape[1])
    return local(
        body,
        (jax.ShapeDtypeStruct(shape, bf16), jax.ShapeDtypeStruct(shape, f32)),
        "halve",
        keep,
        got,
        cost_estimate=chained,
    )


def add(keep, got):
    def body(keep_ref, got_ref, sum_ref):
        sum_ref[...] = (keep_ref[...].astype(f32) + got_ref[...].astype(f32)).astype(bf16)

    return local(body, jax.ShapeDtypeStruct(got.shape, bf16), "add", keep, got, cost_estimate=chained)


def join(mine, got, bit, other=None, **kwargs):
    def body(mine_ref, got_ref, both_ref):
        side = side_of(bit, other)
        both_ref[:, pl.ds(side, 1)] = mine_ref[...][:, None]
        both_ref[:, pl.ds(1 - side, 1)] = got_ref[...][:, None]

    shape = (mine.shape[0], 2, *mine.shape[1:])
    return local(body, jax.ShapeDtypeStruct(shape, mine.dtype), "join", mine, got, **kwargs)


def join_second(mine, got, bit, other, **kwargs):
    def body(mine_ref, got_ref, both_ref):
        parity, side = side_of(0), side_of(bit, other)

        @pl.when(parity == 0)
        def _():
            both_ref[:, pl.ds(side, 1)] = mine_ref[...][:, None]
            both_ref[:, pl.ds(1 - side, 1)] = got_ref[...][:, None]

        @pl.when(parity == 1)
        def _():
            both_ref[:, :, pl.ds(side, 1)] = mine_ref[...][:, :, None]
            both_ref[:, :, pl.ds(1 - side, 1)] = got_ref[...][:, :, None]

    shape = (mine.shape[0], 2, *mine.shape[1:])
    return local(body, jax.ShapeDtypeStruct(shape, mine.dtype), "join_second", mine, got, **kwargs)


def join_cores(mine, other, **kwargs):
    def body(mine_ref, other_ref, both_ref):
        side = side_of(0)
        for chip in range(mine.shape[0]):
            core = lax.rem(side + chip.bit_count(), 2)
            both_ref[chip, pl.ds(core, 1)] = mine_ref[chip][None]
            both_ref[chip, pl.ds(1 - core, 1)] = other_ref[chip][None]

    shape = (mine.shape[0], 2, *mine.shape[1:])
    return local(body, jax.ShapeDtypeStruct(shape, mine.dtype), "join_cores", mine, other, **kwargs)


class Gather:
    def __init__(self, rows):
        self.rows, self.got, self.last = rows, None, None

    def settle(self, after):
        if self.got is None:
            self.rows, _ = lax.optimization_barrier((self.rows, after))
            return
        share = self.rows.shape[-2:]
        got, _ = lax.optimization_barrier((self.got, after))
        bit, other = self.last
        if bit == 0:
            both = join_cores(self.rows, got, cost_estimate=waiting)
        elif other is None or bit < other:
            mine, got = (part.reshape(-1, 1, *share) for part in (self.rows, got))
            both = join(mine, got, bit, other, cost_estimate=waiting)
        else:
            mine, got = (part.reshape(-1, 2, *share) for part in (self.rows, got))
            both = join_second(mine, got, bit, other, cost_estimate=waiting)
        self.rows, self.got = both.reshape(-1, *share), None

    def step(self, after, bit, other=None):
        self.settle(after)
        self.got, self.last = swap(self.rows, bit, other), (bit, other)


def sum_all(send, keep, beside):
    bits = (lax.axis_size("rows") * lax.axis_size("cols")).bit_length() - 1
    halving = [(1, 2), (2, 1)]
    adding = []
    for bit in range(3, bits, 2):
        adding += [(bit, bit + 1), (bit + 1, bit)] if bit + 1 < bits else [(bit, None)]

    got = beside("cores", send, swap(send, 0))
    for n, pair in enumerate(halving):
        send, keep = halve(keep, got, *pair)
        got = beside(f"halve {n}", send, swap(send, *pair))
    mine = add(keep, got)
    for n, pair in enumerate(adding):
        mine = add(mine, beside(f"add {n}", mine, swap(mine, *pair)))
    for n, pair in enumerate(reversed(halving)):
        got = beside(f"join {n}", mine, swap(mine, *pair))
        mine = join(mine[None], got[None], *pair, cost_estimate=chained).reshape(-1, mine.shape[1])
    return mine, beside("halves", mine, swap(mine, 0))


def gelu_pair(value):
    square = value * value
    tangent = jnp.tanh(value * (gelu_scale + gelu_scale * 0.044715 * square))
    half = 0.5 * value
    plus = 0.5 + 0.5 * tangent
    grad = plus + half * (1.0 - tangent * tangent) * (
        gelu_scale + gelu_scale * 3.0 * 0.044715 * square
    )
    return value * plus, grad


def column(value, c):
    return jnp.concatenate([value[r, c : c + 1] for r in range(value.shape[0])], axis=0)


def rim_kernel(canvas_ref, *out_refs):
    even_ref, odd_ref = out_refs[-2:]
    rows, cols, _ = canvas_ref.shape
    begin = canvas_ref[:, 0:16, :].astype(f32)
    end = canvas_ref[:, cols - 16 :, :].astype(f32)
    for c in range(2):
        pair = column(begin, c), column(end, 14 + c)
        if len(out_refs) == 3:
            out_refs[0][c] = jnp.where(lax.axis_index("cols") == 0, pair[1], pair[0]).astype(bf16)
        else:
            out_refs[0][c], out_refs[1][c] = pair[0].astype(bf16), pair[1].astype(bf16)
    odd = lax.rem(lax.axis_index("rows"), 2)
    for case, low_ref, high_ref in ((0, odd_ref, even_ref), (1, even_ref, odd_ref)):

        @pl.when(odd == case)
        def _():
            for k in range(2):
                at = slice(k * cols, (k + 1) * cols)
                low_ref[at, :], high_ref[at, :] = canvas_ref[k], canvas_ref[rows - 2 + k]


def payload_kernel(target_ref, *refs):
    even_ref, odd_ref, left_ref, right_ref, half_ref = refs[-5:]
    half_ref[0] = target_ref[...].astype(bf16)
    if len(refs) == 6:
        here = lax.axis_index("cols")
        other = refs[0][...].astype(f32)
        left_ref[...] = jnp.where(here == 0, 0.0, other).astype(bf16)
        right_ref[...] = jnp.where(here == 0, other, 0.0).astype(bf16)
    else:
        left_ref[...], right_ref[...] = refs[0][...], refs[1][...]
    beyond = [ref[c].astype(f32) for ref in (left_ref, right_ref) for c in range(2)]
    rows, width = beyond[0].shape

    def rim(r):
        parts = [part[r + k : r + k + 1] for k in range(2) for part in beyond]
        return jnp.concatenate([*parts, jnp.zeros((8, width), f32)], axis=0).astype(bf16)

    odd = lax.rem(lax.axis_index("rows"), 2)
    for case, low_ref, high_ref in ((0, odd_ref, even_ref), (1, even_ref, odd_ref)):

        @pl.when(odd == case)
        def _():
            low_ref[...], high_ref[...] = rim(0), rim(rows - 2)


def moved_rows(row, before, after):
    cols = row.shape[0]
    wide = row.astype(f32)
    place = lax.broadcasted_iota(jnp.int32, (8, row.shape[1]), 0)
    right, left = pltpu.roll(wide, 1, 0), pltpu.roll(wide, cols - 1, 0)
    right = jnp.concatenate([jnp.where(place == 0, before, right[:8]), right[8:]], axis=0)
    left = jnp.concatenate([left[:-8], jnp.where(place == 7, after, left[-8:])], axis=0)
    return right.astype(bf16), row.astype(bf16), left.astype(bf16)


def fill_row(cat_ref, r, row, before, after):
    cols, width = row.shape
    for b, part in enumerate(moved_rows(row, before, after)):
        cat_ref[r * cols : (r + 1) * cols, b * width : (b + 1) * width] = part


def gram_tiles(feat, gram_ref, base_ref=None):
    width = feat.shape[1]
    half = width // 2
    product = functools.partial(
        lax.dot_general,
        dimension_numbers=(((0,), (0,)), ((), ())),
        preferred_element_type=f32,
    )
    upper = product(feat[:, :half], feat)
    lower = product(feat[:, half:], feat[:, half:])
    for n, (i, j) in enumerate(tile_pairs(width)):
        at = slice(n * tile, (n + 1) * tile)
        if i * tile < half:
            part = upper[i * tile : (i + 1) * tile, j * tile : (j + 1) * tile]
        else:
            k, m = i * tile - half, j * tile - half
            part = lower[k : k + tile, m : m + tile]
        gram_ref[at, :] = part if base_ref is None else part + base_ref[at, :]


def inner_kernel(
    shape, own_ref, left_ref, right_ref, kernel_ref, bias_ref,
    feat_ref, slope_ref, gram_ref, row_ref, part_ref, cat_ref,
):
    row_ref[...] = bias_ref[...].astype(f32).reshape(row_ref.shape)
    tile_rows, tile_cols, in_width, out_width, step = shape
    lefts, rights = left_ref[1].astype(f32), right_ref[0].astype(f32)
    for r in range(tile_rows):
        fill_row(cat_ref, r, own_ref[r], lefts[r : r + 1], rights[r : r + 1])
    bias = row_ref[...]
    root = 1.0 / math.sqrt(out_width)
    span = 3 * in_width

    def product(begin, count, a):
        return jnp.dot(
            cat_ref[begin * tile_cols : (begin + count) * tile_cols, :],
            kernel_ref[a * span : (a + 1) * span, :],
            preferred_element_type=f32,
        )

    for h in range(0, tile_rows - 2, step):
        total = bias
        for a in range(3):
            total = total + product(h + a, step, a)
        features, slope = gelu_pair(total)
        at = slice(h * tile_cols, (h + step) * tile_cols)
        feat_ref[at, :] = features.astype(bf16)
        slope_ref[at, :] = (slope * root).astype(bf16)
    low, high = product(0, 2, 2), product(tile_rows - 2, 2, 0)
    ends = product(0, 1, 1), product(tile_rows - 1, 1, 1)
    part_ref[0:tile_cols, :] = low[:tile_cols] + bias
    part_ref[tile_cols : 2 * tile_cols, :] = low[tile_cols:] + ends[0] + bias
    part_ref[2 * tile_cols : 3 * tile_cols, :] = high[:tile_cols] + ends[1] + bias
    part_ref[3 * tile_cols :, :] = high[tile_cols:] + bias
    gram_tiles(feat_ref[...], gram_ref)


def halo_rows(halo_refs, low_ref, high_ref):
    even_ref, odd_ref, even_rim_ref, odd_rim_ref = halo_refs
    row = lax.axis_index("rows")
    odd = lax.rem(row, 2)
    main = even_ref.shape[0]
    low_ref[0:main, :] = jnp.where(odd == 0, odd_ref[...], even_ref[...])
    high_ref[0:main, :] = jnp.where(odd == 0, even_ref[...], odd_ref[...])
    low_ref[main:, :] = jnp.where(odd == 0, odd_rim_ref[...], even_rim_ref[...])
    high_ref[main:, :] = jnp.where(odd == 0, even_rim_ref[...], odd_rim_ref[...])

    @pl.when(row == 0)
    def _():
        low_ref[...] = jnp.zeros_like(low_ref)

    @pl.when(row == lax.axis_size("rows") - 1)
    def _():
        high_ref[...] = jnp.zeros_like(high_ref)


def halves(width):
    return slice(0, width // 2), slice(width // 2, width)


def outer_kernel(
    shape, even_ref, odd_ref, even_rim_ref, odd_rim_ref, kernel_ref, base_ref, part_ref,
    feat_ref, slope_ref, send_ref, keep_ref, low_ref, high_ref, cat_ref, gram_ref,
):
    tile_rows, tile_cols, in_width, out_width, step = shape
    span, main = 3 * in_width, 2 * tile_cols
    halo_rows((even_ref, odd_ref, even_rim_ref, odd_rim_ref), low_ref, high_ref)
    for n, (source, at) in enumerate([(low_ref, tile_cols), (high_ref, 0)]):
        rim = source[main:, :].astype(f32)
        k = 4 * (1 - n)
        fill_row(cat_ref, n, source[at : at + tile_cols, :], rim[k + 1 : k + 2], rim[k + 2 : k + 3])
    root = 1.0 / math.sqrt(out_width)
    for at in halves(out_width):
        for n, a in enumerate([0, 2]):
            rows = slice(n * tile_cols, (n + 1) * tile_cols)
            features, slope = gelu_pair(
                part_ref[(n + 1) * tile_cols : (n + 2) * tile_cols, at]
                + jnp.dot(
                    cat_ref[rows, :],
                    kernel_ref[a * span : (a + 1) * span, at],
                    preferred_element_type=f32,
                )
            )
            feat_ref[rows, at] = features.astype(bf16)
            slope_ref[rows, at] = (slope * root).astype(bf16)
    gram_tiles(feat_ref[...], gram_ref, base_ref)
    half = send_ref.shape[0]
    side = side_of(0)
    send_ref[...] = gram_ref[rows_at(1 - side, half), :].astype(bf16)
    keep_ref[...] = gram_ref[rows_at(side, half), :]


def beyond_kernel(
    shape, own_ref, even_ref, odd_ref, even_rim_ref, odd_rim_ref, left_ref, right_ref, kernel_ref, bias_ref,
    part_ref, feat_ref, slope_ref, low_ref, high_ref, cat_ref, edge_ref,
):
    tile_rows, tile_cols, in_width, out_width, step = shape
    halo_rows((even_ref, odd_ref, even_rim_ref, odd_rim_ref), low_ref, high_ref)
    first = (lax.axis_index("rows") > 0).astype(f32)
    last = (lax.axis_index("rows") < lax.axis_size("rows") - 1).astype(f32)
    left = (lax.axis_index("cols") > 0).astype(f32)
    right = (lax.axis_index("cols") < lax.axis_size("cols") - 1).astype(f32)
    main = 2 * tile_cols
    low_rim, high_rim = low_ref[main:, :].astype(f32), high_ref[main:, :].astype(f32)
    own_begin = column(own_ref[:, 0:16, :].astype(f32), 0)
    own_end = column(own_ref[:, tile_cols - 16 :, :].astype(f32), 15)

    def sides(c, own):
        return jnp.concatenate(
            [low_rim[c : c + 1], low_rim[4 + c : 5 + c], own, high_rim[c : c + 1], high_rim[4 + c : 5 + c]],
            axis=0,
        )

    def ends(c, own):
        c16 = c // 16 * 16
        piece = lambda ref, k: ref[k + c16 : k + c16 + 16, :].astype(f32)[c - c16 : c - c16 + 1]
        rows = [piece(low_ref, 0), piece(low_ref, tile_cols), own]
        return jnp.concatenate([*rows, piece(high_ref, 0), piece(high_ref, tile_cols)], axis=0)

    lefts = [
        sides(0, left_ref[0].astype(f32)), sides(1, left_ref[1].astype(f32)), ends(0, own_begin)
    ]
    rights = [
        ends(tile_cols - 1, own_end), sides(2, right_ref[0].astype(f32)), sides(3, right_ref[1].astype(f32))
    ]
    span = 3 * in_width
    for r, line in enumerate([0, 1, tile_rows + 2, tile_rows + 3]):
        source = low_ref if r < 2 else high_ref
        row = source[r % 2 * tile_cols : (r % 2 + 1) * tile_cols, :]
        fill_row(cat_ref, r, row, lefts[1][line : line + 1], rights[1][line : line + 1])
    blank = jnp.zeros((edge - tile_rows - 2, in_width), f32)
    for a in range(3):
        for b in range(3):
            piece = jnp.concatenate(
                [lefts[b][a : a + tile_rows + 2], blank, rights[b][a : a + tile_rows + 2], blank],
                axis=0,
            )
            at = (3 * a + b) * in_width
            edge_ref[:, at : at + in_width] = piece.astype(bf16)
    root = 1.0 / math.sqrt(out_width)
    line = lax.broadcasted_iota(jnp.int32, (2 * edge, out_width // 2), 0)
    weight = jnp.where(line < edge, left, right)
    weight = jnp.where(line % edge == 0, weight * first, weight)
    weight = jnp.where(line % edge == tile_rows + 1, weight * last, weight)
    for at in halves(out_width):

        def product(begin, a):
            return jnp.dot(
                cat_ref[begin * tile_cols : (begin + 1) * tile_cols, :],
                kernel_ref[a * span : (a + 1) * span, at],
                preferred_element_type=f32,
            )

        totals = [
            part_ref[0:tile_cols, at] + product(0, 0) + product(1, 1),
            part_ref[3 * tile_cols :, at] + product(2, 1) + product(3, 2),
            bias_ref[:, at] + jnp.dot(edge_ref[...], kernel_ref[:, at], preferred_element_type=f32),
        ]
        scales = [first * root, last * root, weight * root]
        for n, (total, scale) in enumerate(zip(totals, scales)):
            features, slope = gelu_pair(total)
            rows = slice(n * tile_cols, n * tile_cols + total.shape[0])
            feat_ref[rows, at] = features.astype(bf16)
            slope_ref[rows, at] = (slope * scale).astype(bf16)


def prepare_kernel(kernel_ref, target_ref, turned_ref, both_ref):
    taps, in_width, out_width = 9, kernel_ref.shape[0] // 9, kernel_ref.shape[1]
    for n in range(taps):
        to = (n // 3 * 3 + 2 - n % 3) * out_width
        turned_ref[to : to + out_width, :] = kernel_ref[n * in_width : (n + 1) * in_width, :].T
    for i, j in tile_pairs(out_width):
        at_i, at_j = slice(i * tile, (i + 1) * tile), slice(j * tile, (j + 1) * tile)
        both = target_ref[at_i, at_j].astype(f32) + target_ref[at_j, at_i].astype(f32).T
        both_ref[at_i, at_j] = both
        if i != j:
            both_ref[at_j, at_i] = both.T


def backward_kernel(
    shape, pixel_total, mine_ref, other_ref, both_ref, in_feat_ref, in_slope_ref, out_feat_ref, out_slope_ref,
    far_feat_ref, far_slope_ref, turned_ref, own_gram_ref, out_ref, gram_ref, full_ref, sym_ref, cat_ref,
):
    tile_rows, tile_cols, in_width, out_width, step = shape
    half = mine_ref.shape[0]
    side = side_of(0)
    gram_ref[rows_at(side, half), :] = mine_ref[...].astype(f32)
    gram_ref[rows_at(1 - side, half), :] = other_ref[...].astype(f32)
    for n, (i, j) in enumerate(tile_pairs(out_width)):
        at_i, at_j = slice(i * tile, (i + 1) * tile), slice(j * tile, (j + 1) * tile)
        gram = gram_ref[n * tile : (n + 1) * tile, :] * (1.0 / pixel_total)
        full_ref[at_i, at_j] = gram
        sym_ref[at_i, at_j] = (2.0 * gram - both_ref[at_i, at_j]).astype(bf16)
        if i != j:
            gram = gram.T
            full_ref[at_j, at_i] = gram
            sym_ref[at_j, at_i] = (2.0 * gram - both_ref[at_j, at_i]).astype(bf16)
    share = own_gram_ref.shape[0]
    start = device_index() * share
    if share % 8 == 0:
        own_gram_ref[...] = full_ref[pl.ds(pl.multiple_of(start, 8), share), :]
    else:
        group = full_ref[pl.ds(pl.multiple_of(start // 8 * 8, 8), 8), :]
        picked = group[0:share]
        for k in range(share, 8, share):
            picked = jnp.where(start % 8 == k, group[k : k + share], picked)
        own_gram_ref[...] = picked

    def grad_of(feat_ref, slope_ref, at):
        product = jnp.dot(feat_ref[at, :], sym_ref[...], preferred_element_type=f32)
        return product * slope_ref[at, :].astype(f32)

    main = 2 * tile_cols
    edges = grad_of(far_feat_ref, far_slope_ref, slice(main, None))
    near, far = (out_feat_ref, out_slope_ref), (far_feat_ref, far_slope_ref)
    lines = [[(*far, 0), (*near, 0)]]
    lines += [
        [(in_feat_ref, in_slope_ref, k * tile_cols) for k in range(h, h + step)]
        for h in range(0, tile_rows - 2, step)
    ]
    lines += [[(*near, tile_cols), (*far, tile_cols)]]
    grads = {}

    def upstream(c):
        pieces = lines[c]
        if pieces[0][0] is pieces[1][0]:
            feat_ref, slope_ref, begin = pieces[0]
            grads[c] = grad_of(feat_ref, slope_ref, slice(begin, begin + step * tile_cols))
        else:
            parts = [grad_of(feat, slope, slice(begin, begin + tile_cols)) for feat, slope, begin in pieces]
            grads[c] = jnp.concatenate(parts, axis=0)

    def fill(c):
        for k in range(step):
            r = c * step + k
            fill_row(
                cat_ref, r, grads[c][k * tile_cols : (k + 1) * tile_cols],
                edges[r : r + 1], edges[edge + r : edge + r + 1],
            )

    span = 3 * out_width

    def convolve(begin, count):
        total = 0.0
        for a in range(3):
            total = total + jnp.dot(
                cat_ref[(begin + 2 - a) * tile_cols : (begin + 2 - a + count) * tile_cols, :],
                turned_ref[a * span : (a + 1) * span, :],
                preferred_element_type=f32,
            )
        out_ref[begin * tile_cols : (begin + count) * tile_cols, :] = total.astype(bf16)

    last = len(lines) - 1
    middle = last // 2
    half_rows = middle * step
    upstream(0)
    for c in range(last):
        upstream(c + 1)
        fill(c)
        if c == middle:
            convolve(0, half_rows)
    fill(last)
    convolve(half_rows, tile_rows - half_rows)


def on_device(canvas, conv_weight, conv_bias, target_gram):
    tile_rows, tile_cols, in_width = canvas.shape
    out_width = conv_weight.shape[3]
    pixel_total = tile_rows * tile_cols * lax.axis_size("rows") * lax.axis_size("cols")
    shape = (tile_rows, tile_cols, in_width, out_width, 2)
    kernel = conv_weight.reshape(9 * in_width, out_width)
    params = pltpu.CompilerParams(vmem_limit_bytes=24 * 1024 * 1024)
    vmem = pl.BlockSpec(memory_space=pltpu.VMEM)
    packed_shape = jax.ShapeDtypeStruct((len(tile_pairs(out_width)) * tile, tile), f32)

    rim_shape = jax.ShapeDtypeStruct((2, tile_rows, in_width), bf16)
    two = lax.axis_size("cols") == 2
    count = lax.axis_size("rows")
    main_shape = jax.ShapeDtypeStruct((2 * tile_cols, in_width), bf16)
    *rims, even, odd = local(
        rim_kernel,
        (*(rim_shape,) * (1 if two else 2), main_shape, main_shape),
        "rims",
        canvas,
        cost_estimate=pl.CostEstimate(flops=4_000_000_000, bytes_accessed=600_000, transcendentals=0),
    )
    if two:
        beyond = [lax.ppermute(rims[0], "cols", [(0, 1), (1, 0)])]
    else:
        beyond = shift_cols(rims[1], rims[0])
    evens, odds = range(0, count, 2), range(1, count, 2)
    even, odd = swap_rows(evens, even), swap_rows(odds, odd)
    payload_shape = jax.ShapeDtypeStruct((2 * tile_cols + edge, in_width), bf16)
    end_shape = jax.ShapeDtypeStruct((edge, in_width), bf16)
    half_shape = jax.ShapeDtypeStruct((1, *target_gram.shape), bf16)
    even_rim, odd_rim, left, right, rows = local(
        payload_kernel,
        (end_shape, end_shape, rim_shape, rim_shape, half_shape),
        "row_rims",
        target_gram,
        *beyond,
    )
    halo = [even, odd, swap_rows(evens, even_rim), swap_rows(odds, odd_rim)]
    bits = (lax.axis_size("rows") * lax.axis_size("cols")).bit_length() - 1
    gather = Gather(rows)
    far = list(reversed(range(3, bits)))
    inner = (tile_rows - 2) * tile_cols
    in_feat, in_slope, in_gram, bias, part = pl.pallas_call(
        functools.partial(inner_kernel, shape),
        out_shape=(
            jax.ShapeDtypeStruct((inner, out_width), bf16),
            jax.ShapeDtypeStruct((inner, out_width), bf16),
            packed_shape,
            jax.ShapeDtypeStruct((1, out_width), f32),
            jax.ShapeDtypeStruct((4 * tile_cols, out_width), f32),
        ),
        in_specs=[vmem] * 5,
        scratch_shapes=[pltpu.VMEM((tile_rows * tile_cols, 3 * in_width), bf16)],
        compiler_params=params,
        name="inner_rows",
        cost_estimate=pl.CostEstimate(
            flops=2 * inner * (9 * in_width + out_width) * out_width,
            bytes_accessed=6_000_000,
            transcendentals=inner * out_width,
        ),
    )(canvas, left, right, kernel, conv_bias)

    half_gram = (packed_shape.shape[0] // 2, tile)
    halo_scratch = [pltpu.VMEM(payload_shape.shape, bf16), pltpu.VMEM(payload_shape.shape, bf16)]
    out_feat, out_slope, send, keep = pl.pallas_call(
        functools.partial(outer_kernel, shape),
        out_shape=(
            jax.ShapeDtypeStruct((2 * tile_cols, out_width), bf16),
            jax.ShapeDtypeStruct((2 * tile_cols, out_width), bf16),
            jax.ShapeDtypeStruct(half_gram, bf16),
            jax.ShapeDtypeStruct(half_gram, f32),
        ),
        in_specs=[vmem] * 7,
        scratch_shapes=[
            *halo_scratch,
            pltpu.VMEM((2 * tile_cols, 3 * in_width), bf16),
            pltpu.VMEM(packed_shape.shape, f32),
        ],
        compiler_params=params,
        name="outer_rows",
    )(*halo, kernel, in_gram, part)

    exchanges = {
        "halve 0": [(bit,) for bit in far[:1]],
        "halve 1": [(bit,) for bit in far[1:]],
        "add 0": [(1, 2)],
        "add 1": [(2, 1)],
        "join 0": [(0,)],
    }
    prepared, far_pixels = [], []

    def beside(name, sent, got):
        if name == "join 1":
            outer = 2 * tile_cols + 2 * edge
            rim_sums, _ = lax.optimization_barrier((part, sent))
            far_pixels.extend(
                pl.pallas_call(
                    functools.partial(beyond_kernel, shape),
                    out_shape=(jax.ShapeDtypeStruct((outer, out_width), bf16),) * 2,
                    in_specs=[vmem] * 10,
                    scratch_shapes=[
                        *halo_scratch,
                        pltpu.VMEM((4 * tile_cols, 3 * in_width), bf16),
                        pltpu.VMEM((2 * edge, 9 * in_width), bf16),
                    ],
                    compiler_params=params,
                    name="beyond",
                    cost_estimate=chained,
                )(canvas, *halo, left, right, kernel, bias, rim_sums)
            )
            gather.settle(sent)
            got, gather.rows, *_ = lax.optimization_barrier((got, gather.rows, *far_pixels))
            return got
        for bit in exchanges.get(name, []):
            gather.step(sent, *bit)
        if name == "join 0":
            got, gather.rows = lax.optimization_barrier((got, gather.rows))
        if name != "halves":
            return got
        gather.settle(sent)
        prepared.extend(
            pl.pallas_call(
                prepare_kernel,
                out_shape=(
                    jax.ShapeDtypeStruct((9 * out_width, in_width), bf16),
                    jax.ShapeDtypeStruct((out_width, out_width), f32),
                ),
                in_specs=[vmem] * 2,
                compiler_params=params,
                name="prepare",
                cost_estimate=pl.CostEstimate(
                    flops=2_000_000_000, bytes_accessed=6_000_000, transcendentals=0
                ),
            )(kernel, gather.rows.reshape(out_width, out_width))
        )
        return lax.optimization_barrier((got, *prepared))[0]

    mine, other = sum_all(send, keep, beside)
    turned, both = prepared
    far_feat, far_slope = far_pixels
    own_gram, grad = pl.pallas_call(
        functools.partial(backward_kernel, shape, pixel_total),
        out_shape=(
            jax.ShapeDtypeStruct(target_gram.shape, f32),
            jax.ShapeDtypeStruct((tile_rows * tile_cols, in_width), bf16),
        ),
        in_specs=[vmem] * 10,
        scratch_shapes=[
            pltpu.VMEM(packed_shape.shape, f32),
            pltpu.VMEM((out_width, out_width), f32),
            pltpu.VMEM((out_width, out_width), bf16),
            pltpu.VMEM(((tile_rows + 2) * tile_cols, 3 * out_width), bf16),
        ],
        compiler_params=params,
        name="grad_conv",
    )(mine, other, both, in_feat, in_slope, out_feat, out_slope, far_feat, far_slope, turned)
    return own_gram, grad.reshape(tile_rows, tile_cols, in_width)


def solution(mesh):
    return jax.shard_map(
        on_device,
        mesh=mesh,
        in_specs=(P("rows", "cols", None), P(), P(), P(("rows", "cols"), None)),
        out_specs=(P(("rows", "cols"), None), P("rows", "cols", None)),
        check_vma=False,
    )
```

```python
import functools
import math

import jax
import jax.numpy as jnp
from jax import lax
from jax.experimental import pallas as pl
from jax.experimental.pallas import tpu as pltpu
from jax.sharding import PartitionSpec as P

gelu_scale = math.sqrt(2.0 / math.pi)
tile = 128
edge = 16
f32, bf16 = jnp.float32, jnp.bfloat16


def tile_pairs(width):
    count = width // tile
    return [(i, j) for i in range(count) for j in range(i, count)]


def swap_rows(low, value):
    count, cols = lax.axis_size("rows"), lax.axis_size("cols")
    partner = {i: i + 1 for i in low if i + 1 < count}
    partner.update({i + 1: i for i in low if i + 1 < count})
    perm = [
        (r * cols + c, partner[r] * cols + c if r in partner else r * cols + (c ^ 1))
        for r in range(count)
        for c in range(cols)
    ]
    return lax.ppermute(value, ("rows", "cols"), perm)


def shift_cols(last, first):
    count = lax.axis_size("cols")
    forward = [(i, i + 1) for i in range(count - 1)]
    backward = [(target, source) for source, target in forward]
    return lax.ppermute(last, "cols", forward), lax.ppermute(first, "cols", backward)


def device_index():
    return lax.axis_index("rows") * lax.axis_size("cols") + lax.axis_index("cols")


def swap(value, bit, other=None):
    total = lax.axis_size("rows") * lax.axis_size("cols")
    flip = lambda i: 1 << (other if other is not None and i.bit_count() % 2 else bit) | 1
    return lax.ppermute(value, ("rows", "cols"), [(i, i ^ flip(i)) for i in range(total)])


def local(body, out_shape, name, *operands, **kwargs):
    return pl.pallas_call(
        body,
        out_shape=out_shape,
        in_specs=[pl.BlockSpec(memory_space=pltpu.VMEM)] * len(operands),
        compiler_params=pltpu.CompilerParams(vmem_limit_bytes=8 * 1024 * 1024),
        name=name,
        **kwargs,
    )(*operands)


def side_of(bit, other=None):
    index = device_index()
    if bit > 0:
        side = lax.rem(index // (1 << bit), 2)
        if other is None:
            return side
        return jnp.where(side_of(0) == 0, side, lax.rem(index // (1 << other), 2))
    bits = (lax.axis_size("rows") * lax.axis_size("cols")).bit_length() - 1
    return lax.rem(sum(lax.rem(index // (1 << k), 2) for k in range(bits)), 2)


def rows_at(index, count):
    return pl.ds(pl.multiple_of(index * count, count), count)


waiting = pl.CostEstimate(flops=1_500_000_000, bytes_accessed=100_000, transcendentals=0)
chained = pl.CostEstimate(flops=8_000_000_000, bytes_accessed=100_000, transcendentals=0)


def halve(keep, got, bit, other=None):
    half = keep.shape[0] // 2

    def body(keep_ref, got_ref, send_ref, stay_ref):
        side = side_of(bit, other)
        away, here = rows_at(1 - side, half), rows_at(side, half)
        send_ref[...] = (keep_ref[away, :] + got_ref[away, :].astype(f32)).astype(bf16)
        stay_ref[...] = keep_ref[here, :] + got_ref[here, :].astype(f32)

    shape = (half, keep.shape[1])
    return local(
        body,
        (jax.ShapeDtypeStruct(shape, bf16), jax.ShapeDtypeStruct(shape, f32)),
        "halve",
        keep,
        got,
        cost_estimate=chained,
    )


def add(keep, got):
    def body(keep_ref, got_ref, sum_ref):
        sum_ref[...] = (keep_ref[...].astype(f32) + got_ref[...].astype(f32)).astype(bf16)

    return local(body, jax.ShapeDtypeStruct(got.shape, bf16), "add", keep, got, cost_estimate=chained)


def join(mine, got, bit, other=None, **kwargs):
    def body(mine_ref, got_ref, both_ref):
        side = side_of(bit, other)
        both_ref[:, pl.ds(side, 1)] = mine_ref[...][:, None]
        both_ref[:, pl.ds(1 - side, 1)] = got_ref[...][:, None]

    shape = (mine.shape[0], 2, *mine.shape[1:])
    return local(body, jax.ShapeDtypeStruct(shape, mine.dtype), "join", mine, got, **kwargs)


def join_second(mine, got, bit, other, **kwargs):
    def body(mine_ref, got_ref, both_ref):
        parity, side = side_of(0), side_of(bit, other)

        @pl.when(parity == 0)
        def _():
            both_ref[:, pl.ds(side, 1)] = mine_ref[...][:, None]
            both_ref[:, pl.ds(1 - side, 1)] = got_ref[...][:, None]

        @pl.when(parity == 1)
        def _():
            both_ref[:, :, pl.ds(side, 1)] = mine_ref[...][:, :, None]
            both_ref[:, :, pl.ds(1 - side, 1)] = got_ref[...][:, :, None]

    shape = (mine.shape[0], 2, *mine.shape[1:])
    return local(body, jax.ShapeDtypeStruct(shape, mine.dtype), "join_second", mine, got, **kwargs)


def join_cores(mine, other, **kwargs):
    def body(mine_ref, other_ref, both_ref):
        side = side_of(0)
        for chip in range(mine.shape[0]):
            core = lax.rem(side + chip.bit_count(), 2)
            both_ref[chip, pl.ds(core, 1)] = mine_ref[chip][None]
            both_ref[chip, pl.ds(1 - core, 1)] = other_ref[chip][None]

    shape = (mine.shape[0], 2, *mine.shape[1:])
    return local(body, jax.ShapeDtypeStruct(shape, mine.dtype), "join_cores", mine, other, **kwargs)


class Gather:
    def __init__(self, rows):
        self.rows, self.got, self.last = rows, None, None

    def settle(self, after):
        if self.got is None:
            self.rows, _ = lax.optimization_barrier((self.rows, after))
            return
        share = self.rows.shape[-2:]
        got, _ = lax.optimization_barrier((self.got, after))
        bit, other = self.last
        if bit == 0:
            both = join_cores(self.rows, got, cost_estimate=waiting)
        elif other is None or bit < other:
            mine, got = (part.reshape(-1, 1, *share) for part in (self.rows, got))
            both = join(mine, got, bit, other, cost_estimate=waiting)
        else:
            mine, got = (part.reshape(-1, 2, *share) for part in (self.rows, got))
            both = join_second(mine, got, bit, other, cost_estimate=waiting)
        self.rows, self.got = both.reshape(-1, *share), None

    def step(self, after, bit, other=None):
        self.settle(after)
        self.got, self.last = swap(self.rows, bit, other), (bit, other)


def sum_all(send, keep, beside):
    bits = (lax.axis_size("rows") * lax.axis_size("cols")).bit_length() - 1
    halving = [(1, 2), (2, 1)]
    adding = []
    for bit in range(3, bits, 2):
        adding += [(bit, bit + 1), (bit + 1, bit)] if bit + 1 < bits else [(bit, None)]

    got = beside("cores", send, swap(send, 0))
    for n, pair in enumerate(halving):
        send, keep = halve(keep, got, *pair)
        got = beside(f"halve {n}", send, swap(send, *pair))
    mine = add(keep, got)
    for n, pair in enumerate(adding):
        mine = add(mine, beside(f"add {n}", mine, swap(mine, *pair)))
    for n, pair in enumerate(reversed(halving)):
        got = beside(f"join {n}", mine, swap(mine, *pair))
        mine = join(mine[None], got[None], *pair, cost_estimate=chained).reshape(-1, mine.shape[1])
    return mine, beside("halves", mine, swap(mine, 0))


def gelu_pair(value):
    square = value * value
    tangent = jnp.tanh(value * (gelu_scale + gelu_scale * 0.044715 * square))
    half = 0.5 * value
    plus = 0.5 + 0.5 * tangent
    grad = plus + half * (1.0 - tangent * tangent) * (
        gelu_scale + gelu_scale * 3.0 * 0.044715 * square
    )
    return value * plus, grad


def column(value, c):
    return jnp.concatenate([value[r, c : c + 1] for r in range(value.shape[0])], axis=0)


def rim_kernel(canvas_ref, *out_refs):
    even_ref, odd_ref = out_refs[-2:]
    rows, cols, _ = canvas_ref.shape
    begin = canvas_ref[:, 0:16, :].astype(f32)
    end = canvas_ref[:, cols - 16 :, :].astype(f32)
    for c in range(2):
        pair = column(begin, c), column(end, 14 + c)
        if len(out_refs) == 3:
            out_refs[0][c] = jnp.where(lax.axis_index("cols") == 0, pair[1], pair[0]).astype(bf16)
        else:
            out_refs[0][c], out_refs[1][c] = pair[0].astype(bf16), pair[1].astype(bf16)
    odd = lax.rem(lax.axis_index("rows"), 2)
    for case, low_ref, high_ref in ((0, odd_ref, even_ref), (1, even_ref, odd_ref)):

        @pl.when(odd == case)
        def _():
            for k in range(2):
                at = slice(k * cols, (k + 1) * cols)
                low_ref[at, :], high_ref[at, :] = canvas_ref[k], canvas_ref[rows - 2 + k]


def payload_kernel(target_ref, *refs):
    even_ref, odd_ref, left_ref, right_ref, half_ref = refs[-5:]
    half_ref[0] = target_ref[...].astype(bf16)
    if len(refs) == 6:
        here = lax.axis_index("cols")
        other = refs[0][...].astype(f32)
        left_ref[...] = jnp.where(here == 0, 0.0, other).astype(bf16)
        right_ref[...] = jnp.where(here == 0, other, 0.0).astype(bf16)
    else:
        left_ref[...], right_ref[...] = refs[0][...], refs[1][...]
    beyond = [ref[c].astype(f32) for ref in (left_ref, right_ref) for c in range(2)]
    rows, width = beyond[0].shape

    def rim(r):
        parts = [part[r + k : r + k + 1] for k in range(2) for part in beyond]
        return jnp.concatenate([*parts, jnp.zeros((8, width), f32)], axis=0).astype(bf16)

    odd = lax.rem(lax.axis_index("rows"), 2)
    for case, low_ref, high_ref in ((0, odd_ref, even_ref), (1, even_ref, odd_ref)):

        @pl.when(odd == case)
        def _():
            low_ref[...], high_ref[...] = rim(0), rim(rows - 2)


def moved_rows(row, before, after):
    cols = row.shape[0]
    wide = row.astype(f32)
    place = lax.broadcasted_iota(jnp.int32, (8, row.shape[1]), 0)
    right, left = pltpu.roll(wide, 1, 0), pltpu.roll(wide, cols - 1, 0)
    right = jnp.concatenate([jnp.where(place == 0, before, right[:8]), right[8:]], axis=0)
    left = jnp.concatenate([left[:-8], jnp.where(place == 7, after, left[-8:])], axis=0)
    return right.astype(bf16), row.astype(bf16), left.astype(bf16)


def fill_row(cat_ref, r, row, before, after):
    cols, width = row.shape
    for b, part in enumerate(moved_rows(row, before, after)):
        cat_ref[r * cols : (r + 1) * cols, b * width : (b + 1) * width] = part


def gram_tiles(feat, gram_ref, base_ref=None):
    width = feat.shape[1]
    half = width // 2
    product = functools.partial(
        lax.dot_general,
        dimension_numbers=(((0,), (0,)), ((), ())),
        preferred_element_type=f32,
    )
    upper = product(feat[:, :half], feat)
    lower = product(feat[:, half:], feat[:, half:])
    for n, (i, j) in enumerate(tile_pairs(width)):
        at = slice(n * tile, (n + 1) * tile)
        if i * tile < half:
            part = upper[i * tile : (i + 1) * tile, j * tile : (j + 1) * tile]
        else:
            k, m = i * tile - half, j * tile - half
            part = lower[k : k + tile, m : m + tile]
        gram_ref[at, :] = part if base_ref is None else part + base_ref[at, :]


def inner_kernel(
    shape, own_ref, left_ref, right_ref, kernel_ref, bias_ref,
    feat_ref, slope_ref, gram_ref, row_ref, part_ref, cat_ref,
):
    row_ref[...] = bias_ref[...].astype(f32).reshape(row_ref.shape)
    tile_rows, tile_cols, in_width, out_width, step = shape
    lefts, rights = left_ref[1].astype(f32), right_ref[0].astype(f32)
    for r in range(tile_rows):
        fill_row(cat_ref, r, own_ref[r], lefts[r : r + 1], rights[r : r + 1])
    bias = row_ref[...]
    root = 1.0 / math.sqrt(out_width)
    span = 3 * in_width

    def product(begin, count, a):
        return jnp.dot(
            cat_ref[begin * tile_cols : (begin + count) * tile_cols, :],
            kernel_ref[a * span : (a + 1) * span, :],
            preferred_element_type=f32,
        )

    for h in range(0, tile_rows - 2, step):
        total = bias
        for a in range(3):
            total = total + product(h + a, step, a)
        features, slope = gelu_pair(total)
        at = slice(h * tile_cols, (h + step) * tile_cols)
        feat_ref[at, :] = features.astype(bf16)
        slope_ref[at, :] = (slope * root).astype(bf16)
    low, high = product(0, 2, 2), product(tile_rows - 2, 2, 0)
    ends = product(0, 1, 1), product(tile_rows - 1, 1, 1)
    part_ref[0:tile_cols, :] = low[:tile_cols] + bias
    part_ref[tile_cols : 2 * tile_cols, :] = low[tile_cols:] + ends[0] + bias
    part_ref[2 * tile_cols : 3 * tile_cols, :] = high[:tile_cols] + ends[1] + bias
    part_ref[3 * tile_cols :, :] = high[tile_cols:] + bias
    gram_tiles(feat_ref[...], gram_ref)


def halo_rows(halo_refs, low_ref, high_ref):
    even_ref, odd_ref, even_rim_ref, odd_rim_ref = halo_refs
    row = lax.axis_index("rows")
    odd = lax.rem(row, 2)
    main = even_ref.shape[0]
    low_ref[0:main, :] = jnp.where(odd == 0, odd_ref[...], even_ref[...])
    high_ref[0:main, :] = jnp.where(odd == 0, even_ref[...], odd_ref[...])
    low_ref[main:, :] = jnp.where(odd == 0, odd_rim_ref[...], even_rim_ref[...])
    high_ref[main:, :] = jnp.where(odd == 0, even_rim_ref[...], odd_rim_ref[...])

    @pl.when(row == 0)
    def _():
        low_ref[...] = jnp.zeros_like(low_ref)

    @pl.when(row == lax.axis_size("rows") - 1)
    def _():
        high_ref[...] = jnp.zeros_like(high_ref)


def halves(width):
    return slice(0, width // 2), slice(width // 2, width)


def outer_kernel(
    shape, even_ref, odd_ref, even_rim_ref, odd_rim_ref, kernel_ref, base_ref, part_ref,
    feat_ref, slope_ref, send_ref, keep_ref, low_ref, high_ref, cat_ref, gram_ref,
):
    tile_rows, tile_cols, in_width, out_width, step = shape
    span, main = 3 * in_width, 2 * tile_cols
    halo_rows((even_ref, odd_ref, even_rim_ref, odd_rim_ref), low_ref, high_ref)
    for n, (source, at) in enumerate([(low_ref, tile_cols), (high_ref, 0)]):
        rim = source[main:, :].astype(f32)
        k = 4 * (1 - n)
        fill_row(cat_ref, n, source[at : at + tile_cols, :], rim[k + 1 : k + 2], rim[k + 2 : k + 3])
    root = 1.0 / math.sqrt(out_width)
    for at in halves(out_width):
        for n, a in enumerate([0, 2]):
            rows = slice(n * tile_cols, (n + 1) * tile_cols)
            features, slope = gelu_pair(
                part_ref[(n + 1) * tile_cols : (n + 2) * tile_cols, at]
                + jnp.dot(
                    cat_ref[rows, :],
                    kernel_ref[a * span : (a + 1) * span, at],
                    preferred_element_type=f32,
                )
            )
            feat_ref[rows, at] = features.astype(bf16)
            slope_ref[rows, at] = (slope * root).astype(bf16)
    gram_tiles(feat_ref[...], gram_ref, base_ref)
    half = send_ref.shape[0]
    side = side_of(0)
    send_ref[...] = gram_ref[rows_at(1 - side, half), :].astype(bf16)
    keep_ref[...] = gram_ref[rows_at(side, half), :]


def beyond_kernel(
    shape, own_ref, even_ref, odd_ref, even_rim_ref, odd_rim_ref, left_ref, right_ref, kernel_ref, bias_ref,
    part_ref, feat_ref, slope_ref, low_ref, high_ref, cat_ref, edge_ref,
):
    tile_rows, tile_cols, in_width, out_width, step = shape
    halo_rows((even_ref, odd_ref, even_rim_ref, odd_rim_ref), low_ref, high_ref)
    first = (lax.axis_index("rows") > 0).astype(f32)
    last = (lax.axis_index("rows") < lax.axis_size("rows") - 1).astype(f32)
    left = (lax.axis_index("cols") > 0).astype(f32)
    right = (lax.axis_index("cols") < lax.axis_size("cols") - 1).astype(f32)
    main = 2 * tile_cols
    low_rim, high_rim = low_ref[main:, :].astype(f32), high_ref[main:, :].astype(f32)
    own_begin = column(own_ref[:, 0:16, :].astype(f32), 0)
    own_end = column(own_ref[:, tile_cols - 16 :, :].astype(f32), 15)

    def sides(c, own):
        return jnp.concatenate(
            [low_rim[c : c + 1], low_rim[4 + c : 5 + c], own, high_rim[c : c + 1], high_rim[4 + c : 5 + c]],
            axis=0,
        )

    def ends(c, own):
        c16 = c // 16 * 16
        piece = lambda ref, k: ref[k + c16 : k + c16 + 16, :].astype(f32)[c - c16 : c - c16 + 1]
        rows = [piece(low_ref, 0), piece(low_ref, tile_cols), own]
        return jnp.concatenate([*rows, piece(high_ref, 0), piece(high_ref, tile_cols)], axis=0)

    lefts = [
        sides(0, left_ref[0].astype(f32)), sides(1, left_ref[1].astype(f32)), ends(0, own_begin)
    ]
    rights = [
        ends(tile_cols - 1, own_end), sides(2, right_ref[0].astype(f32)), sides(3, right_ref[1].astype(f32))
    ]
    span = 3 * in_width
    for r, line in enumerate([0, 1, tile_rows + 2, tile_rows + 3]):
        source = low_ref if r < 2 else high_ref
        row = source[r % 2 * tile_cols : (r % 2 + 1) * tile_cols, :]
        fill_row(cat_ref, r, row, lefts[1][line : line + 1], rights[1][line : line + 1])
    blank = jnp.zeros((edge - tile_rows - 2, in_width), f32)
    for a in range(3):
        for b in range(3):
            piece = jnp.concatenate(
                [lefts[b][a : a + tile_rows + 2], blank, rights[b][a : a + tile_rows + 2], blank],
                axis=0,
            )
            at = (3 * a + b) * in_width
            edge_ref[:, at : at + in_width] = piece.astype(bf16)
    root = 1.0 / math.sqrt(out_width)
    line = lax.broadcasted_iota(jnp.int32, (2 * edge, out_width // 2), 0)
    weight = jnp.where(line < edge, left, right)
    weight = jnp.where(line % edge == 0, weight * first, weight)
    weight = jnp.where(line % edge == tile_rows + 1, weight * last, weight)
    for at in halves(out_width):

        def product(begin, a):
            return jnp.dot(
                cat_ref[begin * tile_cols : (begin + 1) * tile_cols, :],
                kernel_ref[a * span : (a + 1) * span, at],
                preferred_element_type=f32,
            )

        totals = [
            part_ref[0:tile_cols, at] + product(0, 0) + product(1, 1),
            part_ref[3 * tile_cols :, at] + product(2, 1) + product(3, 2),
            bias_ref[:, at] + jnp.dot(edge_ref[...], kernel_ref[:, at], preferred_element_type=f32),
        ]
        scales = [first * root, last * root, weight * root]
        for n, (total, scale) in enumerate(zip(totals, scales)):
            features, slope = gelu_pair(total)
            rows = slice(n * tile_cols, n * tile_cols + total.shape[0])
            feat_ref[rows, at] = features.astype(bf16)
            slope_ref[rows, at] = (slope * scale).astype(bf16)


def prepare_kernel(kernel_ref, target_ref, turned_ref, both_ref):
    taps, in_width, out_width = 9, kernel_ref.shape[0] // 9, kernel_ref.shape[1]
    for n in range(taps):
        to = (n // 3 * 3 + 2 - n % 3) * out_width
        turned_ref[to : to + out_width, :] = kernel_ref[n * in_width : (n + 1) * in_width, :].T
    for i, j in tile_pairs(out_width):
        at_i, at_j = slice(i * tile, (i + 1) * tile), slice(j * tile, (j + 1) * tile)
        both = target_ref[at_i, at_j].astype(f32) + target_ref[at_j, at_i].astype(f32).T
        both_ref[at_i, at_j] = both
        if i != j:
            both_ref[at_j, at_i] = both.T


def backward_kernel(
    shape, pixel_total, mine_ref, other_ref, both_ref, in_feat_ref, in_slope_ref, out_feat_ref, out_slope_ref,
    far_feat_ref, far_slope_ref, turned_ref, own_gram_ref, out_ref, gram_ref, full_ref, sym_ref, cat_ref,
):
    tile_rows, tile_cols, in_width, out_width, step = shape
    half = mine_ref.shape[0]
    side = side_of(0)
    gram_ref[rows_at(side, half), :] = mine_ref[...].astype(f32)
    gram_ref[rows_at(1 - side, half), :] = other_ref[...].astype(f32)
    for n, (i, j) in enumerate(tile_pairs(out_width)):
        at_i, at_j = slice(i * tile, (i + 1) * tile), slice(j * tile, (j + 1) * tile)
        gram = gram_ref[n * tile : (n + 1) * tile, :] * (1.0 / pixel_total)
        full_ref[at_i, at_j] = gram
        sym_ref[at_i, at_j] = (2.0 * gram - both_ref[at_i, at_j]).astype(bf16)
        if i != j:
            gram = gram.T
            full_ref[at_j, at_i] = gram
            sym_ref[at_j, at_i] = (2.0 * gram - both_ref[at_j, at_i]).astype(bf16)
    share = own_gram_ref.shape[0]
    start = device_index() * share
    if share % 8 == 0:
        own_gram_ref[...] = full_ref[pl.ds(pl.multiple_of(start, 8), share), :]
    else:
        group = full_ref[pl.ds(pl.multiple_of(start // 8 * 8, 8), 8), :]
        picked = group[0:share]
        for k in range(share, 8, share):
            picked = jnp.where(start % 8 == k, group[k : k + share], picked)
        own_gram_ref[...] = picked

    def grad_of(feat_ref, slope_ref, at):
        product = jnp.dot(feat_ref[at, :], sym_ref[...], preferred_element_type=f32)
        return product * slope_ref[at, :].astype(f32)

    main = 2 * tile_cols
    edges = grad_of(far_feat_ref, far_slope_ref, slice(main, None))
    near, far = (out_feat_ref, out_slope_ref), (far_feat_ref, far_slope_ref)
    lines = [[(*far, 0), (*near, 0)]]
    lines += [
        [(in_feat_ref, in_slope_ref, k * tile_cols) for k in range(h, h + step)]
        for h in range(0, tile_rows - 2, step)
    ]
    lines += [[(*near, tile_cols), (*far, tile_cols)]]
    grads = {}

    def upstream(c):
        pieces = lines[c]
        if pieces[0][0] is pieces[1][0]:
            feat_ref, slope_ref, begin = pieces[0]
            grads[c] = grad_of(feat_ref, slope_ref, slice(begin, begin + step * tile_cols))
        else:
            parts = [grad_of(feat, slope, slice(begin, begin + tile_cols)) for feat, slope, begin in pieces]
            grads[c] = jnp.concatenate(parts, axis=0)

    def fill(c):
        for k in range(step):
            r = c * step + k
            fill_row(
                cat_ref, r, grads[c][k * tile_cols : (k + 1) * tile_cols],
                edges[r : r + 1], edges[edge + r : edge + r + 1],
            )

    span = 3 * out_width

    def convolve(begin, count):
        total = 0.0
        for a in range(3):
            total = total + jnp.dot(
                cat_ref[(begin + 2 - a) * tile_cols : (begin + 2 - a + count) * tile_cols, :],
                turned_ref[a * span : (a + 1) * span, :],
                preferred_element_type=f32,
            )
        out_ref[begin * tile_cols : (begin + count) * tile_cols, :] = total.astype(bf16)

    last = len(lines) - 1
    middle = last // 2
    half_rows = middle * step
    upstream(0)
    for c in range(last):
        upstream(c + 1)
        fill(c)
        if c == middle:
            convolve(0, half_rows)
    fill(last)
    convolve(half_rows, tile_rows - half_rows)


def on_device(canvas, conv_weight, conv_bias, target_gram):
    tile_rows, tile_cols, in_width = canvas.shape
    out_width = conv_weight.shape[3]
    pixel_total = tile_rows * tile_cols * lax.axis_size("rows") * lax.axis_size("cols")
    shape = (tile_rows, tile_cols, in_width, out_width, 2)
    kernel = conv_weight.reshape(9 * in_width, out_width)
    params = pltpu.CompilerParams(vmem_limit_bytes=24 * 1024 * 1024)
    vmem = pl.BlockSpec(memory_space=pltpu.VMEM)
    packed_shape = jax.ShapeDtypeStruct((len(tile_pairs(out_width)) * tile, tile), f32)

    rim_shape = jax.ShapeDtypeStruct((2, tile_rows, in_width), bf16)
    two = lax.axis_size("cols") == 2
    count = lax.axis_size("rows")
    main_shape = jax.ShapeDtypeStruct((2 * tile_cols, in_width), bf16)
    *rims, even, odd = local(
        rim_kernel,
        (*(rim_shape,) * (1 if two else 2), main_shape, main_shape),
        "rims",
        canvas,
        cost_estimate=pl.CostEstimate(flops=4_000_000_000, bytes_accessed=600_000, transcendentals=0),
    )
    if two:
        beyond = [lax.ppermute(rims[0], "cols", [(0, 1), (1, 0)])]
    else:
        beyond = shift_cols(rims[1], rims[0])
    evens, odds = range(0, count, 2), range(1, count, 2)
    even, odd = swap_rows(evens, even), swap_rows(odds, odd)
    payload_shape = jax.ShapeDtypeStruct((2 * tile_cols + edge, in_width), bf16)
    end_shape = jax.ShapeDtypeStruct((edge, in_width), bf16)
    half_shape = jax.ShapeDtypeStruct((1, *target_gram.shape), bf16)
    even_rim, odd_rim, left, right, rows = local(
        payload_kernel,
        (end_shape, end_shape, rim_shape, rim_shape, half_shape),
        "row_rims",
        target_gram,
        *beyond,
    )
    halo = [even, odd, swap_rows(evens, even_rim), swap_rows(odds, odd_rim)]
    bits = (lax.axis_size("rows") * lax.axis_size("cols")).bit_length() - 1
    gather = Gather(rows)
    far = list(reversed(range(3, bits)))
    inner = (tile_rows - 2) * tile_cols
    in_feat, in_slope, in_gram, bias, part = pl.pallas_call(
        functools.partial(inner_kernel, shape),
        out_shape=(
            jax.ShapeDtypeStruct((inner, out_width), bf16),
            jax.ShapeDtypeStruct((inner, out_width), bf16),
            packed_shape,
            jax.ShapeDtypeStruct((1, out_width), f32),
            jax.ShapeDtypeStruct((4 * tile_cols, out_width), f32),
        ),
        in_specs=[vmem] * 5,
        scratch_shapes=[pltpu.VMEM((tile_rows * tile_cols, 3 * in_width), bf16)],
        compiler_params=params,
        name="inner_rows",
        cost_estimate=pl.CostEstimate(
            flops=2 * inner * (9 * in_width + out_width) * out_width,
            bytes_accessed=6_000_000,
            transcendentals=inner * out_width,
        ),
    )(canvas, left, right, kernel, conv_bias)

    half_gram = (packed_shape.shape[0] // 2, tile)
    halo_scratch = [pltpu.VMEM(payload_shape.shape, bf16), pltpu.VMEM(payload_shape.shape, bf16)]
    out_feat, out_slope, send, keep = pl.pallas_call(
        functools.partial(outer_kernel, shape),
        out_shape=(
            jax.ShapeDtypeStruct((2 * tile_cols, out_width), bf16),
            jax.ShapeDtypeStruct((2 * tile_cols, out_width), bf16),
            jax.ShapeDtypeStruct(half_gram, bf16),
            jax.ShapeDtypeStruct(half_gram, f32),
        ),
        in_specs=[vmem] * 7,
        scratch_shapes=[
            *halo_scratch,
            pltpu.VMEM((2 * tile_cols, 3 * in_width), bf16),
            pltpu.VMEM(packed_shape.shape, f32),
        ],
        compiler_params=params,
        name="outer_rows",
    )(*halo, kernel, in_gram, part)

    exchanges = {
        "halve 0": [(bit,) for bit in far[:1]],
        "halve 1": [(bit,) for bit in far[1:]],
        "add 0": [(1, 2)],
        "add 1": [(2, 1)],
        "join 0": [(0,)],
    }
    prepared, far_pixels = [], []

    def beside(name, sent, got):
        if name == "join 1":
            outer = 2 * tile_cols + 2 * edge
            rim_sums, _ = lax.optimization_barrier((part, sent))
            far_pixels.extend(
                pl.pallas_call(
                    functools.partial(beyond_kernel, shape),
                    out_shape=(jax.ShapeDtypeStruct((outer, out_width), bf16),) * 2,
                    in_specs=[vmem] * 10,
                    scratch_shapes=[
                        *halo_scratch,
                        pltpu.VMEM((4 * tile_cols, 3 * in_width), bf16),
                        pltpu.VMEM((2 * edge, 9 * in_width), bf16),
                    ],
                    compiler_params=params,
                    name="beyond",
                    cost_estimate=chained,
                )(canvas, *halo, left, right, kernel, bias, rim_sums)
            )
            gather.settle(sent)
            got, gather.rows, *_ = lax.optimization_barrier((got, gather.rows, *far_pixels))
            return got
        for bit in exchanges.get(name, []):
            gather.step(sent, *bit)
        if name == "join 0":
            got, gather.rows = lax.optimization_barrier((got, gather.rows))
        if name != "halves":
            return got
        gather.settle(sent)
        prepared.extend(
            pl.pallas_call(
                prepare_kernel,
                out_shape=(
                    jax.ShapeDtypeStruct((9 * out_width, in_width), bf16),
                    jax.ShapeDtypeStruct((out_width, out_width), f32),
                ),
                in_specs=[vmem] * 2,
                compiler_params=params,
                name="prepare",
                cost_estimate=pl.CostEstimate(
                    flops=2_000_000_000, bytes_accessed=6_000_000, transcendentals=0
                ),
            )(kernel, gather.rows.reshape(out_width, out_width))
        )
        return lax.optimization_barrier((got, *prepared))[0]

    mine, other = sum_all(send, keep, beside)
    turned, both = prepared
    far_feat, far_slope = far_pixels
    own_gram, grad = pl.pallas_call(
        functools.partial(backward_kernel, shape, pixel_total),
        out_shape=(
            jax.ShapeDtypeStruct(target_gram.shape, f32),
            jax.ShapeDtypeStruct((tile_rows * tile_cols, in_width), bf16),
        ),
        in_specs=[vmem] * 10,
        scratch_shapes=[
            pltpu.VMEM(packed_shape.shape, f32),
            pltpu.VMEM((out_width, out_width), f32),
            pltpu.VMEM((out_width, out_width), bf16),
            pltpu.VMEM(((tile_rows + 2) * tile_cols, 3 * out_width), bf16),
        ],
        compiler_params=params,
        name="grad_conv",
    )(mine, other, both, in_feat, in_slope, out_feat, out_slope, far_feat, far_slope, turned)
    return own_gram, grad.reshape(tile_rows, tile_cols, in_width)


def solution(mesh):
    return jax.shard_map(
        on_device,
        mesh=mesh,
        in_specs=(P("rows", "cols", None), P(), P(), P(("rows", "cols"), None)),
        out_specs=(P(("rows", "cols"), None), P("rows", "cols", None)),
        check_vma=False,
    )
```

```python
import functools
import math

import jax
import jax.numpy as jnp
from jax import lax
from jax.experimental import pallas as pl
from jax.experimental.pallas import tpu as pltpu
from jax.sharding import PartitionSpec as P

gelu_scale = math.sqrt(2.0 / math.pi)
tile = 128
edge = 16
f32, bf16 = jnp.float32, jnp.bfloat16


def tile_pairs(width):
    count = width // tile
    return [(i, j) for i in range(count) for j in range(i, count)]


def swap_rows(low, value):
    count, cols = lax.axis_size("rows"), lax.axis_size("cols")
    partner = {i: i + 1 for i in low if i + 1 < count}
    partner.update({i + 1: i for i in low if i + 1 < count})
    perm = [
        (r * cols + c, partner[r] * cols + c if r in partner else r * cols + (c ^ 1))
        for r in range(count)
        for c in range(cols)
    ]
    return lax.ppermute(value, ("rows", "cols"), perm)


def shift_cols(last, first):
    count = lax.axis_size("cols")
    forward = [(i, i + 1) for i in range(count - 1)]
    backward = [(target, source) for source, target in forward]
    return lax.ppermute(last, "cols", forward), lax.ppermute(first, "cols", backward)


def device_index():
    return lax.axis_index("rows") * lax.axis_size("cols") + lax.axis_index("cols")


def swap(value, bit, other=None):
    total = lax.axis_size("rows") * lax.axis_size("cols")
    flip = lambda i: 1 << (other if other is not None and i.bit_count() % 2 else bit) | 1
    return lax.ppermute(value, ("rows", "cols"), [(i, i ^ flip(i)) for i in range(total)])


def local(body, out_shape, name, *operands, **kwargs):
    return pl.pallas_call(
        body,
        out_shape=out_shape,
        in_specs=[pl.BlockSpec(memory_space=pltpu.VMEM)] * len(operands),
        compiler_params=pltpu.CompilerParams(vmem_limit_bytes=8 * 1024 * 1024),
        name=name,
        **kwargs,
    )(*operands)


def side_of(bit, other=None):
    index = device_index()
    if bit > 0:
        side = lax.rem(index // (1 << bit), 2)
        if other is None:
            return side
        return jnp.where(side_of(0) == 0, side, lax.rem(index // (1 << other), 2))
    bits = (lax.axis_size("rows") * lax.axis_size("cols")).bit_length() - 1
    return lax.rem(sum(lax.rem(index // (1 << k), 2) for k in range(bits)), 2)


def rows_at(index, count):
    return pl.ds(pl.multiple_of(index * count, count), count)


waiting = pl.CostEstimate(flops=1_500_000_000, bytes_accessed=100_000, transcendentals=0)
chained = pl.CostEstimate(flops=8_000_000_000, bytes_accessed=100_000, transcendentals=0)


def halve(keep, got, bit, other=None):
    half = keep.shape[0] // 2

    def body(keep_ref, got_ref, send_ref, stay_ref):
        side = side_of(bit, other)
        away, here = rows_at(1 - side, half), rows_at(side, half)
        send_ref[...] = (keep_ref[away, :] + got_ref[away, :].astype(f32)).astype(bf16)
        stay_ref[...] = keep_ref[here, :] + got_ref[here, :].astype(f32)

    shape = (half, keep.shape[1])
    return local(
        body,
        (jax.ShapeDtypeStruct(shape, bf16), jax.ShapeDtypeStruct(shape, f32)),
        "halve",
        keep,
        got,
        cost_estimate=chained,
    )


def add(keep, got):
    def body(keep_ref, got_ref, sum_ref):
        sum_ref[...] = (keep_ref[...].astype(f32) + got_ref[...].astype(f32)).astype(bf16)

    return local(body, jax.ShapeDtypeStruct(got.shape, bf16), "add", keep, got, cost_estimate=chained)


def join(mine, got, bit, other=None, **kwargs):
    def body(mine_ref, got_ref, both_ref):
        side = side_of(bit, other)
        both_ref[:, pl.ds(side, 1)] = mine_ref[...][:, None]
        both_ref[:, pl.ds(1 - side, 1)] = got_ref[...][:, None]

    shape = (mine.shape[0], 2, *mine.shape[1:])
    return local(body, jax.ShapeDtypeStruct(shape, mine.dtype), "join", mine, got, **kwargs)


def join_second(mine, got, bit, other, **kwargs):
    def body(mine_ref, got_ref, both_ref):
        parity, side = side_of(0), side_of(bit, other)

        @pl.when(parity == 0)
        def _():
            both_ref[:, pl.ds(side, 1)] = mine_ref[...][:, None]
            both_ref[:, pl.ds(1 - side, 1)] = got_ref[...][:, None]

        @pl.when(parity == 1)
        def _():
            both_ref[:, :, pl.ds(side, 1)] = mine_ref[...][:, :, None]
            both_ref[:, :, pl.ds(1 - side, 1)] = got_ref[...][:, :, None]

    shape = (mine.shape[0], 2, *mine.shape[1:])
    return local(body, jax.ShapeDtypeStruct(shape, mine.dtype), "join_second", mine, got, **kwargs)


def join_cores(mine, other, **kwargs):
    def body(mine_ref, other_ref, both_ref):
        side = side_of(0)
        for chip in range(mine.shape[0]):
            core = lax.rem(side + chip.bit_count(), 2)
            both_ref[chip, pl.ds(core, 1)] = mine_ref[chip][None]
            both_ref[chip, pl.ds(1 - core, 1)] = other_ref[chip][None]

    shape = (mine.shape[0], 2, *mine.shape[1:])
    return local(body, jax.ShapeDtypeStruct(shape, mine.dtype), "join_cores", mine, other, **kwargs)


class Gather:
    def __init__(self, rows):
        self.rows, self.got, self.last = rows, None, None

    def settle(self, after):
        if self.got is None:
            self.rows, _ = lax.optimization_barrier((self.rows, after))
            return
        share = self.rows.shape[-2:]
        got, _ = lax.optimization_barrier((self.got, after))
        bit, other = self.last
        if bit == 0:
            both = join_cores(self.rows, got, cost_estimate=waiting)
        elif other is None or bit < other:
            mine, got = (part.reshape(-1, 1, *share) for part in (self.rows, got))
            both = join(mine, got, bit, other, cost_estimate=waiting)
        else:
            mine, got = (part.reshape(-1, 2, *share) for part in (self.rows, got))
            both = join_second(mine, got, bit, other, cost_estimate=waiting)
        self.rows, self.got = both.reshape(-1, *share), None

    def step(self, after, bit, other=None):
        self.settle(after)
        self.got, self.last = swap(self.rows, bit, other), (bit, other)


def sum_all(send, keep, beside):
    bits = (lax.axis_size("rows") * lax.axis_size("cols")).bit_length() - 1
    halving = [(1, 2), (2, 1)]
    adding = []
    for bit in range(3, bits, 2):
        adding += [(bit, bit + 1), (bit + 1, bit)] if bit + 1 < bits else [(bit, None)]

    got = beside("cores", send, swap(send, 0))
    for n, pair in enumerate(halving):
        send, keep = halve(keep, got, *pair)
        got = beside(f"halve {n}", send, swap(send, *pair))
    mine = add(keep, got)
    for n, pair in enumerate(adding):
        mine = add(mine, beside(f"add {n}", mine, swap(mine, *pair)))
    for n, pair in enumerate(reversed(halving)):
        got = beside(f"join {n}", mine, swap(mine, *pair))
        mine = join(mine[None], got[None], *pair, cost_estimate=chained).reshape(-1, mine.shape[1])
    return mine, beside("halves", mine, swap(mine, 0))


def gelu_pair(value):
    square = value * value
    tangent = jnp.tanh(value * (gelu_scale + gelu_scale * 0.044715 * square))
    half = 0.5 * value
    plus = 0.5 + 0.5 * tangent
    grad = plus + half * (1.0 - tangent * tangent) * (
        gelu_scale + gelu_scale * 3.0 * 0.044715 * square
    )
    return value * plus, grad


def column(value, c):
    return jnp.concatenate([value[r, c : c + 1] for r in range(value.shape[0])], axis=0)


def rim_kernel(canvas_ref, *out_refs):
    even_ref, odd_ref = out_refs[-2:]
    rows, cols, _ = canvas_ref.shape
    begin = canvas_ref[:, 0:16, :].astype(f32)
    end = canvas_ref[:, cols - 16 :, :].astype(f32)
    for c in range(2):
        pair = column(begin, c), column(end, 14 + c)
        if len(out_refs) == 3:
            out_refs[0][c] = jnp.where(lax.axis_index("cols") == 0, pair[1], pair[0]).astype(bf16)
        else:
            out_refs[0][c], out_refs[1][c] = pair[0].astype(bf16), pair[1].astype(bf16)
    odd = lax.rem(lax.axis_index("rows"), 2)
    for case, low_ref, high_ref in ((0, odd_ref, even_ref), (1, even_ref, odd_ref)):

        @pl.when(odd == case)
        def _():
            for k in range(2):
                at = slice(k * cols, (k + 1) * cols)
                low_ref[at, :], high_ref[at, :] = canvas_ref[k], canvas_ref[rows - 2 + k]


def payload_kernel(target_ref, rows_ref, *refs):
    even_ref, payload_ref, left_ref, right_ref, half_ref = refs[-5:]
    main = rows_ref.shape[0]
    payload_ref[0:main, :] = rows_ref[...]
    odd_ref = payload_ref.at[main:]
    half_ref[0] = target_ref[...].astype(bf16)
    if len(refs) == 6:
        here = lax.axis_index("cols")
        other = refs[0][...].astype(f32)
        left_ref[...] = jnp.where(here == 0, 0.0, other).astype(bf16)
        right_ref[...] = jnp.where(here == 0, other, 0.0).astype(bf16)
    else:
        left_ref[...], right_ref[...] = refs[0][...], refs[1][...]
    beyond = [ref[c].astype(f32) for ref in (left_ref, right_ref) for c in range(2)]
    rows, width = beyond[0].shape

    def rim(r):
        parts = [part[r + k : r + k + 1] for k in range(2) for part in beyond]
        return jnp.concatenate([*parts, jnp.zeros((8, width), f32)], axis=0).astype(bf16)

    odd = lax.rem(lax.axis_index("rows"), 2)
    for case, low_ref, high_ref in ((0, odd_ref, even_ref), (1, even_ref, odd_ref)):

        @pl.when(odd == case)
        def _():
            low_ref[...], high_ref[...] = rim(0), rim(rows - 2)


def moved_rows(row, before, after):
    cols = row.shape[0]
    wide = row.astype(f32)
    place = lax.broadcasted_iota(jnp.int32, (8, row.shape[1]), 0)
    right, left = pltpu.roll(wide, 1, 0), pltpu.roll(wide, cols - 1, 0)
    right = jnp.concatenate([jnp.where(place == 0, before, right[:8]), right[8:]], axis=0)
    left = jnp.concatenate([left[:-8], jnp.where(place == 7, after, left[-8:])], axis=0)
    return right.astype(bf16), row.astype(bf16), left.astype(bf16)


def fill_row(cat_ref, r, row, before, after):
    cols, width = row.shape
    for b, part in enumerate(moved_rows(row, before, after)):
        cat_ref[r * cols : (r + 1) * cols, b * width : (b + 1) * width] = part


def gram_tiles(feat, gram_ref, base_ref=None):
    width = feat.shape[1]
    half = width // 2
    product = functools.partial(
        lax.dot_general,
        dimension_numbers=(((0,), (0,)), ((), ())),
        preferred_element_type=f32,
    )
    upper = product(feat[:, :half], feat)
    lower = product(feat[:, half:], feat[:, half:])
    for n, (i, j) in enumerate(tile_pairs(width)):
        at = slice(n * tile, (n + 1) * tile)
        if i * tile < half:
            part = upper[i * tile : (i + 1) * tile, j * tile : (j + 1) * tile]
        else:
            k, m = i * tile - half, j * tile - half
            part = lower[k : k + tile, m : m + tile]
        gram_ref[at, :] = part if base_ref is None else part + base_ref[at, :]


def inner_kernel(
    shape, own_ref, left_ref, right_ref, kernel_ref, bias_ref,
    feat_ref, slope_ref, gram_ref, row_ref, part_ref, cat_ref,
):
    row_ref[...] = bias_ref[...].astype(f32).reshape(row_ref.shape)
    tile_rows, tile_cols, in_width, out_width, step = shape
    lefts, rights = left_ref[1].astype(f32), right_ref[0].astype(f32)
    for r in range(tile_rows):
        fill_row(cat_ref, r, own_ref[r], lefts[r : r + 1], rights[r : r + 1])
    bias = row_ref[...]
    root = 1.0 / math.sqrt(out_width)
    span = 3 * in_width

    def product(begin, count, a):
        return jnp.dot(
            cat_ref[begin * tile_cols : (begin + count) * tile_cols, :],
            kernel_ref[a * span : (a + 1) * span, :],
            preferred_element_type=f32,
        )

    for h in range(0, tile_rows - 2, step):
        total = bias
        for a in range(3):
            total = total + product(h + a, step, a)
        features, slope = gelu_pair(total)
        at = slice(h * tile_cols, (h + step) * tile_cols)
        feat_ref[at, :] = features.astype(bf16)
        slope_ref[at, :] = (slope * root).astype(bf16)
    low, high = product(0, 2, 2), product(tile_rows - 2, 2, 0)
    ends = product(0, 1, 1), product(tile_rows - 1, 1, 1)
    part_ref[0:tile_cols, :] = low[:tile_cols] + bias
    part_ref[tile_cols : 2 * tile_cols, :] = low[tile_cols:] + ends[0] + bias
    part_ref[2 * tile_cols : 3 * tile_cols, :] = high[:tile_cols] + ends[1] + bias
    part_ref[3 * tile_cols :, :] = high[tile_cols:] + bias
    gram_tiles(feat_ref[...], gram_ref)


def halo_rows(halo_refs, low_ref, high_ref):
    even_ref, odd_ref, even_rim_ref = halo_refs
    row = lax.axis_index("rows")
    odd = lax.rem(row, 2)
    main = even_ref.shape[0]
    for at, even in ((slice(0, main), even_ref), (slice(main, None), even_rim_ref)):
        low_ref[at, :] = jnp.where(odd == 0, odd_ref[at, :], even[...])
        high_ref[at, :] = jnp.where(odd == 0, even[...], odd_ref[at, :])

    @pl.when(row == 0)
    def _():
        low_ref[...] = jnp.zeros_like(low_ref)

    @pl.when(row == lax.axis_size("rows") - 1)
    def _():
        high_ref[...] = jnp.zeros_like(high_ref)


def halves(width):
    return slice(0, width // 2), slice(width // 2, width)


def outer_kernel(
    shape, even_ref, odd_ref, even_rim_ref, kernel_ref, base_ref, part_ref,
    feat_ref, slope_ref, send_ref, keep_ref, low_ref, high_ref, cat_ref, gram_ref,
):
    tile_rows, tile_cols, in_width, out_width, step = shape
    span, main = 3 * in_width, 2 * tile_cols
    halo_rows((even_ref, odd_ref, even_rim_ref), low_ref, high_ref)
    for n, (source, at) in enumerate([(low_ref, tile_cols), (high_ref, 0)]):
        rim = source[main:, :].astype(f32)
        k = 4 * (1 - n)
        fill_row(cat_ref, n, source[at : at + tile_cols, :], rim[k + 1 : k + 2], rim[k + 2 : k + 3])
    root = 1.0 / math.sqrt(out_width)
    for at in halves(out_width):
        for n, a in enumerate([0, 2]):
            rows = slice(n * tile_cols, (n + 1) * tile_cols)
            features, slope = gelu_pair(
                part_ref[(n + 1) * tile_cols : (n + 2) * tile_cols, at]
                + jnp.dot(
                    cat_ref[rows, :],
                    kernel_ref[a * span : (a + 1) * span, at],
                    preferred_element_type=f32,
                )
            )
            feat_ref[rows, at] = features.astype(bf16)
            slope_ref[rows, at] = (slope * root).astype(bf16)
    gram_tiles(feat_ref[...], gram_ref, base_ref)
    half = send_ref.shape[0]
    side = side_of(0)
    send_ref[...] = gram_ref[rows_at(1 - side, half), :].astype(bf16)
    keep_ref[...] = gram_ref[rows_at(side, half), :]


def beyond_kernel(
    shape, own_ref, even_ref, odd_ref, even_rim_ref, left_ref, right_ref, kernel_ref, bias_ref,
    part_ref, feat_ref, slope_ref, low_ref, high_ref, cat_ref, edge_ref,
):
    tile_rows, tile_cols, in_width, out_width, step = shape
    halo_rows((even_ref, odd_ref, even_rim_ref), low_ref, high_ref)
    first = (lax.axis_index("rows") > 0).astype(f32)
    last = (lax.axis_index("rows") < lax.axis_size("rows") - 1).astype(f32)
    left = (lax.axis_index("cols") > 0).astype(f32)
    right = (lax.axis_index("cols") < lax.axis_size("cols") - 1).astype(f32)
    main = 2 * tile_cols
    low_rim, high_rim = low_ref[main:, :].astype(f32), high_ref[main:, :].astype(f32)
    own_begin = column(own_ref[:, 0:16, :].astype(f32), 0)
    own_end = column(own_ref[:, tile_cols - 16 :, :].astype(f32), 15)

    def sides(c, own):
        return jnp.concatenate(
            [low_rim[c : c + 1], low_rim[4 + c : 5 + c], own, high_rim[c : c + 1], high_rim[4 + c : 5 + c]],
            axis=0,
        )

    def ends(c, own):
        c16 = c // 16 * 16
        piece = lambda ref, k: ref[k + c16 : k + c16 + 16, :].astype(f32)[c - c16 : c - c16 + 1]
        rows = [piece(low_ref, 0), piece(low_ref, tile_cols), own]
        return jnp.concatenate([*rows, piece(high_ref, 0), piece(high_ref, tile_cols)], axis=0)

    lefts = [
        sides(0, left_ref[0].astype(f32)), sides(1, left_ref[1].astype(f32)), ends(0, own_begin)
    ]
    rights = [
        ends(tile_cols - 1, own_end), sides(2, right_ref[0].astype(f32)), sides(3, right_ref[1].astype(f32))
    ]
    span = 3 * in_width
    for r, line in enumerate([0, 1, tile_rows + 2, tile_rows + 3]):
        source = low_ref if r < 2 else high_ref
        row = source[r % 2 * tile_cols : (r % 2 + 1) * tile_cols, :]
        fill_row(cat_ref, r, row, lefts[1][line : line + 1], rights[1][line : line + 1])
    blank = jnp.zeros((edge - tile_rows - 2, in_width), f32)
    for a in range(3):
        for b in range(3):
            piece = jnp.concatenate(
                [lefts[b][a : a + tile_rows + 2], blank, rights[b][a : a + tile_rows + 2], blank],
                axis=0,
            )
            at = (3 * a + b) * in_width
            edge_ref[:, at : at + in_width] = piece.astype(bf16)
    root = 1.0 / math.sqrt(out_width)
    line = lax.broadcasted_iota(jnp.int32, (2 * edge, out_width // 2), 0)
    weight = jnp.where(line < edge, left, right)
    weight = jnp.where(line % edge == 0, weight * first, weight)
    weight = jnp.where(line % edge == tile_rows + 1, weight * last, weight)
    for at in halves(out_width):

        def product(begin, a):
            return jnp.dot(
                cat_ref[begin * tile_cols : (begin + 1) * tile_cols, :],
                kernel_ref[a * span : (a + 1) * span, at],
                preferred_element_type=f32,
            )

        totals = [
            part_ref[0:tile_cols, at] + product(0, 0) + product(1, 1),
            part_ref[3 * tile_cols :, at] + product(2, 1) + product(3, 2),
            bias_ref[:, at] + jnp.dot(edge_ref[...], kernel_ref[:, at], preferred_element_type=f32),
        ]
        scales = [first * root, last * root, weight * root]
        for n, (total, scale) in enumerate(zip(totals, scales)):
            features, slope = gelu_pair(total)
            rows = slice(n * tile_cols, n * tile_cols + total.shape[0])
            feat_ref[rows, at] = features.astype(bf16)
            slope_ref[rows, at] = (slope * scale).astype(bf16)


def prepare_kernel(kernel_ref, target_ref, turned_ref, both_ref):
    taps, in_width, out_width = 9, kernel_ref.shape[0] // 9, kernel_ref.shape[1]
    for n in range(taps):
        to = (n // 3 * 3 + 2 - n % 3) * out_width
        turned_ref[to : to + out_width, :] = kernel_ref[n * in_width : (n + 1) * in_width, :].T
    for i, j in tile_pairs(out_width):
        at_i, at_j = slice(i * tile, (i + 1) * tile), slice(j * tile, (j + 1) * tile)
        both = target_ref[at_i, at_j].astype(f32) + target_ref[at_j, at_i].astype(f32).T
        both_ref[at_i, at_j] = both
        if i != j:
            both_ref[at_j, at_i] = both.T


def backward_kernel(
    shape, pixel_total, mine_ref, other_ref, both_ref, in_feat_ref, in_slope_ref, out_feat_ref, out_slope_ref,
    far_feat_ref, far_slope_ref, turned_ref, own_gram_ref, out_ref, gram_ref, full_ref, sym_ref, cat_ref,
):
    tile_rows, tile_cols, in_width, out_width, step = shape
    half = mine_ref.shape[0]
    side = side_of(0)
    gram_ref[rows_at(side, half), :] = mine_ref[...].astype(f32)
    gram_ref[rows_at(1 - side, half), :] = other_ref[...].astype(f32)
    for n, (i, j) in enumerate(tile_pairs(out_width)):
        at_i, at_j = slice(i * tile, (i + 1) * tile), slice(j * tile, (j + 1) * tile)
        gram = gram_ref[n * tile : (n + 1) * tile, :] * (1.0 / pixel_total)
        full_ref[at_i, at_j] = gram
        sym_ref[at_i, at_j] = (2.0 * gram - both_ref[at_i, at_j]).astype(bf16)
        if i != j:
            gram = gram.T
            full_ref[at_j, at_i] = gram
            sym_ref[at_j, at_i] = (2.0 * gram - both_ref[at_j, at_i]).astype(bf16)
    share = own_gram_ref.shape[0]
    start = device_index() * share
    if share % 8 == 0:
        own_gram_ref[...] = full_ref[pl.ds(pl.multiple_of(start, 8), share), :]
    else:
        group = full_ref[pl.ds(pl.multiple_of(start // 8 * 8, 8), 8), :]
        picked = group[0:share]
        for k in range(share, 8, share):
            picked = jnp.where(start % 8 == k, group[k : k + share], picked)
        own_gram_ref[...] = picked

    def grad_of(feat_ref, slope_ref, at):
        product = jnp.dot(feat_ref[at, :], sym_ref[...], preferred_element_type=f32)
        return product * slope_ref[at, :].astype(f32)

    main = 2 * tile_cols
    edges = grad_of(far_feat_ref, far_slope_ref, slice(main, None))
    near, far = (out_feat_ref, out_slope_ref), (far_feat_ref, far_slope_ref)
    lines = [[(*far, 0), (*near, 0)]]
    lines += [
        [(in_feat_ref, in_slope_ref, k * tile_cols) for k in range(h, h + step)]
        for h in range(0, tile_rows - 2, step)
    ]
    lines += [[(*near, tile_cols), (*far, tile_cols)]]
    grads = {}

    def upstream(c):
        pieces = lines[c]
        if pieces[0][0] is pieces[1][0]:
            feat_ref, slope_ref, begin = pieces[0]
            grads[c] = grad_of(feat_ref, slope_ref, slice(begin, begin + step * tile_cols))
        else:
            parts = [grad_of(feat, slope, slice(begin, begin + tile_cols)) for feat, slope, begin in pieces]
            grads[c] = jnp.concatenate(parts, axis=0)

    def fill(c):
        for k in range(step):
            r = c * step + k
            fill_row(
                cat_ref, r, grads[c][k * tile_cols : (k + 1) * tile_cols],
                edges[r : r + 1], edges[edge + r : edge + r + 1],
            )

    span = 3 * out_width

    def convolve(begin, count):
        total = 0.0
        for a in range(3):
            total = total + jnp.dot(
                cat_ref[(begin + 2 - a) * tile_cols : (begin + 2 - a + count) * tile_cols, :],
                turned_ref[a * span : (a + 1) * span, :],
                preferred_element_type=f32,
            )
        out_ref[begin * tile_cols : (begin + count) * tile_cols, :] = total.astype(bf16)

    last = len(lines) - 1
    middle = last // 2
    half_rows = middle * step
    upstream(0)
    for c in range(last):
        upstream(c + 1)
        fill(c)
        if c == middle:
            convolve(0, half_rows)
    fill(last)
    convolve(half_rows, tile_rows - half_rows)


def on_device(canvas, conv_weight, conv_bias, target_gram):
    tile_rows, tile_cols, in_width = canvas.shape
    out_width = conv_weight.shape[3]
    pixel_total = tile_rows * tile_cols * lax.axis_size("rows") * lax.axis_size("cols")
    shape = (tile_rows, tile_cols, in_width, out_width, 2)
    kernel = conv_weight.reshape(9 * in_width, out_width)
    params = pltpu.CompilerParams(vmem_limit_bytes=24 * 1024 * 1024)
    vmem = pl.BlockSpec(memory_space=pltpu.VMEM)
    packed_shape = jax.ShapeDtypeStruct((len(tile_pairs(out_width)) * tile, tile), f32)

    rim_shape = jax.ShapeDtypeStruct((2, tile_rows, in_width), bf16)
    two = lax.axis_size("cols") == 2
    count = lax.axis_size("rows")
    main_shape = jax.ShapeDtypeStruct((2 * tile_cols, in_width), bf16)
    *rims, even, odd = local(
        rim_kernel,
        (*(rim_shape,) * (1 if two else 2), main_shape, main_shape),
        "rims",
        canvas,
        cost_estimate=pl.CostEstimate(flops=4_000_000_000, bytes_accessed=600_000, transcendentals=0),
    )
    if two:
        beyond = [lax.ppermute(rims[0], "cols", [(0, 1), (1, 0)])]
    else:
        beyond = shift_cols(rims[1], rims[0])
    evens, odds = range(0, count, 2), range(1, count, 2)
    even = swap_rows(evens, even)
    payload_shape = jax.ShapeDtypeStruct((2 * tile_cols + edge, in_width), bf16)
    end_shape = jax.ShapeDtypeStruct((edge, in_width), bf16)
    half_shape = jax.ShapeDtypeStruct((1, *target_gram.shape), bf16)
    even_rim, odd, left, right, rows = local(
        payload_kernel,
        (end_shape, payload_shape, rim_shape, rim_shape, half_shape),
        "row_rims",
        target_gram,
        odd,
        *beyond,
    )
    halo = [even, swap_rows(odds, odd), swap_rows(evens, even_rim)]
    bits = (lax.axis_size("rows") * lax.axis_size("cols")).bit_length() - 1
    gather = Gather(rows)
    far = list(reversed(range(3, bits)))
    inner = (tile_rows - 2) * tile_cols
    in_feat, in_slope, in_gram, bias, part = pl.pallas_call(
        functools.partial(inner_kernel, shape),
        out_shape=(
            jax.ShapeDtypeStruct((inner, out_width), bf16),
            jax.ShapeDtypeStruct((inner, out_width), bf16),
            packed_shape,
            jax.ShapeDtypeStruct((1, out_width), f32),
            jax.ShapeDtypeStruct((4 * tile_cols, out_width), f32),
        ),
        in_specs=[vmem] * 5,
        scratch_shapes=[pltpu.VMEM((tile_rows * tile_cols, 3 * in_width), bf16)],
        compiler_params=params,
        name="inner_rows",
        cost_estimate=pl.CostEstimate(
            flops=2 * inner * (9 * in_width + out_width) * out_width,
            bytes_accessed=6_000_000,
            transcendentals=inner * out_width,
        ),
    )(canvas, left, right, kernel, conv_bias)

    half_gram = (packed_shape.shape[0] // 2, tile)
    halo_scratch = [pltpu.VMEM(payload_shape.shape, bf16), pltpu.VMEM(payload_shape.shape, bf16)]
    out_feat, out_slope, send, keep = pl.pallas_call(
        functools.partial(outer_kernel, shape),
        out_shape=(
            jax.ShapeDtypeStruct((2 * tile_cols, out_width), bf16),
            jax.ShapeDtypeStruct((2 * tile_cols, out_width), bf16),
            jax.ShapeDtypeStruct(half_gram, bf16),
            jax.ShapeDtypeStruct(half_gram, f32),
        ),
        in_specs=[vmem] * 6,
        scratch_shapes=[
            *halo_scratch,
            pltpu.VMEM((2 * tile_cols, 3 * in_width), bf16),
            pltpu.VMEM(packed_shape.shape, f32),
        ],
        compiler_params=params,
        name="outer_rows",
    )(*halo, kernel, in_gram, part)

    exchanges = {
        "halve 0": [(bit,) for bit in far[:1]],
        "halve 1": [(bit,) for bit in far[1:]],
        "add 0": [(1, 2)],
        "add 1": [(2, 1)],
        "join 0": [(0,)],
    }
    prepared, far_pixels = [], []

    def beside(name, sent, got):
        if name == "join 1":
            outer = 2 * tile_cols + 2 * edge
            rim_sums, _ = lax.optimization_barrier((part, sent))
            far_pixels.extend(
                pl.pallas_call(
                    functools.partial(beyond_kernel, shape),
                    out_shape=(jax.ShapeDtypeStruct((outer, out_width), bf16),) * 2,
                    in_specs=[vmem] * 9,
                    scratch_shapes=[
                        *halo_scratch,
                        pltpu.VMEM((4 * tile_cols, 3 * in_width), bf16),
                        pltpu.VMEM((2 * edge, 9 * in_width), bf16),
                    ],
                    compiler_params=params,
                    name="beyond",
                    cost_estimate=chained,
                )(canvas, *halo, left, right, kernel, bias, rim_sums)
            )
            gather.settle(sent)
            got, gather.rows, *_ = lax.optimization_barrier((got, gather.rows, *far_pixels))
            return got
        for bit in exchanges.get(name, []):
            gather.step(sent, *bit)
        if name == "join 0":
            got, gather.rows = lax.optimization_barrier((got, gather.rows))
        if name != "halves":
            return got
        gather.settle(sent)
        prepared.extend(
            pl.pallas_call(
                prepare_kernel,
                out_shape=(
                    jax.ShapeDtypeStruct((9 * out_width, in_width), bf16),
                    jax.ShapeDtypeStruct((out_width, out_width), f32),
                ),
                in_specs=[vmem] * 2,
                compiler_params=params,
                name="prepare",
                cost_estimate=pl.CostEstimate(
                    flops=2_000_000_000, bytes_accessed=6_000_000, transcendentals=0
                ),
            )(kernel, gather.rows.reshape(out_width, out_width))
        )
        return lax.optimization_barrier((got, *prepared))[0]

    mine, other = sum_all(send, keep, beside)
    turned, both = prepared
    far_feat, far_slope = far_pixels
    own_gram, grad = pl.pallas_call(
        functools.partial(backward_kernel, shape, pixel_total),
        out_shape=(
            jax.ShapeDtypeStruct(target_gram.shape, f32),
            jax.ShapeDtypeStruct((tile_rows * tile_cols, in_width), bf16),
        ),
        in_specs=[vmem] * 10,
        scratch_shapes=[
            pltpu.VMEM(packed_shape.shape, f32),
            pltpu.VMEM((out_width, out_width), f32),
            pltpu.VMEM((out_width, out_width), bf16),
            pltpu.VMEM(((tile_rows + 2) * tile_cols, 3 * out_width), bf16),
        ],
        compiler_params=params,
        name="grad_conv",
    )(mine, other, both, in_feat, in_slope, out_feat, out_slope, far_feat, far_slope, turned)
    return own_gram, grad.reshape(tile_rows, tile_cols, in_width)


def solution(mesh):
    return jax.shard_map(
        on_device,
        mesh=mesh,
        in_specs=(P("rows", "cols", None), P(), P(), P(("rows", "cols"), None)),
        out_specs=(P(("rows", "cols"), None), P("rows", "cols", None)),
        check_vma=False,
    )
```

```python
import functools
import math

import jax
import jax.numpy as jnp
from jax import lax
from jax.experimental import pallas as pl
from jax.experimental.pallas import tpu as pltpu
from jax.sharding import PartitionSpec as P

gelu_scale = math.sqrt(2.0 / math.pi)
tile = 128
edge = 16
f32, bf16 = jnp.float32, jnp.bfloat16


def tile_pairs(width):
    count = width // tile
    return [(i, j) for i in range(count) for j in range(i, count)]


def swap_rows(low, value):
    count, cols = lax.axis_size("rows"), lax.axis_size("cols")
    partner = {i: i + 1 for i in low if i + 1 < count}
    partner.update({i + 1: i for i in low if i + 1 < count})
    perm = [
        (r * cols + c, partner[r] * cols + c if r in partner else r * cols + (c ^ 1))
        for r in range(count)
        for c in range(cols)
    ]
    return lax.ppermute(value, ("rows", "cols"), perm)


def shift_cols(last, first):
    count = lax.axis_size("cols")
    forward = [(i, i + 1) for i in range(count - 1)]
    backward = [(target, source) for source, target in forward]
    return lax.ppermute(last, "cols", forward), lax.ppermute(first, "cols", backward)


def device_index():
    return lax.axis_index("rows") * lax.axis_size("cols") + lax.axis_index("cols")


def swap(value, bit, other=None):
    total = lax.axis_size("rows") * lax.axis_size("cols")
    flip = lambda i: 1 << (other if other is not None and i.bit_count() % 2 else bit) | 1
    return lax.ppermute(value, ("rows", "cols"), [(i, i ^ flip(i)) for i in range(total)])


def local(body, out_shape, name, *operands, **kwargs):
    return pl.pallas_call(
        body,
        out_shape=out_shape,
        in_specs=[pl.BlockSpec(memory_space=pltpu.VMEM)] * len(operands),
        compiler_params=pltpu.CompilerParams(vmem_limit_bytes=8 * 1024 * 1024),
        name=name,
        **kwargs,
    )(*operands)


def side_of(bit, other=None):
    index = device_index()
    if bit > 0:
        side = lax.rem(index // (1 << bit), 2)
        if other is None:
            return side
        return jnp.where(side_of(0) == 0, side, lax.rem(index // (1 << other), 2))
    bits = (lax.axis_size("rows") * lax.axis_size("cols")).bit_length() - 1
    return lax.rem(sum(lax.rem(index // (1 << k), 2) for k in range(bits)), 2)


def rows_at(index, count):
    return pl.ds(pl.multiple_of(index * count, count), count)


waiting = pl.CostEstimate(flops=1_500_000_000, bytes_accessed=100_000, transcendentals=0)
chained = pl.CostEstimate(flops=8_000_000_000, bytes_accessed=100_000, transcendentals=0)


def halve(keep, got, bit, other=None):
    half = keep.shape[0] // 2

    def body(keep_ref, got_ref, send_ref, stay_ref):
        side = side_of(bit, other)
        away, here = rows_at(1 - side, half), rows_at(side, half)
        send_ref[...] = (keep_ref[away, :] + got_ref[away, :].astype(f32)).astype(bf16)
        stay_ref[...] = keep_ref[here, :] + got_ref[here, :].astype(f32)

    shape = (half, keep.shape[1])
    return local(
        body,
        (jax.ShapeDtypeStruct(shape, bf16), jax.ShapeDtypeStruct(shape, f32)),
        "halve",
        keep,
        got,
        cost_estimate=chained,
    )


def add(keep, got):
    def body(keep_ref, got_ref, sum_ref):
        sum_ref[...] = (keep_ref[...].astype(f32) + got_ref[...].astype(f32)).astype(bf16)

    return local(body, jax.ShapeDtypeStruct(got.shape, bf16), "add", keep, got, cost_estimate=chained)


def join(mine, got, bit, other=None, **kwargs):
    def body(mine_ref, got_ref, both_ref):
        side = side_of(bit, other)
        both_ref[:, pl.ds(side, 1)] = mine_ref[...][:, None]
        both_ref[:, pl.ds(1 - side, 1)] = got_ref[...][:, None]

    shape = (mine.shape[0], 2, *mine.shape[1:])
    return local(body, jax.ShapeDtypeStruct(shape, mine.dtype), "join", mine, got, **kwargs)


def join_second(mine, got, bit, other, **kwargs):
    def body(mine_ref, got_ref, both_ref):
        parity, side = side_of(0), side_of(bit, other)

        @pl.when(parity == 0)
        def _():
            both_ref[:, pl.ds(side, 1)] = mine_ref[...][:, None]
            both_ref[:, pl.ds(1 - side, 1)] = got_ref[...][:, None]

        @pl.when(parity == 1)
        def _():
            both_ref[:, :, pl.ds(side, 1)] = mine_ref[...][:, :, None]
            both_ref[:, :, pl.ds(1 - side, 1)] = got_ref[...][:, :, None]

    shape = (mine.shape[0], 2, *mine.shape[1:])
    return local(body, jax.ShapeDtypeStruct(shape, mine.dtype), "join_second", mine, got, **kwargs)


def join_cores(mine, other, **kwargs):
    def body(mine_ref, other_ref, both_ref):
        side = side_of(0)
        for chip in range(mine.shape[0]):
            core = lax.rem(side + chip.bit_count(), 2)
            both_ref[chip, pl.ds(core, 1)] = mine_ref[chip][None]
            both_ref[chip, pl.ds(1 - core, 1)] = other_ref[chip][None]

    shape = (mine.shape[0], 2, *mine.shape[1:])
    return local(body, jax.ShapeDtypeStruct(shape, mine.dtype), "join_cores", mine, other, **kwargs)


class Gather:
    def __init__(self, rows):
        self.rows, self.got, self.last = rows, None, None

    def settle(self, after):
        if self.got is None:
            self.rows, _ = lax.optimization_barrier((self.rows, after))
            return
        share = self.rows.shape[-2:]
        got, _ = lax.optimization_barrier((self.got, after))
        bit, other = self.last
        if bit == 0:
            both = join_cores(self.rows, got, cost_estimate=waiting)
        elif other is None or bit < other:
            mine, got = (part.reshape(-1, 1, *share) for part in (self.rows, got))
            both = join(mine, got, bit, other, cost_estimate=waiting)
        else:
            mine, got = (part.reshape(-1, 2, *share) for part in (self.rows, got))
            both = join_second(mine, got, bit, other, cost_estimate=waiting)
        self.rows, self.got = both.reshape(-1, *share), None

    def step(self, after, bit, other=None):
        self.settle(after)
        self.got, self.last = swap(self.rows, bit, other), (bit, other)


def sum_all(send, keep, beside):
    bits = (lax.axis_size("rows") * lax.axis_size("cols")).bit_length() - 1
    halving = [(1, 2), (2, 1)]
    adding = [(bit,) for bit in range(3, bits)]

    got = beside("cores", send, swap(send, 0))
    for n, pair in enumerate(halving):
        send, keep = halve(keep, got, *pair)
        got = beside(f"halve {n}", send, swap(send, *pair))
    mine = add(keep, got)
    for n, pair in enumerate(adding):
        mine = add(mine, beside(f"add {n}", mine, swap(mine, *pair)))
    for n, pair in enumerate(reversed(halving)):
        got = beside(f"join {n}", mine, swap(mine, *pair))
        mine = join(mine[None], got[None], *pair, cost_estimate=chained).reshape(-1, mine.shape[1])
    return mine, beside("halves", mine, swap(mine, 0))


def gelu_pair(value):
    square = value * value
    tangent = jnp.tanh(value * (gelu_scale + gelu_scale * 0.044715 * square))
    half = 0.5 * value
    plus = 0.5 + 0.5 * tangent
    grad = plus + half * (1.0 - tangent * tangent) * (
        gelu_scale + gelu_scale * 3.0 * 0.044715 * square
    )
    return value * plus, grad


def column(value, c):
    return jnp.concatenate([value[r, c : c + 1] for r in range(value.shape[0])], axis=0)


def rim_kernel(canvas_ref, *out_refs):
    even_ref, odd_ref = out_refs[-2:]
    rows, cols, _ = canvas_ref.shape
    begin = canvas_ref[:, 0:16, :].astype(f32)
    end = canvas_ref[:, cols - 16 :, :].astype(f32)
    for c in range(2):
        pair = column(begin, c), column(end, 14 + c)
        if len(out_refs) == 3:
            out_refs[0][c] = jnp.where(lax.axis_index("cols") == 0, pair[1], pair[0]).astype(bf16)
        else:
            out_refs[0][c], out_refs[1][c] = pair[0].astype(bf16), pair[1].astype(bf16)
    odd = lax.rem(lax.axis_index("rows"), 2)
    for case, low_ref, high_ref in ((0, odd_ref, even_ref), (1, even_ref, odd_ref)):

        @pl.when(odd == case)
        def _():
            for k in range(2):
                at = slice(k * cols, (k + 1) * cols)
                low_ref[at, :], high_ref[at, :] = canvas_ref[k], canvas_ref[rows - 2 + k]


def payload_kernel(target_ref, rows_ref, *refs):
    even_ref, payload_ref, left_ref, right_ref, half_ref = refs[-5:]
    main = rows_ref.shape[0]
    payload_ref[0:main, :] = rows_ref[...]
    odd_ref = payload_ref.at[main:]
    half_ref[0] = target_ref[...].astype(bf16)
    if len(refs) == 6:
        here = lax.axis_index("cols")
        other = refs[0][...].astype(f32)
        left_ref[...] = jnp.where(here == 0, 0.0, other).astype(bf16)
        right_ref[...] = jnp.where(here == 0, other, 0.0).astype(bf16)
    else:
        left_ref[...], right_ref[...] = refs[0][...], refs[1][...]
    beyond = [ref[c].astype(f32) for ref in (left_ref, right_ref) for c in range(2)]
    rows, width = beyond[0].shape

    def rim(r):
        parts = [part[r + k : r + k + 1] for k in range(2) for part in beyond]
        return jnp.concatenate([*parts, jnp.zeros((8, width), f32)], axis=0).astype(bf16)

    odd = lax.rem(lax.axis_index("rows"), 2)
    for case, low_ref, high_ref in ((0, odd_ref, even_ref), (1, even_ref, odd_ref)):

        @pl.when(odd == case)
        def _():
            low_ref[...], high_ref[...] = rim(0), rim(rows - 2)


def moved_rows(row, before, after):
    cols = row.shape[0]
    wide = row.astype(f32)
    place = lax.broadcasted_iota(jnp.int32, (8, row.shape[1]), 0)
    right, left = pltpu.roll(wide, 1, 0), pltpu.roll(wide, cols - 1, 0)
    right = jnp.concatenate([jnp.where(place == 0, before, right[:8]), right[8:]], axis=0)
    left = jnp.concatenate([left[:-8], jnp.where(place == 7, after, left[-8:])], axis=0)
    return right.astype(bf16), row.astype(bf16), left.astype(bf16)


def fill_row(cat_ref, r, row, before, after):
    cols, width = row.shape
    for b, part in enumerate(moved_rows(row, before, after)):
        cat_ref[r * cols : (r + 1) * cols, b * width : (b + 1) * width] = part


def gram_tiles(feat, gram_ref, base_ref=None):
    width = feat.shape[1]
    half = width // 2
    product = functools.partial(
        lax.dot_general,
        dimension_numbers=(((0,), (0,)), ((), ())),
        preferred_element_type=f32,
    )
    upper = product(feat[:, :half], feat)
    lower = product(feat[:, half:], feat[:, half:])
    for n, (i, j) in enumerate(tile_pairs(width)):
        at = slice(n * tile, (n + 1) * tile)
        if i * tile < half:
            part = upper[i * tile : (i + 1) * tile, j * tile : (j + 1) * tile]
        else:
            k, m = i * tile - half, j * tile - half
            part = lower[k : k + tile, m : m + tile]
        gram_ref[at, :] = part if base_ref is None else part + base_ref[at, :]


def inner_kernel(
    shape, own_ref, left_ref, right_ref, kernel_ref, bias_ref,
    feat_ref, slope_ref, gram_ref, row_ref, part_ref, cat_ref,
):
    row_ref[...] = bias_ref[...].astype(f32).reshape(row_ref.shape)
    tile_rows, tile_cols, in_width, out_width, step = shape
    lefts, rights = left_ref[1].astype(f32), right_ref[0].astype(f32)
    for r in range(tile_rows):
        fill_row(cat_ref, r, own_ref[r], lefts[r : r + 1], rights[r : r + 1])
    bias = row_ref[...]
    root = 1.0 / math.sqrt(out_width)
    span = 3 * in_width

    def product(begin, count, a):
        return jnp.dot(
            cat_ref[begin * tile_cols : (begin + count) * tile_cols, :],
            kernel_ref[a * span : (a + 1) * span, :],
            preferred_element_type=f32,
        )

    for h in range(0, tile_rows - 2, step):
        total = bias
        for a in range(3):
            total = total + product(h + a, step, a)
        features, slope = gelu_pair(total)
        at = slice(h * tile_cols, (h + step) * tile_cols)
        feat_ref[at, :] = features.astype(bf16)
        slope_ref[at, :] = (slope * root).astype(bf16)
    low, high = product(0, 2, 2), product(tile_rows - 2, 2, 0)
    ends = product(0, 1, 1), product(tile_rows - 1, 1, 1)
    part_ref[0:tile_cols, :] = low[:tile_cols] + bias
    part_ref[tile_cols : 2 * tile_cols, :] = low[tile_cols:] + ends[0] + bias
    part_ref[2 * tile_cols : 3 * tile_cols, :] = high[:tile_cols] + ends[1] + bias
    part_ref[3 * tile_cols :, :] = high[tile_cols:] + bias
    gram_tiles(feat_ref[...], gram_ref)


def halo_rows(halo_refs, low_ref, high_ref):
    even_ref, odd_ref, even_rim_ref = halo_refs
    row = lax.axis_index("rows")
    odd = lax.rem(row, 2)
    main = even_ref.shape[0]
    for at, even in ((slice(0, main), even_ref), (slice(main, None), even_rim_ref)):
        low_ref[at, :] = jnp.where(odd == 0, odd_ref[at, :], even[...])
        high_ref[at, :] = jnp.where(odd == 0, even[...], odd_ref[at, :])

    @pl.when(row == 0)
    def _():
        low_ref[...] = jnp.zeros_like(low_ref)

    @pl.when(row == lax.axis_size("rows") - 1)
    def _():
        high_ref[...] = jnp.zeros_like(high_ref)


def halves(width):
    return slice(0, width // 2), slice(width // 2, width)


def outer_kernel(
    shape, even_ref, odd_ref, even_rim_ref, kernel_ref, base_ref, part_ref,
    feat_ref, slope_ref, send_ref, keep_ref, low_ref, high_ref, cat_ref, gram_ref,
):
    tile_rows, tile_cols, in_width, out_width, step = shape
    span, main = 3 * in_width, 2 * tile_cols
    halo_rows((even_ref, odd_ref, even_rim_ref), low_ref, high_ref)
    for n, (source, at) in enumerate([(low_ref, tile_cols), (high_ref, 0)]):
        rim = source[main:, :].astype(f32)
        k = 4 * (1 - n)
        fill_row(cat_ref, n, source[at : at + tile_cols, :], rim[k + 1 : k + 2], rim[k + 2 : k + 3])
    root = 1.0 / math.sqrt(out_width)
    for at in halves(out_width):
        for n, a in enumerate([0, 2]):
            rows = slice(n * tile_cols, (n + 1) * tile_cols)
            features, slope = gelu_pair(
                part_ref[(n + 1) * tile_cols : (n + 2) * tile_cols, at]
                + jnp.dot(
                    cat_ref[rows, :],
                    kernel_ref[a * span : (a + 1) * span, at],
                    preferred_element_type=f32,
                )
            )
            feat_ref[rows, at] = features.astype(bf16)
            slope_ref[rows, at] = (slope * root).astype(bf16)
    gram_tiles(feat_ref[...], gram_ref, base_ref)
    half = send_ref.shape[0]
    side = side_of(0)
    send_ref[...] = gram_ref[rows_at(1 - side, half), :].astype(bf16)
    keep_ref[...] = gram_ref[rows_at(side, half), :]


def beyond_kernel(
    shape, own_ref, even_ref, odd_ref, even_rim_ref, left_ref, right_ref, kernel_ref, bias_ref,
    part_ref, feat_ref, slope_ref, low_ref, high_ref, cat_ref, edge_ref,
):
    tile_rows, tile_cols, in_width, out_width, step = shape
    halo_rows((even_ref, odd_ref, even_rim_ref), low_ref, high_ref)
    first = (lax.axis_index("rows") > 0).astype(f32)
    last = (lax.axis_index("rows") < lax.axis_size("rows") - 1).astype(f32)
    left = (lax.axis_index("cols") > 0).astype(f32)
    right = (lax.axis_index("cols") < lax.axis_size("cols") - 1).astype(f32)
    main = 2 * tile_cols
    low_rim, high_rim = low_ref[main:, :].astype(f32), high_ref[main:, :].astype(f32)
    own_begin = column(own_ref[:, 0:16, :].astype(f32), 0)
    own_end = column(own_ref[:, tile_cols - 16 :, :].astype(f32), 15)

    def sides(c, own):
        return jnp.concatenate(
            [low_rim[c : c + 1], low_rim[4 + c : 5 + c], own, high_rim[c : c + 1], high_rim[4 + c : 5 + c]],
            axis=0,
        )

    def ends(c, own):
        c16 = c // 16 * 16
        piece = lambda ref, k: ref[k + c16 : k + c16 + 16, :].astype(f32)[c - c16 : c - c16 + 1]
        rows = [piece(low_ref, 0), piece(low_ref, tile_cols), own]
        return jnp.concatenate([*rows, piece(high_ref, 0), piece(high_ref, tile_cols)], axis=0)

    lefts = [
        sides(0, left_ref[0].astype(f32)), sides(1, left_ref[1].astype(f32)), ends(0, own_begin)
    ]
    rights = [
        ends(tile_cols - 1, own_end), sides(2, right_ref[0].astype(f32)), sides(3, right_ref[1].astype(f32))
    ]
    span = 3 * in_width
    for r, line in enumerate([0, 1, tile_rows + 2, tile_rows + 3]):
        source = low_ref if r < 2 else high_ref
        row = source[r % 2 * tile_cols : (r % 2 + 1) * tile_cols, :]
        fill_row(cat_ref, r, row, lefts[1][line : line + 1], rights[1][line : line + 1])
    blank = jnp.zeros((edge - tile_rows - 2, in_width), f32)
    for a in range(3):
        for b in range(3):
            piece = jnp.concatenate(
                [lefts[b][a : a + tile_rows + 2], blank, rights[b][a : a + tile_rows + 2], blank],
                axis=0,
            )
            at = (3 * a + b) * in_width
            edge_ref[:, at : at + in_width] = piece.astype(bf16)
    root = 1.0 / math.sqrt(out_width)
    line = lax.broadcasted_iota(jnp.int32, (2 * edge, out_width // 2), 0)
    weight = jnp.where(line < edge, left, right)
    weight = jnp.where(line % edge == 0, weight * first, weight)
    weight = jnp.where(line % edge == tile_rows + 1, weight * last, weight)
    for at in halves(out_width):

        def product(begin, a):
            return jnp.dot(
                cat_ref[begin * tile_cols : (begin + 1) * tile_cols, :],
                kernel_ref[a * span : (a + 1) * span, at],
                preferred_element_type=f32,
            )

        totals = [
            part_ref[0:tile_cols, at] + product(0, 0) + product(1, 1),
            part_ref[3 * tile_cols :, at] + product(2, 1) + product(3, 2),
            bias_ref[:, at] + jnp.dot(edge_ref[...], kernel_ref[:, at], preferred_element_type=f32),
        ]
        scales = [first * root, last * root, weight * root]
        for n, (total, scale) in enumerate(zip(totals, scales)):
            features, slope = gelu_pair(total)
            rows = slice(n * tile_cols, n * tile_cols + total.shape[0])
            feat_ref[rows, at] = features.astype(bf16)
            slope_ref[rows, at] = (slope * scale).astype(bf16)


def turn_kernel(kernel_ref, turned_ref):
    taps, in_width, out_width = 9, kernel_ref.shape[0] // 9, kernel_ref.shape[1]
    for n in range(taps):
        to = (n // 3 * 3 + 2 - n % 3) * out_width
        turned_ref[to : to + out_width, :] = kernel_ref[n * in_width : (n + 1) * in_width, :].T


def prepare_kernel(target_ref, both_ref):
    for i, j in tile_pairs(target_ref.shape[0]):
        at_i, at_j = slice(i * tile, (i + 1) * tile), slice(j * tile, (j + 1) * tile)
        both = target_ref[at_i, at_j].astype(f32) + target_ref[at_j, at_i].astype(f32).T
        both_ref[at_i, at_j] = both
        if i != j:
            both_ref[at_j, at_i] = both.T


def backward_kernel(
    shape, pixel_total, mine_ref, other_ref, both_ref, in_feat_ref, in_slope_ref, out_feat_ref, out_slope_ref,
    far_feat_ref, far_slope_ref, turned_ref, own_gram_ref, out_ref, gram_ref, full_ref, sym_ref, cat_ref,
):
    tile_rows, tile_cols, in_width, out_width, step = shape
    half = mine_ref.shape[0]
    side = side_of(0)
    gram_ref[rows_at(side, half), :] = mine_ref[...].astype(f32)
    gram_ref[rows_at(1 - side, half), :] = other_ref[...].astype(f32)
    for n, (i, j) in enumerate(tile_pairs(out_width)):
        at_i, at_j = slice(i * tile, (i + 1) * tile), slice(j * tile, (j + 1) * tile)
        gram = gram_ref[n * tile : (n + 1) * tile, :] * (1.0 / pixel_total)
        full_ref[at_i, at_j] = gram
        sym_ref[at_i, at_j] = (2.0 * gram - both_ref[at_i, at_j]).astype(bf16)
        if i != j:
            gram = gram.T
            full_ref[at_j, at_i] = gram
            sym_ref[at_j, at_i] = (2.0 * gram - both_ref[at_j, at_i]).astype(bf16)
    share = own_gram_ref.shape[0]
    start = device_index() * share
    if share % 8 == 0:
        own_gram_ref[...] = full_ref[pl.ds(pl.multiple_of(start, 8), share), :]
    else:
        group = full_ref[pl.ds(pl.multiple_of(start // 8 * 8, 8), 8), :]
        picked = group[0:share]
        for k in range(share, 8, share):
            picked = jnp.where(start % 8 == k, group[k : k + share], picked)
        own_gram_ref[...] = picked

    def grad_of(feat_ref, slope_ref, at):
        product = jnp.dot(feat_ref[at, :], sym_ref[...], preferred_element_type=f32)
        return product * slope_ref[at, :].astype(f32)

    main = 2 * tile_cols
    edges = grad_of(far_feat_ref, far_slope_ref, slice(main, None))
    near, far = (out_feat_ref, out_slope_ref), (far_feat_ref, far_slope_ref)
    lines = [[(*far, 0), (*near, 0)]]
    lines += [
        [(in_feat_ref, in_slope_ref, k * tile_cols) for k in range(h, h + step)]
        for h in range(0, tile_rows - 2, step)
    ]
    lines += [[(*near, tile_cols), (*far, tile_cols)]]
    grads = {}

    def upstream(c):
        pieces = lines[c]
        if pieces[0][0] is pieces[1][0]:
            feat_ref, slope_ref, begin = pieces[0]
            grads[c] = grad_of(feat_ref, slope_ref, slice(begin, begin + step * tile_cols))
        else:
            parts = [grad_of(feat, slope, slice(begin, begin + tile_cols)) for feat, slope, begin in pieces]
            grads[c] = jnp.concatenate(parts, axis=0)

    def fill(c):
        for k in range(step):
            r = c * step + k
            fill_row(
                cat_ref, r, grads[c][k * tile_cols : (k + 1) * tile_cols],
                edges[r : r + 1], edges[edge + r : edge + r + 1],
            )

    span = 3 * out_width

    def convolve(begin, count):
        total = 0.0
        for a in range(3):
            total = total + jnp.dot(
                cat_ref[(begin + 2 - a) * tile_cols : (begin + 2 - a + count) * tile_cols, :],
                turned_ref[a * span : (a + 1) * span, :],
                preferred_element_type=f32,
            )
        out_ref[begin * tile_cols : (begin + count) * tile_cols, :] = total.astype(bf16)

    last = len(lines) - 1
    middle = last // 2
    half_rows = middle * step
    upstream(0)
    for c in range(last):
        upstream(c + 1)
        fill(c)
        if c == middle:
            convolve(0, half_rows)
    fill(last)
    convolve(half_rows, tile_rows - half_rows)


def on_device(canvas, conv_weight, conv_bias, target_gram):
    tile_rows, tile_cols, in_width = canvas.shape
    out_width = conv_weight.shape[3]
    pixel_total = tile_rows * tile_cols * lax.axis_size("rows") * lax.axis_size("cols")
    shape = (tile_rows, tile_cols, in_width, out_width, 2)
    kernel = conv_weight.reshape(9 * in_width, out_width)
    params = pltpu.CompilerParams(vmem_limit_bytes=24 * 1024 * 1024)
    vmem = pl.BlockSpec(memory_space=pltpu.VMEM)
    packed_shape = jax.ShapeDtypeStruct((len(tile_pairs(out_width)) * tile, tile), f32)

    rim_shape = jax.ShapeDtypeStruct((2, tile_rows, in_width), bf16)
    two = lax.axis_size("cols") == 2
    count = lax.axis_size("rows")
    main_shape = jax.ShapeDtypeStruct((2 * tile_cols, in_width), bf16)
    *rims, even, odd = local(
        rim_kernel,
        (*(rim_shape,) * (1 if two else 2), main_shape, main_shape),
        "rims",
        canvas,
        cost_estimate=pl.CostEstimate(flops=4_000_000_000, bytes_accessed=600_000, transcendentals=0),
    )
    if two:
        beyond = [lax.ppermute(rims[0], "cols", [(0, 1), (1, 0)])]
    else:
        beyond = shift_cols(rims[1], rims[0])
    evens, odds = range(0, count, 2), range(1, count, 2)
    even = swap_rows(evens, even)
    payload_shape = jax.ShapeDtypeStruct((2 * tile_cols + edge, in_width), bf16)
    end_shape = jax.ShapeDtypeStruct((edge, in_width), bf16)
    half_shape = jax.ShapeDtypeStruct((1, *target_gram.shape), bf16)
    even_rim, odd, left, right, rows = local(
        payload_kernel,
        (end_shape, payload_shape, rim_shape, rim_shape, half_shape),
        "row_rims",
        target_gram,
        odd,
        *beyond,
    )
    halo = [even, swap_rows(odds, odd), swap_rows(evens, even_rim)]
    bits = (lax.axis_size("rows") * lax.axis_size("cols")).bit_length() - 1
    gather = Gather(rows)
    far = list(reversed(range(3, bits)))
    inner = (tile_rows - 2) * tile_cols
    in_feat, in_slope, in_gram, bias, part = pl.pallas_call(
        functools.partial(inner_kernel, shape),
        out_shape=(
            jax.ShapeDtypeStruct((inner, out_width), bf16),
            jax.ShapeDtypeStruct((inner, out_width), bf16),
            packed_shape,
            jax.ShapeDtypeStruct((1, out_width), f32),
            jax.ShapeDtypeStruct((4 * tile_cols, out_width), f32),
        ),
        in_specs=[vmem] * 5,
        scratch_shapes=[pltpu.VMEM((tile_rows * tile_cols, 3 * in_width), bf16)],
        compiler_params=params,
        name="inner_rows",
        cost_estimate=pl.CostEstimate(
            flops=2 * inner * (9 * in_width + out_width) * out_width,
            bytes_accessed=6_000_000,
            transcendentals=inner * out_width,
        ),
    )(canvas, left, right, kernel, conv_bias)

    weights, in_gram = lax.optimization_barrier((kernel, in_gram))
    turned = local(
        turn_kernel,
        jax.ShapeDtypeStruct((9 * out_width, in_width), bf16),
        "turn",
        weights,
        cost_estimate=waiting,
    )
    in_gram, turned = lax.optimization_barrier((in_gram, turned))
    half_gram = (packed_shape.shape[0] // 2, tile)
    halo_scratch = [pltpu.VMEM(payload_shape.shape, bf16), pltpu.VMEM(payload_shape.shape, bf16)]
    out_feat, out_slope, send, keep = pl.pallas_call(
        functools.partial(outer_kernel, shape),
        out_shape=(
            jax.ShapeDtypeStruct((2 * tile_cols, out_width), bf16),
            jax.ShapeDtypeStruct((2 * tile_cols, out_width), bf16),
            jax.ShapeDtypeStruct(half_gram, bf16),
            jax.ShapeDtypeStruct(half_gram, f32),
        ),
        in_specs=[vmem] * 6,
        scratch_shapes=[
            *halo_scratch,
            pltpu.VMEM((2 * tile_cols, 3 * in_width), bf16),
            pltpu.VMEM(packed_shape.shape, f32),
        ],
        compiler_params=params,
        name="outer_rows",
    )(*halo, kernel, in_gram, part)

    exchanges = {
        "halve 0": [(bit,) for bit in far[:1]],
        "halve 1": [(bit,) for bit in far[1:]],
        "add 0": [(1, 2)],
        "add 1": [(2, 1)],
        "join 0": [(0,)],
    }
    prepared, far_pixels = [], []

    def beside(name, sent, got):
        if name == "join 1":
            outer = 2 * tile_cols + 2 * edge
            rim_sums, _ = lax.optimization_barrier((part, sent))
            far_pixels.extend(
                pl.pallas_call(
                    functools.partial(beyond_kernel, shape),
                    out_shape=(jax.ShapeDtypeStruct((outer, out_width), bf16),) * 2,
                    in_specs=[vmem] * 9,
                    scratch_shapes=[
                        *halo_scratch,
                        pltpu.VMEM((4 * tile_cols, 3 * in_width), bf16),
                        pltpu.VMEM((2 * edge, 9 * in_width), bf16),
                    ],
                    compiler_params=params,
                    name="beyond",
                    cost_estimate=chained,
                )(canvas, *halo, left, right, kernel, bias, rim_sums)
            )
            gather.settle(sent)
            got, gather.rows, *_ = lax.optimization_barrier((got, gather.rows, *far_pixels))
            return got
        for bit in exchanges.get(name, []):
            gather.step(sent, *bit)
        if name == "join 0":
            got, gather.rows = lax.optimization_barrier((got, gather.rows))
        if name != "halves":
            return got
        gather.settle(sent)
        prepared.append(
            local(
                prepare_kernel,
                jax.ShapeDtypeStruct((out_width, out_width), f32),
                "prepare",
                gather.rows.reshape(out_width, out_width),
                cost_estimate=waiting,
            )
        )
        return lax.optimization_barrier((got, *prepared))[0]

    mine, other = sum_all(send, keep, beside)
    (both,) = prepared
    far_feat, far_slope = far_pixels
    own_gram, grad = pl.pallas_call(
        functools.partial(backward_kernel, shape, pixel_total),
        out_shape=(
            jax.ShapeDtypeStruct(target_gram.shape, f32),
            jax.ShapeDtypeStruct((tile_rows * tile_cols, in_width), bf16),
        ),
        in_specs=[vmem] * 10,
        scratch_shapes=[
            pltpu.VMEM(packed_shape.shape, f32),
            pltpu.VMEM((out_width, out_width), f32),
            pltpu.VMEM((out_width, out_width), bf16),
            pltpu.VMEM(((tile_rows + 2) * tile_cols, 3 * out_width), bf16),
        ],
        compiler_params=params,
        name="grad_conv",
    )(mine, other, both, in_feat, in_slope, out_feat, out_slope, far_feat, far_slope, turned)
    return own_gram, grad.reshape(tile_rows, tile_cols, in_width)


def solution(mesh):
    return jax.shard_map(
        on_device,
        mesh=mesh,
        in_specs=(P("rows", "cols", None), P(), P(), P(("rows", "cols"), None)),
        out_specs=(P(("rows", "cols"), None), P("rows", "cols", None)),
        check_vma=False,
    )
```

```python
import functools
import math

import jax
import jax.numpy as jnp
from jax import lax
from jax.experimental import pallas as pl
from jax.experimental.pallas import tpu as pltpu
from jax.sharding import PartitionSpec as P

gelu_scale = math.sqrt(2.0 / math.pi)
tile = 128
edge = 16
f32, bf16 = jnp.float32, jnp.bfloat16


def tile_pairs(width):
    count = width // tile
    return [(i, j) for i in range(count) for j in range(i, count)]


def swap_rows(low, value):
    count, cols = lax.axis_size("rows"), lax.axis_size("cols")
    partner = {i: i + 1 for i in low if i + 1 < count}
    partner.update({i + 1: i for i in low if i + 1 < count})
    perm = [
        (r * cols + c, partner[r] * cols + c if r in partner else r * cols + (c ^ 1))
        for r in range(count)
        for c in range(cols)
    ]
    return lax.ppermute(value, ("rows", "cols"), perm)


def shift_cols(last, first):
    count = lax.axis_size("cols")
    forward = [(i, i + 1) for i in range(count - 1)]
    backward = [(target, source) for source, target in forward]
    return lax.ppermute(last, "cols", forward), lax.ppermute(first, "cols", backward)


def device_index():
    return lax.axis_index("rows") * lax.axis_size("cols") + lax.axis_index("cols")


def swap(value, bit, other=None):
    total = lax.axis_size("rows") * lax.axis_size("cols")
    flip = lambda i: 1 << (other if other is not None and i.bit_count() % 2 else bit) | 1
    return lax.ppermute(value, ("rows", "cols"), [(i, i ^ flip(i)) for i in range(total)])


def local(body, out_shape, name, *operands, **kwargs):
    return pl.pallas_call(
        body,
        out_shape=out_shape,
        in_specs=[pl.BlockSpec(memory_space=pltpu.VMEM)] * len(operands),
        compiler_params=pltpu.CompilerParams(vmem_limit_bytes=8 * 1024 * 1024),
        name=name,
        **kwargs,
    )(*operands)


def side_of(bit, other=None):
    index = device_index()
    if bit > 0:
        side = lax.rem(index // (1 << bit), 2)
        if other is None:
            return side
        return jnp.where(side_of(0) == 0, side, lax.rem(index // (1 << other), 2))
    bits = (lax.axis_size("rows") * lax.axis_size("cols")).bit_length() - 1
    return lax.rem(sum(lax.rem(index // (1 << k), 2) for k in range(bits)), 2)


def rows_at(index, count):
    return pl.ds(pl.multiple_of(index * count, count), count)


waiting = pl.CostEstimate(flops=1_500_000_000, bytes_accessed=100_000, transcendentals=0)
chained = pl.CostEstimate(flops=8_000_000_000, bytes_accessed=100_000, transcendentals=0)


def halve(keep, got, bit, other=None):
    half = keep.shape[0] // 2

    def body(keep_ref, got_ref, send_ref, stay_ref):
        side = side_of(bit, other)
        away, here = rows_at(1 - side, half), rows_at(side, half)
        send_ref[...] = (keep_ref[away, :] + got_ref[away, :].astype(f32)).astype(bf16)
        stay_ref[...] = keep_ref[here, :] + got_ref[here, :].astype(f32)

    shape = (half, keep.shape[1])
    return local(
        body,
        (jax.ShapeDtypeStruct(shape, bf16), jax.ShapeDtypeStruct(shape, f32)),
        "halve",
        keep,
        got,
        cost_estimate=chained,
    )


def add(keep, got):
    def body(keep_ref, got_ref, sum_ref):
        sum_ref[...] = (keep_ref[...].astype(f32) + got_ref[...].astype(f32)).astype(bf16)

    return local(body, jax.ShapeDtypeStruct(got.shape, bf16), "add", keep, got, cost_estimate=chained)


def join(mine, got, bit, other=None, **kwargs):
    def body(mine_ref, got_ref, both_ref):
        side = side_of(bit, other)
        both_ref[:, pl.ds(side, 1)] = mine_ref[...][:, None]
        both_ref[:, pl.ds(1 - side, 1)] = got_ref[...][:, None]

    shape = (mine.shape[0], 2, *mine.shape[1:])
    return local(body, jax.ShapeDtypeStruct(shape, mine.dtype), "join", mine, got, **kwargs)


def join_second(mine, got, bit, other, **kwargs):
    def body(mine_ref, got_ref, both_ref):
        parity, side = side_of(0), side_of(bit, other)

        @pl.when(parity == 0)
        def _():
            both_ref[:, pl.ds(side, 1)] = mine_ref[...][:, None]
            both_ref[:, pl.ds(1 - side, 1)] = got_ref[...][:, None]

        @pl.when(parity == 1)
        def _():
            both_ref[:, :, pl.ds(side, 1)] = mine_ref[...][:, :, None]
            both_ref[:, :, pl.ds(1 - side, 1)] = got_ref[...][:, :, None]

    shape = (mine.shape[0], 2, *mine.shape[1:])
    return local(body, jax.ShapeDtypeStruct(shape, mine.dtype), "join_second", mine, got, **kwargs)


def join_cores(mine, other, **kwargs):
    def body(mine_ref, other_ref, both_ref):
        side = side_of(0)
        for chip in range(mine.shape[0]):
            core = lax.rem(side + chip.bit_count(), 2)
            both_ref[chip, pl.ds(core, 1)] = mine_ref[chip][None]
            both_ref[chip, pl.ds(1 - core, 1)] = other_ref[chip][None]

    shape = (mine.shape[0], 2, *mine.shape[1:])
    return local(body, jax.ShapeDtypeStruct(shape, mine.dtype), "join_cores", mine, other, **kwargs)


class Gather:
    def __init__(self, rows):
        self.rows, self.got, self.last = rows, None, None

    def settle(self, after):
        if self.got is None:
            self.rows, _ = lax.optimization_barrier((self.rows, after))
            return
        share = self.rows.shape[-2:]
        got, _ = lax.optimization_barrier((self.got, after))
        bit, other = self.last
        if bit == 0:
            both = join_cores(self.rows, got, cost_estimate=waiting)
        elif other is None or bit < other:
            mine, got = (part.reshape(-1, 1, *share) for part in (self.rows, got))
            both = join(mine, got, bit, other, cost_estimate=waiting)
        else:
            mine, got = (part.reshape(-1, 2, *share) for part in (self.rows, got))
            both = join_second(mine, got, bit, other, cost_estimate=waiting)
        self.rows, self.got = both.reshape(-1, *share), None

    def step(self, after, bit, other=None):
        self.settle(after)
        self.got, self.last = swap(self.rows, bit, other), (bit, other)


def sum_all(send, keep, beside):
    bits = (lax.axis_size("rows") * lax.axis_size("cols")).bit_length() - 1
    halving = [(1, 2), (2, 1)]
    adding = [(bit,) for bit in range(3, bits)]

    got = beside("cores", send, swap(send, 0))
    for n, pair in enumerate(halving):
        send, keep = halve(keep, got, *pair)
        got = beside(f"halve {n}", send, swap(send, *pair))
    mine = add(keep, got)
    for n, pair in enumerate(adding):
        mine = add(mine, beside(f"add {n}", mine, swap(mine, *pair)))
    for n, pair in enumerate(reversed(halving)):
        got = beside(f"join {n}", mine, swap(mine, *pair))
        mine = join(mine[None], got[None], *pair, cost_estimate=chained).reshape(-1, mine.shape[1])
    return mine, beside("halves", mine, swap(mine, 0))


def gelu_pair(value):
    square = value * value
    tangent = jnp.tanh(value * (gelu_scale + gelu_scale * 0.044715 * square))
    half = 0.5 * value
    plus = 0.5 + 0.5 * tangent
    grad = plus + half * (1.0 - tangent * tangent) * (
        gelu_scale + gelu_scale * 3.0 * 0.044715 * square
    )
    return value * plus, grad


def column(value, c):
    return jnp.concatenate([value[r, c : c + 1] for r in range(value.shape[0])], axis=0)


def rim_kernel(canvas_ref, *out_refs):
    even_ref, odd_ref = out_refs[-2:]
    rows, cols, _ = canvas_ref.shape
    begin = canvas_ref[:, 0:16, :].astype(f32)
    end = canvas_ref[:, cols - 16 :, :].astype(f32)
    for c in range(2):
        pair = column(begin, c), column(end, 14 + c)
        if len(out_refs) == 3:
            out_refs[0][c] = jnp.where(lax.axis_index("cols") == 0, pair[1], pair[0]).astype(bf16)
        else:
            out_refs[0][c], out_refs[1][c] = pair[0].astype(bf16), pair[1].astype(bf16)
    odd = lax.rem(lax.axis_index("rows"), 2)
    for case, low_ref, high_ref in ((0, odd_ref, even_ref), (1, even_ref, odd_ref)):

        @pl.when(odd == case)
        def _():
            for k in range(2):
                at = slice(k * cols, (k + 1) * cols)
                low_ref[at, :], high_ref[at, :] = canvas_ref[k], canvas_ref[rows - 2 + k]


def payload_kernel(target_ref, rows_ref, *refs):
    odd_ref, payload_ref, left_ref, right_ref, half_ref = refs[-5:]
    main = rows_ref.shape[0]
    payload_ref[0:main, :] = rows_ref[...]
    even_ref = payload_ref.at[main:]
    half_ref[0] = target_ref[...].astype(bf16)
    if len(refs) == 6:
        here = lax.axis_index("cols")
        other = refs[0][...].astype(f32)
        left_ref[...] = jnp.where(here == 0, 0.0, other).astype(bf16)
        right_ref[...] = jnp.where(here == 0, other, 0.0).astype(bf16)
    else:
        left_ref[...], right_ref[...] = refs[0][...], refs[1][...]
    beyond = [ref[c].astype(f32) for ref in (left_ref, right_ref) for c in range(2)]
    rows, width = beyond[0].shape

    def rim(r):
        parts = [part[r + k : r + k + 1] for k in range(2) for part in beyond]
        return jnp.concatenate([*parts, jnp.zeros((8, width), f32)], axis=0).astype(bf16)

    odd = lax.rem(lax.axis_index("rows"), 2)
    for case, low_ref, high_ref in ((0, odd_ref, even_ref), (1, even_ref, odd_ref)):

        @pl.when(odd == case)
        def _():
            low_ref[...], high_ref[...] = rim(0), rim(rows - 2)


def moved_rows(row, before, after):
    cols = row.shape[0]
    wide = row.astype(f32)
    place = lax.broadcasted_iota(jnp.int32, (8, row.shape[1]), 0)
    right, left = pltpu.roll(wide, 1, 0), pltpu.roll(wide, cols - 1, 0)
    right = jnp.concatenate([jnp.where(place == 0, before, right[:8]), right[8:]], axis=0)
    left = jnp.concatenate([left[:-8], jnp.where(place == 7, after, left[-8:])], axis=0)
    return right.astype(bf16), row.astype(bf16), left.astype(bf16)


def fill_row(cat_ref, r, row, before, after):
    cols, width = row.shape
    for b, part in enumerate(moved_rows(row, before, after)):
        cat_ref[r * cols : (r + 1) * cols, b * width : (b + 1) * width] = part


def gram_tiles(feat, gram_ref, base_ref=None):
    width = feat.shape[1]
    half = width // 2
    product = functools.partial(
        lax.dot_general,
        dimension_numbers=(((0,), (0,)), ((), ())),
        preferred_element_type=f32,
    )
    upper = product(feat[:, :half], feat)
    lower = product(feat[:, half:], feat[:, half:])
    for n, (i, j) in enumerate(tile_pairs(width)):
        at = slice(n * tile, (n + 1) * tile)
        if i * tile < half:
            part = upper[i * tile : (i + 1) * tile, j * tile : (j + 1) * tile]
        else:
            k, m = i * tile - half, j * tile - half
            part = lower[k : k + tile, m : m + tile]
        gram_ref[at, :] = part if base_ref is None else part + base_ref[at, :]


def inner_kernel(
    shape, own_ref, left_ref, right_ref, kernel_ref, bias_ref,
    feat_ref, slope_ref, gram_ref, row_ref, part_ref, cat_ref,
):
    row_ref[...] = bias_ref[...].astype(f32).reshape(row_ref.shape)
    tile_rows, tile_cols, in_width, out_width, step = shape
    lefts, rights = left_ref[1].astype(f32), right_ref[0].astype(f32)
    for r in range(tile_rows):
        fill_row(cat_ref, r, own_ref[r], lefts[r : r + 1], rights[r : r + 1])
    bias = row_ref[...]
    root = 1.0 / math.sqrt(out_width)
    span = 3 * in_width

    def product(begin, count, a):
        return jnp.dot(
            cat_ref[begin * tile_cols : (begin + count) * tile_cols, :],
            kernel_ref[a * span : (a + 1) * span, :],
            preferred_element_type=f32,
        )

    for h in range(0, tile_rows - 2, step):
        total = bias
        for a in range(3):
            total = total + product(h + a, step, a)
        features, slope = gelu_pair(total)
        at = slice(h * tile_cols, (h + step) * tile_cols)
        feat_ref[at, :] = features.astype(bf16)
        slope_ref[at, :] = (slope * root).astype(bf16)
    low, high = product(0, 2, 2), product(tile_rows - 2, 2, 0)
    ends = product(0, 1, 1), product(tile_rows - 1, 1, 1)
    part_ref[0:tile_cols, :] = low[:tile_cols] + bias
    part_ref[tile_cols : 2 * tile_cols, :] = low[tile_cols:] + ends[0] + bias
    part_ref[2 * tile_cols : 3 * tile_cols, :] = high[:tile_cols] + ends[1] + bias
    part_ref[3 * tile_cols :, :] = high[tile_cols:] + bias
    gram_tiles(feat_ref[...], gram_ref)


def halo_rows(halo_refs, low_ref, high_ref):
    even_ref, odd_ref, odd_rim_ref = halo_refs
    row = lax.axis_index("rows")
    odd = lax.rem(row, 2)
    main = odd_ref.shape[0]
    for at, part in ((slice(0, main), odd_ref), (slice(main, None), odd_rim_ref)):
        low_ref[at, :] = jnp.where(odd == 0, part[...], even_ref[at, :])
        high_ref[at, :] = jnp.where(odd == 0, even_ref[at, :], part[...])

    @pl.when(row == 0)
    def _():
        low_ref[...] = jnp.zeros_like(low_ref)

    @pl.when(row == lax.axis_size("rows") - 1)
    def _():
        high_ref[...] = jnp.zeros_like(high_ref)


def halves(width):
    return slice(0, width // 2), slice(width // 2, width)


def outer_kernel(
    shape, even_ref, odd_ref, odd_rim_ref, kernel_ref, base_ref, part_ref,
    feat_ref, slope_ref, send_ref, keep_ref, low_ref, high_ref, cat_ref, gram_ref,
):
    tile_rows, tile_cols, in_width, out_width, step = shape
    span, main = 3 * in_width, 2 * tile_cols
    halo_rows((even_ref, odd_ref, odd_rim_ref), low_ref, high_ref)
    for n, (source, at) in enumerate([(low_ref, tile_cols), (high_ref, 0)]):
        rim = source[main:, :].astype(f32)
        k = 4 * (1 - n)
        fill_row(cat_ref, n, source[at : at + tile_cols, :], rim[k + 1 : k + 2], rim[k + 2 : k + 3])
    root = 1.0 / math.sqrt(out_width)
    for at in halves(out_width):
        for n, a in enumerate([0, 2]):
            rows = slice(n * tile_cols, (n + 1) * tile_cols)
            features, slope = gelu_pair(
                part_ref[(n + 1) * tile_cols : (n + 2) * tile_cols, at]
                + jnp.dot(
                    cat_ref[rows, :],
                    kernel_ref[a * span : (a + 1) * span, at],
                    preferred_element_type=f32,
                )
            )
            feat_ref[rows, at] = features.astype(bf16)
            slope_ref[rows, at] = (slope * root).astype(bf16)
    gram_tiles(feat_ref[...], gram_ref, base_ref)
    half = send_ref.shape[0]
    side = side_of(0)
    send_ref[...] = gram_ref[rows_at(1 - side, half), :].astype(bf16)
    keep_ref[...] = gram_ref[rows_at(side, half), :]


def beyond_kernel(
    shape, own_ref, even_ref, odd_ref, odd_rim_ref, left_ref, right_ref, kernel_ref, bias_ref,
    part_ref, feat_ref, slope_ref, low_ref, high_ref, cat_ref, edge_ref,
):
    tile_rows, tile_cols, in_width, out_width, step = shape
    halo_rows((even_ref, odd_ref, odd_rim_ref), low_ref, high_ref)
    first = (lax.axis_index("rows") > 0).astype(f32)
    last = (lax.axis_index("rows") < lax.axis_size("rows") - 1).astype(f32)
    left = (lax.axis_index("cols") > 0).astype(f32)
    right = (lax.axis_index("cols") < lax.axis_size("cols") - 1).astype(f32)
    main = 2 * tile_cols
    low_rim, high_rim = low_ref[main:, :].astype(f32), high_ref[main:, :].astype(f32)
    own_begin = column(own_ref[:, 0:16, :].astype(f32), 0)
    own_end = column(own_ref[:, tile_cols - 16 :, :].astype(f32), 15)

    def sides(c, own):
        return jnp.concatenate(
            [low_rim[c : c + 1], low_rim[4 + c : 5 + c], own, high_rim[c : c + 1], high_rim[4 + c : 5 + c]],
            axis=0,
        )

    def ends(c, own):
        c16 = c // 16 * 16
        piece = lambda ref, k: ref[k + c16 : k + c16 + 16, :].astype(f32)[c - c16 : c - c16 + 1]
        rows = [piece(low_ref, 0), piece(low_ref, tile_cols), own]
        return jnp.concatenate([*rows, piece(high_ref, 0), piece(high_ref, tile_cols)], axis=0)

    lefts = [
        sides(0, left_ref[0].astype(f32)), sides(1, left_ref[1].astype(f32)), ends(0, own_begin)
    ]
    rights = [
        ends(tile_cols - 1, own_end), sides(2, right_ref[0].astype(f32)), sides(3, right_ref[1].astype(f32))
    ]
    span = 3 * in_width
    for r, line in enumerate([0, 1, tile_rows + 2, tile_rows + 3]):
        source = low_ref if r < 2 else high_ref
        row = source[r % 2 * tile_cols : (r % 2 + 1) * tile_cols, :]
        fill_row(cat_ref, r, row, lefts[1][line : line + 1], rights[1][line : line + 1])
    blank = jnp.zeros((edge - tile_rows - 2, in_width), f32)
    for a in range(3):
        for b in range(3):
            piece = jnp.concatenate(
                [lefts[b][a : a + tile_rows + 2], blank, rights[b][a : a + tile_rows + 2], blank],
                axis=0,
            )
            at = (3 * a + b) * in_width
            edge_ref[:, at : at + in_width] = piece.astype(bf16)
    root = 1.0 / math.sqrt(out_width)
    line = lax.broadcasted_iota(jnp.int32, (2 * edge, out_width // 2), 0)
    weight = jnp.where(line < edge, left, right)
    weight = jnp.where(line % edge == 0, weight * first, weight)
    weight = jnp.where(line % edge == tile_rows + 1, weight * last, weight)
    for at in halves(out_width):

        def product(begin, a):
            return jnp.dot(
                cat_ref[begin * tile_cols : (begin + 1) * tile_cols, :],
                kernel_ref[a * span : (a + 1) * span, at],
                preferred_element_type=f32,
            )

        totals = [
            part_ref[0:tile_cols, at] + product(0, 0) + product(1, 1),
            part_ref[3 * tile_cols :, at] + product(2, 1) + product(3, 2),
            bias_ref[:, at] + jnp.dot(edge_ref[...], kernel_ref[:, at], preferred_element_type=f32),
        ]
        scales = [first * root, last * root, weight * root]
        for n, (total, scale) in enumerate(zip(totals, scales)):
            features, slope = gelu_pair(total)
            rows = slice(n * tile_cols, n * tile_cols + total.shape[0])
            feat_ref[rows, at] = features.astype(bf16)
            slope_ref[rows, at] = (slope * scale).astype(bf16)


def turn_kernel(kernel_ref, turned_ref):
    taps, in_width, out_width = 9, kernel_ref.shape[0] // 9, kernel_ref.shape[1]
    for n in range(taps):
        to = (n // 3 * 3 + 2 - n % 3) * out_width
        turned_ref[to : to + out_width, :] = kernel_ref[n * in_width : (n + 1) * in_width, :].T


def prepare_kernel(target_ref, both_ref):
    for i, j in tile_pairs(target_ref.shape[0]):
        at_i, at_j = slice(i * tile, (i + 1) * tile), slice(j * tile, (j + 1) * tile)
        both = target_ref[at_i, at_j].astype(f32) + target_ref[at_j, at_i].astype(f32).T
        both_ref[at_i, at_j] = both
        if i != j:
            both_ref[at_j, at_i] = both.T


def backward_kernel(
    shape, pixel_total, mine_ref, other_ref, both_ref, in_feat_ref, in_slope_ref, out_feat_ref, out_slope_ref,
    far_feat_ref, far_slope_ref, turned_ref, own_gram_ref, out_ref, gram_ref, full_ref, sym_ref, cat_ref,
):
    tile_rows, tile_cols, in_width, out_width, step = shape
    half = mine_ref.shape[0]
    side = side_of(0)
    gram_ref[rows_at(side, half), :] = mine_ref[...].astype(f32)
    gram_ref[rows_at(1 - side, half), :] = other_ref[...].astype(f32)
    for n, (i, j) in enumerate(tile_pairs(out_width)):
        at_i, at_j = slice(i * tile, (i + 1) * tile), slice(j * tile, (j + 1) * tile)
        gram = gram_ref[n * tile : (n + 1) * tile, :] * (1.0 / pixel_total)
        full_ref[at_i, at_j] = gram
        sym_ref[at_i, at_j] = (2.0 * gram - both_ref[at_i, at_j]).astype(bf16)
        if i != j:
            gram = gram.T
            full_ref[at_j, at_i] = gram
            sym_ref[at_j, at_i] = (2.0 * gram - both_ref[at_j, at_i]).astype(bf16)
    share = own_gram_ref.shape[0]
    start = device_index() * share
    if share % 8 == 0:
        own_gram_ref[...] = full_ref[pl.ds(pl.multiple_of(start, 8), share), :]
    else:
        group = full_ref[pl.ds(pl.multiple_of(start // 8 * 8, 8), 8), :]
        picked = group[0:share]
        for k in range(share, 8, share):
            picked = jnp.where(start % 8 == k, group[k : k + share], picked)
        own_gram_ref[...] = picked

    def grad_of(feat_ref, slope_ref, at):
        product = jnp.dot(feat_ref[at, :], sym_ref[...], preferred_element_type=f32)
        return product * slope_ref[at, :].astype(f32)

    main = 2 * tile_cols
    edges = grad_of(far_feat_ref, far_slope_ref, slice(main, None))
    near, far = (out_feat_ref, out_slope_ref), (far_feat_ref, far_slope_ref)
    lines = [[(*far, 0), (*near, 0)]]
    lines += [
        [(in_feat_ref, in_slope_ref, k * tile_cols) for k in range(h, h + step)]
        for h in range(0, tile_rows - 2, step)
    ]
    lines += [[(*near, tile_cols), (*far, tile_cols)]]
    grads = {}

    def upstream(c):
        pieces = lines[c]
        if pieces[0][0] is pieces[1][0]:
            feat_ref, slope_ref, begin = pieces[0]
            grads[c] = grad_of(feat_ref, slope_ref, slice(begin, begin + step * tile_cols))
        else:
            parts = [grad_of(feat, slope, slice(begin, begin + tile_cols)) for feat, slope, begin in pieces]
            grads[c] = jnp.concatenate(parts, axis=0)

    def fill(c):
        for k in range(step):
            r = c * step + k
            fill_row(
                cat_ref, r, grads[c][k * tile_cols : (k + 1) * tile_cols],
                edges[r : r + 1], edges[edge + r : edge + r + 1],
            )

    span = 3 * out_width

    def convolve(begin, count):
        total = 0.0
        for a in range(3):
            total = total + jnp.dot(
                cat_ref[(begin + 2 - a) * tile_cols : (begin + 2 - a + count) * tile_cols, :],
                turned_ref[a * span : (a + 1) * span, :],
                preferred_element_type=f32,
            )
        out_ref[begin * tile_cols : (begin + count) * tile_cols, :] = total.astype(bf16)

    last = len(lines) - 1
    middle = last // 2
    half_rows = middle * step
    upstream(0)
    for c in range(last):
        upstream(c + 1)
        fill(c)
        if c == middle:
            convolve(0, half_rows)
    fill(last)
    convolve(half_rows, tile_rows - half_rows)


def on_device(canvas, conv_weight, conv_bias, target_gram):
    tile_rows, tile_cols, in_width = canvas.shape
    out_width = conv_weight.shape[3]
    pixel_total = tile_rows * tile_cols * lax.axis_size("rows") * lax.axis_size("cols")
    shape = (tile_rows, tile_cols, in_width, out_width, 2)
    kernel = conv_weight.reshape(9 * in_width, out_width)
    params = pltpu.CompilerParams(vmem_limit_bytes=24 * 1024 * 1024)
    vmem = pl.BlockSpec(memory_space=pltpu.VMEM)
    packed_shape = jax.ShapeDtypeStruct((len(tile_pairs(out_width)) * tile, tile), f32)

    rim_shape = jax.ShapeDtypeStruct((2, tile_rows, in_width), bf16)
    two = lax.axis_size("cols") == 2
    count = lax.axis_size("rows")
    main_shape = jax.ShapeDtypeStruct((2 * tile_cols, in_width), bf16)
    *rims, even, odd = local(
        rim_kernel,
        (*(rim_shape,) * (1 if two else 2), main_shape, main_shape),
        "rims",
        canvas,
        cost_estimate=pl.CostEstimate(flops=4_000_000_000, bytes_accessed=600_000, transcendentals=0),
    )
    if two:
        beyond = [lax.ppermute(rims[0], "cols", [(0, 1), (1, 0)])]
    else:
        beyond = shift_cols(rims[1], rims[0])
    evens, odds = range(0, count, 2), range(1, count, 2)
    odd = swap_rows(odds, odd)
    payload_shape = jax.ShapeDtypeStruct((2 * tile_cols + edge, in_width), bf16)
    end_shape = jax.ShapeDtypeStruct((edge, in_width), bf16)
    half_shape = jax.ShapeDtypeStruct((1, *target_gram.shape), bf16)
    odd_rim, even, left, right, rows = local(
        payload_kernel,
        (end_shape, payload_shape, rim_shape, rim_shape, half_shape),
        "row_rims",
        target_gram,
        even,
        *beyond,
    )
    halo = [swap_rows(evens, even), odd, swap_rows(odds, odd_rim)]
    bits = (lax.axis_size("rows") * lax.axis_size("cols")).bit_length() - 1
    gather = Gather(rows)
    far = list(reversed(range(3, bits)))
    inner = (tile_rows - 2) * tile_cols
    in_feat, in_slope, in_gram, bias, part = pl.pallas_call(
        functools.partial(inner_kernel, shape),
        out_shape=(
            jax.ShapeDtypeStruct((inner, out_width), bf16),
            jax.ShapeDtypeStruct((inner, out_width), bf16),
            packed_shape,
            jax.ShapeDtypeStruct((1, out_width), f32),
            jax.ShapeDtypeStruct((4 * tile_cols, out_width), f32),
        ),
        in_specs=[vmem] * 5,
        scratch_shapes=[pltpu.VMEM((tile_rows * tile_cols, 3 * in_width), bf16)],
        compiler_params=params,
        name="inner_rows",
        cost_estimate=pl.CostEstimate(
            flops=2 * inner * (9 * in_width + out_width) * out_width,
            bytes_accessed=6_000_000,
            transcendentals=inner * out_width,
        ),
    )(canvas, left, right, kernel, conv_bias)

    weights, in_gram = lax.optimization_barrier((kernel, in_gram))
    turned = local(
        turn_kernel,
        jax.ShapeDtypeStruct((9 * out_width, in_width), bf16),
        "turn",
        weights,
        cost_estimate=waiting,
    )
    in_gram, turned = lax.optimization_barrier((in_gram, turned))
    half_gram = (packed_shape.shape[0] // 2, tile)
    halo_scratch = [pltpu.VMEM(payload_shape.shape, bf16), pltpu.VMEM(payload_shape.shape, bf16)]
    out_feat, out_slope, send, keep = pl.pallas_call(
        functools.partial(outer_kernel, shape),
        out_shape=(
            jax.ShapeDtypeStruct((2 * tile_cols, out_width), bf16),
            jax.ShapeDtypeStruct((2 * tile_cols, out_width), bf16),
            jax.ShapeDtypeStruct(half_gram, bf16),
            jax.ShapeDtypeStruct(half_gram, f32),
        ),
        in_specs=[vmem] * 6,
        scratch_shapes=[
            *halo_scratch,
            pltpu.VMEM((2 * tile_cols, 3 * in_width), bf16),
            pltpu.VMEM(packed_shape.shape, f32),
        ],
        compiler_params=params,
        name="outer_rows",
    )(*halo, kernel, in_gram, part)

    exchanges = {
        "halve 0": [(bit,) for bit in far[:1]],
        "halve 1": [(bit,) for bit in far[1:]],
        "add 0": [(1, 2)],
        "add 1": [(2, 1)],
        "join 0": [(0,)],
    }
    prepared, far_pixels = [], []

    def beside(name, sent, got):
        if name == "join 1":
            outer = 2 * tile_cols + 2 * edge
            rim_sums, _ = lax.optimization_barrier((part, sent))
            far_pixels.extend(
                pl.pallas_call(
                    functools.partial(beyond_kernel, shape),
                    out_shape=(jax.ShapeDtypeStruct((outer, out_width), bf16),) * 2,
                    in_specs=[vmem] * 9,
                    scratch_shapes=[
                        *halo_scratch,
                        pltpu.VMEM((4 * tile_cols, 3 * in_width), bf16),
                        pltpu.VMEM((2 * edge, 9 * in_width), bf16),
                    ],
                    compiler_params=params,
                    name="beyond",
                    cost_estimate=chained,
                )(canvas, *halo, left, right, kernel, bias, rim_sums)
            )
            gather.settle(sent)
            got, gather.rows, *_ = lax.optimization_barrier((got, gather.rows, *far_pixels))
            return got
        for bit in exchanges.get(name, []):
            gather.step(sent, *bit)
        if name == "join 0":
            got, gather.rows = lax.optimization_barrier((got, gather.rows))
        if name != "halves":
            return got
        gather.settle(sent)
        prepared.append(
            local(
                prepare_kernel,
                jax.ShapeDtypeStruct((out_width, out_width), f32),
                "prepare",
                gather.rows.reshape(out_width, out_width),
                cost_estimate=waiting,
            )
        )
        return lax.optimization_barrier((got, *prepared))[0]

    mine, other = sum_all(send, keep, beside)
    (both,) = prepared
    far_feat, far_slope = far_pixels
    own_gram, grad = pl.pallas_call(
        functools.partial(backward_kernel, shape, pixel_total),
        out_shape=(
            jax.ShapeDtypeStruct(target_gram.shape, f32),
            jax.ShapeDtypeStruct((tile_rows * tile_cols, in_width), bf16),
        ),
        in_specs=[vmem] * 10,
        scratch_shapes=[
            pltpu.VMEM(packed_shape.shape, f32),
            pltpu.VMEM((out_width, out_width), f32),
            pltpu.VMEM((out_width, out_width), bf16),
            pltpu.VMEM(((tile_rows + 2) * tile_cols, 3 * out_width), bf16),
        ],
        compiler_params=params,
        name="grad_conv",
    )(mine, other, both, in_feat, in_slope, out_feat, out_slope, far_feat, far_slope, turned)
    return own_gram, grad.reshape(tile_rows, tile_cols, in_width)


def solution(mesh):
    return jax.shard_map(
        on_device,
        mesh=mesh,
        in_specs=(P("rows", "cols", None), P(), P(), P(("rows", "cols"), None)),
        out_specs=(P(("rows", "cols"), None), P("rows", "cols", None)),
        check_vma=False,
    )
```

```python
import functools
import math

import jax
import jax.numpy as jnp
from jax import lax
from jax.experimental import pallas as pl
from jax.experimental.pallas import tpu as pltpu
from jax.sharding import PartitionSpec as P

gelu_scale = math.sqrt(2.0 / math.pi)
tile = 128
edge = 16
f32, bf16 = jnp.float32, jnp.bfloat16


def tile_pairs(width):
    count = width // tile
    return [(i, j) for i in range(count) for j in range(i, count)]


def swap_rows(low, value):
    count, cols = lax.axis_size("rows"), lax.axis_size("cols")
    partner = {i: i + 1 for i in low if i + 1 < count}
    partner.update({i + 1: i for i in low if i + 1 < count})
    perm = [
        (r * cols + c, partner[r] * cols + c if r in partner else r * cols + (c ^ 1))
        for r in range(count)
        for c in range(cols)
    ]
    return lax.ppermute(value, ("rows", "cols"), perm)


def shift_cols(last, first):
    count = lax.axis_size("cols")
    forward = [(i, i + 1) for i in range(count - 1)]
    backward = [(target, source) for source, target in forward]
    return lax.ppermute(last, "cols", forward), lax.ppermute(first, "cols", backward)


def device_index():
    return lax.axis_index("rows") * lax.axis_size("cols") + lax.axis_index("cols")


def swap(value, bit, other=None):
    total = lax.axis_size("rows") * lax.axis_size("cols")
    flip = lambda i: 1 << (other if other is not None and i.bit_count() % 2 else bit) | 1
    return lax.ppermute(value, ("rows", "cols"), [(i, i ^ flip(i)) for i in range(total)])


def local(body, out_shape, name, *operands, **kwargs):
    return pl.pallas_call(
        body,
        out_shape=out_shape,
        in_specs=[pl.BlockSpec(memory_space=pltpu.VMEM)] * len(operands),
        compiler_params=pltpu.CompilerParams(vmem_limit_bytes=8 * 1024 * 1024),
        name=name,
        **kwargs,
    )(*operands)


def side_of(bit, other=None):
    index = device_index()
    if bit > 0:
        side = lax.rem(index // (1 << bit), 2)
        if other is None:
            return side
        return jnp.where(side_of(0) == 0, side, lax.rem(index // (1 << other), 2))
    bits = (lax.axis_size("rows") * lax.axis_size("cols")).bit_length() - 1
    return lax.rem(sum(lax.rem(index // (1 << k), 2) for k in range(bits)), 2)


def rows_at(index, count):
    return pl.ds(pl.multiple_of(index * count, count), count)


waiting = pl.CostEstimate(flops=1_500_000_000, bytes_accessed=100_000, transcendentals=0)
chained = pl.CostEstimate(flops=8_000_000_000, bytes_accessed=100_000, transcendentals=0)


def halve(keep, got, bit, other=None):
    half = keep.shape[0] // 2

    def body(keep_ref, got_ref, send_ref, stay_ref):
        side = side_of(bit, other)
        away, here = rows_at(1 - side, half), rows_at(side, half)
        send_ref[...] = (keep_ref[away, :] + got_ref[away, :].astype(f32)).astype(bf16)
        stay_ref[...] = keep_ref[here, :] + got_ref[here, :].astype(f32)

    shape = (half, keep.shape[1])
    return local(
        body,
        (jax.ShapeDtypeStruct(shape, bf16), jax.ShapeDtypeStruct(shape, f32)),
        "halve",
        keep,
        got,
        cost_estimate=chained,
    )


def add(keep, got):
    def body(keep_ref, got_ref, sum_ref):
        sum_ref[...] = (keep_ref[...].astype(f32) + got_ref[...].astype(f32)).astype(bf16)

    return local(body, jax.ShapeDtypeStruct(got.shape, bf16), "add", keep, got, cost_estimate=chained)


def join(mine, got, bit, other=None, **kwargs):
    def body(mine_ref, got_ref, both_ref):
        side = side_of(bit, other)
        both_ref[:, pl.ds(side, 1)] = mine_ref[...][:, None]
        both_ref[:, pl.ds(1 - side, 1)] = got_ref[...][:, None]

    shape = (mine.shape[0], 2, *mine.shape[1:])
    return local(body, jax.ShapeDtypeStruct(shape, mine.dtype), "join", mine, got, **kwargs)


def join_second(mine, got, bit, other, **kwargs):
    def body(mine_ref, got_ref, both_ref):
        parity, side = side_of(0), side_of(bit, other)

        @pl.when(parity == 0)
        def _():
            both_ref[:, pl.ds(side, 1)] = mine_ref[...][:, None]
            both_ref[:, pl.ds(1 - side, 1)] = got_ref[...][:, None]

        @pl.when(parity == 1)
        def _():
            both_ref[:, :, pl.ds(side, 1)] = mine_ref[...][:, :, None]
            both_ref[:, :, pl.ds(1 - side, 1)] = got_ref[...][:, :, None]

    shape = (mine.shape[0], 2, *mine.shape[1:])
    return local(body, jax.ShapeDtypeStruct(shape, mine.dtype), "join_second", mine, got, **kwargs)


def join_cores(mine, other, **kwargs):
    def body(mine_ref, other_ref, both_ref):
        side = side_of(0)
        for chip in range(mine.shape[0]):
            core = lax.rem(side + chip.bit_count(), 2)
            both_ref[chip, pl.ds(core, 1)] = mine_ref[chip][None]
            both_ref[chip, pl.ds(1 - core, 1)] = other_ref[chip][None]

    shape = (mine.shape[0], 2, *mine.shape[1:])
    return local(body, jax.ShapeDtypeStruct(shape, mine.dtype), "join_cores", mine, other, **kwargs)


class Gather:
    def __init__(self, rows):
        self.rows, self.got, self.last = rows, None, None

    def settle(self, after):
        if self.got is None:
            self.rows, _ = lax.optimization_barrier((self.rows, after))
            return
        share = self.rows.shape[-2:]
        got, _ = lax.optimization_barrier((self.got, after))
        bit, other = self.last
        if bit == 0:
            both = join_cores(self.rows, got, cost_estimate=waiting)
        elif other is None or bit < other:
            mine, got = (part.reshape(-1, 1, *share) for part in (self.rows, got))
            both = join(mine, got, bit, other, cost_estimate=waiting)
        else:
            mine, got = (part.reshape(-1, 2, *share) for part in (self.rows, got))
            both = join_second(mine, got, bit, other, cost_estimate=waiting)
        self.rows, self.got = both.reshape(-1, *share), None

    def step(self, after, bit, other=None):
        self.settle(after)
        self.got, self.last = swap(self.rows, bit, other), (bit, other)


def sum_all(send, keep, beside):
    bits = (lax.axis_size("rows") * lax.axis_size("cols")).bit_length() - 1
    halving = [(1, 2), (2, 1)]
    adding = [(bit,) for bit in range(3, bits)]

    got = beside("cores", send, swap(send, 0))
    for n, pair in enumerate(halving):
        send, keep = halve(keep, got, *pair)
        got = beside(f"halve {n}", send, swap(send, *pair))
    mine = add(keep, got)
    for n, pair in enumerate(adding):
        mine = add(mine, beside(f"add {n}", mine, swap(mine, *pair)))
    for n, pair in enumerate(reversed(halving)):
        got = beside(f"join {n}", mine, swap(mine, *pair))
        mine = join(mine[None], got[None], *pair, cost_estimate=chained).reshape(-1, mine.shape[1])
    return mine, beside("halves", mine, swap(mine, 0))


def gelu_pair(value):
    square = value * value
    tangent = jnp.tanh(value * (gelu_scale + gelu_scale * 0.044715 * square))
    half = 0.5 * value
    plus = 0.5 + 0.5 * tangent
    grad = plus + half * (1.0 - tangent * tangent) * (
        gelu_scale + gelu_scale * 3.0 * 0.044715 * square
    )
    return value * plus, grad


def column(value, c):
    return jnp.concatenate([value[r, c : c + 1] for r in range(value.shape[0])], axis=0)


def rim_kernel(canvas_ref, *out_refs):
    even_ref, odd_ref = out_refs[-2:]
    rows, cols, _ = canvas_ref.shape
    begin = canvas_ref[:, 0:16, :].astype(f32)
    end = canvas_ref[:, cols - 16 :, :].astype(f32)
    for c in range(2):
        pair = column(begin, c), column(end, 14 + c)
        if len(out_refs) == 3:
            out_refs[0][c] = jnp.where(lax.axis_index("cols") == 0, pair[1], pair[0]).astype(bf16)
        else:
            out_refs[0][c], out_refs[1][c] = pair[0].astype(bf16), pair[1].astype(bf16)
    odd = lax.rem(lax.axis_index("rows"), 2)
    for case, low_ref, high_ref in ((0, odd_ref, even_ref), (1, even_ref, odd_ref)):

        @pl.when(odd == case)
        def _():
            for k in range(2):
                at = slice(k * cols, (k + 1) * cols)
                low_ref[at, :], high_ref[at, :] = canvas_ref[k], canvas_ref[rows - 2 + k]


def payload_kernel(target_ref, rows_ref, *refs):
    payload_ref, left_ref, right_ref, half_ref = refs[-4:]
    main = rows_ref.shape[0]
    payload_ref[0:main, :] = rows_ref[...]
    odd_ref = payload_ref.at[main:]
    half_ref[0] = target_ref[...].astype(bf16)
    if len(refs) == 5:
        here = lax.axis_index("cols")
        other = refs[0][...].astype(f32)
        left_ref[...] = jnp.where(here == 0, 0.0, other).astype(bf16)
        right_ref[...] = jnp.where(here == 0, other, 0.0).astype(bf16)
    else:
        left_ref[...], right_ref[...] = refs[0][...], refs[1][...]
    odd_ref[...] = row_rim(left_ref, right_ref, 1)


def row_rim(left_ref, right_ref, last):
    beyond = [ref[c].astype(f32) for ref in (left_ref, right_ref) for c in range(2)]
    rows, width = beyond[0].shape

    def rim(r):
        parts = [part[r + k : r + k + 1] for k in range(2) for part in beyond]
        return jnp.concatenate([*parts, jnp.zeros((8, width), f32)], axis=0)

    parity = lax.rem(lax.axis_index("rows"), 2)
    return jnp.where(parity == last, rim(rows - 2), rim(0)).astype(bf16)


def even_rim_kernel(left_ref, right_ref, _, even_ref):
    even_ref[...] = row_rim(left_ref, right_ref, 0)


def moved_rows(row, before, after):
    cols = row.shape[0]
    wide = row.astype(f32)
    place = lax.broadcasted_iota(jnp.int32, (8, row.shape[1]), 0)
    right, left = pltpu.roll(wide, 1, 0), pltpu.roll(wide, cols - 1, 0)
    right = jnp.concatenate([jnp.where(place == 0, before, right[:8]), right[8:]], axis=0)
    left = jnp.concatenate([left[:-8], jnp.where(place == 7, after, left[-8:])], axis=0)
    return right.astype(bf16), row.astype(bf16), left.astype(bf16)


def fill_row(cat_ref, r, row, before, after):
    cols, width = row.shape
    for b, part in enumerate(moved_rows(row, before, after)):
        cat_ref[r * cols : (r + 1) * cols, b * width : (b + 1) * width] = part


def gram_tiles(feat, gram_ref, base_ref=None):
    width = feat.shape[1]
    half = width // 2
    product = functools.partial(
        lax.dot_general,
        dimension_numbers=(((0,), (0,)), ((), ())),
        preferred_element_type=f32,
    )
    upper = product(feat[:, :half], feat)
    lower = product(feat[:, half:], feat[:, half:])
    for n, (i, j) in enumerate(tile_pairs(width)):
        at = slice(n * tile, (n + 1) * tile)
        if i * tile < half:
            part = upper[i * tile : (i + 1) * tile, j * tile : (j + 1) * tile]
        else:
            k, m = i * tile - half, j * tile - half
            part = lower[k : k + tile, m : m + tile]
        gram_ref[at, :] = part if base_ref is None else part + base_ref[at, :]


def inner_kernel(
    shape, own_ref, left_ref, right_ref, kernel_ref, bias_ref,
    feat_ref, slope_ref, gram_ref, row_ref, part_ref, cat_ref,
):
    row_ref[...] = bias_ref[...].astype(f32).reshape(row_ref.shape)
    tile_rows, tile_cols, in_width, out_width, step = shape
    lefts, rights = left_ref[1].astype(f32), right_ref[0].astype(f32)
    for r in range(tile_rows):
        fill_row(cat_ref, r, own_ref[r], lefts[r : r + 1], rights[r : r + 1])
    bias = row_ref[...]
    root = 1.0 / math.sqrt(out_width)
    span = 3 * in_width

    def product(begin, count, a):
        return jnp.dot(
            cat_ref[begin * tile_cols : (begin + count) * tile_cols, :],
            kernel_ref[a * span : (a + 1) * span, :],
            preferred_element_type=f32,
        )

    for h in range(0, tile_rows - 2, step):
        total = bias
        for a in range(3):
            total = total + product(h + a, step, a)
        features, slope = gelu_pair(total)
        at = slice(h * tile_cols, (h + step) * tile_cols)
        feat_ref[at, :] = features.astype(bf16)
        slope_ref[at, :] = (slope * root).astype(bf16)
    low, high = product(0, 2, 2), product(tile_rows - 2, 2, 0)
    ends = product(0, 1, 1), product(tile_rows - 1, 1, 1)
    part_ref[0:tile_cols, :] = low[:tile_cols] + bias
    part_ref[tile_cols : 2 * tile_cols, :] = low[tile_cols:] + ends[0] + bias
    part_ref[2 * tile_cols : 3 * tile_cols, :] = high[:tile_cols] + ends[1] + bias
    part_ref[3 * tile_cols :, :] = high[tile_cols:] + bias
    gram_tiles(feat_ref[...], gram_ref)


def halo_rows(halo_refs, low_ref, high_ref):
    even_ref, odd_ref, even_rim_ref = halo_refs
    row = lax.axis_index("rows")
    odd = lax.rem(row, 2)
    main = even_ref.shape[0]
    for at, even in ((slice(0, main), even_ref), (slice(main, None), even_rim_ref)):
        low_ref[at, :] = jnp.where(odd == 0, odd_ref[at, :], even[...])
        high_ref[at, :] = jnp.where(odd == 0, even[...], odd_ref[at, :])

    @pl.when(row == 0)
    def _():
        low_ref[...] = jnp.zeros_like(low_ref)

    @pl.when(row == lax.axis_size("rows") - 1)
    def _():
        high_ref[...] = jnp.zeros_like(high_ref)


def halves(width):
    return slice(0, width // 2), slice(width // 2, width)


def outer_kernel(
    shape, even_ref, odd_ref, even_rim_ref, kernel_ref, base_ref, part_ref,
    feat_ref, slope_ref, send_ref, keep_ref, low_ref, high_ref, cat_ref, gram_ref,
):
    tile_rows, tile_cols, in_width, out_width, step = shape
    span, main = 3 * in_width, 2 * tile_cols
    halo_rows((even_ref, odd_ref, even_rim_ref), low_ref, high_ref)
    for n, (source, at) in enumerate([(low_ref, tile_cols), (high_ref, 0)]):
        rim = source[main:, :].astype(f32)
        k = 4 * (1 - n)
        fill_row(cat_ref, n, source[at : at + tile_cols, :], rim[k + 1 : k + 2], rim[k + 2 : k + 3])
    root = 1.0 / math.sqrt(out_width)
    for at in halves(out_width):
        for n, a in enumerate([0, 2]):
            rows = slice(n * tile_cols, (n + 1) * tile_cols)
            features, slope = gelu_pair(
                part_ref[(n + 1) * tile_cols : (n + 2) * tile_cols, at]
                + jnp.dot(
                    cat_ref[rows, :],
                    kernel_ref[a * span : (a + 1) * span, at],
                    preferred_element_type=f32,
                )
            )
            feat_ref[rows, at] = features.astype(bf16)
            slope_ref[rows, at] = (slope * root).astype(bf16)
    gram_tiles(feat_ref[...], gram_ref, base_ref)
    half = send_ref.shape[0]
    side = side_of(0)
    send_ref[...] = gram_ref[rows_at(1 - side, half), :].astype(bf16)
    keep_ref[...] = gram_ref[rows_at(side, half), :]


def beyond_kernel(
    shape, own_ref, even_ref, odd_ref, even_rim_ref, left_ref, right_ref, kernel_ref, bias_ref,
    part_ref, feat_ref, slope_ref, low_ref, high_ref, cat_ref, edge_ref,
):
    tile_rows, tile_cols, in_width, out_width, step = shape
    halo_rows((even_ref, odd_ref, even_rim_ref), low_ref, high_ref)
    first = (lax.axis_index("rows") > 0).astype(f32)
    last = (lax.axis_index("rows") < lax.axis_size("rows") - 1).astype(f32)
    left = (lax.axis_index("cols") > 0).astype(f32)
    right = (lax.axis_index("cols") < lax.axis_size("cols") - 1).astype(f32)
    main = 2 * tile_cols
    low_rim, high_rim = low_ref[main:, :].astype(f32), high_ref[main:, :].astype(f32)
    own_begin = column(own_ref[:, 0:16, :].astype(f32), 0)
    own_end = column(own_ref[:, tile_cols - 16 :, :].astype(f32), 15)

    def sides(c, own):
        return jnp.concatenate(
            [low_rim[c : c + 1], low_rim[4 + c : 5 + c], own, high_rim[c : c + 1], high_rim[4 + c : 5 + c]],
            axis=0,
        )

    def ends(c, own):
        c16 = c // 16 * 16
        piece = lambda ref, k: ref[k + c16 : k + c16 + 16, :].astype(f32)[c - c16 : c - c16 + 1]
        rows = [piece(low_ref, 0), piece(low_ref, tile_cols), own]
        return jnp.concatenate([*rows, piece(high_ref, 0), piece(high_ref, tile_cols)], axis=0)

    lefts = [
        sides(0, left_ref[0].astype(f32)), sides(1, left_ref[1].astype(f32)), ends(0, own_begin)
    ]
    rights = [
        ends(tile_cols - 1, own_end), sides(2, right_ref[0].astype(f32)), sides(3, right_ref[1].astype(f32))
    ]
    span = 3 * in_width
    for r, line in enumerate([0, 1, tile_rows + 2, tile_rows + 3]):
        source = low_ref if r < 2 else high_ref
        row = source[r % 2 * tile_cols : (r % 2 + 1) * tile_cols, :]
        fill_row(cat_ref, r, row, lefts[1][line : line + 1], rights[1][line : line + 1])
    blank = jnp.zeros((edge - tile_rows - 2, in_width), f32)
    for a in range(3):
        for b in range(3):
            piece = jnp.concatenate(
                [lefts[b][a : a + tile_rows + 2], blank, rights[b][a : a + tile_rows + 2], blank],
                axis=0,
            )
            at = (3 * a + b) * in_width
            edge_ref[:, at : at + in_width] = piece.astype(bf16)
    root = 1.0 / math.sqrt(out_width)
    line = lax.broadcasted_iota(jnp.int32, (2 * edge, out_width // 2), 0)
    weight = jnp.where(line < edge, left, right)
    weight = jnp.where(line % edge == 0, weight * first, weight)
    weight = jnp.where(line % edge == tile_rows + 1, weight * last, weight)
    for at in halves(out_width):

        def product(begin, a):
            return jnp.dot(
                cat_ref[begin * tile_cols : (begin + 1) * tile_cols, :],
                kernel_ref[a * span : (a + 1) * span, at],
                preferred_element_type=f32,
            )

        totals = [
            part_ref[0:tile_cols, at] + product(0, 0) + product(1, 1),
            part_ref[3 * tile_cols :, at] + product(2, 1) + product(3, 2),
            bias_ref[:, at] + jnp.dot(edge_ref[...], kernel_ref[:, at], preferred_element_type=f32),
        ]
        scales = [first * root, last * root, weight * root]
        for n, (total, scale) in enumerate(zip(totals, scales)):
            features, slope = gelu_pair(total)
            rows = slice(n * tile_cols, n * tile_cols + total.shape[0])
            feat_ref[rows, at] = features.astype(bf16)
            slope_ref[rows, at] = (slope * scale).astype(bf16)


def turn_kernel(kernel_ref, turned_ref):
    taps, in_width, out_width = 9, kernel_ref.shape[0] // 9, kernel_ref.shape[1]
    for n in range(taps):
        to = (n // 3 * 3 + 2 - n % 3) * out_width
        turned_ref[to : to + out_width, :] = kernel_ref[n * in_width : (n + 1) * in_width, :].T


def prepare_kernel(target_ref, both_ref):
    for i, j in tile_pairs(target_ref.shape[0]):
        at_i, at_j = slice(i * tile, (i + 1) * tile), slice(j * tile, (j + 1) * tile)
        both = target_ref[at_i, at_j].astype(f32) + target_ref[at_j, at_i].astype(f32).T
        both_ref[at_i, at_j] = both
        if i != j:
            both_ref[at_j, at_i] = both.T


def backward_kernel(
    shape, pixel_total, mine_ref, other_ref, both_ref, in_feat_ref, in_slope_ref, out_feat_ref, out_slope_ref,
    far_feat_ref, far_slope_ref, turned_ref, own_gram_ref, out_ref, gram_ref, full_ref, sym_ref, cat_ref,
):
    tile_rows, tile_cols, in_width, out_width, step = shape
    half = mine_ref.shape[0]
    side = side_of(0)
    gram_ref[rows_at(side, half), :] = mine_ref[...].astype(f32)
    gram_ref[rows_at(1 - side, half), :] = other_ref[...].astype(f32)
    for n, (i, j) in enumerate(tile_pairs(out_width)):
        at_i, at_j = slice(i * tile, (i + 1) * tile), slice(j * tile, (j + 1) * tile)
        gram = gram_ref[n * tile : (n + 1) * tile, :] * (1.0 / pixel_total)
        full_ref[at_i, at_j] = gram
        sym_ref[at_i, at_j] = (2.0 * gram - both_ref[at_i, at_j]).astype(bf16)
        if i != j:
            gram = gram.T
            full_ref[at_j, at_i] = gram
            sym_ref[at_j, at_i] = (2.0 * gram - both_ref[at_j, at_i]).astype(bf16)
    share = own_gram_ref.shape[0]
    start = device_index() * share
    if share % 8 == 0:
        own_gram_ref[...] = full_ref[pl.ds(pl.multiple_of(start, 8), share), :]
    else:
        group = full_ref[pl.ds(pl.multiple_of(start // 8 * 8, 8), 8), :]
        picked = group[0:share]
        for k in range(share, 8, share):
            picked = jnp.where(start % 8 == k, group[k : k + share], picked)
        own_gram_ref[...] = picked

    def grad_of(feat_ref, slope_ref, at):
        product = jnp.dot(feat_ref[at, :], sym_ref[...], preferred_element_type=f32)
        return product * slope_ref[at, :].astype(f32)

    main = 2 * tile_cols
    edges = grad_of(far_feat_ref, far_slope_ref, slice(main, None))
    near, far = (out_feat_ref, out_slope_ref), (far_feat_ref, far_slope_ref)
    lines = [[(*far, 0), (*near, 0)]]
    lines += [
        [(in_feat_ref, in_slope_ref, k * tile_cols) for k in range(h, h + step)]
        for h in range(0, tile_rows - 2, step)
    ]
    lines += [[(*near, tile_cols), (*far, tile_cols)]]
    grads = {}

    def upstream(c):
        pieces = lines[c]
        if pieces[0][0] is pieces[1][0]:
            feat_ref, slope_ref, begin = pieces[0]
            grads[c] = grad_of(feat_ref, slope_ref, slice(begin, begin + step * tile_cols))
        else:
            parts = [grad_of(feat, slope, slice(begin, begin + tile_cols)) for feat, slope, begin in pieces]
            grads[c] = jnp.concatenate(parts, axis=0)

    def fill(c):
        for k in range(step):
            r = c * step + k
            fill_row(
                cat_ref, r, grads[c][k * tile_cols : (k + 1) * tile_cols],
                edges[r : r + 1], edges[edge + r : edge + r + 1],
            )

    span = 3 * out_width

    def convolve(begin, count):
        total = 0.0
        for a in range(3):
            total = total + jnp.dot(
                cat_ref[(begin + 2 - a) * tile_cols : (begin + 2 - a + count) * tile_cols, :],
                turned_ref[a * span : (a + 1) * span, :],
                preferred_element_type=f32,
            )
        out_ref[begin * tile_cols : (begin + count) * tile_cols, :] = total.astype(bf16)

    last = len(lines) - 1
    middle = last // 2
    half_rows = middle * step
    upstream(0)
    for c in range(last):
        upstream(c + 1)
        fill(c)
        if c == middle:
            convolve(0, half_rows)
    fill(last)
    convolve(half_rows, tile_rows - half_rows)


def on_device(canvas, conv_weight, conv_bias, target_gram):
    tile_rows, tile_cols, in_width = canvas.shape
    out_width = conv_weight.shape[3]
    pixel_total = tile_rows * tile_cols * lax.axis_size("rows") * lax.axis_size("cols")
    shape = (tile_rows, tile_cols, in_width, out_width, 2)
    kernel = conv_weight.reshape(9 * in_width, out_width)
    params = pltpu.CompilerParams(vmem_limit_bytes=24 * 1024 * 1024)
    vmem = pl.BlockSpec(memory_space=pltpu.VMEM)
    packed_shape = jax.ShapeDtypeStruct((len(tile_pairs(out_width)) * tile, tile), f32)

    rim_shape = jax.ShapeDtypeStruct((2, tile_rows, in_width), bf16)
    two = lax.axis_size("cols") == 2
    count = lax.axis_size("rows")
    main_shape = jax.ShapeDtypeStruct((2 * tile_cols, in_width), bf16)
    *rims, even, odd = local(
        rim_kernel,
        (*(rim_shape,) * (1 if two else 2), main_shape, main_shape),
        "rims",
        canvas,
        cost_estimate=pl.CostEstimate(flops=4_000_000_000, bytes_accessed=600_000, transcendentals=0),
    )
    if two:
        beyond = [lax.ppermute(rims[0], "cols", [(0, 1), (1, 0)])]
    else:
        beyond = shift_cols(rims[1], rims[0])
    evens, odds = range(0, count, 2), range(1, count, 2)
    even = swap_rows(evens, even)
    payload_shape = jax.ShapeDtypeStruct((2 * tile_cols + edge, in_width), bf16)
    end_shape = jax.ShapeDtypeStruct((edge, in_width), bf16)
    half_shape = jax.ShapeDtypeStruct((1, *target_gram.shape), bf16)
    odd, left, right, rows = local(
        payload_kernel,
        (payload_shape, rim_shape, rim_shape, half_shape),
        "row_rims",
        target_gram,
        odd,
        *beyond,
    )
    odd = swap_rows(odds, odd)
    weights, _ = lax.optimization_barrier((kernel, left))
    turned = local(
        turn_kernel,
        jax.ShapeDtypeStruct((9 * out_width, in_width), bf16),
        "turn",
        weights,
        cost_estimate=chained,
    )
    even_rim = local(even_rim_kernel, end_shape, "even_rim", left, right, turned)
    halo = [even, odd, swap_rows(evens, even_rim)]
    bits = (lax.axis_size("rows") * lax.axis_size("cols")).bit_length() - 1
    gather = Gather(rows)
    far = list(reversed(range(3, bits)))
    inner = (tile_rows - 2) * tile_cols
    in_feat, in_slope, in_gram, bias, part = pl.pallas_call(
        functools.partial(inner_kernel, shape),
        out_shape=(
            jax.ShapeDtypeStruct((inner, out_width), bf16),
            jax.ShapeDtypeStruct((inner, out_width), bf16),
            packed_shape,
            jax.ShapeDtypeStruct((1, out_width), f32),
            jax.ShapeDtypeStruct((4 * tile_cols, out_width), f32),
        ),
        in_specs=[vmem] * 5,
        scratch_shapes=[pltpu.VMEM((tile_rows * tile_cols, 3 * in_width), bf16)],
        compiler_params=params,
        name="inner_rows",
        cost_estimate=pl.CostEstimate(
            flops=2 * inner * (9 * in_width + out_width) * out_width,
            bytes_accessed=6_000_000,
            transcendentals=inner * out_width,
        ),
    )(canvas, left, right, kernel, conv_bias)

    half_gram = (packed_shape.shape[0] // 2, tile)
    halo_scratch = [pltpu.VMEM(payload_shape.shape, bf16), pltpu.VMEM(payload_shape.shape, bf16)]
    out_feat, out_slope, send, keep = pl.pallas_call(
        functools.partial(outer_kernel, shape),
        out_shape=(
            jax.ShapeDtypeStruct((2 * tile_cols, out_width), bf16),
            jax.ShapeDtypeStruct((2 * tile_cols, out_width), bf16),
            jax.ShapeDtypeStruct(half_gram, bf16),
            jax.ShapeDtypeStruct(half_gram, f32),
        ),
        in_specs=[vmem] * 6,
        scratch_shapes=[
            *halo_scratch,
            pltpu.VMEM((2 * tile_cols, 3 * in_width), bf16),
            pltpu.VMEM(packed_shape.shape, f32),
        ],
        compiler_params=params,
        name="outer_rows",
    )(*halo, kernel, in_gram, part)

    exchanges = {
        "halve 0": [(bit,) for bit in far[:1]],
        "halve 1": [(bit,) for bit in far[1:]],
        "add 0": [(1, 2)],
        "add 1": [(2, 1)],
        "join 0": [(0,)],
    }
    prepared, far_pixels = [], []

    def beside(name, sent, got):
        if name == "join 1":
            outer = 2 * tile_cols + 2 * edge
            rim_sums, _ = lax.optimization_barrier((part, sent))
            far_pixels.extend(
                pl.pallas_call(
                    functools.partial(beyond_kernel, shape),
                    out_shape=(jax.ShapeDtypeStruct((outer, out_width), bf16),) * 2,
                    in_specs=[vmem] * 9,
                    scratch_shapes=[
                        *halo_scratch,
                        pltpu.VMEM((4 * tile_cols, 3 * in_width), bf16),
                        pltpu.VMEM((2 * edge, 9 * in_width), bf16),
                    ],
                    compiler_params=params,
                    name="beyond",
                    cost_estimate=chained,
                )(canvas, *halo, left, right, kernel, bias, rim_sums)
            )
            gather.settle(sent)
            got, gather.rows, *_ = lax.optimization_barrier((got, gather.rows, *far_pixels))
            return got
        for bit in exchanges.get(name, []):
            gather.step(sent, *bit)
        if name == "join 0":
            got, gather.rows = lax.optimization_barrier((got, gather.rows))
        if name != "halves":
            return got
        gather.settle(sent)
        prepared.append(
            local(
                prepare_kernel,
                jax.ShapeDtypeStruct((out_width, out_width), f32),
                "prepare",
                gather.rows.reshape(out_width, out_width),
                cost_estimate=waiting,
            )
        )
        return lax.optimization_barrier((got, *prepared))[0]

    mine, other = sum_all(send, keep, beside)
    (both,) = prepared
    far_feat, far_slope = far_pixels
    own_gram, grad = pl.pallas_call(
        functools.partial(backward_kernel, shape, pixel_total),
        out_shape=(
            jax.ShapeDtypeStruct(target_gram.shape, f32),
            jax.ShapeDtypeStruct((tile_rows * tile_cols, in_width), bf16),
        ),
        in_specs=[vmem] * 10,
        scratch_shapes=[
            pltpu.VMEM(packed_shape.shape, f32),
            pltpu.VMEM((out_width, out_width), f32),
            pltpu.VMEM((out_width, out_width), bf16),
            pltpu.VMEM(((tile_rows + 2) * tile_cols, 3 * out_width), bf16),
        ],
        compiler_params=params,
        name="grad_conv",
    )(mine, other, both, in_feat, in_slope, out_feat, out_slope, far_feat, far_slope, turned)
    return own_gram, grad.reshape(tile_rows, tile_cols, in_width)


def solution(mesh):
    return jax.shard_map(
        on_device,
        mesh=mesh,
        in_specs=(P("rows", "cols", None), P(), P(), P(("rows", "cols"), None)),
        out_specs=(P(("rows", "cols"), None), P("rows", "cols", None)),
        check_vma=False,
    )
```

```python
import functools
import math

import jax
import jax.numpy as jnp
from jax import lax
from jax.experimental import pallas as pl
from jax.experimental.pallas import tpu as pltpu
from jax.sharding import PartitionSpec as P

gelu_scale = math.sqrt(2.0 / math.pi)
tile = 128
edge = 16
f32, bf16 = jnp.float32, jnp.bfloat16


def tile_pairs(width):
    count = width // tile
    return [(i, j) for i in range(count) for j in range(i, count)]


def swap_rows(low, value):
    count, cols = lax.axis_size("rows"), lax.axis_size("cols")
    partner = {i: i + 1 for i in low if i + 1 < count}
    partner.update({i + 1: i for i in low if i + 1 < count})
    perm = [
        (r * cols + c, partner[r] * cols + c if r in partner else r * cols + (c ^ 1))
        for r in range(count)
        for c in range(cols)
    ]
    return lax.ppermute(value, ("rows", "cols"), perm)


def shift_cols(last, first):
    count = lax.axis_size("cols")
    forward = [(i, i + 1) for i in range(count - 1)]
    backward = [(target, source) for source, target in forward]
    return lax.ppermute(last, "cols", forward), lax.ppermute(first, "cols", backward)


def device_index():
    return lax.axis_index("rows") * lax.axis_size("cols") + lax.axis_index("cols")


def swap(value, bit, other=None):
    total = lax.axis_size("rows") * lax.axis_size("cols")
    flip = lambda i: 1 << (other if other is not None and i.bit_count() % 2 else bit) | 1
    return lax.ppermute(value, ("rows", "cols"), [(i, i ^ flip(i)) for i in range(total)])


def local(body, out_shape, name, *operands, **kwargs):
    return pl.pallas_call(
        body,
        out_shape=out_shape,
        in_specs=[pl.BlockSpec(memory_space=pltpu.VMEM)] * len(operands),
        compiler_params=pltpu.CompilerParams(vmem_limit_bytes=8 * 1024 * 1024),
        name=name,
        **kwargs,
    )(*operands)


def side_of(bit, other=None):
    index = device_index()
    if bit > 0:
        side = lax.rem(index // (1 << bit), 2)
        if other is None:
            return side
        return jnp.where(side_of(0) == 0, side, lax.rem(index // (1 << other), 2))
    bits = (lax.axis_size("rows") * lax.axis_size("cols")).bit_length() - 1
    return lax.rem(sum(lax.rem(index // (1 << k), 2) for k in range(bits)), 2)


def rows_at(index, count):
    return pl.ds(pl.multiple_of(index * count, count), count)


waiting = pl.CostEstimate(flops=1_500_000_000, bytes_accessed=100_000, transcendentals=0)
chained = pl.CostEstimate(flops=8_000_000_000, bytes_accessed=100_000, transcendentals=0)


def halve(keep, got, bit, other=None):
    half = keep.shape[0] // 2

    def body(keep_ref, got_ref, send_ref, stay_ref):
        side = side_of(bit, other)
        away, here = rows_at(1 - side, half), rows_at(side, half)
        send_ref[...] = (keep_ref[away, :] + got_ref[away, :].astype(f32)).astype(bf16)
        stay_ref[...] = keep_ref[here, :] + got_ref[here, :].astype(f32)

    shape = (half, keep.shape[1])
    return local(
        body,
        (jax.ShapeDtypeStruct(shape, bf16), jax.ShapeDtypeStruct(shape, f32)),
        "halve",
        keep,
        got,
        cost_estimate=chained,
    )


def add(keep, got):
    def body(keep_ref, got_ref, sum_ref):
        sum_ref[...] = (keep_ref[...].astype(f32) + got_ref[...].astype(f32)).astype(bf16)

    return local(body, jax.ShapeDtypeStruct(got.shape, bf16), "add", keep, got, cost_estimate=chained)


def join(mine, got, bit, other=None, **kwargs):
    def body(mine_ref, got_ref, both_ref):
        side = side_of(bit, other)
        both_ref[:, pl.ds(side, 1)] = mine_ref[...][:, None]
        both_ref[:, pl.ds(1 - side, 1)] = got_ref[...][:, None]

    shape = (mine.shape[0], 2, *mine.shape[1:])
    return local(body, jax.ShapeDtypeStruct(shape, mine.dtype), "join", mine, got, **kwargs)


def join_second(mine, got, bit, other, **kwargs):
    def body(mine_ref, got_ref, both_ref):
        parity, side = side_of(0), side_of(bit, other)

        @pl.when(parity == 0)
        def _():
            both_ref[:, pl.ds(side, 1)] = mine_ref[...][:, None]
            both_ref[:, pl.ds(1 - side, 1)] = got_ref[...][:, None]

        @pl.when(parity == 1)
        def _():
            both_ref[:, :, pl.ds(side, 1)] = mine_ref[...][:, :, None]
            both_ref[:, :, pl.ds(1 - side, 1)] = got_ref[...][:, :, None]

    shape = (mine.shape[0], 2, *mine.shape[1:])
    return local(body, jax.ShapeDtypeStruct(shape, mine.dtype), "join_second", mine, got, **kwargs)


def join_cores(mine, other, **kwargs):
    def body(mine_ref, other_ref, both_ref):
        side = side_of(0)
        for chip in range(mine.shape[0]):
            core = lax.rem(side + chip.bit_count(), 2)
            both_ref[chip, pl.ds(core, 1)] = mine_ref[chip][None]
            both_ref[chip, pl.ds(1 - core, 1)] = other_ref[chip][None]

    shape = (mine.shape[0], 2, *mine.shape[1:])
    return local(body, jax.ShapeDtypeStruct(shape, mine.dtype), "join_cores", mine, other, **kwargs)


class Gather:
    def __init__(self, rows):
        self.rows, self.got, self.last = rows, None, None

    def settle(self, after):
        if self.got is None:
            self.rows, _ = lax.optimization_barrier((self.rows, after))
            return
        share = self.rows.shape[-2:]
        got, _ = lax.optimization_barrier((self.got, after))
        bit, other = self.last
        if bit == 0:
            both = join_cores(self.rows, got, cost_estimate=waiting)
        elif other is None or bit < other:
            mine, got = (part.reshape(-1, 1, *share) for part in (self.rows, got))
            both = join(mine, got, bit, other, cost_estimate=waiting)
        else:
            mine, got = (part.reshape(-1, 2, *share) for part in (self.rows, got))
            both = join_second(mine, got, bit, other, cost_estimate=waiting)
        self.rows, self.got = both.reshape(-1, *share), None

    def step(self, after, bit, other=None):
        self.settle(after)
        self.got, self.last = swap(self.rows, bit, other), (bit, other)


def sum_all(send, keep, beside):
    bits = (lax.axis_size("rows") * lax.axis_size("cols")).bit_length() - 1
    halving = [(1, 2), (2, 1)]
    adding = [(bit,) for bit in reversed(range(3, bits))]

    got = beside("cores", send, swap(send, 0))
    for n, pair in enumerate(halving):
        send, keep = halve(keep, got, *pair)
        got = beside(f"halve {n}", send, swap(send, *pair))
    mine = add(keep, got)
    for n, pair in enumerate(adding):
        mine = add(mine, beside(f"add {n}", mine, swap(mine, *pair)))
    for n, pair in enumerate(reversed(halving)):
        got = beside(f"join {n}", mine, swap(mine, *pair))
        mine = join(mine[None], got[None], *pair, cost_estimate=chained).reshape(-1, mine.shape[1])
    return mine, beside("halves", mine, swap(mine, 0))


def gelu_pair(value):
    square = value * value
    tangent = jnp.tanh(value * (gelu_scale + gelu_scale * 0.044715 * square))
    half = 0.5 * value
    plus = 0.5 + 0.5 * tangent
    grad = plus + half * (1.0 - tangent * tangent) * (
        gelu_scale + gelu_scale * 3.0 * 0.044715 * square
    )
    return value * plus, grad


def column(value, c):
    return jnp.concatenate([value[r, c : c + 1] for r in range(value.shape[0])], axis=0)


def rim_kernel(canvas_ref, *out_refs):
    even_ref, odd_ref = out_refs[-2:]
    rows, cols, _ = canvas_ref.shape
    begin = canvas_ref[:, 0:16, :].astype(f32)
    end = canvas_ref[:, cols - 16 :, :].astype(f32)
    for c in range(2):
        pair = column(begin, c), column(end, 14 + c)
        if len(out_refs) == 3:
            out_refs[0][c] = jnp.where(lax.axis_index("cols") == 0, pair[1], pair[0]).astype(bf16)
        else:
            out_refs[0][c], out_refs[1][c] = pair[0].astype(bf16), pair[1].astype(bf16)
    odd = lax.rem(lax.axis_index("rows"), 2)
    for case, low_ref, high_ref in ((0, odd_ref, even_ref), (1, even_ref, odd_ref)):

        @pl.when(odd == case)
        def _():
            for k in range(2):
                at = slice(k * cols, (k + 1) * cols)
                low_ref[at, :], high_ref[at, :] = canvas_ref[k], canvas_ref[rows - 2 + k]


def payload_kernel(target_ref, rows_ref, *refs):
    even_ref, payload_ref, left_ref, right_ref, half_ref = refs[-5:]
    main = rows_ref.shape[0]
    payload_ref[0:main, :] = rows_ref[...]
    odd_ref = payload_ref.at[main:]
    half_ref[0] = target_ref[...].astype(bf16)
    if len(refs) == 6:
        here = lax.axis_index("cols")
        other = refs[0][...].astype(f32)
        left_ref[...] = jnp.where(here == 0, 0.0, other).astype(bf16)
        right_ref[...] = jnp.where(here == 0, other, 0.0).astype(bf16)
    else:
        left_ref[...], right_ref[...] = refs[0][...], refs[1][...]
    beyond = [ref[c].astype(f32) for ref in (left_ref, right_ref) for c in range(2)]
    rows, width = beyond[0].shape

    def rim(r):
        parts = [part[r + k : r + k + 1] for k in range(2) for part in beyond]
        return jnp.concatenate([*parts, jnp.zeros((8, width), f32)], axis=0).astype(bf16)

    odd = lax.rem(lax.axis_index("rows"), 2)
    for case, low_ref, high_ref in ((0, odd_ref, even_ref), (1, even_ref, odd_ref)):

        @pl.when(odd == case)
        def _():
            low_ref[...], high_ref[...] = rim(0), rim(rows - 2)


def moved_rows(row, before, after):
    cols = row.shape[0]
    wide = row.astype(f32)
    place = lax.broadcasted_iota(jnp.int32, (8, row.shape[1]), 0)
    right, left = pltpu.roll(wide, 1, 0), pltpu.roll(wide, cols - 1, 0)
    right = jnp.concatenate([jnp.where(place == 0, before, right[:8]), right[8:]], axis=0)
    left = jnp.concatenate([left[:-8], jnp.where(place == 7, after, left[-8:])], axis=0)
    return right.astype(bf16), row.astype(bf16), left.astype(bf16)


def fill_row(cat_ref, r, row, before, after):
    cols, width = row.shape
    for b, part in enumerate(moved_rows(row, before, after)):
        cat_ref[r * cols : (r + 1) * cols, b * width : (b + 1) * width] = part


def gram_tiles(feat, gram_ref, base_ref=None):
    width = feat.shape[1]
    half = width // 2
    product = functools.partial(
        lax.dot_general,
        dimension_numbers=(((0,), (0,)), ((), ())),
        preferred_element_type=f32,
    )
    upper = product(feat[:, :half], feat)
    lower = product(feat[:, half:], feat[:, half:])
    for n, (i, j) in enumerate(tile_pairs(width)):
        at = slice(n * tile, (n + 1) * tile)
        if i * tile < half:
            part = upper[i * tile : (i + 1) * tile, j * tile : (j + 1) * tile]
        else:
            k, m = i * tile - half, j * tile - half
            part = lower[k : k + tile, m : m + tile]
        gram_ref[at, :] = part if base_ref is None else part + base_ref[at, :]


def inner_kernel(
    shape, own_ref, left_ref, right_ref, kernel_ref, bias_ref,
    feat_ref, slope_ref, gram_ref, row_ref, part_ref, cat_ref,
):
    row_ref[...] = bias_ref[...].astype(f32).reshape(row_ref.shape)
    tile_rows, tile_cols, in_width, out_width, step = shape
    lefts, rights = left_ref[1].astype(f32), right_ref[0].astype(f32)
    for r in range(tile_rows):
        fill_row(cat_ref, r, own_ref[r], lefts[r : r + 1], rights[r : r + 1])
    bias = row_ref[...]
    root = 1.0 / math.sqrt(out_width)
    span = 3 * in_width

    def product(begin, count, a):
        return jnp.dot(
            cat_ref[begin * tile_cols : (begin + count) * tile_cols, :],
            kernel_ref[a * span : (a + 1) * span, :],
            preferred_element_type=f32,
        )

    for h in range(0, tile_rows - 2, step):
        total = bias
        for a in range(3):
            total = total + product(h + a, step, a)
        features, slope = gelu_pair(total)
        at = slice(h * tile_cols, (h + step) * tile_cols)
        feat_ref[at, :] = features.astype(bf16)
        slope_ref[at, :] = (slope * root).astype(bf16)
    low, high = product(0, 2, 2), product(tile_rows - 2, 2, 0)
    ends = product(0, 1, 1), product(tile_rows - 1, 1, 1)
    part_ref[0:tile_cols, :] = low[:tile_cols] + bias
    part_ref[tile_cols : 2 * tile_cols, :] = low[tile_cols:] + ends[0] + bias
    part_ref[2 * tile_cols : 3 * tile_cols, :] = high[:tile_cols] + ends[1] + bias
    part_ref[3 * tile_cols :, :] = high[tile_cols:] + bias
    gram_tiles(feat_ref[...], gram_ref)


def halo_rows(halo_refs, low_ref, high_ref):
    even_ref, odd_ref, even_rim_ref = halo_refs
    row = lax.axis_index("rows")
    odd = lax.rem(row, 2)
    main = even_ref.shape[0]
    for at, even in ((slice(0, main), even_ref), (slice(main, None), even_rim_ref)):
        low_ref[at, :] = jnp.where(odd == 0, odd_ref[at, :], even[...])
        high_ref[at, :] = jnp.where(odd == 0, even[...], odd_ref[at, :])

    @pl.when(row == 0)
    def _():
        low_ref[...] = jnp.zeros_like(low_ref)

    @pl.when(row == lax.axis_size("rows") - 1)
    def _():
        high_ref[...] = jnp.zeros_like(high_ref)


def halves(width):
    return slice(0, width // 2), slice(width // 2, width)


def outer_kernel(
    shape, even_ref, odd_ref, even_rim_ref, kernel_ref, base_ref, part_ref,
    feat_ref, slope_ref, send_ref, keep_ref, low_ref, high_ref, cat_ref, gram_ref,
):
    tile_rows, tile_cols, in_width, out_width, step = shape
    span, main = 3 * in_width, 2 * tile_cols
    halo_rows((even_ref, odd_ref, even_rim_ref), low_ref, high_ref)
    for n, (source, at) in enumerate([(low_ref, tile_cols), (high_ref, 0)]):
        rim = source[main:, :].astype(f32)
        k = 4 * (1 - n)
        fill_row(cat_ref, n, source[at : at + tile_cols, :], rim[k + 1 : k + 2], rim[k + 2 : k + 3])
    root = 1.0 / math.sqrt(out_width)
    for at in halves(out_width):
        for n, a in enumerate([0, 2]):
            rows = slice(n * tile_cols, (n + 1) * tile_cols)
            features, slope = gelu_pair(
                part_ref[(n + 1) * tile_cols : (n + 2) * tile_cols, at]
                + jnp.dot(
                    cat_ref[rows, :],
                    kernel_ref[a * span : (a + 1) * span, at],
                    preferred_element_type=f32,
                )
            )
            feat_ref[rows, at] = features.astype(bf16)
            slope_ref[rows, at] = (slope * root).astype(bf16)
    gram_tiles(feat_ref[...], gram_ref, base_ref)
    half = send_ref.shape[0]
    side = side_of(0)
    send_ref[...] = gram_ref[rows_at(1 - side, half), :].astype(bf16)
    keep_ref[...] = gram_ref[rows_at(side, half), :]


def beyond_kernel(
    shape, own_ref, even_ref, odd_ref, even_rim_ref, left_ref, right_ref, kernel_ref, bias_ref,
    part_ref, feat_ref, slope_ref, low_ref, high_ref, cat_ref, edge_ref,
):
    tile_rows, tile_cols, in_width, out_width, step = shape
    halo_rows((even_ref, odd_ref, even_rim_ref), low_ref, high_ref)
    first = (lax.axis_index("rows") > 0).astype(f32)
    last = (lax.axis_index("rows") < lax.axis_size("rows") - 1).astype(f32)
    left = (lax.axis_index("cols") > 0).astype(f32)
    right = (lax.axis_index("cols") < lax.axis_size("cols") - 1).astype(f32)
    main = 2 * tile_cols
    low_rim, high_rim = low_ref[main:, :].astype(f32), high_ref[main:, :].astype(f32)
    own_begin = column(own_ref[:, 0:16, :].astype(f32), 0)
    own_end = column(own_ref[:, tile_cols - 16 :, :].astype(f32), 15)

    def sides(c, own):
        return jnp.concatenate(
            [low_rim[c : c + 1], low_rim[4 + c : 5 + c], own, high_rim[c : c + 1], high_rim[4 + c : 5 + c]],
            axis=0,
        )

    def ends(c, own):
        c16 = c // 16 * 16
        piece = lambda ref, k: ref[k + c16 : k + c16 + 16, :].astype(f32)[c - c16 : c - c16 + 1]
        rows = [piece(low_ref, 0), piece(low_ref, tile_cols), own]
        return jnp.concatenate([*rows, piece(high_ref, 0), piece(high_ref, tile_cols)], axis=0)

    lefts = [
        sides(0, left_ref[0].astype(f32)), sides(1, left_ref[1].astype(f32)), ends(0, own_begin)
    ]
    rights = [
        ends(tile_cols - 1, own_end), sides(2, right_ref[0].astype(f32)), sides(3, right_ref[1].astype(f32))
    ]
    span = 3 * in_width
    for r, line in enumerate([0, 1, tile_rows + 2, tile_rows + 3]):
        source = low_ref if r < 2 else high_ref
        row = source[r % 2 * tile_cols : (r % 2 + 1) * tile_cols, :]
        fill_row(cat_ref, r, row, lefts[1][line : line + 1], rights[1][line : line + 1])
    blank = jnp.zeros((edge - tile_rows - 2, in_width), f32)
    for a in range(3):
        for b in range(3):
            piece = jnp.concatenate(
                [lefts[b][a : a + tile_rows + 2], blank, rights[b][a : a + tile_rows + 2], blank],
                axis=0,
            )
            at = (3 * a + b) * in_width
            edge_ref[:, at : at + in_width] = piece.astype(bf16)
    root = 1.0 / math.sqrt(out_width)
    line = lax.broadcasted_iota(jnp.int32, (2 * edge, out_width // 2), 0)
    weight = jnp.where(line < edge, left, right)
    weight = jnp.where(line % edge == 0, weight * first, weight)
    weight = jnp.where(line % edge == tile_rows + 1, weight * last, weight)
    for at in halves(out_width):

        def product(begin, a):
            return jnp.dot(
                cat_ref[begin * tile_cols : (begin + 1) * tile_cols, :],
                kernel_ref[a * span : (a + 1) * span, at],
                preferred_element_type=f32,
            )

        totals = [
            part_ref[0:tile_cols, at] + product(0, 0) + product(1, 1),
            part_ref[3 * tile_cols :, at] + product(2, 1) + product(3, 2),
            bias_ref[:, at] + jnp.dot(edge_ref[...], kernel_ref[:, at], preferred_element_type=f32),
        ]
        scales = [first * root, last * root, weight * root]
        for n, (total, scale) in enumerate(zip(totals, scales)):
            features, slope = gelu_pair(total)
            rows = slice(n * tile_cols, n * tile_cols + total.shape[0])
            feat_ref[rows, at] = features.astype(bf16)
            slope_ref[rows, at] = (slope * scale).astype(bf16)


def turn_kernel(kernel_ref, turned_ref):
    taps, in_width, out_width = 9, kernel_ref.shape[0] // 9, kernel_ref.shape[1]
    for n in range(taps):
        to = (n // 3 * 3 + 2 - n % 3) * out_width
        turned_ref[to : to + out_width, :] = kernel_ref[n * in_width : (n + 1) * in_width, :].T


def prepare_kernel(target_ref, both_ref):
    for i, j in tile_pairs(target_ref.shape[0]):
        at_i, at_j = slice(i * tile, (i + 1) * tile), slice(j * tile, (j + 1) * tile)
        both = target_ref[at_i, at_j].astype(f32) + target_ref[at_j, at_i].astype(f32).T
        both_ref[at_i, at_j] = both
        if i != j:
            both_ref[at_j, at_i] = both.T


def backward_kernel(
    shape, pixel_total, mine_ref, other_ref, both_ref, in_feat_ref, in_slope_ref, out_feat_ref, out_slope_ref,
    far_feat_ref, far_slope_ref, turned_ref, own_gram_ref, out_ref, gram_ref, full_ref, sym_ref, cat_ref,
):
    tile_rows, tile_cols, in_width, out_width, step = shape
    half = mine_ref.shape[0]
    side = side_of(0)
    gram_ref[rows_at(side, half), :] = mine_ref[...].astype(f32)
    gram_ref[rows_at(1 - side, half), :] = other_ref[...].astype(f32)
    for n, (i, j) in enumerate(tile_pairs(out_width)):
        at_i, at_j = slice(i * tile, (i + 1) * tile), slice(j * tile, (j + 1) * tile)
        gram = gram_ref[n * tile : (n + 1) * tile, :] * (1.0 / pixel_total)
        full_ref[at_i, at_j] = gram
        sym_ref[at_i, at_j] = (2.0 * gram - both_ref[at_i, at_j]).astype(bf16)
        if i != j:
            gram = gram.T
            full_ref[at_j, at_i] = gram
            sym_ref[at_j, at_i] = (2.0 * gram - both_ref[at_j, at_i]).astype(bf16)
    share = own_gram_ref.shape[0]
    start = device_index() * share
    if share % 8 == 0:
        own_gram_ref[...] = full_ref[pl.ds(pl.multiple_of(start, 8), share), :]
    else:
        group = full_ref[pl.ds(pl.multiple_of(start // 8 * 8, 8), 8), :]
        picked = group[0:share]
        for k in range(share, 8, share):
            picked = jnp.where(start % 8 == k, group[k : k + share], picked)
        own_gram_ref[...] = picked

    def grad_of(feat_ref, slope_ref, at):
        product = jnp.dot(feat_ref[at, :], sym_ref[...], preferred_element_type=f32)
        return product * slope_ref[at, :].astype(f32)

    main = 2 * tile_cols
    edges = grad_of(far_feat_ref, far_slope_ref, slice(main, None))
    near, far = (out_feat_ref, out_slope_ref), (far_feat_ref, far_slope_ref)
    lines = [[(*far, 0), (*near, 0)]]
    lines += [
        [(in_feat_ref, in_slope_ref, k * tile_cols) for k in range(h, h + step)]
        for h in range(0, tile_rows - 2, step)
    ]
    lines += [[(*near, tile_cols), (*far, tile_cols)]]
    grads = {}

    def upstream(c):
        pieces = lines[c]
        if pieces[0][0] is pieces[1][0]:
            feat_ref, slope_ref, begin = pieces[0]
            grads[c] = grad_of(feat_ref, slope_ref, slice(begin, begin + step * tile_cols))
        else:
            parts = [grad_of(feat, slope, slice(begin, begin + tile_cols)) for feat, slope, begin in pieces]
            grads[c] = jnp.concatenate(parts, axis=0)

    def fill(c):
        for k in range(step):
            r = c * step + k
            fill_row(
                cat_ref, r, grads[c][k * tile_cols : (k + 1) * tile_cols],
                edges[r : r + 1], edges[edge + r : edge + r + 1],
            )

    span = 3 * out_width

    def convolve(begin, count):
        total = 0.0
        for a in range(3):
            total = total + jnp.dot(
                cat_ref[(begin + 2 - a) * tile_cols : (begin + 2 - a + count) * tile_cols, :],
                turned_ref[a * span : (a + 1) * span, :],
                preferred_element_type=f32,
            )
        out_ref[begin * tile_cols : (begin + count) * tile_cols, :] = total.astype(bf16)

    last = len(lines) - 1
    middle = last // 2
    half_rows = middle * step
    upstream(0)
    for c in range(last):
        upstream(c + 1)
        fill(c)
        if c == middle:
            convolve(0, half_rows)
    fill(last)
    convolve(half_rows, tile_rows - half_rows)


def on_device(canvas, conv_weight, conv_bias, target_gram):
    tile_rows, tile_cols, in_width = canvas.shape
    out_width = conv_weight.shape[3]
    pixel_total = tile_rows * tile_cols * lax.axis_size("rows") * lax.axis_size("cols")
    shape = (tile_rows, tile_cols, in_width, out_width, 2)
    kernel = conv_weight.reshape(9 * in_width, out_width)
    params = pltpu.CompilerParams(vmem_limit_bytes=24 * 1024 * 1024)
    vmem = pl.BlockSpec(memory_space=pltpu.VMEM)
    packed_shape = jax.ShapeDtypeStruct((len(tile_pairs(out_width)) * tile, tile), f32)

    rim_shape = jax.ShapeDtypeStruct((2, tile_rows, in_width), bf16)
    two = lax.axis_size("cols") == 2
    count = lax.axis_size("rows")
    main_shape = jax.ShapeDtypeStruct((2 * tile_cols, in_width), bf16)
    *rims, even, odd = local(
        rim_kernel,
        (*(rim_shape,) * (1 if two else 2), main_shape, main_shape),
        "rims",
        canvas,
        cost_estimate=pl.CostEstimate(flops=4_000_000_000, bytes_accessed=600_000, transcendentals=0),
    )
    if two:
        beyond = [lax.ppermute(rims[0], "cols", [(0, 1), (1, 0)])]
    else:
        beyond = shift_cols(rims[1], rims[0])
    evens, odds = range(0, count, 2), range(1, count, 2)
    even = swap_rows(evens, even)
    payload_shape = jax.ShapeDtypeStruct((2 * tile_cols + edge, in_width), bf16)
    end_shape = jax.ShapeDtypeStruct((edge, in_width), bf16)
    half_shape = jax.ShapeDtypeStruct((1, *target_gram.shape), bf16)
    even_rim, odd, left, right, rows = local(
        payload_kernel,
        (end_shape, payload_shape, rim_shape, rim_shape, half_shape),
        "row_rims",
        target_gram,
        odd,
        *beyond,
    )
    halo = [even, swap_rows(odds, odd), swap_rows(evens, even_rim)]
    bits = (lax.axis_size("rows") * lax.axis_size("cols")).bit_length() - 1
    gather = Gather(rows)
    far = list(reversed(range(3, bits)))
    inner = (tile_rows - 2) * tile_cols
    in_feat, in_slope, in_gram, bias, part = pl.pallas_call(
        functools.partial(inner_kernel, shape),
        out_shape=(
            jax.ShapeDtypeStruct((inner, out_width), bf16),
            jax.ShapeDtypeStruct((inner, out_width), bf16),
            packed_shape,
            jax.ShapeDtypeStruct((1, out_width), f32),
            jax.ShapeDtypeStruct((4 * tile_cols, out_width), f32),
        ),
        in_specs=[vmem] * 5,
        scratch_shapes=[pltpu.VMEM((tile_rows * tile_cols, 3 * in_width), bf16)],
        compiler_params=params,
        name="inner_rows",
        cost_estimate=pl.CostEstimate(
            flops=2 * inner * (9 * in_width + out_width) * out_width,
            bytes_accessed=6_000_000,
            transcendentals=inner * out_width,
        ),
    )(canvas, left, right, kernel, conv_bias)

    weights, in_gram = lax.optimization_barrier((kernel, in_gram))
    turned = local(
        turn_kernel,
        jax.ShapeDtypeStruct((9 * out_width, in_width), bf16),
        "turn",
        weights,
        cost_estimate=waiting,
    )
    in_gram, turned = lax.optimization_barrier((in_gram, turned))
    half_gram = (packed_shape.shape[0] // 2, tile)
    halo_scratch = [pltpu.VMEM(payload_shape.shape, bf16), pltpu.VMEM(payload_shape.shape, bf16)]
    out_feat, out_slope, send, keep = pl.pallas_call(
        functools.partial(outer_kernel, shape),
        out_shape=(
            jax.ShapeDtypeStruct((2 * tile_cols, out_width), bf16),
            jax.ShapeDtypeStruct((2 * tile_cols, out_width), bf16),
            jax.ShapeDtypeStruct(half_gram, bf16),
            jax.ShapeDtypeStruct(half_gram, f32),
        ),
        in_specs=[vmem] * 6,
        scratch_shapes=[
            *halo_scratch,
            pltpu.VMEM((2 * tile_cols, 3 * in_width), bf16),
            pltpu.VMEM(packed_shape.shape, f32),
        ],
        compiler_params=params,
        name="outer_rows",
    )(*halo, kernel, in_gram, part)

    exchanges = {
        "halve 0": [(bit,) for bit in far[:1]],
        "halve 1": [(bit,) for bit in far[1:]],
        "add 0": [(1, 2)],
        "add 1": [(2, 1)],
        "join 0": [(0,)],
    }
    prepared, far_pixels = [], []

    def beside(name, sent, got):
        if name == "join 1":
            outer = 2 * tile_cols + 2 * edge
            rim_sums, _ = lax.optimization_barrier((part, sent))
            far_pixels.extend(
                pl.pallas_call(
                    functools.partial(beyond_kernel, shape),
                    out_shape=(jax.ShapeDtypeStruct((outer, out_width), bf16),) * 2,
                    in_specs=[vmem] * 9,
                    scratch_shapes=[
                        *halo_scratch,
                        pltpu.VMEM((4 * tile_cols, 3 * in_width), bf16),
                        pltpu.VMEM((2 * edge, 9 * in_width), bf16),
                    ],
                    compiler_params=params,
                    name="beyond",
                    cost_estimate=chained,
                )(canvas, *halo, left, right, kernel, bias, rim_sums)
            )
            gather.settle(sent)
            got, gather.rows, *_ = lax.optimization_barrier((got, gather.rows, *far_pixels))
            return got
        for bit in exchanges.get(name, []):
            gather.step(sent, *bit)
        if name == "join 0":
            got, gather.rows = lax.optimization_barrier((got, gather.rows))
        if name != "halves":
            return got
        gather.settle(sent)
        prepared.append(
            local(
                prepare_kernel,
                jax.ShapeDtypeStruct((out_width, out_width), f32),
                "prepare",
                gather.rows.reshape(out_width, out_width),
                cost_estimate=waiting,
            )
        )
        return lax.optimization_barrier((got, *prepared))[0]

    mine, other = sum_all(send, keep, beside)
    (both,) = prepared
    far_feat, far_slope = far_pixels
    own_gram, grad = pl.pallas_call(
        functools.partial(backward_kernel, shape, pixel_total),
        out_shape=(
            jax.ShapeDtypeStruct(target_gram.shape, f32),
            jax.ShapeDtypeStruct((tile_rows * tile_cols, in_width), bf16),
        ),
        in_specs=[vmem] * 10,
        scratch_shapes=[
            pltpu.VMEM(packed_shape.shape, f32),
            pltpu.VMEM((out_width, out_width), f32),
            pltpu.VMEM((out_width, out_width), bf16),
            pltpu.VMEM(((tile_rows + 2) * tile_cols, 3 * out_width), bf16),
        ],
        compiler_params=params,
        name="grad_conv",
    )(mine, other, both, in_feat, in_slope, out_feat, out_slope, far_feat, far_slope, turned)
    return own_gram, grad.reshape(tile_rows, tile_cols, in_width)


def solution(mesh):
    return jax.shard_map(
        on_device,
        mesh=mesh,
        in_specs=(P("rows", "cols", None), P(), P(), P(("rows", "cols"), None)),
        out_specs=(P(("rows", "cols"), None), P("rows", "cols", None)),
        check_vma=False,
    )
```
